32 devices in a mesh: dp: 8 (over y, x, core), fsdp: 4 (over z).
Axes of the slice: x: 2, y: 2, z: 4, core: 2. Of those that a mesh axis runs over, the one named last changes fastest.
Arguments:
- frames: bfloat16 [16, 1024, 1024], P('dp', 'fsdp'), may hold values from -6 to 6
- cotangent: bfloat16 [16, 1024, 1024], P('dp', 'fsdp'), may hold values from -6 to 6
- adapter_ids: int32 [16], P('dp'), may hold values from 0 to 7
- norm_gains: float32 [6, 1024], replicated, may hold values from 0.5 to 1.5
- norm_biases: float32 [6, 1024], replicated, may hold values from -1 to 1
- rel_table: bfloat16 [73, 64], replicated, may hold values from -5 to 5
- w_up: bfloat16 [2, 1024, 4096], P(None, ('dp', 'fsdp')), may hold values from -0.1875 to 0.1875
- w_down: bfloat16 [2, 4096, 1024], P(None, ('dp', 'fsdp')), may hold values from -0.09375 to 0.09375
- w_qkv: bfloat16 [1024, 3072], P(('dp', 'fsdp')), may hold values from -0.1875 to 0.1875
- w_out: bfloat16 [1024, 1024], P(('dp', 'fsdp')), may hold values from -0.75 to 0.75
- w_pw1: bfloat16 [1024, 2048], P(('dp', 'fsdp')), may hold values from -0.1875 to 0.1875
- w_depth: bfloat16 [31, 1024], P(None, ('dp', 'fsdp')), may hold values from -1 to 1
- w_pw2: bfloat16 [1024, 1024], P(('dp', 'fsdp')), may hold values from -0.1875 to 0.1875
- ad_a_model: bfloat16 [8, 1024, 128], P(None, 'fsdp'), may hold values from -0.1875 to 0.1875
- ad_a_hidden: bfloat16 [2, 4096, 128], P(None, 'fsdp'), may hold values from -0.09375 to 0.09375
- ad_b_model: bfloat16 [9, 128, 1024], P(None, None, 'fsdp'), may hold values from -1.5 to 1.5
- ad_b_hidden: bfloat16 [2, 128, 4096], P(None, None, 'fsdp'), may hold values from -1.5 to 1.5
Outputs:
- layer_out: bfloat16 [16, 1024, 1024], P('dp', 'fsdp')
- grad_frames: bfloat16 [16, 1024, 1024], P('dp', 'fsdp')
- grad_a_model: float32 [8, 1024, 128], P(None, ('dp', 'fsdp'))
- grad_a_hidden: float32 [2, 4096, 128], P(None, ('dp', 'fsdp'))
- grad_b_model: float32 [9, 128, 1024], P(None, None, ('dp', 'fsdp'))
- grad_b_hidden: float32 [2, 128, 4096], P(None, None, ('dp', 'fsdp'))
The draws below stay inside these ranges and needn't reach their ends.
Inputs may be any that keep to these rules, and one draw needn't show every extreme that they name: `adapter_ids`: each clip's adapter.
All inputs are finite; a program needn't handle non-finite values.
Results may differ from the reference program's by a relative error of at most 0.024.
The reference program's roundings to bfloat16 on the way count: a program that leaves them out, or rounds other values in their place, can miss the bound.
Values may be sent and summed in bfloat16 or wider, within the bound.
No kernel may reach another device: no remote copies, remote signals or barrier semaphores. Data moves between devices by JAX's collectives and lax.ppermute only.
A program may use at most 640 MiB of HBM per device.

```python
import math
import jax
import jax.numpy as jnp
from jax import lax

D = 1024
HEADS = 16
HD = 64
FF = 4096
KERNEL = 31
REL_LEFT = 64
REL_RIGHT = 8
REL = 73
ADAPT = 8
RANK = 16
SLOTS = 128
LEN = 1024
CLIPS = 16


def place_ends(drawn, own_key, smallest, largest):
    longest = drawn.shape.index(max(drawn.shape))
    spots = []
    for shift in (0, 1):
        where = [jax.random.randint(jax.random.fold_in(own_key, axis), (), 0, length) for axis, length in enumerate(drawn.shape)]
        where[longest] = (where[longest] + shift) % drawn.shape[longest]
        spots.append(tuple(where))
    return drawn.at[spots[0]].set(smallest).at[spots[1]].set(largest)


def shard_levels(stream_key, dims, cuts, least, top_value):
    def one(position, blocks):
        steps = jax.random.uniform(jax.random.fold_in(jax.random.fold_in(stream_key, 6), position), (blocks,), jnp.float32, least / len(cuts), top_value / len(cuts))
        return jnp.repeat(jnp.exp(steps), dims[position] // blocks).reshape((-1,) + (1,) * (len(dims) - position - 1))

    factor_of = one(*cuts[0])
    for cut in cuts[1:]:
        factor_of = factor_of * one(*cut)
    return factor_of


def normal_values(key, dims, deviation, most, cuts=(), held_as=jnp.bfloat16):
    entries = jax.random.normal(key, dims, jnp.float32) * deviation
    if len(cuts) > 0:
        entries = shard_levels(key, dims, cuts, -0.22, 0.18) * entries
    return jnp.clip(entries, min=-most, max=most).astype(held_as)


def setup_inputs(seed: int = 0) -> dict:
    arg_keys = jax.random.split(jax.random.key(seed), 18)
    frames = normal_values(arg_keys[0], (CLIPS, LEN, D), 1.0, 6.0, ((0, 8), (1, 4)))
    cotangent = normal_values(arg_keys[1], (CLIPS, LEN, D), 1.0, 6.0, ((0, 8), (1, 4)))
    adapter_ids = place_ends(jax.random.randint(arg_keys[2], (CLIPS,), 0, ADAPT), jax.random.fold_in(arg_keys[2], 1), 0, ADAPT - 1).astype(jnp.int32)
    norm_gains = jnp.clip(1.0 + 0.1 * jax.random.normal(arg_keys[3], (6, D), jnp.float32), 0.5, 1.5)
    norm_biases = normal_values(arg_keys[4], (6, D), 0.2, 1.0, (), jnp.float32)
    rel_table = normal_values(arg_keys[5], (REL, HD), 1.0, 5.0)
    w_up = normal_values(arg_keys[6], (2, D, FF), D ** -0.5, 0.1875, ((1, 32),))
    w_down = normal_values(arg_keys[7], (2, FF, D), FF ** -0.5, 0.09375, ((1, 32),))
    w_qkv = normal_values(arg_keys[8], (D, 3 * D), D ** -0.5, 0.1875, ((0, 32),))
    w_out = normal_values(arg_keys[9], (D, D), (D // 16) ** -0.5, 0.75, ((0, 32),))
    w_pw1 = normal_values(arg_keys[10], (D, 2 * D), D ** -0.5, 0.1875, ((0, 32),))
    w_depth = normal_values(arg_keys[11], (KERNEL, D), KERNEL ** -0.5, 1.0, ((1, 32),))
    w_pw2 = normal_values(arg_keys[12], (D, D), D ** -0.5, 0.1875, ((0, 32),))
    ad_a_model = normal_values(arg_keys[13], (8, D, SLOTS), D ** -0.5, 0.1875, ((1, 4),))
    ad_a_hidden = normal_values(arg_keys[14], (2, FF, SLOTS), FF ** -0.5, 0.09375, ((1, 4),))
    ad_b_model = normal_values(arg_keys[15], (9, SLOTS, D), RANK ** -0.5, 1.5, ((2, 4),))
    ad_b_hidden = normal_values(arg_keys[16], (2, SLOTS, FF), RANK ** -0.5, 1.5, ((2, 4),))
    return {"frames": frames, "cotangent": cotangent, "adapter_ids": adapter_ids, "norm_gains": norm_gains, "norm_biases": norm_biases, "rel_table": rel_table, "w_up": w_up, "w_down": w_down, "w_qkv": w_qkv, "w_out": w_out, "w_pw1": w_pw1, "w_depth": w_depth, "w_pw2": w_pw2, "ad_a_model": ad_a_model, "ad_a_hidden": ad_a_hidden, "ad_b_model": ad_b_model, "ad_b_hidden": ad_b_hidden}


HIGHEST = lax.Precision.HIGHEST
EPSILON = 1e-05

@jax.custom_vjp
def low(v):
    return lax.optimization_barrier(v.astype(jnp.bfloat16)).astype(jnp.float32)

@jax.custom_vjp
def low_back(v):
    return v

def low_keep(v):
    return (low(v), None)

def low_pass(kept, grad):
    return (grad,)

def back_keep(v):
    return (v, None)

def back_low(kept, grad):
    return (low(grad),)
low.defvjp(low_keep, low_pass)
low_back.defvjp(back_keep, back_low)

def layer_norm(field, gain, shift):
    centre = lax.optimization_barrier(jnp.mean(field, -1, keepdims=True))
    centred = field - centre
    spread = lax.optimization_barrier(jnp.mean(centred * centred, -1, keepdims=True))
    return centred * lax.rsqrt(spread + EPSILON) * gain + shift

def project(inputs, weight, a_stack, b_stack, slot_mask):
    slot_acts = jnp.einsum('ni,pie->pne', inputs, a_stack, precision=HIGHEST) * slot_mask
    slot_acts = low(low_back(slot_acts))
    adapted = jnp.einsum('pne,peo->npo', slot_acts, b_stack, precision=HIGHEST)
    frozen_part = jnp.dot(inputs, weight, precision=HIGHEST)
    return low_back(frozen_part + adapted.reshape(frozen_part.shape))

def layer(layer_in, slot_mask, consts, adapters):
    gains, shifts, rel_table, w_up, w_down, w_qkv, w_out, w_pw1, w_depth, w_pw2 = consts
    a_model, a_hidden, b_model, b_hidden = adapters
    scale = 1.0 / math.sqrt(HD)
    first_in = low(layer_norm(layer_in, gains[0], shifts[0]))
    hidden_one = project(first_in, w_up[0], a_model[0:1], b_hidden[0:1], slot_mask)
    act_one = low(jax.nn.silu(hidden_one))
    after_ffn = layer_in + 0.5 * project(act_one, w_down[0], a_hidden[0:1], b_model[0:1], slot_mask)
    attn_in = low(layer_norm(after_ffn, gains[1], shifts[1]))
    joined = project(attn_in, w_qkv, a_model[1:4], b_model[1:4], slot_mask)
    query = low(joined[:, :D]).reshape(LEN, HEADS, HD)
    keys = low(joined[:, D:2 * D]).reshape(LEN, HEADS, HD)
    values = low(joined[:, 2 * D:]).reshape(LEN, HEADS, HD)
    table = jnp.einsum('qhd,rd->hqr', query, rel_table, precision=HIGHEST)
    positions = jnp.arange(LEN, dtype=jnp.int32)
    offsets = jnp.clip(positions[None, :] - positions[:, None], -REL_LEFT, REL_RIGHT) + REL_LEFT
    spots = jnp.broadcast_to(offsets[None], (HEADS, LEN, LEN))
    near = jnp.take_along_axis(table, spots, axis=2)
    plain = jnp.einsum('qhd,khd->hqk', query, keys, precision=HIGHEST)
    scores = low_back((plain + near) * scale)
    probs = low(jax.nn.softmax(scores, axis=-1))
    attended = low(low_back(jnp.einsum('hqk,khd->qhd', probs, values, precision=HIGHEST))).reshape(LEN, D)
    after_attn = after_ffn + project(attended, w_out, a_model[4:5], b_model[4:5], slot_mask)
    conv_in = low(layer_norm(after_attn, gains[2], shifts[2]))
    b_glu = jnp.concatenate([b_model[7], b_model[8]], axis=1)[None]
    gated = project(conv_in, w_pw1, a_model[5:6], b_glu, slot_mask)
    gated_val = low(gated[:, :D] * jax.nn.sigmoid(gated[:, D:]))
    padded = jnp.concatenate([jnp.zeros((KERNEL - 1, D), jnp.float32), gated_val], axis=0)
    conv_out = padded[0:LEN] * w_depth[0]
    for tap_index in range(1, KERNEL):
        conv_out = conv_out + padded[tap_index:tap_index + LEN] * w_depth[tap_index]
    conv_act = low(jax.nn.silu(layer_norm(conv_out, gains[3], shifts[3])))
    after_conv = after_attn + project(conv_act, w_pw2, a_model[6:7], b_model[5:6], slot_mask)
    second_in = low(layer_norm(after_conv, gains[4], shifts[4]))
    hidden_two = project(second_in, w_up[1], a_model[7:8], b_hidden[1:2], slot_mask)
    act_two = low(jax.nn.silu(hidden_two))
    after_second = after_conv + 0.5 * project(act_two, w_down[1], a_hidden[1:2], b_model[6:7], slot_mask)
    return layer_norm(after_second, gains[5], shifts[5])

def reference(frames, cotangent, adapter_ids, norm_gains, norm_biases, rel_table, w_up, w_down, w_qkv, w_out, w_pw1, w_depth, w_pw2, ad_a_model, ad_a_hidden, ad_b_model, ad_b_hidden):
    consts = tuple((item.astype(jnp.float32) for item in (norm_gains, norm_biases, rel_table, w_up, w_down, w_qkv, w_out, w_pw1, w_depth, w_pw2)))
    adapters = tuple((item.astype(jnp.float32) for item in (ad_a_model, ad_a_hidden, ad_b_model, ad_b_hidden)))
    slot_owner = jnp.arange(ADAPT * RANK, dtype=jnp.int32) // RANK

    def step(totals, item):
        clip_in, clip_cot, ident = item
        slot_mask = (slot_owner == ident).astype(jnp.float32)
        result, back = jax.vjp(lambda field, params: layer(field, slot_mask, consts, params), clip_in.astype(jnp.float32), adapters)
        d_clip, d_params = back(clip_cot.astype(jnp.float32))
        totals = tuple((total + part for total, part in zip(totals, d_params)))
        return (totals, (result.astype(jnp.bfloat16), d_clip.astype(jnp.bfloat16)))
    zeros = tuple((jnp.zeros(item.shape, jnp.float32) for item in adapters))
    totals, (layer_out, grad_frames) = lax.scan(step, zeros, (frames, cotangent, adapter_ids))
    return (layer_out, grad_frames, totals[0], totals[1], totals[2], totals[3])
```

```python
import functools
import math

import jax
import jax.numpy as jnp
from jax import lax
from jax.experimental import pallas as pl
from jax.experimental.pallas import tpu as pltpu
from jax.sharding import Mesh
from jax.sharding import PartitionSpec as P

HEADS = 16
KERNEL = 31
RANK = 16
EPSILON = 1e-05
EVERYWHERE = ("chip", "core", "fz", "fh")

HD = 64
REL_LEFT = 64
REL_RIGHT = 8
TILE = 128
WIDE = 4 * TILE
BAND = 3 * TILE
VMEM = 48 * 1024 * 1024


def dot_nn(a, b):
    return lax.dot_general(a, b, (((1,), (0,)), ((), ())), preferred_element_type=jnp.float32)


def dot_nt(a, b):
    return lax.dot_general(a, b, (((1,), (1,)), ((), ())), preferred_element_type=jnp.float32)


def chunk_plan(tile, chunks):
    return [{chunks - 1: 0, 0: 1, 1: 2}.get((c - tile) % chunks) for c in range(chunks)]


def far_left(c, tile, chunks, own):
    return jnp.logical_or(c + own >= chunks, c < tile)


def wrapped_band(c, tile, chunks, own):
    if tile == 0 and c == chunks - 1:
        return own > 0
    if c == tile + 1:
        return c + own < chunks
    return None


def tile_scores(q_head, keys, rel_wide, tile, own):
    scores = dot_nt(q_head, keys)
    wide = dot_nt(q_head, rel_wide)
    band = pltpu.roll(wide, BAND, 1, stride=1, stride_axis=0)[:, :BAND]
    first, last = wide[:, 0:1], wide[:, WIDE - 1 : WIDE]
    chunks = scores.shape[1] // TILE
    parts = []
    for c, spot in enumerate(chunk_plan(tile, chunks)):
        part = scores[:, c * TILE : (c + 1) * TILE]
        if spot is None:
            part = part + jnp.where(far_left(c, tile, chunks, own), first, last)
        else:
            bias = band[:, spot * TILE : (spot + 1) * TILE]
            near = wrapped_band(c, tile, chunks, own)
            if near is not None:
                bias = jnp.where(near, bias, jnp.where(far_left(c, tile, chunks, own), first, last))
            part = part + bias
        parts.append(part)
    return parts


def attn_fwd_kernel(own_ref, q_ref, k_ref, v_ref, rel_ref, o_ref, lse_ref):
    own = own_ref[0]
    keys, values, rel_wide = k_ref[...], v_ref[...], rel_ref[...]
    low_lanes = lax.broadcasted_iota(jnp.int32, (TILE, 2 * HD), 1) < HD
    for tile in range(q_ref.shape[0] // TILE):
        rows = slice(tile * TILE, (tile + 1) * TILE)
        q_pair = q_ref[rows, :] * jnp.bfloat16(0.125)
        outs = []
        for lanes in (low_lanes, jnp.logical_not(low_lanes)):
            q_head = jnp.where(lanes, q_pair, jnp.zeros_like(q_pair))
            parts = tile_scores(q_head, keys, rel_wide, tile, own)
            top = functools.reduce(jnp.maximum, parts)
            top = jnp.max(top, axis=1, keepdims=True)
            expo = [jnp.exp(part - top) for part in parts]
            total = jnp.sum(functools.reduce(jnp.add, expo), axis=1, keepdims=True)
            expo_low = jnp.concatenate([e.astype(jnp.bfloat16) for e in expo], axis=1)
            outs.append((dot_nn(expo_low, values) / total, top + jnp.log(total)))
        o_ref[rows, :] = jnp.where(low_lanes, outs[0][0], outs[1][0]).astype(jnp.bfloat16)
        lse_ref[rows, :] = jnp.where(low_lanes, outs[0][1], outs[1][1])


def attn_bwd_kernel(
    own_ref, q_ref, k_ref, v_ref, do_ref, lse_ref, rel_ref, rev_ref, flip_ref,
    dq_ref, dk_own_ref, dv_own_ref, dk_far_ref, dv_far_ref, ds_ref, p_ref,
):
    own = own_ref[0]
    keys, values, rel_wide = k_ref[...], v_ref[...], rel_ref[...]
    rows_n, keys_n = q_ref.shape[0], k_ref.shape[0]
    chunks = keys_n // TILE
    low_lanes = lax.broadcasted_iota(jnp.int32, (TILE, 2 * HD), 1) < HD
    lane = lax.broadcasted_iota(jnp.int32, (TILE, TILE), 1)
    for tile in range(rows_n // TILE):
        rows = slice(tile * TILE, (tile + 1) * TILE)
        q_pair = q_ref[rows, :] * jnp.bfloat16(0.125)
        do_pair = do_ref[rows, :]
        plan = chunk_plan(tile, chunks)
        marks = []
        for c, spot in enumerate(plan):
            left = far_left(c, tile, chunks, own)
            lane_on = jnp.where(left, 0, 1)
            if spot is not None:
                near = wrapped_band(c, tile, chunks, own)
                lane_on = jnp.int32(-1) if near is None else jnp.where(near, -1, lane_on)
            marks.append(jnp.where(lane == lane_on, 1.0, 0.0).astype(jnp.bfloat16))
        keys_marked = jnp.concatenate([keys, jnp.concatenate(marks, axis=0)], axis=1)
        dqs = []
        for head, lanes in enumerate((low_lanes, jnp.logical_not(low_lanes))):
            q_head = jnp.where(lanes, q_pair, jnp.zeros_like(q_pair))
            do_head = jnp.where(lanes, do_pair, jnp.zeros_like(do_pair))
            log_total = lse_ref[rows, head * HD : head * HD + 1]
            parts = tile_scores(q_head, keys, rel_wide, tile, own)
            d_probs = dot_nt(do_head, values)
            probs = [jnp.exp(part - log_total) for part in parts]
            d_parts = [d_probs[:, c * TILE : (c + 1) * TILE] for c in range(chunks)]
            inner = functools.reduce(jnp.add, [p * d for p, d in zip(probs, d_parts)])
            inner = jnp.sum(inner, axis=1, keepdims=True)
            d_scores = [(p * (d - inner)).astype(jnp.bfloat16) for p, d in zip(probs, d_parts)]
            p_ref[head, rows, :] = jnp.concatenate([p.astype(jnp.bfloat16) for p in probs], axis=1)
            joined = jnp.concatenate(d_scores, axis=1)
            ds_ref[head, rows, :] = joined
            band = [None, None, None]
            for c, spot in enumerate(plan):
                if spot is not None:
                    near = wrapped_band(c, tile, chunks, own)
                    piece = d_scores[c]
                    if near is not None:
                        piece = jnp.where(near, piece, jnp.zeros_like(piece))
                    band[spot] = piece
            turned = dot_nn(jnp.concatenate(band, axis=1), flip_ref[...])
            turned = pltpu.roll(turned, BAND, 1, stride=1, stride_axis=0).astype(jnp.bfloat16)
            marked = dot_nn(joined, keys_marked)
            d_query = marked[:, :TILE] + dot_nn(turned, rev_ref[...])
            d_query = d_query + marked[:, TILE : TILE + 1] * rel_wide[0:1, :].astype(jnp.float32)
            d_query = d_query + marked[:, TILE + 1 : TILE + 2] * rel_wide[WIDE - 1 : WIDE, :].astype(jnp.float32)
            dqs.append(d_query * 0.125)
        dq_ref[rows, :] = jnp.where(low_lanes, dqs[0], dqs[1]).astype(dq_ref.dtype)
    q_turned = jnp.transpose(q_ref[...] * jnp.bfloat16(0.125))
    do_turned = jnp.transpose(do_ref[...])
    for turned, kept, own_out, far_out in (
        (q_turned, ds_ref, dk_own_ref, dk_far_ref),
        (do_turned, p_ref, dv_own_ref, dv_far_ref),
    ):
        both = jnp.concatenate(
            [dot_nn(turned[head * HD : (head + 1) * HD, :], kept[head]) for head in range(2)], axis=0
        )
        both = jnp.transpose(both)
        own_out[...] = both[:rows_n]
        far_out[...] = both[rows_n:].astype(far_out.dtype)


def rel_tables(rel_table):
    places = jnp.clip(jnp.arange(WIDE, dtype=jnp.int32) - WIDE // 2, -REL_LEFT, REL_RIGHT) + REL_LEFT
    table_rows = jnp.arange(rel_table.shape[0], dtype=jnp.int32)
    picker = (places[:, None] == table_rows[None, :]).astype(jnp.bfloat16)
    wide = jnp.dot(picker, rel_table, preferred_element_type=jnp.float32).astype(jnp.bfloat16)
    wide = jnp.concatenate([wide, wide], axis=1)
    flip = jnp.arange(BAND)[:, None] + jnp.arange(WIDE)[None, :] == WIDE - 1
    return wide, wide[::-1], flip.astype(jnp.bfloat16)


def attention_forward(own, query, keys, values, rel_wide):
    rows, width = query.shape
    keys_n = keys.shape[0]
    pair = 2 * HD
    cost = pl.CostEstimate(flops=6 * rows * keys_n * width, bytes_accessed=8 * keys_n * width, transcendentals=0)
    return pl.pallas_call(
        attn_fwd_kernel,
        grid=(width // pair,),
        in_specs=[
            pl.BlockSpec(memory_space=pltpu.SMEM),
            pl.BlockSpec((rows, pair), lambda h: (0, h)),
            pl.BlockSpec((keys_n, pair), lambda h: (0, h)),
            pl.BlockSpec((keys_n, pair), lambda h: (0, h)),
            pl.BlockSpec((WIDE, pair), lambda h: (0, 0)),
        ],
        out_specs=[pl.BlockSpec((rows, pair), lambda h: (0, h))] * 2,
        out_shape=[
            jax.ShapeDtypeStruct((rows, width), jnp.bfloat16),
            jax.ShapeDtypeStruct((rows, width), jnp.float32),
        ],
        compiler_params=pltpu.CompilerParams(vmem_limit_bytes=VMEM),
        cost_estimate=cost,
        name="attention_forward",
    )(own, query, keys, values, rel_wide)


def attention_backward(own, query, keys, values, d_out, log_total, tables):
    rows, width = query.shape
    keys_n = keys.shape[0]
    pair = 2 * HD
    far = keys_n - rows
    row_block = pl.BlockSpec((rows, pair), lambda h: (0, h))
    key_block = pl.BlockSpec((keys_n, pair), lambda h: (0, h))
    far_block = pl.BlockSpec((far, pair), lambda h: (0, h))
    cost = pl.CostEstimate(flops=14 * rows * keys_n * width, bytes_accessed=16 * keys_n * width, transcendentals=0)
    return pl.pallas_call(
        attn_bwd_kernel,
        grid=(width // pair,),
        in_specs=[
            pl.BlockSpec(memory_space=pltpu.SMEM),
            row_block, key_block, key_block, row_block, row_block,
            pl.BlockSpec((WIDE, pair), lambda h: (0, 0)),
            pl.BlockSpec((WIDE, pair), lambda h: (0, 0)),
            pl.BlockSpec((BAND, WIDE), lambda h: (0, 0)),
        ],
        out_specs=[row_block, row_block, row_block, far_block, far_block],
        out_shape=[
            jax.ShapeDtypeStruct((rows, width), jnp.bfloat16),
            jax.ShapeDtypeStruct((rows, width), jnp.float32),
            jax.ShapeDtypeStruct((rows, width), jnp.float32),
            jax.ShapeDtypeStruct((far, width), jnp.bfloat16),
            jax.ShapeDtypeStruct((far, width), jnp.bfloat16),
        ],
        scratch_shapes=[
            pltpu.VMEM((2, rows, keys_n), jnp.bfloat16),
            pltpu.VMEM((2, rows, keys_n), jnp.bfloat16),
        ],
        compiler_params=pltpu.CompilerParams(vmem_limit_bytes=VMEM),
        cost_estimate=cost,
        name="attention_backward",
    )(own, query, keys, values, d_out, log_total, *tables)


def layer_norm(field, gain, shift):
    centre = jnp.mean(field, -1, keepdims=True)
    centred = field - centre
    spread = jnp.mean(centred * centred, -1, keepdims=True)
    return centred * lax.rsqrt(spread + EPSILON) * gain + shift


def glu_gate(joined):
    half_width = joined.shape[1] // 2
    return joined[:, :half_width] * jax.nn.sigmoid(joined[:, half_width:])


def dot_tn(a, b):
    return lax.dot_general(a, b, (((0,), (0,)), ((), ())), preferred_element_type=jnp.float32)


def project_fwd(inputs, weight, down, up):
    slot_acts = dot_nt(inputs, down).astype(jnp.bfloat16)
    return dot_nn(inputs, weight) + dot_nn(slot_acts, up), slot_acts


def project_bwd(grad, inputs, slot_acts, weight, down, up):
    grad_low = grad.astype(jnp.bfloat16)
    d_slots = dot_nt(grad_low, up).astype(jnp.bfloat16)
    d_inputs = dot_nt(grad_low, weight) + dot_nn(d_slots, down)
    return d_inputs, dot_tn(d_slots, inputs), dot_tn(slot_acts, grad_low)


class Layout:
    def __init__(self, together, fsdp):
        self.fsdp = fsdp
        self.inner = fsdp // together
        self.group = 2 * self.inner

    def place(self, core, f):
        return core * self.fsdp + f

    def round_route(self, turn):
        route = []
        for core in range(2):
            for f in range(self.fsdp):
                clip = (f % 2 + turn) % 2
                spot = f // 2
                target = self.place(spot % 2, (2 * core + clip) * self.inner + spot // 2)
                route.append((self.place(core, f), target))
        return route

    def gather_rows(self, blocks):
        parity = (lax.axis_index("fz") * self.inner + lax.axis_index("fh")) % 2
        clip = lax.axis_index("fz") % 2
        got = []
        for turn in range(2):
            sent = lax.dynamic_index_in_dim(blocks, (parity + turn) % 2, 0, keepdims=False)
            got.append(lax.ppermute(sent, ("core", "fz", "fh"), self.round_route(turn)))
        swap = clip == 1
        return jnp.concatenate(
            [jnp.where(swap, got[1], got[0]), jnp.where(swap, got[0], got[1])], axis=0
        )

    def scatter_rows(self, rows):
        parity = (lax.axis_index("fz") * self.inner + lax.axis_index("fh")) % 2
        clip = lax.axis_index("fz") % 2
        halves = rows.reshape(2, rows.shape[0] // 2, rows.shape[1])
        got = []
        for turn in range(2):
            sent = lax.dynamic_index_in_dim(halves, (clip + turn) % 2, 0, keepdims=False)
            route = [(target, source) for source, target in self.round_route(turn)]
            got.append(lax.ppermute(sent, ("core", "fz", "fh"), route))
        swap = parity == 1
        return jnp.stack([jnp.where(swap, got[1], got[0]), jnp.where(swap, got[0], got[1])])

    def spot_index(self, spot):
        return (spot % 2) * self.inner + spot // 2

    def from_spot(self, block, distance, cyclic):
        route = []
        for spot in range(self.group):
            source = spot + distance
            if cyclic:
                source %= self.group
            if 0 <= source < self.group:
                route.append((self.spot_index(source), self.spot_index(spot)))
        return lax.ppermute(block, ("core", "fh"), route)


def pick_adapters(layout, ids, a_model, a_hidden, b_model, b_hidden):
    slots = a_model.shape[2]
    wanted = ids[:, None] * RANK + jnp.arange(RANK, dtype=jnp.int32)[None, :]
    picker = (wanted[:, :, None] == jnp.arange(slots, dtype=jnp.int32)).astype(jnp.bfloat16)
    down = lambda a: jnp.einsum("jrs,pks->jprk", picker, a, preferred_element_type=jnp.float32)
    up = lambda b: jnp.einsum("jrs,psn->jprn", picker, b, preferred_element_type=jnp.float32)
    packs = (
        jnp.concatenate([down(a_model), up(b_model)], axis=1).astype(jnp.bfloat16),
        jnp.concatenate([down(a_hidden), up(b_hidden)], axis=1).astype(jnp.bfloat16),
    )
    count = layout.fsdp
    here = lax.axis_index("fz") * layout.inner + lax.axis_index("fh")
    whole = []
    for pack in packs:
        span = pack.shape[3]
        full = jnp.zeros(pack.shape[1:3] + (span * count,), jnp.bfloat16)
        for step in range(count):
            target = (here + step) % count
            piece = lax.dynamic_index_in_dim(pack, target // layout.inner, 0, keepdims=False)
            if step:
                route = [(f, (f + step) % count) for f in range(count)]
                piece = lax.ppermute(piece, ("fz", "fh"), route)
            source = (here - step) % count
            full = lax.dynamic_update_slice(full, piece, (0, 0, source * span))
        whole.append(full)
    models = a_model.shape[0]
    return whole[0][:models], whole[1][:2], whole[0][models:], whole[1][2:]


def send_grads(grads):
    devices = lax.axis_size(EVERYWHERE)
    packed = []
    for grad in grads:
        count, rank, features = grad.shape
        cut = grad.astype(jnp.bfloat16).reshape(count * rank, devices, features // devices)
        packed.append(jnp.transpose(cut, (1, 0, 2)).reshape(devices, -1))
    got = lax.all_to_all(jnp.concatenate(packed, axis=1), EVERYWHERE, 0, 0, tiled=True)
    parts = []
    begin = 0
    for grad, pack in zip(grads, packed):
        count, rank, features = grad.shape
        size = pack.shape[1]
        part = got[:, begin : begin + size].reshape(devices, count, rank, features // devices)
        parts.append(part)
        begin += size
    return parts


def local(
    frames,
    cotangent,
    adapter_ids,
    norm_gains,
    norm_biases,
    rel_table,
    w_up,
    w_down,
    w_qkv,
    w_out,
    w_pw1,
    w_depth,
    w_pw2,
    ad_a_model,
    ad_a_hidden,
    ad_b_model,
    ad_b_hidden,
):
    group_clips, frame_span, width = frames.shape
    together = 2 * group_clips
    layout = Layout(together, lax.axis_size("fz") * lax.axis_size("fh"))
    rows = 2 * frame_span
    slots = ad_a_model.shape[2]
    spot = lax.axis_index("fh") * 2 + lax.axis_index("core")
    own = (spot * (rows // TILE)).astype(jnp.int32).reshape(1)
    other_ids = lax.ppermute(adapter_ids, "core", [(0, 1), (1, 0)])
    at_zero = lax.axis_index("core") == 0
    near_ids = jnp.concatenate(
        [jnp.where(at_zero, adapter_ids, other_ids), jnp.where(at_zero, other_ids, adapter_ids)]
    )
    all_ids = lax.all_gather(adapter_ids, ("chip", "core"), axis=0, tiled=True)
    layer_in = layout.gather_rows(frames).astype(jnp.float32)
    a_model, a_hidden, b_model, b_hidden = pick_adapters(
        layout, near_ids, ad_a_model, ad_a_hidden, ad_b_model, ad_b_hidden
    )
    up0_w = lax.all_gather(w_up[0], EVERYWHERE, axis=0, tiled=True)
    down0_w = lax.all_gather(w_down[0], EVERYWHERE, axis=0, tiled=True)
    qkv_w = lax.all_gather(w_qkv, EVERYWHERE, axis=0, tiled=True)
    out_w = lax.all_gather(w_out, EVERYWHERE, axis=0, tiled=True)
    pw1_w = lax.all_gather(w_pw1, EVERYWHERE, axis=0, tiled=True)
    depth_w = lax.all_gather(w_depth, EVERYWHERE, axis=1, tiled=True)
    pw2_w = lax.all_gather(w_pw2, EVERYWHERE, axis=0, tiled=True)
    up1_w = lax.all_gather(w_up[1], EVERYWHERE, axis=0, tiled=True)
    down1_w = lax.all_gather(w_down[1], EVERYWHERE, axis=0, tiled=True)
    depth = depth_w.astype(jnp.float32)
    tables = rel_tables(rel_table)
    blank = jnp.zeros((RANK, width), jnp.bfloat16)
    qkv_down = a_model[1:4].reshape(3 * RANK, width)
    qkv_up = jnp.concatenate(
        [
            jnp.concatenate([b_model[1], blank, blank], axis=1),
            jnp.concatenate([blank, b_model[2], blank], axis=1),
            jnp.concatenate([blank, blank, b_model[3]], axis=1),
        ]
    )
    glu_up = jnp.concatenate([b_model[7], b_model[8]], axis=1)

    def norm_of(index):
        return lambda field: layer_norm(field, norm_gains[index], norm_biases[index])

    normed, back_norm_zero = jax.vjp(norm_of(0), layer_in)
    first_in = normed.astype(jnp.bfloat16)
    hidden_one, slots_up_one = project_fwd(first_in, up0_w, a_model[0], b_hidden[0])
    act_one, back_silu_one = jax.vjp(jax.nn.silu, hidden_one)
    act_one = act_one.astype(jnp.bfloat16)
    ffn_one, slots_down_one = project_fwd(act_one, down0_w, a_hidden[0], b_model[0])
    after_ffn = layer_in + 0.5 * ffn_one
    normed, back_norm_one = jax.vjp(norm_of(1), after_ffn)
    attn_in = normed.astype(jnp.bfloat16)
    joined, slots_qkv = project_fwd(attn_in, qkv_w, qkv_down, qkv_up)
    joined = joined.astype(jnp.bfloat16)
    query, own_kv = joined[:, :width], joined[:, width:]
    kv = jnp.concatenate(
        [own_kv] + [layout.from_spot(own_kv, step, True) for step in range(1, layout.group)], axis=0
    )
    keys, values = kv[:, :width], kv[:, width:]
    mixed, log_total = attention_forward(own, query, keys, values, tables[0])
    attn_out, slots_out = project_fwd(mixed, out_w, a_model[4], b_model[4])
    after_attn = after_ffn + attn_out
    normed, back_norm_two = jax.vjp(norm_of(2), after_attn)
    conv_in = normed.astype(jnp.bfloat16)
    gated, slots_glu = project_fwd(conv_in, pw1_w, a_model[5], glu_up)
    gated_val, back_glu = jax.vjp(glu_gate, gated)
    gated_low = gated_val.astype(jnp.bfloat16)
    earlier = layout.from_spot(gated_low[rows - KERNEL + 1 :], -1, False)
    extended = jnp.concatenate([earlier, gated_low], axis=0).astype(jnp.float32)
    conv_out = extended[0:rows] * depth[0]
    for tap_index in range(1, KERNEL):
        conv_out = conv_out + extended[tap_index : tap_index + rows] * depth[tap_index]
    conv_act, back_conv_norm = jax.vjp(
        lambda field: jax.nn.silu(layer_norm(field, norm_gains[3], norm_biases[3])), conv_out
    )
    conv_act = conv_act.astype(jnp.bfloat16)
    conv_proj, slots_pw2 = project_fwd(conv_act, pw2_w, a_model[6], b_model[5])
    after_conv = after_attn + conv_proj
    normed, back_norm_four = jax.vjp(norm_of(4), after_conv)
    second_in = normed.astype(jnp.bfloat16)
    hidden_two, slots_up_two = project_fwd(second_in, up1_w, a_model[7], b_hidden[1])
    act_two, back_silu_two = jax.vjp(jax.nn.silu, hidden_two)
    act_two = act_two.astype(jnp.bfloat16)
    ffn_two, slots_down_two = project_fwd(act_two, down1_w, a_hidden[1], b_model[6])
    after_second = after_conv + 0.5 * ffn_two
    result, back_final = jax.vjp(norm_of(5), after_second)
    layer_out = layout.scatter_rows(result.astype(jnp.bfloat16))

    d_out = layout.gather_rows(cotangent).astype(jnp.float32)
    (d_fourth,) = back_final(d_out)
    d_act, da_down1, db_down1 = project_bwd(
        0.5 * d_fourth, act_two, slots_down_two, down1_w, a_hidden[1], b_model[6]
    )
    (d_hidden,) = back_silu_two(d_act)
    d_inputs, da_up1, db_up1 = project_bwd(
        d_hidden, second_in, slots_up_two, up1_w, a_model[7], b_hidden[1]
    )
    (d_normed,) = back_norm_four(d_inputs)
    d_third = d_fourth + d_normed
    d_inputs, da_pw2, db_pw2 = project_bwd(
        d_third, conv_act, slots_pw2, pw2_w, a_model[6], b_model[5]
    )
    (d_conv,) = back_conv_norm(d_inputs)
    later = layout.from_spot(d_conv[: KERNEL - 1].astype(jnp.bfloat16), 1, False)
    extended_grad = jnp.concatenate([d_conv, later.astype(jnp.float32)], axis=0)
    d_gated = extended_grad[KERNEL - 1 : KERNEL - 1 + rows] * depth[0]
    for tap_index in range(1, KERNEL):
        begin = KERNEL - 1 - tap_index
        d_gated = d_gated + extended_grad[begin : begin + rows] * depth[tap_index]
    (d_joined,) = back_glu(d_gated)
    d_inputs, da_pw1, db_pw1 = project_bwd(d_joined, conv_in, slots_glu, pw1_w, a_model[5], glu_up)
    (d_normed,) = back_norm_two(d_inputs)
    d_second = d_third + d_normed
    d_mixed, da_out, db_out = project_bwd(
        d_second, mixed, slots_out, out_w, a_model[4], b_model[4]
    )
    d_query, dk_own, dv_own, dk_far, dv_far = attention_backward(
        own, query, keys, values, d_mixed.astype(jnp.bfloat16), log_total, tables
    )
    for step in range(1, layout.group):
        part = slice((step - 1) * rows, step * rows)
        dk_own = dk_own + layout.from_spot(dk_far[part], -step, True).astype(jnp.float32)
        dv_own = dv_own + layout.from_spot(dv_far[part], -step, True).astype(jnp.float32)
    d_joined = jnp.concatenate(
        [d_query, dk_own.astype(jnp.bfloat16), dv_own.astype(jnp.bfloat16)], axis=1
    )
    d_inputs, da_qkv, db_qkv = project_bwd(d_joined, attn_in, slots_qkv, qkv_w, qkv_down, qkv_up)
    (d_normed,) = back_norm_one(d_inputs)
    d_first = d_second + d_normed
    d_act, da_down0, db_down0 = project_bwd(
        0.5 * d_first, act_one, slots_down_one, down0_w, a_hidden[0], b_model[0]
    )
    (d_hidden,) = back_silu_one(d_act)
    d_inputs, da_up0, db_up0 = project_bwd(
        d_hidden, first_in, slots_up_one, up0_w, a_model[0], b_hidden[0]
    )
    (d_normed,) = back_norm_zero(d_inputs)
    grad_frames = layout.scatter_rows((d_first + d_normed).astype(jnp.bfloat16))

    da_qkv = da_qkv.reshape(3, RANK, width)
    db_qkv = [
        db_qkv[index * RANK : (index + 1) * RANK, index * width : (index + 1) * width]
        for index in range(3)
    ]
    grads = (
        jnp.concatenate([da_up0[None], da_qkv, jnp.stack([da_out, da_pw1, da_pw2, da_up1])]),
        jnp.stack([da_down0, da_down1]),
        jnp.stack(
            [db_down0, *db_qkv, db_out, db_pw2, db_down1, db_pw1[:, :width], db_pw1[:, width:]]
        ),
        jnp.stack([db_up0, db_up1]),
    )
    parts = send_grads(grads)
    chips = lax.axis_size("chip")
    clip_ids = all_ids.reshape(chips, 1, together, 1)
    clip_ids = jnp.broadcast_to(clip_ids, (chips, 2, together, layout.inner)).reshape(-1)
    wanted = clip_ids[:, None] * RANK + jnp.arange(RANK, dtype=jnp.int32)[None, :]
    picker = (wanted[:, :, None] == jnp.arange(slots, dtype=jnp.int32)).astype(jnp.bfloat16)
    sums = [
        jnp.einsum(form, part, picker, preferred_element_type=jnp.float32)
        for form, part in zip(("dprk,drs->pks", "dprk,drs->pks", "dprk,drs->psk", "dprk,drs->psk"), parts)
    ]
    return (layer_out, grad_frames, *sums)


def solution(mesh):
    every = ("chip", "core", "fz", "fh")
    clips, spread = ("chip", "core"), ("fz", "fh")
    in_specs = (
        P(clips, spread, None),
        P(clips, spread, None),
        P(clips),
        P(),
        P(),
        P(),
        P(None, every, None),
        P(None, every, None),
        P(every, None),
        P(every, None),
        P(every, None),
        P(None, every),
        P(every, None),
        P(None, spread, None),
        P(None, spread, None),
        P(None, None, spread),
        P(None, None, spread),
    )
    out_specs = (
        P(clips, spread, None),
        P(clips, spread, None),
        P(None, every, None),
        P(None, every, None),
        P(None, None, every),
        P(None, None, every),
    )

    def run(frames, *rest):
        dp, fsdp = mesh.shape["dp"], mesh.shape["fsdp"]
        together = 2 * frames.shape[0] // dp
        cut = Mesh(
            mesh.devices.reshape(dp // 2, 2, together, fsdp // together), EVERYWHERE
        )
        return jax.shard_map(
            local, mesh=cut, in_specs=in_specs, out_specs=out_specs, check_vma=False
        )(frames, *rest)

    return run
```

```python
import functools
import math

import jax
import jax.numpy as jnp
from jax import lax
from jax.experimental import pallas as pl
from jax.experimental.pallas import tpu as pltpu
from jax.sharding import Mesh
from jax.sharding import PartitionSpec as P

HEADS = 16
KERNEL = 31
RANK = 16
EPSILON = 1e-05
EVERYWHERE = ("chip", "core", "fz", "fh")

HD = 64
REL_LEFT = 64
REL_RIGHT = 8
TILE = 128
WIDE = 4 * TILE
BAND = 3 * TILE
VMEM = 32 * 1024 * 1024


def dot_nn(a, b):
    return lax.dot_general(a, b, (((1,), (0,)), ((), ())), preferred_element_type=jnp.float32)


def dot_nt(a, b):
    return lax.dot_general(a, b, (((1,), (1,)), ((), ())), preferred_element_type=jnp.float32)


def chunk_plan(tile, chunks):
    return [{chunks - 1: 0, 0: 1, 1: 2}.get((c - tile) % chunks) for c in range(chunks)]


def far_left(c, tile, chunks, own):
    return jnp.logical_or(c + own >= chunks, c < tile)


def wrapped_band(c, tile, chunks, own):
    if tile == 0 and c == chunks - 1:
        return own > 0
    if c == tile + 1:
        return c + own < chunks
    return None


def tile_scores(q_head, keys, rel_wide, tile, own):
    scores = dot_nt(q_head, keys)
    wide = dot_nt(q_head, rel_wide)
    band = pltpu.roll(wide, BAND, 1, stride=1, stride_axis=0)[:, :BAND]
    first, last = wide[:, 0:1], wide[:, WIDE - 1 : WIDE]
    chunks = scores.shape[1] // TILE
    parts = []
    for c, spot in enumerate(chunk_plan(tile, chunks)):
        part = scores[:, c * TILE : (c + 1) * TILE]
        if spot is None:
            part = part + jnp.where(far_left(c, tile, chunks, own), first, last)
        else:
            bias = band[:, spot * TILE : (spot + 1) * TILE]
            near = wrapped_band(c, tile, chunks, own)
            if near is not None:
                bias = jnp.where(near, bias, jnp.where(far_left(c, tile, chunks, own), first, last))
            part = part + bias
        parts.append(part)
    return parts


def stacked(refs):
    return jnp.concatenate([ref[...] for ref in refs], axis=0)


def attn_fwd_kernel(group, own_ref, q_ref, rel_ref, *refs):
    own = own_ref[0]
    keys, values, rel_wide = stacked(refs[:group]), stacked(refs[group : 2 * group]), rel_ref[...]
    o_ref, lse_ref = refs[2 * group :]
    low_lanes = lax.broadcasted_iota(jnp.int32, (TILE, 2 * HD), 1) < HD
    for tile in range(q_ref.shape[0] // TILE):
        rows = slice(tile * TILE, (tile + 1) * TILE)
        q_pair = q_ref[rows, :] * jnp.bfloat16(0.125)
        outs = []
        for lanes in (low_lanes, jnp.logical_not(low_lanes)):
            q_head = jnp.where(lanes, q_pair, jnp.zeros_like(q_pair))
            parts = tile_scores(q_head, keys, rel_wide, tile, own)
            top = functools.reduce(jnp.maximum, parts)
            top = jnp.max(top, axis=1, keepdims=True)
            expo = [jnp.exp(part - top) for part in parts]
            total = jnp.sum(functools.reduce(jnp.add, expo), axis=1, keepdims=True)
            expo_low = jnp.concatenate([e.astype(jnp.bfloat16) for e in expo], axis=1)
            outs.append((dot_nn(expo_low, values) / total, top + jnp.log(total)))
        o_ref[rows, :] = jnp.where(low_lanes, outs[0][0], outs[1][0]).astype(jnp.bfloat16)
        lse_ref[rows, :] = jnp.where(low_lanes, outs[0][1], outs[1][1])


def attn_bwd_kernel(group, own_ref, q_ref, do_ref, lse_ref, rel_ref, rev_ref, flip_ref, *refs):
    own = own_ref[0]
    keys, values, rel_wide = stacked(refs[:group]), stacked(refs[group : 2 * group]), rel_ref[...]
    dq_ref, own_out, far_out, ds_ref, p_ref = refs[2 * group :]
    rows_n, keys_n = q_ref.shape[0], keys.shape[0]
    chunks = keys_n // TILE
    low_lanes = lax.broadcasted_iota(jnp.int32, (TILE, 2 * HD), 1) < HD
    lane = lax.broadcasted_iota(jnp.int32, (TILE, TILE), 1)
    for tile in range(rows_n // TILE):
        rows = slice(tile * TILE, (tile + 1) * TILE)
        q_pair = q_ref[rows, :] * jnp.bfloat16(0.125)
        do_pair = do_ref[rows, :]
        plan = chunk_plan(tile, chunks)
        marks = []
        for c, spot in enumerate(plan):
            left = far_left(c, tile, chunks, own)
            lane_on = jnp.where(left, 0, 1)
            if spot is not None:
                near = wrapped_band(c, tile, chunks, own)
                lane_on = jnp.int32(-1) if near is None else jnp.where(near, -1, lane_on)
            marks.append(jnp.where(lane == lane_on, 1.0, 0.0).astype(jnp.bfloat16))
        keys_marked = jnp.concatenate([keys, jnp.concatenate(marks, axis=0)], axis=1)
        dqs = []
        for head, lanes in enumerate((low_lanes, jnp.logical_not(low_lanes))):
            q_head = jnp.where(lanes, q_pair, jnp.zeros_like(q_pair))
            do_head = jnp.where(lanes, do_pair, jnp.zeros_like(do_pair))
            log_total = lse_ref[rows, head * HD : head * HD + 1]
            parts = tile_scores(q_head, keys, rel_wide, tile, own)
            d_probs = dot_nt(do_head, values)
            probs = [jnp.exp(part - log_total) for part in parts]
            d_parts = [d_probs[:, c * TILE : (c + 1) * TILE] for c in range(chunks)]
            inner = functools.reduce(jnp.add, [p * d for p, d in zip(probs, d_parts)])
            inner = jnp.sum(inner, axis=1, keepdims=True)
            d_scores = [(p * (d - inner)).astype(jnp.bfloat16) for p, d in zip(probs, d_parts)]
            p_ref[head, rows, :] = jnp.concatenate([p.astype(jnp.bfloat16) for p in probs], axis=1)
            joined = jnp.concatenate(d_scores, axis=1)
            ds_ref[head, rows, :] = joined
            band = [None, None, None]
            for c, spot in enumerate(plan):
                if spot is not None:
                    near = wrapped_band(c, tile, chunks, own)
                    piece = d_scores[c]
                    if near is not None:
                        piece = jnp.where(near, piece, jnp.zeros_like(piece))
                    band[spot] = piece
            turned = dot_nn(jnp.concatenate(band, axis=1), flip_ref[...])
            turned = pltpu.roll(turned, BAND, 1, stride=1, stride_axis=0).astype(jnp.bfloat16)
            marked = dot_nn(joined, keys_marked)
            d_query = marked[:, :TILE] + dot_nn(turned, rev_ref[...])
            d_query = d_query + marked[:, TILE : TILE + 1] * rel_wide[0:1, :].astype(jnp.float32)
            d_query = d_query + marked[:, TILE + 1 : TILE + 2] * rel_wide[WIDE - 1 : WIDE, :].astype(jnp.float32)
            dqs.append(d_query * 0.125)
        dq_ref[rows, :] = jnp.where(low_lanes, dqs[0], dqs[1]).astype(dq_ref.dtype)
    q_turned = jnp.transpose(q_ref[...] * jnp.bfloat16(0.125))
    do_turned = jnp.transpose(do_ref[...])
    for which, (turned, kept) in enumerate(((q_turned, ds_ref), (do_turned, p_ref))):
        both = jnp.concatenate(
            [dot_nn(turned[head * HD : (head + 1) * HD, :], kept[head]) for head in range(2)], axis=0
        )
        both = jnp.transpose(both)
        own_out[which] = both[:rows_n]
        far_out[which] = both[rows_n:].astype(far_out.dtype)


def rel_tables(rel_table):
    places = jnp.clip(jnp.arange(WIDE, dtype=jnp.int32) - WIDE // 2, -REL_LEFT, REL_RIGHT) + REL_LEFT
    table_rows = jnp.arange(rel_table.shape[0], dtype=jnp.int32)
    picker = (places[:, None] == table_rows[None, :]).astype(jnp.bfloat16)
    wide = jnp.dot(picker, rel_table, preferred_element_type=jnp.float32).astype(jnp.bfloat16)
    wide = jnp.concatenate([wide, wide], axis=1)
    flip = jnp.arange(BAND)[:, None] + jnp.arange(WIDE)[None, :] == WIDE - 1
    return wide, wide[::-1], flip.astype(jnp.bfloat16)


def pair_blocks(rows, width, group):
    pairs = width // (2 * HD)
    one = pl.BlockSpec((rows, 2 * HD), lambda h: (0, h))
    two = pl.BlockSpec((rows, 2 * HD), lambda h: (0, pairs + h))
    return pairs, one, [one] * group + [two] * group


def fixed(array):
    return pl.BlockSpec(array.shape, lambda h: (0, 0))


def attention_forward(own, query, kv, rel_wide):
    rows, width = query.shape
    pairs, block, kv_blocks = pair_blocks(rows, width, len(kv))
    size = rows * rows * len(kv) * width
    return pl.pallas_call(
        functools.partial(attn_fwd_kernel, len(kv)),
        grid=(pairs,),
        in_specs=[pl.BlockSpec(memory_space=pltpu.SMEM), block, fixed(rel_wide)] + kv_blocks,
        out_specs=[block] * 2,
        out_shape=[
            jax.ShapeDtypeStruct((rows, width), jnp.bfloat16),
            jax.ShapeDtypeStruct((rows, width), jnp.float32),
        ],
        compiler_params=pltpu.CompilerParams(vmem_limit_bytes=VMEM),
        cost_estimate=pl.CostEstimate(flops=12 * size, bytes_accessed=rows * width * 16, transcendentals=0),
        name="attention_forward",
    )(own, query, rel_wide, *kv, *kv)


def attention_backward(own, query, kv, d_out, log_total, tables):
    rows, width = query.shape
    keys_n = rows * len(kv)
    pairs, block, kv_blocks = pair_blocks(rows, width, len(kv))
    size = rows * keys_n * width
    return pl.pallas_call(
        functools.partial(attn_bwd_kernel, len(kv)),
        grid=(pairs,),
        in_specs=[pl.BlockSpec(memory_space=pltpu.SMEM), block, block, block]
        + [fixed(table) for table in tables]
        + kv_blocks,
        out_specs=[
            block,
            pl.BlockSpec((2, rows, 2 * HD), lambda h: (0, 0, h)),
            pl.BlockSpec((2, keys_n - rows, 2 * HD), lambda h: (0, 0, h)),
        ],
        out_shape=[
            jax.ShapeDtypeStruct((rows, width), jnp.bfloat16),
            jax.ShapeDtypeStruct((2, rows, width), jnp.float32),
            jax.ShapeDtypeStruct((2, keys_n - rows, width), jnp.bfloat16),
        ],
        scratch_shapes=[pltpu.VMEM((2, rows, keys_n), jnp.bfloat16)] * 2,
        compiler_params=pltpu.CompilerParams(vmem_limit_bytes=VMEM),
        cost_estimate=pl.CostEstimate(flops=24 * size, bytes_accessed=rows * width * 32, transcendentals=0),
        name="attention_backward",
    )(own, query, d_out, log_total, *tables, *kv, *kv)


HBM = pl.BlockSpec(memory_space=pltpu.HBM)
SCALARS = pl.BlockSpec(memory_space=pltpu.SMEM)


def assemble_kernel(spans, count, places_ref, *refs):
    pieces, outs, sems = refs[:count], refs[count:-1], refs[-1]
    copies = [
        pltpu.make_async_copy(
            piece.at[:, pl.ds(begin, width)], out.at[places_ref[index]], sems.at[index, which]
        )
        for index, piece in enumerate(pieces)
        for which, (out, (begin, width)) in enumerate(zip(outs, spans))
    ]
    for copy in copies:
        copy.start()
    for copy in copies:
        copy.wait()


def assemble(places, pieces, widths):
    rows, count = pieces[0].shape[0], len(pieces)
    spans = [(sum(widths[:k]), width) for k, width in enumerate(widths)]
    outs = pl.pallas_call(
        functools.partial(assemble_kernel, spans, count),
        in_specs=[SCALARS] + [HBM] * count,
        out_specs=[pl.BlockSpec(memory_space=pltpu.VMEM)] * len(spans),
        out_shape=[jax.ShapeDtypeStruct((count, rows, w), pieces[0].dtype) for w in widths],
        scratch_shapes=[pltpu.SemaphoreType.DMA((count, len(spans)))],
        compiler_params=pltpu.CompilerParams(vmem_limit_bytes=20 * 1024 * 1024),
        cost_estimate=pl.CostEstimate(
            flops=0, bytes_accessed=4 * count * rows * sum(widths), transcendentals=0
        ),
        name="assemble",
    )(places, *pieces)
    return [out.reshape(count * rows, out.shape[2]) for out in outs]


class Gather:
    def __init__(self):
        self.chips = lax.axis_size("chip")
        side = math.isqrt(self.chips)
        self.first, self.second = (side, side) if side * side == self.chips else (self.chips, 1)
        chip, core = lax.axis_index("chip"), lax.axis_index("core")
        places = []
        for owner in (core, 1 - core):
            for early, late in self.steps():
                one = self.moved(chip, early, late)
                two = self.moved(chip, late, early)
                places.append(jnp.where(owner == 0, one, two) * 2 + owner)
        self.places = jnp.stack(places).astype(jnp.int32)

    def steps(self):
        steps = [(early, 0) for early in range(self.first)]
        steps += [(0, late) for late in range(1, self.second)]
        return steps + [(e, l) for l in range(1, self.second) for e in range(1, self.first)]

    def moved(self, chip, along_first, along_second):
        return chip ^ (along_first * self.second + along_second)

    def hop(self, block, early, late):
        route = []
        for chip in range(self.chips):
            route.append((self.moved(chip, early, late) * 2, chip * 2))
            route.append((self.moved(chip, late, early) * 2 + 1, chip * 2 + 1))
        return lax.ppermute(block, ("chip", "core"), route)

    def stages(self, shards, used):
        swap = lambda block: lax.ppermute(block, "core", [(0, 1), (1, 0)])
        collect = lambda shard: lax.all_gather(shard, ("fz", "fh"), axis=0, tiled=True)
        count = len(shards)
        shards = list(shards)
        blocks = [collect(shard) for shard in shards[:2]]
        kept, traded, last = [[] for _ in shards], [[] for _ in shards], []
        complete = 0
        for turn in range(count + 1):
            onward = kept[turn - 1][1 : self.first] if turn else []
            if turn > 1:
                late = kept[turn - 2]
                self.held = yield [kept[which] + traded[which] for which in range(complete)]
                (onward, late), last, self.held = lax.optimization_barrier(
                    ((onward, late), last, list(self.held))
                )
                further = [self.hop(block, 0, step) for step in range(1, self.second) for block in onward]
                kept[turn - 1] = kept[turn - 1] + further
                traded[turn - 2] = [swap(block) for block in late]
                last = further + traded[turn - 2]
                complete += 1
            self.held = yield [kept[which] + traded[which] for which in range(complete)]
            if turn < count:
                fresh = blocks[turn][:, : used[turn]]
                coming = shards[turn + 2 : turn + 3]
                (fresh, onward, coming), last, self.held = lax.optimization_barrier(
                    ((fresh, onward, coming), last, list(self.held))
                )
                blocks += [collect(shard) for shard in coming]
                early = [self.hop(fresh, step, 0) for step in range(1, self.first)]
                other = [self.hop(fresh, 0, step) for step in range(1, self.second)]
                kept[turn] = [fresh] + early + other
                last = early + other
                if turn == 1:
                    further = [self.hop(block, 0, step) for step in range(1, self.second) for block in onward]
                    kept[0] = kept[0] + further
                    last = last + further
            else:
                late, last, self.held = lax.optimization_barrier((kept[-1], last, list(self.held)))
                traded[-1] = [swap(block) for block in late]
        yield [own + other for own, other in zip(kept, traded)]


VMEM_SPEC = pl.BlockSpec(memory_space=pltpu.VMEM)
TALL = 512


def dot_tn(a, b):
    return lax.dot_general(a, b, (((0,), (0,)), ((), ())), preferred_element_type=jnp.float32)


def norm_rows(field):
    centred = field - jnp.mean(field, -1, keepdims=True)
    rate = lax.rsqrt(jnp.mean(centred * centred, -1, keepdims=True) + EPSILON)
    return centred * rate, rate


def norm_back(grad, gain, normed, rate):
    scaled = grad * gain
    inner = jnp.mean(scaled * normed, -1, keepdims=True)
    return (scaled - jnp.mean(scaled, -1, keepdims=True) - normed * inner) * rate


def each_rows(rows, step, body):
    def one(index, carry):
        body(pl.ds(pl.multiple_of(index * step, step), step))
        return carry

    lax.fori_loop(0, rows // step, one, 0)


def shape_of(rows, width, dtype=jnp.bfloat16):
    return jax.ShapeDtypeStruct((rows, width), dtype)


class Weight:
    def __init__(self, places, pieces, begin, width):
        self.places, self.pieces, self.begin, self.width = places, pieces, begin, width
        self.depth = sum(piece.shape[0] for piece in pieces)
        self.block = self.depth // places.shape[0]
        self.count = len(pieces)
        self.bytes = 2 * self.depth * width

    def blocks(self, pieces):
        return [
            piece.at[pl.ds(begin, self.block)]
            for piece in pieces
            for begin in range(0, piece.shape[0], self.block)
        ]

    def loads(self, places_ref, pieces, store, sems, runs):
        copies = []
        for tile, spans in enumerate(runs):
            here = []
            for which, (begin, span) in enumerate(spans):
                for index, piece in enumerate(self.blocks(pieces)):
                    row = pl.multiple_of(places_ref[index] * self.block, self.block)
                    here.append(
                        pltpu.make_async_copy(
                            piece.at[:, pl.ds(self.begin + begin, span)],
                            store.at[pl.ds(row, self.block), pl.ds(begin, span)],
                            sems.at[tile, which, index],
                        )
                    )
            copies.append(here)
        for here in copies:
            for copy in here:
                copy.start()
        return copies

    def scratch(self, runs):
        return [
            pltpu.VMEM((self.depth, self.width), jnp.bfloat16),
            pltpu.SemaphoreType.DMA((len(runs), len(runs[0]), self.depth // self.block)),
        ]


def fused(kernel, name, weight, runs, scratch, outs, *operands):
    moved = sum(math.prod(item.shape) * item.dtype.itemsize for item in (*operands, *outs))
    rows = operands[0].shape[0]

    def body(places_ref, *refs):
        kernel(places_ref, refs[: weight.count], *refs[weight.count :])

    return pl.pallas_call(
        body,
        in_specs=[SCALARS] + [HBM] * weight.count + [VMEM_SPEC] * len(operands),
        out_specs=[VMEM_SPEC] * len(outs),
        out_shape=outs,
        scratch_shapes=weight.scratch(runs) + scratch,
        compiler_params=pltpu.CompilerParams(vmem_limit_bytes=weight.bytes + 14 * 1024 * 1024),
        cost_estimate=pl.CostEstimate(
            flops=rows * weight.bytes, bytes_accessed=moved + weight.bytes, transcendentals=0
        ),
        name=name,
    )(weight.places, *weight.pieces, *operands)


def wait_all(copies):
    for here in copies:
        for copy in here:
            copy.wait()


def wide_kernel(kind, weight, runs, places_ref, pieces, u_ref, down_ref, up_ref, z_ref, *rest):
    outs, (store, sems) = rest[:-2], rest[-2:]
    copies = weight.loads(places_ref, pieces, store, sems, runs)
    z_ref[...] = dot_nt(u_ref[...], down_ref[...]).astype(jnp.bfloat16)
    wait_all(copies)
    for spans in runs:
        result = [
            dot_nn(u_ref[...], store[:, begin : begin + span])
            + dot_nn(z_ref[...], up_ref[:, begin : begin + span])
            for begin, span in spans
        ]
        at = slice(spans[0][0], spans[0][0] + spans[0][1])
        if kind == "silu":
            gate = jax.nn.sigmoid(result[0])
            active = result[0] * gate
            outs[0][:, at] = active.astype(jnp.bfloat16)
            outs[1][:, at] = (gate + active * (1.0 - gate)).astype(jnp.bfloat16)
        elif kind == "glu":
            gate = jax.nn.sigmoid(result[1])
            gated = result[0] * gate
            outs[0][:, at] = gated.astype(jnp.bfloat16)
            outs[1][:, at] = gate.astype(jnp.bfloat16)
            outs[2][:, at] = (gated * (1.0 - gate)).astype(jnp.bfloat16)
        else:
            which = min(at.start // outs[0].shape[1], 1)
            first = which * outs[0].shape[1]
            outs[which][:, at.start - first : at.stop - first] = result[0].astype(jnp.bfloat16)


def project_wide(kind, inputs, weight, down, up):
    rows = inputs.shape[0]
    width = weight.width
    out_width = width // 2 if kind == "glu" else width
    sizes = {"silu": [width] * 2, "glu": [out_width] * 3, "plain": [width // 3, width - width // 3]}[kind]
    span = min(TALL, out_width)
    runs = [[(base + begin, span) for base in range(0, width, out_width)] for begin in range(0, out_width, span)]
    return fused(
        functools.partial(wide_kernel, kind, weight, runs), "project_" + kind, weight, runs, [],
        [shape_of(rows, down.shape[0])] + [shape_of(rows, size) for size in sizes],
        inputs, down, up,
    )


def narrow_kernel(factor, weight, runs, last, places_ref, pieces, u_ref, down_ref, up_ref, field_ref, gain_ref, bias_ref, *rest):
    cot_ref = rest[0] if last else None
    z_ref, field_out, normed_out, store, sems = rest[1 if last else 0 :]
    copies = weight.loads(places_ref, pieces, store, sems, runs)
    z_ref[...] = dot_nt(u_ref[...], down_ref[...]).astype(jnp.bfloat16)
    wait_all(copies)
    for ((begin, span),) in runs:
        at = slice(begin, begin + span)
        result = dot_nn(u_ref[...], store[:, at]) + dot_nn(z_ref[...], up_ref[:, at])
        field_out[:, at] = field_ref[:, at].astype(jnp.float32) + factor * result
    gain, bias = gain_ref[...], bias_ref[...]

    def finish(at):
        normed, rate = norm_rows(field_out[at, :])
        normed_out[at, :] = (normed * gain + bias).astype(jnp.bfloat16)
        if last:
            field_out[at, :] = norm_back(cot_ref[at, :].astype(jnp.float32), gain, normed, rate)

    each_rows(u_ref.shape[0], 128, finish)


def project_narrow(inputs, weight, down, up, field, gain, bias, factor, cotangent=None):
    rows, width = inputs.shape[0], weight.width
    span = min(TALL, width)
    runs = [[(begin, span)] for begin in range(0, width, span)]
    extra = [] if cotangent is None else [cotangent]
    return fused(
        functools.partial(narrow_kernel, factor, weight, runs, bool(extra)), "project_next", weight, runs, [],
        [shape_of(rows, down.shape[0]), shape_of(rows, width, jnp.float32), shape_of(rows, width)],
        inputs, down, up, field, gain, bias, *extra,
    )


def adapter_grads(grad_ref, z_ref, up_ref, u_ref, dz_ref, da_ref, db_ref):
    dz_ref[...] = dot_nt(grad_ref[...], up_ref[...]).astype(jnp.bfloat16)
    db_ref[...] = dot_tn(z_ref[...], grad_ref[...]).astype(jnp.bfloat16)
    da_ref[...] = dot_tn(dz_ref[...], u_ref[...]).astype(jnp.bfloat16)


def hidden_back_kernel(factor, weight, runs, places_ref, pieces, d_ref, down_ref, up_ref, u_ref, z_ref,
                       slope_ref, out_ref, da_ref, db_ref, store, sems, grad, dz):
    copies = weight.loads(places_ref, pieces, store, sems, runs)
    grad[...] = (factor * d_ref[...]).astype(jnp.bfloat16)
    adapter_grads(grad, z_ref, up_ref, u_ref, dz, da_ref, db_ref)
    wait_all(copies)
    tall = min(TALL, weight.depth)
    for begin in range(0, weight.depth, tall):
        at = slice(begin, begin + tall)
        result = dot_nt(grad[...], store[at, :]) + dot_nn(dz[...], down_ref[:, at])
        out_ref[:, at] = (result * slope_ref[:, at].astype(jnp.float32)).astype(jnp.bfloat16)


def hidden_back(d_field, factor, weight, down, up, inputs, slot_acts, slope):
    rows, width = d_field.shape
    depth, rank = weight.depth, down.shape[0]
    runs = [[(0, width)]]
    return fused(
        functools.partial(hidden_back_kernel, factor, weight, runs), "hidden_back", weight, runs,
        [pltpu.VMEM((rows, width), jnp.bfloat16), pltpu.VMEM((rows, rank), jnp.bfloat16)],
        [shape_of(rows, depth), shape_of(rank, depth), shape_of(rank, width)],
        d_field, down, up, inputs, slot_acts, slope,
    )


def field_back_kernel(kind, weight, runs, share_count, places_ref, pieces, d_ref, down_ref, up_ref, u_ref, z_ref, *rest):
    extra = {"norm": 3, "conv": 3, "plain": 0}[kind]
    shares, rest = rest[:share_count], rest[share_count:]
    extras, (out_ref, da_ref, db_ref, store, sems, grad, dz, d_inputs) = rest[:extra], rest[extra:]
    copies = weight.loads(places_ref, pieces, store, sems, runs)
    if shares:
        width = d_ref.shape[1]
        grad[:, :width] = d_ref[...]
        for which in range(2):
            total = shares[0][which]
            for share in shares[1:]:
                total = total + share[which].astype(jnp.float32)
            grad[:, (1 + which) * width : (2 + which) * width] = total.astype(jnp.bfloat16)
    elif d_ref.dtype == jnp.bfloat16:
        grad = d_ref
    else:
        grad[...] = d_ref[...].astype(jnp.bfloat16)
    adapter_grads(grad, z_ref, up_ref, u_ref, dz, da_ref, db_ref)
    wait_all(copies)
    tall = min(TALL, weight.depth)
    for begin in range(0, weight.depth, tall):
        at = slice(begin, begin + tall)
        result = dot_nt(grad[...], store[at, :]) + dot_nn(dz[...], down_ref[:, at])
        if kind == "plain":
            out_ref[:, at] = result.astype(out_ref.dtype)
        else:
            d_inputs[:, at] = result

    def finish(at):
        if kind == "norm":
            prior_ref, field_ref, gain_ref = extras
            normed, rate = norm_rows(field_ref[at, :].astype(jnp.float32))
            moved = norm_back(d_inputs[at, :], gain_ref[...], normed, rate)
            out_ref[at, :] = (prior_ref[at, :] + moved).astype(out_ref.dtype)
        else:
            field_ref, gain_ref, bias_ref = extras
            gain = gain_ref[...]
            normed, rate = norm_rows(field_ref[at, :])
            shifted = normed * gain + bias_ref[...]
            gate = jax.nn.sigmoid(shifted)
            slope = gate + shifted * gate * (1.0 - gate)
            out_ref[at, :] = norm_back(d_inputs[at, :] * slope, gain, normed, rate)

    if kind != "plain":
        each_rows(d_ref.shape[0], 128, finish)


def field_back(
    kind, grad, weight, down, up, inputs, slot_acts, extras=(), out_dtype=jnp.float32, shares=()
):
    rows, width = grad.shape[0], weight.width
    depth, rank = weight.depth, down.shape[0]
    runs = [[(0, width)]]
    scratch = shares or grad.dtype != jnp.bfloat16
    return fused(
        functools.partial(field_back_kernel, kind, weight, runs, len(shares)), "field_back_" + kind, weight, runs,
        [
            pltpu.VMEM((rows, width) if scratch else (16, 128), jnp.bfloat16),
            pltpu.VMEM((rows, rank), jnp.bfloat16),
            pltpu.VMEM((rows, depth) if kind != "plain" else (8, 128), jnp.float32),
        ],
        [shape_of(rows, depth, out_dtype), shape_of(rank, depth), shape_of(rank, width)],
        grad, down, up, inputs, slot_acts, *shares, *extras,
    )


HALO = 32


def taps_kernel(weight, runs, places_ref, *refs):
    pieces, (out_ref, store, sems) = refs[: weight.count], refs[weight.count :]
    wait_all(weight.loads(places_ref, pieces, store, sems, runs))
    out_ref[...] = jnp.transpose(store[...].astype(jnp.float32))[: out_ref.shape[0], :]


def gather_taps(weight):
    runs = [[(0, TILE)]]
    return pl.pallas_call(
        functools.partial(taps_kernel, weight, runs),
        in_specs=[SCALARS] + [HBM] * weight.count,
        out_specs=VMEM_SPEC,
        out_shape=jax.ShapeDtypeStruct((HALO, weight.depth), jnp.float32),
        scratch_shapes=weight.scratch(runs),
        compiler_params=pltpu.CompilerParams(vmem_limit_bytes=8 * 1024 * 1024),
        name="gather_taps",
    )(weight.places, *weight.pieces)


def slide(lanes, parts, shifted, taps_ref, shifts, rows, store):
    begin = 0
    for part in parts:
        shifted[0, begin : begin + part.shape[0], :] = part
        begin += part.shape[0]
    length = begin - 8
    for turn in range(1, 8):
        shifted[turn, 0:length, :] = shifted[0, turn : turn + length, :]
    step = 64
    for at in range(0, rows, step):
        total = None
        for tap, shift in enumerate(shifts):
            base = shift - shift % 8 + at
            term = shifted[shift % 8, base : base + step, :] * taps_ref[tap : tap + 1, lanes]
            total = term if total is None else total + term
        store(slice(at, at + step), total)


def each_tile(width, body):
    def one(index, carry):
        body(pl.ds(pl.multiple_of(index * TILE, TILE), TILE))
        return carry

    lax.fori_loop(0, width // TILE, one, 0)


def conv_kernel(val_ref, earlier_ref, taps_ref, gain_ref, bias_ref, conv_ref, act_ref, shifted):
    rows, width = val_ref.shape

    def one(lanes):
        parts = [earlier_ref[:, lanes].astype(jnp.float32), val_ref[:, lanes].astype(jnp.float32)]

        def store(at, total):
            conv_ref[at, lanes] = total

        shifts = [HALO - KERNEL + 1 + tap for tap in range(KERNEL)]
        slide(lanes, parts, shifted, taps_ref, shifts, rows, store)

    each_tile(width, one)

    def finish(at):
        shifted_field = norm_rows(conv_ref[at, :])[0] * gain_ref[...] + bias_ref[...]
        act_ref[at, :] = (shifted_field * jax.nn.sigmoid(shifted_field)).astype(jnp.bfloat16)

    each_rows(rows, 128, finish)


def conv_back_kernel(d_ref, later_ref, taps_ref, gate_ref, slope_ref, out_ref, shifted):
    rows, width = d_ref.shape

    def one(lanes):
        parts = [d_ref[:, lanes], later_ref[:, lanes].astype(jnp.float32)]
        high = pl.ds(pl.multiple_of(lanes.start + width, TILE), TILE)

        def store(at, total):
            out_ref[at, lanes] = (total * gate_ref[at, lanes].astype(jnp.float32)).astype(jnp.bfloat16)
            out_ref[at, high] = (total * slope_ref[at, lanes].astype(jnp.float32)).astype(jnp.bfloat16)

        slide(lanes, parts, shifted, taps_ref, [KERNEL - 1 - tap for tap in range(KERNEL)], rows, store)

    each_tile(width, one)


def conv_call(kernel, name, outs, rows, *operands):
    return pl.pallas_call(
        kernel,
        in_specs=[VMEM_SPEC] * len(operands),
        out_specs=[VMEM_SPEC] * len(outs),
        out_shape=outs,
        scratch_shapes=[pltpu.VMEM((8, rows + HALO, TILE), jnp.float32)],
        compiler_params=pltpu.CompilerParams(vmem_limit_bytes=16 * 1024 * 1024),
        cost_estimate=pl.CostEstimate(flops=0, bytes_accessed=32 * rows * operands[0].shape[1], transcendentals=0),
        name=name,
    )(*operands)


def conv_forward(value, earlier, taps, gain, bias):
    rows, width = value.shape
    outs = [shape_of(rows, width, jnp.float32), shape_of(rows, width)]
    return conv_call(conv_kernel, "conv_forward", outs, rows, value, earlier, taps, gain, bias)


def conv_backward(d_conv, later, taps, gate, slope):
    rows, width = d_conv.shape
    outs = [shape_of(rows, 2 * width)]
    return conv_call(conv_back_kernel, "conv_backward", outs, rows, d_conv, later, taps, gate, slope)[0]


class Layout:
    def __init__(self, together, fsdp):
        self.fsdp = fsdp
        self.inner = fsdp // together
        self.group = 2 * self.inner

    def place(self, core, f):
        return core * self.fsdp + f

    def round_route(self, turn):
        route = []
        for core in range(2):
            for f in range(self.fsdp):
                clip = (f % 2 + turn) % 2
                spot = f // 2
                target = self.place(spot % 2, (2 * core + clip) * self.inner + spot // 2)
                route.append((self.place(core, f), target))
        return route

    def gather_rows(self, blocks):
        parity = (lax.axis_index("fz") * self.inner + lax.axis_index("fh")) % 2
        clip = lax.axis_index("fz") % 2
        got = []
        for turn in range(2):
            sent = lax.dynamic_index_in_dim(blocks, (parity + turn) % 2, 0, keepdims=False)
            got.append(lax.ppermute(sent, ("core", "fz", "fh"), self.round_route(turn)))
        swap = clip == 1
        return jnp.concatenate(
            [jnp.where(swap, got[1], got[0]), jnp.where(swap, got[0], got[1])], axis=0
        )

    def scatter_rows(self, rows):
        parity = (lax.axis_index("fz") * self.inner + lax.axis_index("fh")) % 2
        clip = lax.axis_index("fz") % 2
        halves = rows.reshape(2, rows.shape[0] // 2, rows.shape[1])
        got = []
        for turn in range(2):
            sent = lax.dynamic_index_in_dim(halves, (clip + turn) % 2, 0, keepdims=False)
            route = [(target, source) for source, target in self.round_route(turn)]
            got.append(lax.ppermute(sent, ("core", "fz", "fh"), route))
        swap = parity == 1
        return jnp.stack([jnp.where(swap, got[1], got[0]), jnp.where(swap, got[0], got[1])])

    def spot_index(self, spot):
        return (spot % 2) * self.inner + spot // 2

    def from_spot(self, block, distance, cyclic):
        route = []
        for spot in range(self.group):
            source = spot + distance
            if cyclic:
                source %= self.group
            if 0 <= source < self.group:
                route.append((self.spot_index(source), self.spot_index(spot)))
        return lax.ppermute(block, ("core", "fh"), route)


def pick_adapters(layout, ids, a_model, a_hidden, b_model, b_hidden):
    slots = a_model.shape[2]
    half = RANK // 2
    core = lax.axis_index("core")
    ranks = core * half + jnp.arange(half, dtype=jnp.int32)
    wanted = ids[:, None] * RANK + ranks[None, :]
    picker = (wanted[:, :, None] == jnp.arange(slots, dtype=jnp.int32)).astype(jnp.bfloat16)
    down = lambda a: jnp.einsum("jrs,pks->jprk", picker, a, preferred_element_type=jnp.float32)
    up = lambda b: jnp.einsum("jrs,psn->jprn", picker, b, preferred_element_type=jnp.float32)
    cut = a_hidden.shape[1] // a_model.shape[1]
    span = a_model.shape[1]

    def short(pack):
        rows = pack.reshape(pack.shape[0], pack.shape[1], half, cut, span)
        return jnp.swapaxes(rows, 2, 3).reshape(pack.shape[0], pack.shape[1] * cut, half, span)

    pack = jnp.concatenate(
        [down(a_model), up(b_model), short(down(a_hidden)), short(up(b_hidden))], axis=1
    ).astype(jnp.bfloat16)
    count = layout.fsdp
    here = lax.axis_index("fz") * layout.inner + lax.axis_index("fh")
    full = jnp.zeros(pack.shape[1:3] + (span * count,), jnp.bfloat16)
    for step in range(count):
        target = (here + step) % count
        piece = lax.dynamic_index_in_dim(pack, target // layout.inner, 0, keepdims=False)
        if step:
            route = [(f, (f + step) % count) for f in range(count)]
            piece = lax.ppermute(piece, ("fz", "fh"), route)
        source = (here - step) % count
        full = lax.dynamic_update_slice(full, piece, (0, 0, source * span))
    other = lax.ppermute(full, "core", [(0, 1), (1, 0)])
    low, high = jnp.where(core == 0, full, other), jnp.where(core == 0, other, full)
    full = jnp.concatenate([low, high], axis=1)
    models = a_model.shape[0] + b_model.shape[0]
    hidden = full[models:].reshape(-1, cut, RANK, count, span)
    hidden = jnp.transpose(hidden, (0, 2, 3, 1, 4)).reshape(-1, RANK, cut * count * span)
    first = a_model.shape[0]
    return full[:first], hidden[: a_hidden.shape[0]], full[first:models], hidden[a_hidden.shape[0] :]


def send_grads(model, hidden):
    devices = lax.axis_size(EVERYWHERE)
    groups, width = model.shape
    share, hidden_share = width // devices, hidden.shape[1] // devices
    tiles = -(-groups // TILE)
    if groups % TILE:
        model = jnp.concatenate([model, jnp.zeros((tiles * TILE - groups, width), model.dtype)])
    turned = model.T
    split = jnp.transpose(hidden.reshape(hidden.shape[0], devices, hidden_share), (1, 0, 2))
    parts = [turned[:, k * TILE : (k + 1) * TILE].reshape(devices, share, TILE) for k in range(tiles)]
    parts.append(split.reshape(devices, -1, TILE))
    chips, others = lax.axis_size("chip"), lax.axis_size("fz") * lax.axis_size("fh")
    part = jnp.concatenate(parts, axis=1).reshape(chips, 2, others, -1, TILE)
    core = lax.axis_index("core")
    ours = lax.dynamic_index_in_dim(part, core, 1, keepdims=False)
    theirs = lax.dynamic_index_in_dim(part, 1 - core, 1, keepdims=False)
    came = lax.ppermute(theirs, "core", [(0, 1), (1, 0)])
    both = (ours.astype(jnp.float32) + came.astype(jnp.float32)).astype(jnp.bfloat16)
    both = both.reshape(chips * others, -1, TILE)
    got = lax.all_to_all(both, ("chip", "fz", "fh"), 0, 0, tiled=True)
    return got[:, : tiles * share], got[:, tiles * share :].reshape(-1, hidden.shape[0], hidden_share)


def place_grads_kernel(groups, ids_ref, model_ref, hidden_ref, model_out, hidden_out):
    model_out[...] = jnp.zeros_like(model_out)
    hidden_out[...] = jnp.zeros_like(hidden_out)
    share = model_out.shape[1]
    slot = lax.broadcasted_iota(jnp.int32, (share, TILE), 1) // RANK
    in_tile = TILE // RANK

    def one(sender, carry):
        owner = ids_ref[sender]
        for group in range(groups):
            tile, local_group = divmod(group, in_tile)
            block = model_ref[sender, tile * share : (tile + 1) * share, :].astype(jnp.float32)
            turn = lax.rem(owner - local_group + in_tile, in_tile) * RANK
            block = jnp.where(slot == owner, pltpu.roll(block, turn, 1), 0.0)
            model_out[group] += block
        at = pl.ds(pl.multiple_of(owner * RANK, RANK), RANK)
        for group in range(hidden_out.shape[0]):
            rows = hidden_ref[sender, group * RANK : (group + 1) * RANK, :]
            hidden_out[group, at, :] += rows.astype(jnp.float32)
        return carry

    lax.fori_loop(0, model_ref.shape[0], one, 0)


def place_grads(ids, model, hidden, groups, slots):
    share = model.shape[1] // -(-groups * RANK // TILE)
    return pl.pallas_call(
        functools.partial(place_grads_kernel, groups),
        in_specs=[SCALARS, VMEM_SPEC, VMEM_SPEC],
        out_specs=[VMEM_SPEC, VMEM_SPEC],
        out_shape=[
            jax.ShapeDtypeStruct((groups, share, slots), jnp.float32),
            jax.ShapeDtypeStruct((hidden.shape[1] // RANK, slots, hidden.shape[2]), jnp.float32),
        ],
        compiler_params=pltpu.CompilerParams(vmem_limit_bytes=16 * 1024 * 1024),
        name="place_grads",
    )(ids, model, hidden)


def local(
    frames,
    cotangent,
    adapter_ids,
    norm_gains,
    norm_biases,
    rel_table,
    w_up,
    w_down,
    w_qkv,
    w_out,
    w_pw1,
    w_depth,
    w_pw2,
    ad_a_model,
    ad_a_hidden,
    ad_b_model,
    ad_b_hidden,
):
    group_clips, frame_span, width = frames.shape
    together = 2 * group_clips
    layout = Layout(together, lax.axis_size("fz") * lax.axis_size("fh"))
    rows = 2 * frame_span
    slots = ad_a_model.shape[2]
    spot = lax.axis_index("fh") * 2 + lax.axis_index("core")
    own = (spot * (rows // TILE)).astype(jnp.int32).reshape(1)
    other_ids = lax.ppermute(adapter_ids, "core", [(0, 1), (1, 0)])
    at_zero = lax.axis_index("core") == 0
    near_ids = jnp.concatenate(
        [jnp.where(at_zero, adapter_ids, other_ids), jnp.where(at_zero, other_ids, adapter_ids)]
    )
    layer_in = layout.gather_rows(frames)
    first_four, other_four = (
        pick_adapters(layout, near_ids, *[factor[at] for factor in factors])
        for factors in [(ad_a_model, ad_a_hidden, ad_b_model, ad_b_hidden)]
        for at in (slice(0, 1), slice(1, None))
    )
    gather = Gather()
    taps = jnp.pad(w_depth.T, ((0, 0), (0, width - KERNEL)))
    shards = [
        w_up[0],
        w_down[0],
        jnp.concatenate([w_qkv, w_out], axis=1),
        jnp.concatenate([w_pw1, w_pw2, taps], axis=1),
        w_up[1],
        w_down[1],
    ]
    used = [shard.shape[1] for shard in shards]
    used[3] = 3 * width + TILE
    turns = gather.stages(shards, used)
    next(turns)

    def weight_of(units, which, begin=0, columns=None):
        return Weight(gather.places, units[which], begin, columns or used[which])

    gains = [norm_gains[index : index + 1] for index in range(6)]
    biases = [norm_biases[index : index + 1] for index in range(6)]

    turns.send([])
    turns.send([])
    turns.send([layer_in, *rel_tables(rel_table)])
    layer_in, *tables = gather.held
    field = layer_in.astype(jnp.float32)
    first_in = (norm_rows(field)[0] * gains[0] + biases[0]).astype(jnp.bfloat16)
    units = turns.send([first_in, *first_four])
    first_in, *first_four = gather.held
    a_up0, a_down0, b_down0, b_up0 = [factor[0] for factor in first_four]
    up0_w = weight_of(units, 0)
    z_up0, act_one, slope_one = project_wide("silu", first_in, up0_w, a_up0, b_up0)
    units = turns.send([act_one, slope_one])
    act_one, slope_one = gather.held
    units = turns.send([])
    down0_w = weight_of(units, 1)
    z_down0, after_ffn, attn_in = project_narrow(
        act_one, down0_w, a_down0, b_down0, layer_in, gains[1], biases[1], 0.5
    )
    units = turns.send([after_ffn, attn_in, *other_four])
    after_ffn, attn_in, a_model, a_hidden, b_model, b_hidden = gather.held
    blank = jnp.zeros((RANK, width), jnp.bfloat16)
    qkv_down = a_model[0:3].reshape(3 * RANK, width)
    qkv_up = jnp.concatenate(
        [
            jnp.concatenate([b_model[0], blank, blank], axis=1),
            jnp.concatenate([blank, b_model[1], blank], axis=1),
            jnp.concatenate([blank, blank, b_model[2]], axis=1),
        ]
    )
    glu_up = jnp.concatenate([b_model[6], b_model[7]], axis=1)
    a_out, a_pw1, a_pw2, a_up1 = [a_model[index] for index in range(3, 7)]
    b_out, b_pw2, b_down1 = [b_model[index] for index in range(3, 6)]
    a_down1, b_up1 = a_hidden[0], b_hidden[0]
    units = turns.send([qkv_down, qkv_up, glu_up])
    qkv_down, qkv_up, glu_up = gather.held
    qkv_w, out_w = weight_of(units, 2, 0, 3 * width), weight_of(units, 2, 3 * width, width)
    z_qkv, query, own_kv = project_wide("plain", attn_in, qkv_w, qkv_down, qkv_up)
    units = turns.send([query, own_kv])
    query, own_kv = gather.held
    units = turns.send([])
    pw1_w, pw2_w = weight_of(units, 3, 0, 2 * width), weight_of(units, 3, 2 * width, width)
    taps = gather_taps(weight_of(units, 3, 3 * width, TILE))
    kv = [own_kv] + [layout.from_spot(own_kv, step, True) for step in range(1, layout.group)]
    mixed, log_total = attention_forward(own, query, kv, tables[0])
    turns.send([])
    units = turns.send([])
    up1_w, down1_w = weight_of(units, 4), weight_of(units, 5)
    mixed, cotangent = lax.optimization_barrier((mixed, cotangent))
    d_out = layout.gather_rows(cotangent)
    z_out, after_attn, conv_in = project_narrow(
        mixed, out_w, a_out, b_out, after_ffn, gains[2], biases[2], 1.0
    )
    z_pw1, gated, gate, gate_slope = project_wide("glu", conv_in, pw1_w, a_pw1, glu_up)
    earlier = layout.from_spot(gated[rows - HALO :], -1, False)
    conv_out, conv_act = conv_forward(gated, earlier, taps, gains[3], biases[3])
    z_pw2, after_conv, second_in = project_narrow(
        conv_act, pw2_w, a_pw2, b_pw2, after_attn, gains[4], biases[4], 1.0
    )
    z_up1, act_two, slope_two = project_wide("silu", second_in, up1_w, a_up1, b_up1)
    z_down1, d_fourth, result = project_narrow(
        act_two, down1_w, a_down1, b_down1, after_conv, gains[5], biases[5], 0.5, d_out
    )
    layer_out = layout.scatter_rows(result)

    d_hidden, da_down1, db_down1 = hidden_back(
        d_fourth, 0.5, down1_w, a_down1, b_down1, act_two, z_down1, slope_two
    )
    d_third, da_up1, db_up1 = field_back(
        "norm", d_hidden, up1_w, a_up1, b_up1, second_in, z_up1,
        (d_fourth, after_conv, gains[4]),
    )
    d_conv, da_pw2, db_pw2 = field_back(
        "conv", d_third, pw2_w, a_pw2, b_pw2, conv_act, z_pw2,
        (conv_out, gains[3], biases[3]),
    )
    later = layout.from_spot(d_conv[:HALO].astype(jnp.bfloat16), 1, False)
    d_joined = conv_backward(d_conv, later, taps, gate, gate_slope)
    d_second, da_pw1, db_pw1 = field_back(
        "norm", d_joined, pw1_w, a_pw1, glu_up, conv_in, z_pw1, (d_third, after_attn, gains[2])
    )
    d_mixed, da_out, db_out = field_back(
        "plain", d_second, out_w, a_out, b_out, mixed, z_out, (), jnp.bfloat16
    )
    label = jnp.full((RANK, width), near_ids[lax.axis_index("fz")]).astype(jnp.bfloat16)
    early = send_grads(
        jnp.concatenate(
            [da_out, da_pw1, da_pw2, da_up1, db_out, db_pw2, db_down1]
            + [db_pw1[:, :width], db_pw1[:, width:], label]
        ),
        jnp.concatenate([da_down1, db_up1]),
    )
    d_query, d_own, d_far = attention_backward(own, query, kv, d_mixed, log_total, tables)
    shares = [d_own]
    for step in range(1, layout.group):
        shares.append(layout.from_spot(d_far[:, (step - 1) * rows : step * rows], -step, True))
    d_first, da_qkv, db_qkv = field_back(
        "norm", d_query, qkv_w, qkv_down, qkv_up, attn_in, z_qkv, (d_second, after_ffn, gains[1]),
        shares=shares,
    )
    db_three = [
        db_qkv[index * RANK : (index + 1) * RANK, index * width : (index + 1) * width]
        for index in range(3)
    ]
    d_hidden, da_down0, db_down0 = hidden_back(
        d_first, 0.5, down0_w, a_down0, b_down0, act_one, z_down0, slope_one
    )
    grad_field, da_up0, db_up0 = field_back(
        "norm", d_hidden, up0_w, a_up0, b_up0, first_in, z_up0,
        (d_first, layer_in, gains[0]), jnp.bfloat16,
    )
    grad_frames = layout.scatter_rows(grad_field)
    late = send_grads(
        jnp.concatenate([da_up0, da_qkv, db_down0, *db_three]), jnp.concatenate([da_down0, db_up0])
    )
    ids = (early[0][:, early[0].shape[1] // 2, RANK] * jnp.bfloat16(0.5)).astype(jnp.int32)
    early_model, early_hidden = place_grads(ids, *early, 9, slots)
    late_model, late_hidden = place_grads(ids, *late, 8, slots)
    grad_a_model = jnp.concatenate([late_model[:4], early_model[:4]])
    grad_b_model = jnp.swapaxes(jnp.concatenate([late_model[4:], early_model[4:]]), 1, 2)
    grad_a_hidden = jnp.swapaxes(jnp.stack([late_hidden[0], early_hidden[0]]), 1, 2)
    grad_b_hidden = jnp.stack([late_hidden[1], early_hidden[1]])
    return (layer_out, grad_frames, grad_a_model, grad_a_hidden, grad_b_model, grad_b_hidden)


def solution(mesh):
    every = ("chip", "core", "fz", "fh")
    clips, spread = ("chip", "core"), ("fz", "fh")
    in_specs = (
        P(clips, spread, None),
        P(clips, spread, None),
        P(clips),
        P(),
        P(),
        P(),
        P(None, every, None),
        P(None, every, None),
        P(every, None),
        P(every, None),
        P(every, None),
        P(None, every),
        P(every, None),
        P(None, spread, None),
        P(None, spread, None),
        P(None, None, spread),
        P(None, None, spread),
    )
    out_specs = (
        P(clips, spread, None),
        P(clips, spread, None),
        P(None, every, None),
        P(None, every, None),
        P(None, None, every),
        P(None, None, every),
    )

    def run(frames, *rest):
        dp, fsdp = mesh.shape["dp"], mesh.shape["fsdp"]
        together = 2 * frames.shape[0] // dp
        cut = Mesh(
            mesh.devices.reshape(dp // 2, 2, together, fsdp // together), EVERYWHERE
        )
        return jax.shard_map(
            local, mesh=cut, in_specs=in_specs, out_specs=out_specs, check_vma=False
        )(frames, *rest)

    return run
```

```python
import functools
import math

import jax
import jax.numpy as jnp
from jax import lax
from jax.experimental import pallas as pl
from jax.experimental.pallas import tpu as pltpu
from jax.sharding import Mesh
from jax.sharding import PartitionSpec as P

HEADS = 16
KERNEL = 31
RANK = 16
EPSILON = 1e-05
EVERYWHERE = ("chip", "core", "fz", "fh")

HD = 64
REL_LEFT = 64
REL_RIGHT = 8
TILE = 128
WIDE = 3 * TILE
VMEM = 32 * 1024 * 1024


def dot_nn(a, b):
    return lax.dot_general(a, b, (((1,), (0,)), ((), ())), preferred_element_type=jnp.float32)


def dot_nt(a, b):
    return lax.dot_general(a, b, (((1,), (1,)), ((), ())), preferred_element_type=jnp.float32)


def chunk_plan(tile, chunks):
    return [{chunks - 1: 0, 0: 1, 1: 2}.get((c - tile) % chunks) for c in range(chunks)]


def far_left(c, tile, chunks, own):
    return jnp.logical_or(c + own >= chunks, c < tile)


def wrapped_band(c, tile, chunks, own):
    if tile == 0 and c == chunks - 1:
        return own > 0
    if c == tile + 1:
        return c + own < chunks
    return None


def tile_scores(scores, table, tile, own):
    near = pltpu.roll(table[:, :TILE], TILE // 2, 1, stride=1, stride_axis=0)
    first, last = table[:, TILE : 2 * TILE], table[:, 2 * TILE :]
    ahead = lane_ahead()
    bands = [
        jnp.where(ahead >= TILE // 2, near, first),
        jnp.where(ahead < -(TILE // 2), first, jnp.where(ahead >= TILE // 2, last, near)),
        jnp.where(ahead < -(TILE // 2), near, last),
    ]
    chunks = scores.shape[1] // TILE
    parts = []
    for c, spot in enumerate(chunk_plan(tile, chunks)):
        part = scores[:, c * TILE : (c + 1) * TILE]
        if spot is None:
            bias = first if c < tile else jnp.where(c + own >= chunks, first, last)
        else:
            bias = bands[spot]
            true_band = wrapped_band(c, tile, chunks, own)
            if true_band is not None:
                bias = jnp.where(true_band, bias, jnp.where(far_left(c, tile, chunks, own), first, last))
        parts.append(part + bias)
    return parts


def lane_ahead():
    lane = lax.broadcasted_iota(jnp.int32, (TILE, TILE), 1)
    return lane - lax.broadcasted_iota(jnp.int32, (TILE, TILE), 0)


def stacked(refs):
    return jnp.concatenate([ref[...] for ref in refs], axis=0)


def head_lanes(rows):
    low = lax.broadcasted_iota(jnp.int32, (rows, 2 * HD), 1) < HD
    return low, (low, jnp.logical_not(low))


def row_tiles(rows):
    return [(tile, slice(tile * TILE, (tile + 1) * TILE)) for tile in range(rows // TILE)]


def attn_fwd_kernel(group, own_ref, q_ref, rel_ref, *refs):
    own = own_ref[0]
    keys, values, rel_wide = stacked(refs[:group]), stacked(refs[group : 2 * group]), rel_ref[...]
    o_ref, lse_ref, s_ref, w_ref, p_ref = refs[2 * group :]
    rows_n = q_ref.shape[0]
    low, heads = head_lanes(rows_n)
    q_pair = q_ref[...] * jnp.bfloat16(0.125)
    for head, lanes in enumerate(heads):
        q_head = jnp.where(lanes, q_pair, jnp.zeros_like(q_pair))
        s_ref[head] = dot_nt(q_head, keys)
        w_ref[head] = dot_nt(q_head, rel_wide)
    ones = jnp.ones_like(values)
    values_ones = jnp.concatenate([values, ones], axis=1)
    outs = []
    for head in range(2):
        for tile, rows in row_tiles(rows_n):
            parts = tile_scores(s_ref[head, rows, :], w_ref[head, rows, :], tile, own)
            top = jnp.max(functools.reduce(jnp.maximum, parts), axis=1, keepdims=True)
            top = jnp.broadcast_to(top, (TILE, TILE))
            expo = [jnp.exp(part - top).astype(jnp.bfloat16) for part in parts]
            p_ref[head, rows, :] = jnp.concatenate(expo, axis=1)
            lse_ref[rows, head * TILE : (head + 1) * TILE] = top
        outs.append(dot_nn(p_ref[head], values_ones))
        total = outs[head][:, 2 * HD :]
        at = slice(head * TILE, (head + 1) * TILE)
        lse_ref[:, at] = lse_ref[:, at] + jnp.log(total)
        outs[head] = outs[head][:, : 2 * HD] / total
    o_ref[...] = jnp.where(low, outs[0], outs[1]).astype(jnp.bfloat16)


def attn_bwd_kernel(group, own_ref, q_ref, do_ref, lse_ref, rel_ref, rev_ref, flip_ref, mark_ref, *refs):
    own = own_ref[0]
    keys, values, rel_wide = stacked(refs[:group]), stacked(refs[group : 2 * group]), rel_ref[...]
    dq_ref, own_out, far_out, s_ref, w_ref, dp_ref, ds_ref, p_ref, band_ref = refs[2 * group :]
    rows_n, keys_n = q_ref.shape[0], keys.shape[0]
    chunks = keys_n // TILE
    low, heads = head_lanes(rows_n)
    lane = lax.broadcasted_iota(jnp.int32, (1, TILE), 1)
    q_pair = q_ref[...] * jnp.bfloat16(0.125)
    do_pair = do_ref[...]
    keys_marked = jnp.concatenate([keys, mark_ref[...]], axis=1)
    for head, lanes in enumerate(heads):
        q_head = jnp.where(lanes, q_pair, jnp.zeros_like(q_pair))
        s_ref[head] = dot_nt(q_head, keys)
        w_ref[head] = dot_nt(q_head, rel_wide)
        dp_ref[head] = dot_nt(jnp.where(lanes, do_pair, jnp.zeros_like(do_pair)), values)
    dqs = []
    ahead = lane_ahead()
    for head in range(2):
        edges = []
        for tile, rows in row_tiles(rows_n):
            log_total = lse_ref[rows, head * TILE : (head + 1) * TILE]
            parts = tile_scores(s_ref[head, rows, :], w_ref[head, rows, :], tile, own)
            probs = [jnp.exp(part - log_total) for part in parts]
            d_parts = [dp_ref[head, rows, c * TILE : (c + 1) * TILE] for c in range(chunks)]
            inner = functools.reduce(jnp.add, [p * d for p, d in zip(probs, d_parts)])
            inner = jnp.sum(inner, axis=1, keepdims=True)
            d_scores = [(p * (d - inner)).astype(jnp.bfloat16) for p, d in zip(probs, d_parts)]
            p_ref[head, rows, :] = jnp.concatenate([p.astype(jnp.bfloat16) for p in probs], axis=1)
            ds_ref[head, rows, :] = jnp.concatenate(d_scores, axis=1)
            band = [None, None, None]
            for c, spot in enumerate(chunk_plan(tile, chunks)):
                if spot is not None:
                    near = wrapped_band(c, tile, chunks, own)
                    piece = d_scores[c]
                    band[spot] = piece if near is None else jnp.where(near, piece, jnp.zeros_like(piece))
            behind, beyond = ahead < -(TILE // 2), ahead >= TILE // 2
            none = jnp.zeros_like(band[0])
            band_ref[head, rows, :] = jnp.where(beyond, band[0], jnp.where(behind, band[2], band[1]))
            sides = (
                (jnp.where(beyond, none, band[0]), jnp.where(behind, band[1], none)),
                (jnp.where(behind, none, band[2]), jnp.where(beyond, band[1], none)),
            )
            edges.append([a.astype(jnp.float32) + b.astype(jnp.float32) for a, b in sides])
        turned = dot_nn(band_ref[head], flip_ref[...])
        turned = jnp.concatenate(
            [
                pltpu.roll(turned[rows, :], TILE // 2, 1, stride=1, stride_axis=0).astype(jnp.bfloat16)
                for _, rows in row_tiles(rows_n)
            ],
            axis=0,
        )
        marked = dot_nn(ds_ref[head], keys_marked)
        near_part = dot_nn(turned, rev_ref[...])
        outs = []
        for tile, rows in row_tiles(rows_n):
            weights = [jnp.zeros((1, TILE), jnp.float32)] * 2
            for c, spot in enumerate(chunk_plan(tile, chunks)):
                near = wrapped_band(c, tile, chunks, own)
                if spot is not None and near is None:
                    continue
                left = far_left(c, tile, chunks, own)
                far = 1.0 if spot is None else jnp.where(near, 0.0, 1.0)
                for side, on in enumerate((left, jnp.logical_not(left))):
                    here = jnp.where(on, far, 0.0)
                    weights[side] = weights[side] + jnp.where(lane == c, here, 0.0)
            sums = marked[rows, TILE:]
            before, after = [
                jnp.sum(sums * weight + edge, axis=1, keepdims=True)
                for weight, edge in zip(weights, edges[tile])
            ]
            d_query = marked[rows, :TILE] + near_part[rows, :]
            d_query = d_query + before * rev_ref[TILE - 1 : TILE, :].astype(jnp.float32)
            d_query = d_query + after * rev_ref[0:1, :].astype(jnp.float32)
            outs.append(d_query * 0.125)
        dqs.append(outs)
    for tile, rows in row_tiles(rows_n):
        dq_ref[rows, :] = jnp.where(low[rows, :], dqs[0][tile], dqs[1][tile]).astype(dq_ref.dtype)
    q_turned = jnp.transpose(q_pair)
    do_turned = jnp.transpose(do_pair)
    for which, (turned, kept) in enumerate(((q_turned, ds_ref), (do_turned, p_ref))):
        both = jnp.concatenate(
            [dot_nn(turned[head * HD : (head + 1) * HD, :], kept[head]) for head in range(2)], axis=0
        )
        both = jnp.transpose(both)
        own_out[which] = both[:rows_n]
        far_out[which] = both[rows_n:].astype(far_out.dtype)


def rel_tables(rel_table, keys_n):
    count = rel_table.shape[0]
    rows = jnp.concatenate([rel_table, jnp.broadcast_to(rel_table[-1:], (TILE - count, HD))])
    rows = jnp.concatenate([rows, rows], axis=1)
    wide = jnp.concatenate(
        [rows, jnp.broadcast_to(rows[:1], rows.shape), jnp.broadcast_to(rows[-1:], rows.shape)]
    )
    flip = jnp.arange(TILE)[:, None] + jnp.arange(TILE)[None, :] == TILE - 1
    marks = jnp.arange(keys_n)[:, None] // TILE == jnp.arange(TILE)[None, :]
    return wide, rows[::-1], flip.astype(jnp.bfloat16), marks.astype(jnp.bfloat16)


def pair_blocks(rows, width, group):
    pairs = width // (2 * HD)
    one = pl.BlockSpec((rows, 2 * HD), lambda h: (0, h))
    two = pl.BlockSpec((rows, 2 * HD), lambda h: (0, pairs + h))
    return pairs, one, [one] * group + [two] * group


def fixed(array):
    return pl.BlockSpec(array.shape, lambda h: (0, 0))


def attention_forward(own, query, kv, rel_wide):
    rows, width = query.shape
    pairs, block, kv_blocks = pair_blocks(rows, width, len(kv))
    size = rows * rows * len(kv) * width
    return pl.pallas_call(
        functools.partial(attn_fwd_kernel, len(kv)),
        grid=(pairs,),
        in_specs=[pl.BlockSpec(memory_space=pltpu.SMEM), block, fixed(rel_wide)] + kv_blocks,
        out_specs=[block, pl.BlockSpec((rows, 2 * TILE), lambda h: (0, h))],
        out_shape=[
            jax.ShapeDtypeStruct((rows, width), jnp.bfloat16),
            jax.ShapeDtypeStruct((rows, width // HD * TILE), jnp.float32),
        ],
        scratch_shapes=[
            pltpu.VMEM((2, rows, rows * len(kv)), jnp.float32),
            pltpu.VMEM((2, rows, WIDE), jnp.float32),
            pltpu.VMEM((2, rows, rows * len(kv)), jnp.bfloat16),
        ],
        compiler_params=pltpu.CompilerParams(vmem_limit_bytes=VMEM),
        cost_estimate=pl.CostEstimate(flops=12 * size, bytes_accessed=rows * width * 16, transcendentals=0),
        name="attention_forward",
    )(own, query, rel_wide, *kv, *kv)


def attention_backward(own, query, kv, d_out, log_total, tables):
    rows, width = query.shape
    keys_n = rows * len(kv)
    pairs, block, kv_blocks = pair_blocks(rows, width, len(kv))
    size = rows * keys_n * width
    return pl.pallas_call(
        functools.partial(attn_bwd_kernel, len(kv)),
        grid=(pairs,),
        in_specs=[pl.BlockSpec(memory_space=pltpu.SMEM), block, block]
        + [pl.BlockSpec((rows, 2 * TILE), lambda h: (0, h))]
        + [fixed(table) for table in tables]
        + kv_blocks,
        out_specs=[
            block,
            pl.BlockSpec((2, rows, 2 * HD), lambda h: (0, 0, h)),
            pl.BlockSpec((2, keys_n - rows, 2 * HD), lambda h: (0, 0, h)),
        ],
        out_shape=[
            jax.ShapeDtypeStruct((rows, width), jnp.bfloat16),
            jax.ShapeDtypeStruct((2, rows, width), jnp.float32),
            jax.ShapeDtypeStruct((2, keys_n - rows, width), jnp.bfloat16),
        ],
        scratch_shapes=[
            pltpu.VMEM((2, rows, keys_n), jnp.float32),
            pltpu.VMEM((2, rows, WIDE), jnp.float32),
            pltpu.VMEM((2, rows, keys_n), jnp.float32),
            pltpu.VMEM((2, rows, keys_n), jnp.bfloat16),
            pltpu.VMEM((2, rows, keys_n), jnp.bfloat16),
            pltpu.VMEM((2, rows, TILE), jnp.bfloat16),
        ],
        compiler_params=pltpu.CompilerParams(vmem_limit_bytes=VMEM),
        cost_estimate=pl.CostEstimate(flops=24 * size, bytes_accessed=rows * width * 32, transcendentals=0),
        name="attention_backward",
    )(own, query, d_out, log_total, *tables, *kv, *kv)


HBM = pl.BlockSpec(memory_space=pltpu.HBM)
SCALARS = pl.BlockSpec(memory_space=pltpu.SMEM)


def assemble_kernel(spans, count, places_ref, *refs):
    pieces, outs, sems = refs[:count], refs[count:-1], refs[-1]
    copies = [
        pltpu.make_async_copy(
            piece.at[:, pl.ds(begin, width)], out.at[places_ref[index]], sems.at[index, which]
        )
        for index, piece in enumerate(pieces)
        for which, (out, (begin, width)) in enumerate(zip(outs, spans))
    ]
    for copy in copies:
        copy.start()
    for copy in copies:
        copy.wait()


def assemble(places, pieces, widths):
    rows, count = pieces[0].shape[0], len(pieces)
    spans = [(sum(widths[:k]), width) for k, width in enumerate(widths)]
    outs = pl.pallas_call(
        functools.partial(assemble_kernel, spans, count),
        in_specs=[SCALARS] + [HBM] * count,
        out_specs=[pl.BlockSpec(memory_space=pltpu.VMEM)] * len(spans),
        out_shape=[jax.ShapeDtypeStruct((count, rows, w), pieces[0].dtype) for w in widths],
        scratch_shapes=[pltpu.SemaphoreType.DMA((count, len(spans)))],
        compiler_params=pltpu.CompilerParams(vmem_limit_bytes=20 * 1024 * 1024),
        cost_estimate=pl.CostEstimate(
            flops=0, bytes_accessed=4 * count * rows * sum(widths), transcendentals=0
        ),
        name="assemble",
    )(places, *pieces)
    return [out.reshape(count * rows, out.shape[2]) for out in outs]


class Gather:
    def __init__(self):
        self.chips = lax.axis_size("chip")
        side = math.isqrt(self.chips)
        self.first, self.second = (side, side) if side * side == self.chips else (self.chips, 1)
        chip, core = lax.axis_index("chip"), lax.axis_index("core")
        places = []
        for owner in (core, 1 - core):
            for early, late in self.steps():
                one = self.moved(chip, early, late)
                two = self.moved(chip, late, early)
                places.append(jnp.where(owner == 0, one, two) * 2 + owner)
        self.places = jnp.stack(places).astype(jnp.int32)

    def steps(self):
        steps = [(early, 0) for early in range(self.first)]
        steps += [(0, late) for late in range(1, self.second)]
        return steps + [(e, l) for l in range(1, self.second) for e in range(1, self.first)]

    def moved(self, chip, along_first, along_second):
        return chip ^ (along_first * self.second + along_second)

    def hop(self, block, early, late):
        route = []
        for chip in range(self.chips):
            route.append((self.moved(chip, early, late) * 2, chip * 2))
            route.append((self.moved(chip, late, early) * 2 + 1, chip * 2 + 1))
        return lax.ppermute(block, ("chip", "core"), route)

    def stages(self, shards, used):
        swap = lambda block: lax.ppermute(block, "core", [(0, 1), (1, 0)])
        collect = lambda shard: lax.all_gather(shard, ("fz", "fh"), axis=0, tiled=True)
        count = len(shards)
        shards = list(shards)
        blocks = [collect(shard) for shard in shards[:3]]
        kept, traded, last = [[] for _ in shards], [[] for _ in shards], []
        complete = 0
        for turn in range(count + 1):
            onward = kept[turn - 1][1 : self.first] if turn else []
            if turn > 1:
                late, due = kept[turn - 2], blocks[turn : turn + 1]
                self.held = yield [kept[which] + traded[which] for which in range(complete)]
                (onward, late, due), last, self.held = lax.optimization_barrier(
                    ((onward, late, due), last, list(self.held))
                )
                blocks[turn : turn + 1] = due
                further = [self.hop(block, 0, step) for step in range(1, self.second) for block in onward]
                kept[turn - 1] = kept[turn - 1] + further
                traded[turn - 2] = [swap(block) for block in late]
                last = further + traded[turn - 2]
                complete += 1
            self.held = yield [kept[which] + traded[which] for which in range(complete)]
            if turn < count:
                fresh = blocks[turn][:, : used[turn]]
                coming = shards[turn + 3 : turn + 4]
                (fresh, onward, coming), last, self.held = lax.optimization_barrier(
                    ((fresh, onward, coming), last, list(self.held))
                )
                blocks += [collect(shard) for shard in coming]
                early = [self.hop(fresh, step, 0) for step in range(1, self.first)]
                other = [self.hop(fresh, 0, step) for step in range(1, self.second)]
                kept[turn] = [fresh] + early + other
                last = early + other
                if turn == 1:
                    further = [self.hop(block, 0, step) for step in range(1, self.second) for block in onward]
                    kept[0] = kept[0] + further
                    last = last + further
            else:
                late, last, self.held = lax.optimization_barrier((kept[-1], last, list(self.held)))
                traded[-1] = [swap(block) for block in late]
        yield [own + other for own, other in zip(kept, traded)]


VMEM_SPEC = pl.BlockSpec(memory_space=pltpu.VMEM)
TALL = 512


def dot_tn(a, b):
    return lax.dot_general(a, b, (((0,), (0,)), ((), ())), preferred_element_type=jnp.float32)


def norm_rows(field):
    centred = field - jnp.mean(field, -1, keepdims=True)
    rate = lax.rsqrt(jnp.mean(centred * centred, -1, keepdims=True) + EPSILON)
    return centred * rate, rate


def norm_back(grad, gain, normed, rate):
    scaled = grad * gain
    inner = jnp.mean(scaled * normed, -1, keepdims=True)
    return (scaled - jnp.mean(scaled, -1, keepdims=True) - normed * inner) * rate


def each_rows(rows, step, body):
    def one(index, carry):
        body(pl.ds(pl.multiple_of(index * step, step), step))
        return carry

    lax.fori_loop(0, rows // step, one, 0)


def shape_of(rows, width, dtype=jnp.bfloat16):
    return jax.ShapeDtypeStruct((rows, width), dtype)


class Weight:
    def __init__(self, places, pieces, begin, width):
        self.places, self.pieces, self.begin, self.width = places, pieces, begin, width
        self.depth = sum(piece.shape[0] for piece in pieces)
        self.block = self.depth // places.shape[0]
        self.count = len(pieces)
        self.bytes = 2 * self.depth * width

    def blocks(self, pieces):
        return [
            piece.at[pl.ds(begin, self.block)]
            for piece in pieces
            for begin in range(0, piece.shape[0], self.block)
        ]

    def loads(self, places_ref, pieces, store, sems, runs):
        copies = []
        for tile, spans in enumerate(runs):
            here = []
            for which, (begin, span) in enumerate(spans):
                for index, piece in enumerate(self.blocks(pieces)):
                    row = pl.multiple_of(places_ref[index] * self.block, self.block)
                    here.append(
                        pltpu.make_async_copy(
                            piece.at[:, pl.ds(self.begin + begin, span)],
                            store.at[pl.ds(row, self.block), pl.ds(begin, span)],
                            sems.at[tile, which, index],
                        )
                    )
            copies.append(here)
        for here in copies:
            for copy in here:
                copy.start()
        return copies

    def scratch(self, runs):
        return [
            pltpu.VMEM((self.depth, self.width), jnp.bfloat16),
            pltpu.SemaphoreType.DMA((len(runs), len(runs[0]), self.depth // self.block)),
        ]


def fused(kernel, name, weight, runs, scratch, outs, *operands):
    moved = sum(math.prod(item.shape) * item.dtype.itemsize for item in (*operands, *outs))
    rows = operands[0].shape[0]

    def body(places_ref, *refs):
        kernel(places_ref, refs[: weight.count], *refs[weight.count :])

    return pl.pallas_call(
        body,
        in_specs=[SCALARS] + [HBM] * weight.count + [VMEM_SPEC] * len(operands),
        out_specs=[VMEM_SPEC] * len(outs),
        out_shape=outs,
        scratch_shapes=weight.scratch(runs) + scratch,
        compiler_params=pltpu.CompilerParams(vmem_limit_bytes=weight.bytes + 14 * 1024 * 1024),
        cost_estimate=pl.CostEstimate(
            flops=rows * weight.bytes, bytes_accessed=moved + weight.bytes, transcendentals=0
        ),
        name=name,
    )(weight.places, *weight.pieces, *operands)


def wait_all(copies):
    for here in copies:
        for copy in here:
            copy.wait()


def wide_kernel(kind, weight, runs, places_ref, pieces, u_ref, down_ref, up_ref, z_ref, *rest):
    outs, (store, sems) = rest[:-2], rest[-2:]
    copies = weight.loads(places_ref, pieces, store, sems, runs)
    z_ref[...] = dot_nt(u_ref[...], down_ref[...]).astype(jnp.bfloat16)
    wait_all(copies)
    for spans in runs:
        result = [
            dot_nn(u_ref[...], store[:, begin : begin + span])
            + dot_nn(z_ref[...], up_ref[:, begin : begin + span])
            for begin, span in spans
        ]
        at = slice(spans[0][0], spans[0][0] + spans[0][1])
        if kind == "silu":
            gate = jax.nn.sigmoid(result[0])
            active = result[0] * gate
            outs[0][:, at] = active.astype(jnp.bfloat16)
            outs[1][:, at] = (gate + active * (1.0 - gate)).astype(jnp.bfloat16)
        elif kind == "glu":
            gate = jax.nn.sigmoid(result[1])
            gated = result[0] * gate
            outs[0][:, at] = gated.astype(jnp.bfloat16)
            outs[1][:, at] = gate.astype(jnp.bfloat16)
            outs[2][:, at] = (gated * (1.0 - gate)).astype(jnp.bfloat16)
        else:
            which = min(at.start // outs[0].shape[1], 1)
            first = which * outs[0].shape[1]
            outs[which][:, at.start - first : at.stop - first] = result[0].astype(jnp.bfloat16)


def project_wide(kind, inputs, weight, down, up):
    rows = inputs.shape[0]
    width = weight.width
    out_width = width // 2 if kind == "glu" else width
    sizes = {"silu": [width] * 2, "glu": [out_width] * 3, "plain": [width // 3, width - width // 3]}[kind]
    span = min(TALL, out_width)
    runs = [[(base + begin, span) for base in range(0, width, out_width)] for begin in range(0, out_width, span)]
    return fused(
        functools.partial(wide_kernel, kind, weight, runs), "project_" + kind, weight, runs, [],
        [shape_of(rows, down.shape[0])] + [shape_of(rows, size) for size in sizes],
        inputs, down, up,
    )


def narrow_kernel(factor, weight, runs, places_ref, pieces, u_ref, down_ref, up_ref, field_ref, gain_ref,
                  bias_ref, z_ref, field_out, normed_out, store, sems):
    copies = weight.loads(places_ref, pieces, store, sems, runs)
    z_ref[...] = dot_nt(u_ref[...], down_ref[...]).astype(jnp.bfloat16)
    wait_all(copies)
    for ((begin, span),) in runs:
        at = slice(begin, begin + span)
        result = dot_nn(u_ref[...], store[:, at]) + dot_nn(z_ref[...], up_ref[:, at])
        field_out[:, at] = field_ref[:, at].astype(jnp.float32) + factor * result
    gain, bias = gain_ref[...], bias_ref[...]

    def finish(at):
        normed_out[at, :] = (norm_rows(field_out[at, :])[0] * gain + bias).astype(jnp.bfloat16)

    each_rows(u_ref.shape[0], 128, finish)


def project_narrow(inputs, weight, down, up, field, gain, bias, factor):
    rows, width = inputs.shape[0], weight.width
    span = min(TALL, width)
    runs = [[(begin, span)] for begin in range(0, width, span)]
    return fused(
        functools.partial(narrow_kernel, factor, weight, runs), "project_next", weight, runs, [],
        [shape_of(rows, down.shape[0]), shape_of(rows, width, jnp.float32), shape_of(rows, width)],
        inputs, down, up, field, gain, bias,
    )


def adapter_grads(grad_ref, z_ref, up_ref, u_ref, dz_ref, da_ref, db_ref):
    dz_ref[...] = dot_nt(grad_ref[...], up_ref[...]).astype(jnp.bfloat16)
    db_ref[...] = dot_tn(z_ref[...], grad_ref[...]).astype(jnp.bfloat16)
    da_ref[...] = dot_tn(dz_ref[...], u_ref[...]).astype(jnp.bfloat16)


def field_back_kernel(kind, weight, runs, share_count, places_ref, pieces, d_ref, down_ref, up_ref, u_ref, z_ref, *rest):
    extra = {"norm": 3, "conv": 3, "plain": 0}[kind]
    shares, rest = rest[:share_count], rest[share_count:]
    extras, (out_ref, da_ref, db_ref, store, sems, grad, dz, d_inputs) = rest[:extra], rest[extra:]
    copies = weight.loads(places_ref, pieces, store, sems, runs)
    if shares:
        width = d_ref.shape[1]
        grad[:, :width] = d_ref[...]
        for which in range(2):
            total = shares[0][which]
            for share in shares[1:]:
                total = total + share[which].astype(jnp.float32)
            grad[:, (1 + which) * width : (2 + which) * width] = total.astype(jnp.bfloat16)
    elif d_ref.dtype == jnp.bfloat16:
        grad = d_ref
    else:
        grad[...] = d_ref[...].astype(jnp.bfloat16)
    adapter_grads(grad, z_ref, up_ref, u_ref, dz, da_ref, db_ref)
    wait_all(copies)
    tall = min(TALL, weight.depth)
    for begin in range(0, weight.depth, tall):
        at = slice(begin, begin + tall)
        result = dot_nt(grad[...], store[at, :]) + dot_nn(dz[...], down_ref[:, at])
        if kind == "plain":
            out_ref[:, at] = result.astype(out_ref.dtype)
        else:
            d_inputs[:, at] = result

    def finish(at):
        if kind == "norm":
            prior_ref, field_ref, gain_ref = extras
            normed, rate = norm_rows(field_ref[at, :].astype(jnp.float32))
            moved = norm_back(d_inputs[at, :], gain_ref[...], normed, rate)
            out_ref[at, :] = (prior_ref[at, :] + moved).astype(out_ref.dtype)
        else:
            field_ref, gain_ref, bias_ref = extras
            gain = gain_ref[...]
            normed, rate = norm_rows(field_ref[at, :])
            shifted = normed * gain + bias_ref[...]
            gate = jax.nn.sigmoid(shifted)
            slope = gate + shifted * gate * (1.0 - gate)
            out_ref[at, :] = norm_back(d_inputs[at, :] * slope, gain, normed, rate)

    if kind != "plain":
        each_rows(d_ref.shape[0], 128, finish)


def field_back(
    kind, grad, weight, down, up, inputs, slot_acts, extras=(), out_dtype=jnp.float32, shares=()
):
    rows, width = grad.shape[0], weight.width
    depth, rank = weight.depth, down.shape[0]
    runs = [[(0, width)]]
    scratch = shares or grad.dtype != jnp.bfloat16
    return fused(
        functools.partial(field_back_kernel, kind, weight, runs, len(shares)), "field_back_" + kind, weight, runs,
        [
            pltpu.VMEM((rows, width) if scratch else (16, 128), jnp.bfloat16),
            pltpu.VMEM((rows, rank), jnp.bfloat16),
            pltpu.VMEM((rows, depth) if kind != "plain" else (8, 128), jnp.float32),
        ],
        [shape_of(rows, depth, out_dtype), shape_of(rank, depth), shape_of(rank, width)],
        grad, down, up, inputs, slot_acts, *shares, *extras,
    )


class Pair:
    def __init__(self, *weights):
        self.weights = weights
        self.places = weights[0].places
        self.pieces = [piece for weight in weights for piece in weight.pieces]
        self.bytes = sum(weight.bytes for weight in weights)

    def split(self, refs):
        middle = self.weights[0].count
        return refs[:middle], refs[middle:]


def pair_call(kernel, name, pair, hbm_in, vmem_in, outs, hbm_out, scratch, limit):
    rows = vmem_in[0].shape[0]
    moved = sum(math.prod(x.shape) * x.dtype.itemsize for x in (*hbm_in, *vmem_in, *outs))

    def body(places_ref, *refs):
        count = len(pair.pieces)
        kernel(places_ref, *pair.split(refs[:count]), *refs[count:])

    return pl.pallas_call(
        body,
        in_specs=[SCALARS] + [HBM] * (len(pair.pieces) + len(hbm_in)) + [VMEM_SPEC] * len(vmem_in),
        out_specs=[HBM] * hbm_out + [VMEM_SPEC] * (len(outs) - hbm_out),
        out_shape=outs,
        scratch_shapes=scratch,
        compiler_params=pltpu.CompilerParams(vmem_limit_bytes=limit),
        cost_estimate=pl.CostEstimate(
            flops=rows * pair.bytes, bytes_accessed=moved + pair.bytes, transcendentals=0
        ),
        name=name,
    )(pair.places, *pair.pieces, *hbm_in, *vmem_in)


def ffn_kernel(up, down, places_ref, up_pieces, down_pieces,
               u_ref, a_up_ref, b_up_ref, a_down_ref, b_down_ref, field_ref, gain_ref, bias_ref, cot_ref,
               act_out, slope_out, z_up_ref, z_down_ref, d_out, normed_out,
               up_store, up_sems, down_store, down_sems, act, slope, out_sems):
    whole_up, whole_down = [[(0, up.width)]], [[(0, down.width)]]
    up_copies = up.loads(places_ref, up_pieces, up_store, up_sems, whole_up)
    z_up_ref[...] = dot_nt(u_ref[...], a_up_ref[...]).astype(jnp.bfloat16)
    wait_all(up_copies)
    down_copies = down.loads(places_ref, down_pieces, down_store, down_sems, whole_down)
    leaving = []
    for begin in range(0, up.width, TALL):
        at = slice(begin, begin + TALL)
        hidden = dot_nn(u_ref[...], up_store[:, at]) + dot_nn(z_up_ref[...], b_up_ref[:, at])
        gate = jax.nn.sigmoid(hidden)
        active = hidden * gate
        act[:, at] = active.astype(jnp.bfloat16)
        slope[:, at] = (gate + active * (1.0 - gate)).astype(jnp.bfloat16)
    for which, (held, out) in enumerate(((act, act_out), (slope, slope_out))):
        leaving.append(pltpu.make_async_copy(held, out, out_sems.at[which]))
        leaving[-1].start()
    z_down_ref[...] = dot_nt(act[...], a_down_ref[...]).astype(jnp.bfloat16)
    wait_all(down_copies)
    for begin in range(0, down.width, TALL):
        at = slice(begin, begin + TALL)
        result = dot_nn(act[...], down_store[:, at]) + dot_nn(z_down_ref[...], b_down_ref[:, at])
        d_out[:, at] = field_ref[:, at] + 0.5 * result
    gain, bias = gain_ref[...], bias_ref[...]

    def finish(at):
        normed, rate = norm_rows(d_out[at, :])
        normed_out[at, :] = (normed * gain + bias).astype(jnp.bfloat16)
        d_out[at, :] = norm_back(cot_ref[at, :].astype(jnp.float32), gain, normed, rate)

    each_rows(u_ref.shape[0], 128, finish)
    for copy in leaving:
        copy.wait()


def feed_forward_last(inputs, up, down, factors, field, gain, bias, cotangent):
    rows, width = inputs.shape
    a_up, b_up, a_down, b_down = factors
    rank, hidden = a_up.shape[0], up.width
    return pair_call(
        functools.partial(ffn_kernel, up, down), "feed_forward_last", Pair(up, down), [],
        [inputs, a_up, b_up, a_down, b_down, field, gain, bias, cotangent],
        [shape_of(rows, hidden)] * 2
        + [shape_of(rows, rank)] * 2
        + [shape_of(rows, width, jnp.float32), shape_of(rows, width)],
        2,
        up.scratch([[(0, hidden)]]) + down.scratch([[(0, width)]])
        + [pltpu.VMEM((rows, hidden), jnp.bfloat16)] * 2 + [pltpu.SemaphoreType.DMA((2,))],
        up.bytes + down.bytes + 24 * 1024 * 1024,
    )


def ffn_back_kernel(up, down, places_ref, up_pieces, down_pieces, act_ref, slope_ref,
                    d_ref, a_up_ref, b_up_ref, a_down_ref, b_down_ref, z_up_ref, z_down_ref, u_ref,
                    field_ref, gain_ref,
                    out_ref, da_up_ref, db_up_ref, da_down_ref, db_down_ref,
                    up_store, up_sems, down_store, down_sems, act, slope, in_sems,
                    grad, dz, d_hidden, d_inputs):
    whole_up, whole_down = [[(0, up.width)]], [[(0, down.width)]]
    down_copies = down.loads(places_ref, down_pieces, down_store, down_sems, whole_down)
    coming = [
        pltpu.make_async_copy(ref, held, in_sems.at[which])
        for which, (ref, held) in enumerate(((slope_ref, slope), (act_ref, act)))
    ]
    coming[0].start()
    grad[...] = (0.5 * d_ref[...]).astype(jnp.bfloat16)
    dz[...] = dot_nt(grad[...], b_down_ref[...]).astype(jnp.bfloat16)
    db_down_ref[...] = dot_tn(z_down_ref[...], grad[...]).astype(jnp.bfloat16)
    wait_all(down_copies)
    coming[0].wait()
    coming[1].start()
    up_copies = up.loads(places_ref, up_pieces, up_store, up_sems, whole_up)
    for begin in range(0, down.depth, TALL):
        at = slice(begin, begin + TALL)
        result = dot_nt(grad[...], down_store[at, :]) + dot_nn(dz[...], a_down_ref[:, at])
        d_hidden[:, at] = (result * slope[:, at].astype(jnp.float32)).astype(jnp.bfloat16)
    coming[1].wait()
    da_down_ref[...] = dot_tn(dz[...], act[...]).astype(jnp.bfloat16)
    dz[...] = dot_nt(d_hidden[...], b_up_ref[...]).astype(jnp.bfloat16)
    wait_all(up_copies)
    for begin in range(0, up.depth, TALL):
        at = slice(begin, begin + TALL)
        d_inputs[:, at] = dot_nt(d_hidden[...], up_store[at, :]) + dot_nn(dz[...], a_up_ref[:, at])
    db_up_ref[...] = dot_tn(z_up_ref[...], d_hidden[...]).astype(jnp.bfloat16)
    da_up_ref[...] = dot_tn(dz[...], u_ref[...]).astype(jnp.bfloat16)

    def finish(at):
        normed, rate = norm_rows(field_ref[at, :].astype(jnp.float32))
        moved = norm_back(d_inputs[at, :], gain_ref[...], normed, rate)
        out_ref[at, :] = (d_ref[at, :] + moved).astype(out_ref.dtype)

    each_rows(d_ref.shape[0], 128, finish)


def feed_forward_back(d_field, up, down, factors, kept, field, gain, out_dtype):
    rows, width = d_field.shape
    inputs, act, slope, z_up, z_down = kept
    a_up, b_up, a_down, b_down = factors
    rank, hidden = a_up.shape[0], up.width
    return pair_call(
        functools.partial(ffn_back_kernel, up, down), "feed_forward_back", Pair(up, down), [act, slope],
        [d_field, a_up, b_up, a_down, b_down, z_up, z_down, inputs, field, gain],
        [shape_of(rows, width, out_dtype), shape_of(rank, width), shape_of(rank, hidden)]
        + [shape_of(rank, hidden), shape_of(rank, width)],
        0,
        up.scratch([[(0, hidden)]]) + down.scratch([[(0, width)]])
        + [pltpu.VMEM((rows, hidden), jnp.bfloat16)] * 2
        + [
            pltpu.SemaphoreType.DMA((2,)),
            pltpu.VMEM((rows, width), jnp.bfloat16),
            pltpu.VMEM((rows, rank), jnp.bfloat16),
            pltpu.VMEM((rows, hidden), jnp.bfloat16),
            pltpu.VMEM((rows, width), jnp.float32),
        ],
        up.bytes + down.bytes + 28 * 1024 * 1024,
    )


HALO = 32


def taps_kernel(weight, runs, places_ref, *refs):
    pieces, (out_ref, store, sems) = refs[: weight.count], refs[weight.count :]
    wait_all(weight.loads(places_ref, pieces, store, sems, runs))
    out_ref[...] = jnp.transpose(store[...].astype(jnp.float32))[: out_ref.shape[0], :]


def gather_taps(weight):
    runs = [[(0, TILE)]]
    return pl.pallas_call(
        functools.partial(taps_kernel, weight, runs),
        in_specs=[SCALARS] + [HBM] * weight.count,
        out_specs=VMEM_SPEC,
        out_shape=jax.ShapeDtypeStruct((HALO, weight.depth), jnp.float32),
        scratch_shapes=weight.scratch(runs),
        compiler_params=pltpu.CompilerParams(vmem_limit_bytes=8 * 1024 * 1024),
        name="gather_taps",
    )(weight.places, *weight.pieces)


def slide(lanes, parts, shifted, taps_ref, shifts, rows, store):
    begin = 0
    for part in parts:
        shifted[0, begin : begin + part.shape[0], :] = part
        begin += part.shape[0]
    length = begin - 8
    for turn in range(1, 8):
        shifted[turn, 0:length, :] = shifted[0, turn : turn + length, :]
    step = 64
    for at in range(0, rows, step):
        total = None
        for tap, shift in enumerate(shifts):
            base = shift - shift % 8 + at
            term = shifted[shift % 8, base : base + step, :] * taps_ref[tap : tap + 1, lanes]
            total = term if total is None else total + term
        store(slice(at, at + step), total)


def each_tile(width, body):
    def one(index, carry):
        body(pl.ds(pl.multiple_of(index * TILE, TILE), TILE))
        return carry

    lax.fori_loop(0, width // TILE, one, 0)


def conv_kernel(val_ref, earlier_ref, taps_ref, gain_ref, bias_ref, conv_ref, act_ref, shifted):
    rows, width = val_ref.shape

    def one(lanes):
        parts = [earlier_ref[:, lanes].astype(jnp.float32), val_ref[:, lanes].astype(jnp.float32)]

        def store(at, total):
            conv_ref[at, lanes] = total

        shifts = [HALO - KERNEL + 1 + tap for tap in range(KERNEL)]
        slide(lanes, parts, shifted, taps_ref, shifts, rows, store)

    each_tile(width, one)

    def finish(at):
        shifted_field = norm_rows(conv_ref[at, :])[0] * gain_ref[...] + bias_ref[...]
        act_ref[at, :] = (shifted_field * jax.nn.sigmoid(shifted_field)).astype(jnp.bfloat16)

    each_rows(rows, 128, finish)


def conv_back_kernel(d_ref, later_ref, taps_ref, gate_ref, slope_ref, out_ref, shifted):
    rows, width = d_ref.shape

    def one(lanes):
        parts = [d_ref[:, lanes], later_ref[:, lanes].astype(jnp.float32)]
        high = pl.ds(pl.multiple_of(lanes.start + width, TILE), TILE)

        def store(at, total):
            out_ref[at, lanes] = (total * gate_ref[at, lanes].astype(jnp.float32)).astype(jnp.bfloat16)
            out_ref[at, high] = (total * slope_ref[at, lanes].astype(jnp.float32)).astype(jnp.bfloat16)

        slide(lanes, parts, shifted, taps_ref, [KERNEL - 1 - tap for tap in range(KERNEL)], rows, store)

    each_tile(width, one)


def conv_call(kernel, name, outs, rows, *operands):
    return pl.pallas_call(
        kernel,
        in_specs=[VMEM_SPEC] * len(operands),
        out_specs=[VMEM_SPEC] * len(outs),
        out_shape=outs,
        scratch_shapes=[pltpu.VMEM((8, rows + HALO, TILE), jnp.float32)],
        compiler_params=pltpu.CompilerParams(vmem_limit_bytes=16 * 1024 * 1024),
        cost_estimate=pl.CostEstimate(flops=0, bytes_accessed=32 * rows * operands[0].shape[1], transcendentals=0),
        name=name,
    )(*operands)


def conv_forward(value, earlier, taps, gain, bias):
    rows, width = value.shape
    outs = [shape_of(rows, width, jnp.float32), shape_of(rows, width)]
    return conv_call(conv_kernel, "conv_forward", outs, rows, value, earlier, taps, gain, bias)


def conv_backward(d_conv, later, taps, gate, slope):
    rows, width = d_conv.shape
    outs = [shape_of(rows, 2 * width)]
    return conv_call(conv_back_kernel, "conv_backward", outs, rows, d_conv, later, taps, gate, slope)[0]


class Layout:
    def __init__(self, together, fsdp):
        self.fsdp = fsdp
        self.inner = fsdp // together
        self.group = 2 * self.inner

    def place(self, core, f):
        return core * self.fsdp + f

    def round_route(self, turn):
        route = []
        for core in range(2):
            for f in range(self.fsdp):
                clip = (f % 2 + turn) % 2
                spot = f // 2
                target = self.place(spot % 2, (2 * core + clip) * self.inner + spot // 2)
                route.append((self.place(core, f), target))
        return route

    def gather_rows(self, blocks):
        parity = (lax.axis_index("fz") * self.inner + lax.axis_index("fh")) % 2
        clip = lax.axis_index("fz") % 2
        got = []
        for turn in range(2):
            sent = lax.dynamic_index_in_dim(blocks, (parity + turn) % 2, 0, keepdims=False)
            got.append(lax.ppermute(sent, ("core", "fz", "fh"), self.round_route(turn)))
        swap = clip == 1
        return jnp.concatenate(
            [jnp.where(swap, got[1], got[0]), jnp.where(swap, got[0], got[1])], axis=0
        )

    def scatter_rows(self, rows):
        parity = (lax.axis_index("fz") * self.inner + lax.axis_index("fh")) % 2
        clip = lax.axis_index("fz") % 2
        halves = rows.reshape(2, rows.shape[0] // 2, rows.shape[1])
        got = []
        for turn in range(2):
            sent = lax.dynamic_index_in_dim(halves, (clip + turn) % 2, 0, keepdims=False)
            route = [(target, source) for source, target in self.round_route(turn)]
            got.append(lax.ppermute(sent, ("core", "fz", "fh"), route))
        swap = parity == 1
        return jnp.stack([jnp.where(swap, got[1], got[0]), jnp.where(swap, got[0], got[1])])

    def spot_index(self, spot):
        return (spot % 2) * self.inner + spot // 2

    def from_spot(self, block, distance, cyclic):
        route = []
        for spot in range(self.group):
            source = spot + distance
            if cyclic:
                source %= self.group
            if 0 <= source < self.group:
                route.append((self.spot_index(source), self.spot_index(spot)))
        return lax.ppermute(block, ("core", "fh"), route)


def pack_adapters(ids, a_model, a_hidden, b_model, b_hidden):
    slots = a_model.shape[2]
    half = RANK // 2
    core = lax.axis_index("core")
    ranks = core * half + jnp.arange(half, dtype=jnp.int32)
    wanted = ids[:, None] * RANK + ranks[None, :]
    picker = (wanted[:, :, None] == jnp.arange(slots, dtype=jnp.int32)).astype(jnp.bfloat16)
    down = lambda a: jnp.einsum("jrs,pks->jprk", picker, a, preferred_element_type=jnp.float32)
    up = lambda b: jnp.einsum("jrs,psn->jprn", picker, b, preferred_element_type=jnp.float32)
    cut = a_hidden.shape[1] // a_model.shape[1]
    span = a_model.shape[1]

    def short(pack):
        rows = pack.reshape(pack.shape[0], pack.shape[1], half, cut, span)
        return jnp.swapaxes(rows, 2, 3).reshape(pack.shape[0], pack.shape[1] * cut, half, span)

    return jnp.concatenate(
        [down(a_model), up(b_model), short(down(a_hidden)), short(up(b_hidden))], axis=1
    ).astype(jnp.bfloat16)


def move_adapters(layout, pack, counts, cut):
    a_models, a_hiddens, b_models = counts
    core, half, span = lax.axis_index("core"), pack.shape[2], pack.shape[3]
    count = layout.fsdp
    here = lax.axis_index("fz") * layout.inner + lax.axis_index("fh")
    full = jnp.zeros(pack.shape[1:3] + (span * count,), jnp.bfloat16)
    for step in range(count):
        target = (here + step) % count
        piece = lax.dynamic_index_in_dim(pack, target // layout.inner, 0, keepdims=False)
        if step:
            route = [(f, (f + step) % count) for f in range(count)]
            piece = lax.ppermute(piece, ("fz", "fh"), route)
        source = (here - step) % count
        full = lax.dynamic_update_slice(full, piece, (0, 0, source * span))
    other = lax.ppermute(full, "core", [(0, 1), (1, 0)])
    low, high = jnp.where(core == 0, full, other), jnp.where(core == 0, other, full)
    full = jnp.concatenate([low, high], axis=1)
    models = a_models + b_models
    hidden = full[models:].reshape(-1, cut, RANK, count, span)
    hidden = jnp.transpose(hidden, (0, 2, 3, 1, 4)).reshape(-1, RANK, cut * count * span)
    return full[:a_models], hidden[:a_hiddens], full[a_models:models], hidden[a_hiddens:]


def pack_grads_kernel(models, fsdp, *refs):
    model_refs, hidden_refs, out_ref = refs[:models], refs[models:-1], refs[-1]
    _, count, _, lanes = out_ref.shape
    model = jnp.concatenate([ref[...].astype(jnp.float32) for ref in model_refs], axis=0)
    tiles = -(-model.shape[0] // TILE)
    if model.shape[0] % TILE:
        rest = jnp.zeros((tiles * TILE - model.shape[0], model.shape[1]), jnp.float32)
        model = jnp.concatenate([model, rest], axis=0)
    turned = [jnp.transpose(model[k * TILE : (k + 1) * TILE]).astype(jnp.bfloat16) for k in range(tiles)]
    share = model.shape[1] // (2 * count)
    for device in range(2 * count):
        chip, other = divmod(device, 2 * fsdp)
        core, f = divmod(other, fsdp)
        place = chip * fsdp + f
        row = 0
        for part in turned:
            out_ref[core, place, row : row + share, :] = part[device * share : (device + 1) * share]
            row += share
        for ref in hidden_refs:
            out_ref[core, place, row : row + RANK, :] = ref[:, device * lanes : (device + 1) * lanes]
            row += RANK


def pack_grads(model, hidden):
    devices, fsdp = lax.axis_size(EVERYWHERE), lax.axis_size("fz") * lax.axis_size("fh")
    width = model[0].shape[1]
    share, hidden_share = width // devices, hidden[0].shape[1] // devices
    groups = sum(part.shape[0] for part in model)
    tiles = -(-groups // TILE)
    if hidden_share == TILE and share % RANK == 0:
        rows = tiles * share + RANK * len(hidden)
        return pl.pallas_call(
            functools.partial(pack_grads_kernel, len(model), fsdp),
            in_specs=[VMEM_SPEC] * (len(model) + len(hidden)),
            out_specs=VMEM_SPEC,
            out_shape=jax.ShapeDtypeStruct((2, devices // 2, rows, TILE), jnp.bfloat16),
            compiler_params=pltpu.CompilerParams(vmem_limit_bytes=16 * 1024 * 1024),
            name="pack_grads",
        )(*model, *hidden)
    rest = jnp.zeros((tiles * TILE - groups, width), jnp.bfloat16)
    turned = jnp.concatenate([*model, rest]).T
    split = jnp.concatenate(hidden).reshape(-1, devices, hidden_share)
    parts = [turned[:, k * TILE : (k + 1) * TILE].reshape(devices, share, TILE) for k in range(tiles)]
    parts.append(jnp.transpose(split, (1, 0, 2)).reshape(devices, -1, TILE))
    part = jnp.concatenate(parts, axis=1).reshape(devices // (2 * fsdp), 2, fsdp, -1, TILE)
    return jnp.swapaxes(part, 0, 1).reshape(2, devices // 2, -1, TILE)


def send_grads(model, hidden):
    part = pack_grads(model, hidden)
    core = lax.axis_index("core")
    ours = lax.dynamic_index_in_dim(part, core, 0, keepdims=False)
    theirs = lax.dynamic_index_in_dim(part, 1 - core, 0, keepdims=False)
    came = lax.ppermute(theirs, "core", [(0, 1), (1, 0)])
    both = (ours.astype(jnp.float32) + came.astype(jnp.float32)).astype(jnp.bfloat16)
    got = lax.all_to_all(both, ("chip", "fz", "fh"), 0, 0, tiled=True)
    devices = lax.axis_size(EVERYWHERE)
    share, hidden_share = model[0].shape[1] // devices, hidden[0].shape[1] // devices
    tiles = -(-sum(item.shape[0] for item in model) // TILE)
    return got[:, : tiles * share], got[:, tiles * share :].reshape(-1, RANK * len(hidden), hidden_share)


def place_grads_kernel(groups, ids_ref, model_ref, hidden_ref, model_out, hidden_out):
    model_out[...] = jnp.zeros_like(model_out)
    hidden_out[...] = jnp.zeros_like(hidden_out)
    share = model_out.shape[1]
    slot = lax.broadcasted_iota(jnp.int32, (share, TILE), 1) // RANK
    in_tile = TILE // RANK

    def one(sender, carry):
        owner = ids_ref[sender]
        for group in range(groups):
            tile, local_group = divmod(group, in_tile)
            block = model_ref[sender, tile * share : (tile + 1) * share, :].astype(jnp.float32)
            turn = lax.rem(owner - local_group + in_tile, in_tile) * RANK
            block = jnp.where(slot == owner, pltpu.roll(block, turn, 1), 0.0)
            model_out[group] += block
        at = pl.ds(pl.multiple_of(owner * RANK, RANK), RANK)
        for group in range(hidden_out.shape[0]):
            rows = hidden_ref[sender, group * RANK : (group + 1) * RANK, :]
            hidden_out[group, at, :] += rows.astype(jnp.float32)
        return carry

    lax.fori_loop(0, model_ref.shape[0], one, 0)


def place_grads(ids, model, hidden, groups, slots):
    share = model.shape[1] // -(-groups * RANK // TILE)
    return pl.pallas_call(
        functools.partial(place_grads_kernel, groups),
        in_specs=[SCALARS, VMEM_SPEC, VMEM_SPEC],
        out_specs=[VMEM_SPEC, VMEM_SPEC],
        out_shape=[
            jax.ShapeDtypeStruct((groups, share, slots), jnp.float32),
            jax.ShapeDtypeStruct((hidden.shape[1] // RANK, slots, hidden.shape[2]), jnp.float32),
        ],
        compiler_params=pltpu.CompilerParams(vmem_limit_bytes=16 * 1024 * 1024),
        name="place_grads",
    )(ids, model, hidden)


def local(
    frames,
    cotangent,
    adapter_ids,
    norm_gains,
    norm_biases,
    rel_table,
    w_up,
    w_down,
    w_qkv,
    w_out,
    w_pw1,
    w_depth,
    w_pw2,
    ad_a_model,
    ad_a_hidden,
    ad_b_model,
    ad_b_hidden,
):
    group_clips, frame_span, width = frames.shape
    together = 2 * group_clips
    layout = Layout(together, lax.axis_size("fz") * lax.axis_size("fh"))
    rows = 2 * frame_span
    slots = ad_a_model.shape[2]
    spot = lax.axis_index("fh") * 2 + lax.axis_index("core")
    own = (spot * (rows // TILE)).astype(jnp.int32).reshape(1)
    other_ids = lax.ppermute(adapter_ids, "core", [(0, 1), (1, 0)])
    at_zero = lax.axis_index("core") == 0
    near_ids = jnp.concatenate(
        [jnp.where(at_zero, adapter_ids, other_ids), jnp.where(at_zero, other_ids, adapter_ids)]
    )
    factors = (ad_a_model, ad_a_hidden, ad_b_model, ad_b_hidden)
    cut = ad_a_hidden.shape[1] // ad_a_model.shape[1]
    first_pack = pack_adapters(near_ids, *[factor[:1] for factor in factors])
    other_pack = pack_adapters(near_ids, *[factor[1:] for factor in factors])
    gather = Gather()
    taps = jnp.pad(w_depth.T, ((0, 0), (0, width - KERNEL)))
    shards = [
        w_up[0],
        w_down[0],
        jnp.concatenate([w_qkv, w_out], axis=1),
        jnp.concatenate([w_pw1, w_pw2, taps], axis=1),
        w_up[1],
        w_down[1],
    ]
    used = [shard.shape[1] for shard in shards]
    used[3] = 3 * width + TILE
    turns = gather.stages(shards, used)
    next(turns)

    def weight_of(units, which, begin=0, columns=None):
        return Weight(gather.places, units[which], begin, columns or used[which])

    gains = [norm_gains[index : index + 1] for index in range(6)]
    biases = [norm_biases[index : index + 1] for index in range(6)]

    turns.send([first_pack, other_pack])
    first_pack, other_pack = gather.held
    turns.send([frames, first_pack, other_pack, *rel_tables(rel_table, rows * layout.group)])
    frames, first_pack, other_pack, *tables = gather.held
    layer_in = layout.gather_rows(frames)
    turns.send([])
    first_four = move_adapters(layout, first_pack, (1, 1, 1), cut)
    units = turns.send([layer_in, *first_four])
    layer_in, *first_four = gather.held
    field = layer_in.astype(jnp.float32)
    first_in = (norm_rows(field)[0] * gains[0] + biases[0]).astype(jnp.bfloat16)
    a_up0, a_down0, b_down0, b_up0 = [factor[0] for factor in first_four]
    up0_w = weight_of(units, 0)
    z_up0, act_one, slope_one = project_wide("silu", first_in, up0_w, a_up0, b_up0)
    units = turns.send([act_one, slope_one, other_pack])
    act_one, slope_one, other_pack = gather.held
    counts = [factor.shape[0] - 1 for factor in factors[:3]]
    other_four = move_adapters(layout, other_pack, counts, cut)
    units = turns.send([])
    down0_w = weight_of(units, 1)
    z_down0, after_ffn, attn_in = project_narrow(
        act_one, down0_w, a_down0, b_down0, layer_in, gains[1], biases[1], 0.5
    )
    units = turns.send([after_ffn, attn_in, *other_four])
    after_ffn, attn_in, a_model, a_hidden, b_model, b_hidden = gather.held
    blank = jnp.zeros((RANK, width), jnp.bfloat16)
    qkv_down = a_model[0:3].reshape(3 * RANK, width)
    qkv_up = jnp.concatenate(
        [
            jnp.concatenate([b_model[0], blank, blank], axis=1),
            jnp.concatenate([blank, b_model[1], blank], axis=1),
            jnp.concatenate([blank, blank, b_model[2]], axis=1),
        ]
    )
    glu_up = jnp.concatenate([b_model[6], b_model[7]], axis=1)
    a_out, a_pw1, a_pw2, a_up1 = [a_model[index] for index in range(3, 7)]
    b_out, b_pw2, b_down1 = [b_model[index] for index in range(3, 6)]
    a_down1, b_up1 = a_hidden[0], b_hidden[0]
    units = turns.send([qkv_down, qkv_up, glu_up])
    qkv_down, qkv_up, glu_up = gather.held
    qkv_w, out_w = weight_of(units, 2, 0, 3 * width), weight_of(units, 2, 3 * width, width)
    z_qkv, query, own_kv = project_wide("plain", attn_in, qkv_w, qkv_down, qkv_up)
    units = turns.send([query, own_kv])
    query, own_kv = gather.held
    units = turns.send([])
    pw1_w, pw2_w = weight_of(units, 3, 0, 2 * width), weight_of(units, 3, 2 * width, width)
    taps = gather_taps(weight_of(units, 3, 3 * width, TILE))
    kv = [own_kv] + [layout.from_spot(own_kv, step, True) for step in range(1, layout.group)]
    mixed, log_total = attention_forward(own, query, kv, tables[0])
    turns.send([mixed, log_total])
    mixed, log_total = gather.held
    units = turns.send([])
    up1_w, down1_w = weight_of(units, 4), weight_of(units, 5)
    mixed, cotangent = lax.optimization_barrier((mixed, cotangent))
    d_out = layout.gather_rows(cotangent)
    z_out, after_attn, conv_in = project_narrow(
        mixed, out_w, a_out, b_out, after_ffn, gains[2], biases[2], 1.0
    )
    z_pw1, gated, gate, gate_slope = project_wide("glu", conv_in, pw1_w, a_pw1, glu_up)
    earlier = layout.from_spot(gated[rows - HALO :], -1, False)
    conv_out, conv_act = conv_forward(gated, earlier, taps, gains[3], biases[3])
    z_pw2, after_conv, second_in = project_narrow(
        conv_act, pw2_w, a_pw2, b_pw2, after_attn, gains[4], biases[4], 1.0
    )
    factors_two = (a_up1, b_up1, a_down1, b_down1)
    act_two, slope_two, z_up1, z_down1, d_fourth, result = feed_forward_last(
        second_in, up1_w, down1_w, factors_two, after_conv, gains[5], biases[5], d_out
    )
    layer_out = layout.scatter_rows(result)

    d_third, da_up1, db_up1, da_down1, db_down1 = feed_forward_back(
        d_fourth, up1_w, down1_w, factors_two, (second_in, act_two, slope_two, z_up1, z_down1),
        after_conv, gains[4], jnp.float32,
    )
    d_conv, da_pw2, db_pw2 = field_back(
        "conv", d_third, pw2_w, a_pw2, b_pw2, conv_act, z_pw2,
        (conv_out, gains[3], biases[3]),
    )
    d_conv, layer_out = lax.optimization_barrier((d_conv, layer_out))
    later = layout.from_spot(d_conv[:HALO].astype(jnp.bfloat16), 1, False)
    d_joined = conv_backward(d_conv, later, taps, gate, gate_slope)
    d_second, da_pw1, db_pw1 = field_back(
        "norm", d_joined, pw1_w, a_pw1, glu_up, conv_in, z_pw1, (d_third, after_attn, gains[2])
    )
    d_mixed, da_out, db_out = field_back(
        "plain", d_second, out_w, a_out, b_out, mixed, z_out, (), jnp.bfloat16
    )
    label = jnp.full((RANK, width), near_ids[lax.axis_index("fz")]).astype(jnp.bfloat16)
    early = send_grads(
        [da_out, da_pw1, da_pw2, da_up1, db_out, db_pw2, db_down1]
        + [db_pw1[:, :width], db_pw1[:, width:], label],
        [da_down1, db_up1],
    )
    d_query, d_own, d_far = attention_backward(own, query, kv, d_mixed, log_total, tables)
    shares = [d_own]
    for step in range(1, layout.group):
        shares.append(layout.from_spot(d_far[:, (step - 1) * rows : step * rows], -step, True))
    d_first, da_qkv, db_qkv = field_back(
        "norm", d_query, qkv_w, qkv_down, qkv_up, attn_in, z_qkv, (d_second, after_ffn, gains[1]),
        shares=shares,
    )
    db_three = [
        db_qkv[index * RANK : (index + 1) * RANK, index * width : (index + 1) * width]
        for index in range(3)
    ]
    grad_field, da_up0, db_up0, da_down0, db_down0 = feed_forward_back(
        d_first, up0_w, down0_w, (a_up0, b_up0, a_down0, b_down0),
        (first_in, act_one, slope_one, z_up0, z_down0), layer_in, gains[0], jnp.bfloat16,
    )
    grad_frames = layout.scatter_rows(grad_field)
    late = send_grads([da_up0, da_qkv, db_down0, *db_three], [da_down0, db_up0])
    ids = (early[0][:, early[0].shape[1] // 2, RANK] * jnp.bfloat16(0.5)).astype(jnp.int32)
    early_model, early_hidden = place_grads(ids, *early, 9, slots)
    late_model, late_hidden = place_grads(ids, *late, 8, slots)
    grad_a_model = jnp.concatenate([late_model[:4], early_model[:4]])
    grad_b_model = jnp.swapaxes(jnp.concatenate([late_model[4:], early_model[4:]]), 1, 2)
    grad_a_hidden = jnp.swapaxes(jnp.stack([late_hidden[0], early_hidden[0]]), 1, 2)
    grad_b_hidden = jnp.stack([late_hidden[1], early_hidden[1]])
    return (layer_out, grad_frames, grad_a_model, grad_a_hidden, grad_b_model, grad_b_hidden)


def solution(mesh):
    every = ("chip", "core", "fz", "fh")
    clips, spread = ("chip", "core"), ("fz", "fh")
    in_specs = (
        P(clips, spread, None),
        P(clips, spread, None),
        P(clips),
        P(),
        P(),
        P(),
        P(None, every, None),
        P(None, every, None),
        P(every, None),
        P(every, None),
        P(every, None),
        P(None, every),
        P(every, None),
        P(None, spread, None),
        P(None, spread, None),
        P(None, None, spread),
        P(None, None, spread),
    )
    out_specs = (
        P(clips, spread, None),
        P(clips, spread, None),
        P(None, every, None),
        P(None, every, None),
        P(None, None, every),
        P(None, None, every),
    )

    def run(frames, *rest):
        dp, fsdp = mesh.shape["dp"], mesh.shape["fsdp"]
        together = 2 * frames.shape[0] // dp
        cut = Mesh(
            mesh.devices.reshape(dp // 2, 2, together, fsdp // together), EVERYWHERE
        )
        return jax.shard_map(
            local, mesh=cut, in_specs=in_specs, out_specs=out_specs, check_vma=False
        )(frames, *rest)

    return run
```

```python
import functools
import math

import jax
import jax.numpy as jnp
from jax import lax
from jax.experimental import pallas as pl
from jax.experimental.pallas import tpu as pltpu
from jax.sharding import Mesh
from jax.sharding import PartitionSpec as P

HEADS = 16
KERNEL = 31
RANK = 16
EPSILON = 1e-05
PACK_ROOM = 56 * 1024 * 1024
EVERYWHERE = ("chip", "core", "fz", "fh")

HD = 64
REL_LEFT = 64
REL_RIGHT = 8
TILE = 128
WIDE = 3 * TILE
VMEM = 32 * 1024 * 1024


def dot_nn(a, b):
    return lax.dot_general(a, b, (((1,), (0,)), ((), ())), preferred_element_type=jnp.float32)


def dot_nt(a, b):
    return lax.dot_general(a, b, (((1,), (1,)), ((), ())), preferred_element_type=jnp.float32)


def chunk_plan(tile, chunks):
    return [{chunks - 1: 0, 0: 1, 1: 2}.get((c - tile) % chunks) for c in range(chunks)]


def far_left(c, tile, chunks, own):
    return jnp.logical_or(c + own >= chunks, c < tile)


def wrapped_band(c, tile, chunks, own):
    if tile == 0 and c == chunks - 1:
        return own > 0
    if c == tile + 1:
        return c + own < chunks
    return None


def tile_scores(scores, table, tile, own):
    near = pltpu.roll(table[:, :TILE], TILE // 2, 1, stride=1, stride_axis=0)
    first, last = table[:, TILE : 2 * TILE], table[:, 2 * TILE :]
    ahead = lane_ahead()
    bands = [
        jnp.where(ahead >= TILE // 2, near, first),
        jnp.where(ahead < -(TILE // 2), first, jnp.where(ahead >= TILE // 2, last, near)),
        jnp.where(ahead < -(TILE // 2), near, last),
    ]
    chunks = scores.shape[1] // TILE
    parts = []
    for c, spot in enumerate(chunk_plan(tile, chunks)):
        part = scores[:, c * TILE : (c + 1) * TILE]
        if spot is None:
            bias = first if c < tile else jnp.where(c + own >= chunks, first, last)
        else:
            bias = bands[spot]
            true_band = wrapped_band(c, tile, chunks, own)
            if true_band is not None:
                bias = jnp.where(true_band, bias, jnp.where(far_left(c, tile, chunks, own), first, last))
        parts.append(part + bias)
    return parts


def lane_ahead():
    lane = lax.broadcasted_iota(jnp.int32, (TILE, TILE), 1)
    return lane - lax.broadcasted_iota(jnp.int32, (TILE, TILE), 0)


def stacked(refs):
    return jnp.concatenate([ref[...] for ref in refs], axis=0)


def head_lanes(rows):
    low = lax.broadcasted_iota(jnp.int32, (rows, 2 * HD), 1) < HD
    return low, (low, jnp.logical_not(low))


def row_tiles(rows):
    return [(tile, slice(tile * TILE, (tile + 1) * TILE)) for tile in range(rows // TILE)]


def attn_fwd_kernel(group, own_ref, q_ref, rel_ref, *refs):
    own = own_ref[0]
    keys, values, rel_wide = stacked(refs[:group]), stacked(refs[group : 2 * group]), rel_ref[...]
    o_ref, lse_ref, s_ref, w_ref, p_ref = refs[2 * group :]
    rows_n = q_ref.shape[0]
    low, heads = head_lanes(rows_n)
    q_pair = q_ref[...] * jnp.bfloat16(0.125)
    for head, lanes in enumerate(heads):
        q_head = jnp.where(lanes, q_pair, jnp.zeros_like(q_pair))
        s_ref[head] = dot_nt(q_head, keys)
        w_ref[head] = dot_nt(q_head, rel_wide)
    ones = jnp.ones_like(values)
    values_ones = jnp.concatenate([values, ones], axis=1)
    outs = []
    for head in range(2):
        for tile, rows in row_tiles(rows_n):
            parts = tile_scores(s_ref[head, rows, :], w_ref[head, rows, :], tile, own)
            top = jnp.max(functools.reduce(jnp.maximum, parts), axis=1, keepdims=True)
            top = jnp.broadcast_to(top, (TILE, TILE))
            expo = [jnp.exp(part - top).astype(jnp.bfloat16) for part in parts]
            p_ref[head, rows, :] = jnp.concatenate(expo, axis=1)
            lse_ref[rows, head * TILE : (head + 1) * TILE] = top
        outs.append(dot_nn(p_ref[head], values_ones))
        total = outs[head][:, 2 * HD :]
        at = slice(head * TILE, (head + 1) * TILE)
        lse_ref[:, at] = lse_ref[:, at] + jnp.log(total)
        outs[head] = outs[head][:, : 2 * HD] / total
    o_ref[...] = jnp.where(low, outs[0], outs[1]).astype(jnp.bfloat16)


def attn_bwd_kernel(group, own_ref, q_ref, do_ref, lse_ref, rel_ref, rev_ref, flip_ref, mark_ref, *refs):
    own = own_ref[0]
    keys, values, rel_wide = stacked(refs[:group]), stacked(refs[group : 2 * group]), rel_ref[...]
    dq_ref, own_out, far_out, s_ref, w_ref, dp_ref, ds_ref, p_ref, band_ref = refs[2 * group :]
    rows_n, keys_n = q_ref.shape[0], keys.shape[0]
    chunks = keys_n // TILE
    low, heads = head_lanes(rows_n)
    lane = lax.broadcasted_iota(jnp.int32, (1, TILE), 1)
    q_pair = q_ref[...] * jnp.bfloat16(0.125)
    do_pair = do_ref[...]
    keys_marked = jnp.concatenate([keys, mark_ref[...]], axis=1)
    for head, lanes in enumerate(heads):
        q_head = jnp.where(lanes, q_pair, jnp.zeros_like(q_pair))
        s_ref[head] = dot_nt(q_head, keys)
        w_ref[head] = dot_nt(q_head, rel_wide)
        dp_ref[head] = dot_nt(jnp.where(lanes, do_pair, jnp.zeros_like(do_pair)), values)
    dqs = []
    ahead = lane_ahead()
    for head in range(2):
        edges = []
        for tile, rows in row_tiles(rows_n):
            log_total = lse_ref[rows, head * TILE : (head + 1) * TILE]
            parts = tile_scores(s_ref[head, rows, :], w_ref[head, rows, :], tile, own)
            probs = [jnp.exp(part - log_total) for part in parts]
            d_parts = [dp_ref[head, rows, c * TILE : (c + 1) * TILE] for c in range(chunks)]
            inner = functools.reduce(jnp.add, [p * d for p, d in zip(probs, d_parts)])
            inner = jnp.sum(inner, axis=1, keepdims=True)
            d_scores = [(p * (d - inner)).astype(jnp.bfloat16) for p, d in zip(probs, d_parts)]
            p_ref[head, rows, :] = jnp.concatenate([p.astype(jnp.bfloat16) for p in probs], axis=1)
            ds_ref[head, rows, :] = jnp.concatenate(d_scores, axis=1)
            band = [None, None, None]
            for c, spot in enumerate(chunk_plan(tile, chunks)):
                if spot is not None:
                    near = wrapped_band(c, tile, chunks, own)
                    piece = d_scores[c]
                    band[spot] = piece if near is None else jnp.where(near, piece, jnp.zeros_like(piece))
            behind, beyond = ahead < -(TILE // 2), ahead >= TILE // 2
            none = jnp.zeros_like(band[0])
            band_ref[head, rows, :] = jnp.where(beyond, band[0], jnp.where(behind, band[2], band[1]))
            sides = (
                (jnp.where(beyond, none, band[0]), jnp.where(behind, band[1], none)),
                (jnp.where(behind, none, band[2]), jnp.where(beyond, band[1], none)),
            )
            edges.append([a.astype(jnp.float32) + b.astype(jnp.float32) for a, b in sides])
        turned = dot_nn(band_ref[head], flip_ref[...])
        turned = jnp.concatenate(
            [
                pltpu.roll(turned[rows, :], TILE // 2, 1, stride=1, stride_axis=0).astype(jnp.bfloat16)
                for _, rows in row_tiles(rows_n)
            ],
            axis=0,
        )
        marked = dot_nn(ds_ref[head], keys_marked)
        near_part = dot_nn(turned, rev_ref[...])
        outs = []
        for tile, rows in row_tiles(rows_n):
            weights = [jnp.zeros((1, TILE), jnp.float32)] * 2
            for c, spot in enumerate(chunk_plan(tile, chunks)):
                near = wrapped_band(c, tile, chunks, own)
                if spot is not None and near is None:
                    continue
                left = far_left(c, tile, chunks, own)
                far = 1.0 if spot is None else jnp.where(near, 0.0, 1.0)
                for side, on in enumerate((left, jnp.logical_not(left))):
                    here = jnp.where(on, far, 0.0)
                    weights[side] = weights[side] + jnp.where(lane == c, here, 0.0)
            sums = marked[rows, TILE:]
            before, after = [
                jnp.sum(sums * weight + edge, axis=1, keepdims=True)
                for weight, edge in zip(weights, edges[tile])
            ]
            d_query = marked[rows, :TILE] + near_part[rows, :]
            d_query = d_query + before * rev_ref[TILE - 1 : TILE, :].astype(jnp.float32)
            d_query = d_query + after * rev_ref[0:1, :].astype(jnp.float32)
            outs.append(d_query * 0.125)
        dqs.append(outs)
    for tile, rows in row_tiles(rows_n):
        dq_ref[rows, :] = jnp.where(low[rows, :], dqs[0][tile], dqs[1][tile]).astype(dq_ref.dtype)
    q_turned = jnp.transpose(q_pair)
    do_turned = jnp.transpose(do_pair)
    for which, (turned, kept) in enumerate(((q_turned, ds_ref), (do_turned, p_ref))):
        both = jnp.concatenate(
            [dot_nn(turned[head * HD : (head + 1) * HD, :], kept[head]) for head in range(2)], axis=0
        )
        both = jnp.transpose(both)
        own_out[which] = both[:rows_n].astype(own_out.dtype)
        far_out[which] = both[rows_n:].astype(far_out.dtype)


def rel_tables(rel_table, keys_n):
    count = rel_table.shape[0]
    rows = jnp.concatenate([rel_table, jnp.broadcast_to(rel_table[-1:], (TILE - count, HD))])
    rows = jnp.concatenate([rows, rows], axis=1)
    wide = jnp.concatenate(
        [rows, jnp.broadcast_to(rows[:1], rows.shape), jnp.broadcast_to(rows[-1:], rows.shape)]
    )
    flip = jnp.arange(TILE)[:, None] + jnp.arange(TILE)[None, :] == TILE - 1
    marks = jnp.arange(keys_n)[:, None] // TILE == jnp.arange(TILE)[None, :]
    return wide, rows[::-1], flip.astype(jnp.bfloat16), marks.astype(jnp.bfloat16)


def pair_blocks(rows, width, group):
    pairs = width // (2 * HD)
    one = pl.BlockSpec((rows, 2 * HD), lambda h: (0, h))
    two = pl.BlockSpec((rows, 2 * HD), lambda h: (0, pairs + h))
    return pairs, one, [one] * group + [two] * group


def fixed(array):
    return pl.BlockSpec(array.shape, lambda h: (0, 0))


def attention_forward(own, query, kv, rel_wide):
    rows, width = query.shape
    pairs, block, kv_blocks = pair_blocks(rows, width, len(kv))
    size = rows * rows * len(kv) * width
    return pl.pallas_call(
        functools.partial(attn_fwd_kernel, len(kv)),
        grid=(pairs,),
        in_specs=[pl.BlockSpec(memory_space=pltpu.SMEM), block, fixed(rel_wide)] + kv_blocks,
        out_specs=[block, pl.BlockSpec((rows, 2 * TILE), lambda h: (0, h))],
        out_shape=[
            jax.ShapeDtypeStruct((rows, width), jnp.bfloat16),
            jax.ShapeDtypeStruct((rows, width // HD * TILE), jnp.float32),
        ],
        scratch_shapes=[
            pltpu.VMEM((2, rows, rows * len(kv)), jnp.float32),
            pltpu.VMEM((2, rows, WIDE), jnp.float32),
            pltpu.VMEM((2, rows, rows * len(kv)), jnp.bfloat16),
        ],
        compiler_params=pltpu.CompilerParams(vmem_limit_bytes=VMEM),
        cost_estimate=pl.CostEstimate(flops=12 * size, bytes_accessed=rows * width * 16, transcendentals=0),
        name="attention_forward",
    )(own, query, rel_wide, *kv, *kv)


def attention_backward(own, query, kv, d_out, log_total, tables):
    rows, width = query.shape
    keys_n = rows * len(kv)
    pairs, block, kv_blocks = pair_blocks(rows, width, len(kv))
    size = rows * keys_n * width
    return pl.pallas_call(
        functools.partial(attn_bwd_kernel, len(kv)),
        grid=(pairs,),
        in_specs=[pl.BlockSpec(memory_space=pltpu.SMEM), block, block]
        + [pl.BlockSpec((rows, 2 * TILE), lambda h: (0, h))]
        + [fixed(table) for table in tables]
        + kv_blocks,
        out_specs=[
            block,
            pl.BlockSpec((2, rows, 2 * HD), lambda h: (0, 0, h)),
            pl.BlockSpec((2, keys_n - rows, 2 * HD), lambda h: (0, 0, h)),
        ],
        out_shape=[
            jax.ShapeDtypeStruct((rows, width), jnp.bfloat16),
            jax.ShapeDtypeStruct((2, rows, width), jnp.bfloat16),
            jax.ShapeDtypeStruct((2, keys_n - rows, width), jnp.bfloat16),
        ],
        scratch_shapes=[
            pltpu.VMEM((2, rows, keys_n), jnp.float32),
            pltpu.VMEM((2, rows, WIDE), jnp.float32),
            pltpu.VMEM((2, rows, keys_n), jnp.float32),
            pltpu.VMEM((2, rows, keys_n), jnp.bfloat16),
            pltpu.VMEM((2, rows, keys_n), jnp.bfloat16),
            pltpu.VMEM((2, rows, TILE), jnp.bfloat16),
        ],
        compiler_params=pltpu.CompilerParams(vmem_limit_bytes=VMEM),
        cost_estimate=pl.CostEstimate(flops=24 * size, bytes_accessed=rows * width * 32, transcendentals=0),
        name="attention_backward",
    )(own, query, d_out, log_total, *tables, *kv, *kv)


HBM = pl.BlockSpec(memory_space=pltpu.HBM)
SCALARS = pl.BlockSpec(memory_space=pltpu.SMEM)


def assemble_kernel(spans, count, places_ref, *refs):
    pieces, outs, sems = refs[:count], refs[count:-1], refs[-1]
    copies = [
        pltpu.make_async_copy(
            piece.at[:, pl.ds(begin, width)], out.at[places_ref[index]], sems.at[index, which]
        )
        for index, piece in enumerate(pieces)
        for which, (out, (begin, width)) in enumerate(zip(outs, spans))
    ]
    for copy in copies:
        copy.start()
    for copy in copies:
        copy.wait()


def assemble(places, pieces, widths):
    rows, count = pieces[0].shape[0], len(pieces)
    spans = [(sum(widths[:k]), width) for k, width in enumerate(widths)]
    outs = pl.pallas_call(
        functools.partial(assemble_kernel, spans, count),
        in_specs=[SCALARS] + [HBM] * count,
        out_specs=[pl.BlockSpec(memory_space=pltpu.VMEM)] * len(spans),
        out_shape=[jax.ShapeDtypeStruct((count, rows, w), pieces[0].dtype) for w in widths],
        scratch_shapes=[pltpu.SemaphoreType.DMA((count, len(spans)))],
        compiler_params=pltpu.CompilerParams(vmem_limit_bytes=20 * 1024 * 1024),
        cost_estimate=pl.CostEstimate(
            flops=0, bytes_accessed=4 * count * rows * sum(widths), transcendentals=0
        ),
        name="assemble",
    )(places, *pieces)
    return [out.reshape(count * rows, out.shape[2]) for out in outs]


class Gather:
    def __init__(self):
        self.chips = lax.axis_size("chip")
        side = math.isqrt(self.chips)
        self.first, self.second = (side, side) if side * side == self.chips else (self.chips, 1)
        chip, core = lax.axis_index("chip"), lax.axis_index("core")
        places = []
        for owner in (core, 1 - core):
            for early, late in self.steps():
                one = self.moved(chip, early, late)
                two = self.moved(chip, late, early)
                places.append(jnp.where(owner == 0, one, two) * 2 + owner)
        self.places = jnp.stack(places).astype(jnp.int32)

    def steps(self):
        steps = [(early, 0) for early in range(self.first)]
        steps += [(0, late) for late in range(1, self.second)]
        return steps + [(e, l) for l in range(1, self.second) for e in range(1, self.first)]

    def moved(self, chip, along_first, along_second):
        return chip ^ (along_first * self.second + along_second)

    def hop(self, block, early, late):
        route = []
        for chip in range(self.chips):
            route.append((self.moved(chip, early, late) * 2, chip * 2))
            route.append((self.moved(chip, late, early) * 2 + 1, chip * 2 + 1))
        return lax.ppermute(block, ("chip", "core"), route)

    def stages(self, shards, used):
        swap = lambda block: lax.ppermute(block, "core", [(0, 1), (1, 0)])
        collect = lambda shard: lax.all_gather(shard, ("fz", "fh"), axis=0, tiled=True)
        count = len(shards)
        shards = list(shards)
        blocks = [collect(shard) for shard in shards[:3]]
        kept, traded, last = [[] for _ in shards], [[] for _ in shards], []
        complete = 0
        for turn in range(count + 1):
            onward = kept[turn - 1][1 : self.first] if turn else []
            if turn > 1:
                late, due = kept[turn - 2], blocks[turn : turn + 1] if turn > 2 else []
                self.held = yield [kept[which] + traded[which] for which in range(complete)]
                (onward, late, due), last, self.held = lax.optimization_barrier(
                    ((onward, late, due), last, list(self.held))
                )
                if due:
                    blocks[turn] = due[0]
                further = [self.hop(block, 0, step) for step in range(1, self.second) for block in onward]
                kept[turn - 1] = kept[turn - 1] + further
                traded[turn - 2] = [swap(block) for block in late]
                last = further + traded[turn - 2]
                complete += 1
            self.held = yield [kept[which] + traded[which] for which in range(complete)]
            if turn < count:
                fresh = blocks[turn][:, : used[turn]]
                coming = shards[turn + 3 : turn + 4]
                (fresh, onward, coming), last, self.held = lax.optimization_barrier(
                    ((fresh, onward, coming), last, list(self.held))
                )
                blocks += [collect(shard) for shard in coming]
                early = [self.hop(fresh, step, 0) for step in range(1, self.first)]
                other = [self.hop(fresh, 0, step) for step in range(1, self.second)]
                kept[turn] = [fresh] + early + other
                last = early + other
                if turn == 1:
                    further = [self.hop(block, 0, step) for step in range(1, self.second) for block in onward]
                    kept[0] = kept[0] + further
                    last = last + further
            else:
                late, last, self.held = lax.optimization_barrier((kept[-1], last, list(self.held)))
                traded[-1] = [swap(block) for block in late]
        yield [own + other for own, other in zip(kept, traded)]


VMEM_SPEC = pl.BlockSpec(memory_space=pltpu.VMEM)
TALL = 512


def dot_tn(a, b):
    return lax.dot_general(a, b, (((0,), (0,)), ((), ())), preferred_element_type=jnp.float32)


def norm_rows(field):
    centred = field - jnp.mean(field, -1, keepdims=True)
    rate = lax.rsqrt(jnp.mean(centred * centred, -1, keepdims=True) + EPSILON)
    return centred * rate, rate


def norm_back(grad, gain, normed, rate):
    scaled = grad * gain
    inner = jnp.mean(scaled * normed, -1, keepdims=True)
    return (scaled - jnp.mean(scaled, -1, keepdims=True) - normed * inner) * rate


def each_rows(rows, step, body):
    def one(index, carry):
        body(pl.ds(pl.multiple_of(index * step, step), step))
        return carry

    lax.fori_loop(0, rows // step, one, 0)


def shape_of(rows, width, dtype=jnp.bfloat16):
    return jax.ShapeDtypeStruct((rows, width), dtype)


class Weight:
    def __init__(self, places, pieces, begin, width):
        self.places, self.pieces, self.begin, self.width = places, pieces, begin, width
        self.depth = sum(piece.shape[0] for piece in pieces)
        self.block = self.depth // places.shape[0]
        self.count = len(pieces)
        self.bytes = 2 * self.depth * width

    def blocks(self, pieces):
        return [
            piece.at[pl.ds(begin, self.block)]
            for piece in pieces
            for begin in range(0, piece.shape[0], self.block)
        ]

    def loads(self, places_ref, pieces, store, sems, runs):
        copies = []
        for tile, spans in enumerate(runs):
            here = []
            for which, (begin, span) in enumerate(spans):
                for index, piece in enumerate(self.blocks(pieces)):
                    row = pl.multiple_of(places_ref[index] * self.block, self.block)
                    here.append(
                        pltpu.make_async_copy(
                            piece.at[:, pl.ds(self.begin + begin, span)],
                            store.at[pl.ds(row, self.block), pl.ds(begin, span)],
                            sems.at[tile, which, index],
                        )
                    )
            copies.append(here)
        for here in copies:
            for copy in here:
                copy.start()
        return copies

    def scratch(self, runs):
        return [
            pltpu.VMEM((self.depth, self.width), jnp.bfloat16),
            pltpu.SemaphoreType.DMA((len(runs), len(runs[0]), self.depth // self.block)),
        ]


def fused(kernel, name, weight, runs, scratch, outs, *operands):
    moved = sum(math.prod(item.shape) * item.dtype.itemsize for item in (*operands, *outs))
    rows = operands[0].shape[0]

    def body(places_ref, *refs):
        kernel(places_ref, refs[: weight.count], *refs[weight.count :])

    return pl.pallas_call(
        body,
        in_specs=[SCALARS] + [HBM] * weight.count + [VMEM_SPEC] * len(operands),
        out_specs=[VMEM_SPEC] * len(outs),
        out_shape=outs,
        scratch_shapes=weight.scratch(runs) + scratch,
        compiler_params=pltpu.CompilerParams(vmem_limit_bytes=weight.bytes + 14 * 1024 * 1024),
        cost_estimate=pl.CostEstimate(
            flops=rows * weight.bytes, bytes_accessed=moved + weight.bytes, transcendentals=0
        ),
        name=name,
    )(weight.places, *weight.pieces, *operands)


class Rows:
    def __init__(self, array, begin, count):
        self.array, self.at, self.count = array, slice(begin, begin + count), count


def wait_all(copies):
    for here in copies:
        for copy in here:
            copy.wait()


def wide_kernel(kind, weight, runs, down, up, places_ref, pieces, u_ref, down_ref, up_ref, z_ref, *rest):
    outs, (store, sems) = rest[:-2], rest[-2:]
    copies = weight.loads(places_ref, pieces, store, sems, runs)
    z_ref[...] = dot_nt(u_ref[...], down_ref[down, :]).astype(jnp.bfloat16)
    wait_all(copies)
    for spans in runs:
        result = [
            dot_nn(u_ref[...], store[:, begin : begin + span])
            + dot_nn(z_ref[...], up_ref[up, begin : begin + span])
            for begin, span in spans
        ]
        at = slice(spans[0][0], spans[0][0] + spans[0][1])
        if kind == "silu":
            gate = jax.nn.sigmoid(result[0])
            active = result[0] * gate
            outs[0][:, at] = active.astype(jnp.bfloat16)
            outs[1][:, at] = (gate + active * (1.0 - gate)).astype(jnp.bfloat16)
        elif kind == "glu":
            gate = jax.nn.sigmoid(result[1])
            gated = result[0] * gate
            outs[0][:, at] = gated.astype(jnp.bfloat16)
            outs[1][:, at] = gate.astype(jnp.bfloat16)
            outs[2][:, at] = (gated * (1.0 - gate)).astype(jnp.bfloat16)
        else:
            which = min(at.start // outs[0].shape[1], 1)
            first = which * outs[0].shape[1]
            outs[which][:, at.start - first : at.stop - first] = result[0].astype(jnp.bfloat16)


def project_wide(kind, inputs, weight, down, up):
    rows = inputs.shape[0]
    width = weight.width
    out_width = width // 2 if kind == "glu" else width
    sizes = {"silu": [width] * 2, "glu": [out_width] * 3, "plain": [width // 3, width - width // 3]}[kind]
    span = min(TALL, out_width)
    runs = [[(base + begin, span) for base in range(0, width, out_width)] for begin in range(0, out_width, span)]
    return fused(
        functools.partial(wide_kernel, kind, weight, runs, down.at, up.at), "project_" + kind, weight, runs, [],
        [shape_of(rows, down.count)] + [shape_of(rows, size) for size in sizes],
        inputs, down.array, up.array,
    )


def narrow_kernel(factor, weight, runs, down, up, places_ref, pieces, u_ref, down_ref, up_ref, field_ref, gain_ref,
                  bias_ref, z_ref, field_out, normed_out, store, sems):
    copies = weight.loads(places_ref, pieces, store, sems, runs)
    z_ref[...] = dot_nt(u_ref[...], down_ref[down, :]).astype(jnp.bfloat16)
    wait_all(copies)
    for ((begin, span),) in runs:
        at = slice(begin, begin + span)
        result = dot_nn(u_ref[...], store[:, at]) + dot_nn(z_ref[...], up_ref[up, at])
        field_out[:, at] = field_ref[:, at].astype(jnp.float32) + factor * result
    gain, bias = gain_ref[...], bias_ref[...]

    def finish(at):
        normed_out[at, :] = (norm_rows(field_out[at, :])[0] * gain + bias).astype(jnp.bfloat16)

    each_rows(u_ref.shape[0], 128, finish)


def project_narrow(inputs, weight, down, up, field, gain, bias, factor):
    rows, width = inputs.shape[0], weight.width
    span = min(TALL, width)
    runs = [[(begin, span)] for begin in range(0, width, span)]
    return fused(
        functools.partial(narrow_kernel, factor, weight, runs, down.at, up.at), "project_next", weight, runs, [],
        [shape_of(rows, down.count), shape_of(rows, width, jnp.float32), shape_of(rows, width)],
        inputs, down.array, up.array, field, gain, bias,
    )


def adapter_grads(up, grad_ref, z_ref, up_ref, u_ref, dz_ref, da_ref, db_ref):
    dz_ref[...] = dot_nt(grad_ref[...], up_ref[up, :]).astype(jnp.bfloat16)
    db_ref[...] = dot_tn(z_ref[...], grad_ref[...]).astype(jnp.bfloat16)
    da_ref[...] = dot_tn(dz_ref[...], u_ref[...]).astype(jnp.bfloat16)


def field_back_kernel(kind, weight, runs, share_count, down, up, places_ref, pieces, d_ref, down_ref, up_ref, u_ref, z_ref, *rest):
    extra = {"norm": 3, "conv": 3, "plain": 0}[kind]
    shares, rest = rest[:share_count], rest[share_count:]
    extras, (out_ref, da_ref, db_ref, store, sems, grad, dz, d_inputs) = rest[:extra], rest[extra:]
    copies = weight.loads(places_ref, pieces, store, sems, runs)
    if shares:
        width = d_ref.shape[1]
        grad[:, :width] = d_ref[...]
        for which in range(2):
            total = shares[0][which].astype(jnp.float32)
            for share in shares[1:]:
                total = total + share[which].astype(jnp.float32)
            grad[:, (1 + which) * width : (2 + which) * width] = total.astype(jnp.bfloat16)
    elif d_ref.dtype == jnp.bfloat16:
        grad = d_ref
    else:
        grad[...] = d_ref[...].astype(jnp.bfloat16)
    adapter_grads(up, grad, z_ref, up_ref, u_ref, dz, da_ref, db_ref)
    wait_all(copies)
    tall = min(TALL, weight.depth)
    for begin in range(0, weight.depth, tall):
        at = slice(begin, begin + tall)
        result = dot_nt(grad[...], store[at, :]) + dot_nn(dz[...], down_ref[down, at])
        if kind == "plain":
            out_ref[:, at] = result.astype(out_ref.dtype)
        else:
            d_inputs[:, at] = result

    def finish(at):
        if kind == "norm":
            prior_ref, field_ref, gain_ref = extras
            normed, rate = norm_rows(field_ref[at, :].astype(jnp.float32))
            moved = norm_back(d_inputs[at, :], gain_ref[...], normed, rate)
            out_ref[at, :] = (prior_ref[at, :] + moved).astype(out_ref.dtype)
        else:
            field_ref, gain_ref, bias_ref = extras
            gain = gain_ref[...]
            normed, rate = norm_rows(field_ref[at, :])
            shifted = normed * gain + bias_ref[...]
            gate = jax.nn.sigmoid(shifted)
            slope = gate + shifted * gate * (1.0 - gate)
            out_ref[at, :] = norm_back(d_inputs[at, :] * slope, gain, normed, rate)

    if kind != "plain":
        each_rows(d_ref.shape[0], 128, finish)


def field_back(
    kind, grad, weight, down, up, inputs, slot_acts, extras=(), out_dtype=jnp.float32, shares=()
):
    rows, width = grad.shape[0], weight.width
    depth, rank = weight.depth, down.count
    runs = [[(0, width)]]
    scratch = shares or grad.dtype != jnp.bfloat16
    return fused(
        functools.partial(field_back_kernel, kind, weight, runs, len(shares), down.at, up.at), "field_back_" + kind, weight, runs,
        [
            pltpu.VMEM((rows, width) if scratch else (16, 128), jnp.bfloat16),
            pltpu.VMEM((rows, rank), jnp.bfloat16),
            pltpu.VMEM((rows, depth) if kind != "plain" else (8, 128), jnp.float32),
        ],
        [shape_of(rows, depth, out_dtype), shape_of(rank, depth), shape_of(rank, width)],
        grad, down.array, up.array, inputs, slot_acts, *shares, *extras,
    )


class Pair:
    def __init__(self, *weights):
        self.weights = weights
        self.places = weights[0].places
        self.pieces = [piece for weight in weights for piece in weight.pieces]
        self.bytes = sum(weight.bytes for weight in weights)

    def split(self, refs):
        middle = self.weights[0].count
        return refs[:middle], refs[middle:]


def halves(turn_ref, first_out, second_out, rows_of):
    half = first_out.shape[0]
    step = half // 2
    for begin in range(0, 2 * half, step):
        made = rows_of(slice(begin, begin + step)).astype(first_out.dtype)
        at = slice(begin % half, begin % half + step)
        for out, turn in ((first_out, begin // half), (second_out, 1 - begin // half)):

            @pl.when(turn_ref[0] == turn)
            def _(out=out):
                out[at, :] = made


def pair_call(kernel, name, pair, hbm_in, vmem_in, turn, outs, hbm_out, scratch, limit):
    rows = vmem_in[0].shape[0]
    moved = sum(math.prod(x.shape) * x.dtype.itemsize for x in (*hbm_in, *vmem_in, *outs))

    def body(places_ref, *refs):
        count = len(pair.pieces)
        kernel(places_ref, *pair.split(refs[:count]), *refs[count:])

    return pl.pallas_call(
        body,
        in_specs=[SCALARS] + [HBM] * (len(pair.pieces) + len(hbm_in)) + [VMEM_SPEC] * len(vmem_in) + [SCALARS] * len(turn),
        out_specs=[HBM] * hbm_out + [VMEM_SPEC] * (len(outs) - hbm_out),
        out_shape=outs,
        scratch_shapes=scratch,
        compiler_params=pltpu.CompilerParams(vmem_limit_bytes=limit),
        cost_estimate=pl.CostEstimate(
            flops=rows * pair.bytes, bytes_accessed=moved + pair.bytes, transcendentals=0
        ),
        name=name,
    )(pair.places, *pair.pieces, *hbm_in, *vmem_in, *turn)


def ffn_kernel(up, down, rows, places_ref, up_pieces, down_pieces,
               u_ref, a_up_ref, b_up_ref, a_down_ref, b_down_ref, field_ref, gain_ref, bias_ref, cot_ref, turn_ref,
               act_out, slope_out, z_up_ref, z_down_ref, d_out, first_out, second_out,
               up_store, up_sems, down_store, down_sems, act, slope, out_sems):
    whole_up, whole_down = [[(0, up.width)]], [[(0, down.width)]]
    a_up, b_up, a_down, b_down = rows
    up_copies = up.loads(places_ref, up_pieces, up_store, up_sems, whole_up)
    z_up_ref[...] = dot_nt(u_ref[...], a_up_ref[a_up, :]).astype(jnp.bfloat16)
    wait_all(up_copies)
    down_copies = down.loads(places_ref, down_pieces, down_store, down_sems, whole_down)
    leaving = []
    for begin in range(0, up.width, TALL):
        at = slice(begin, begin + TALL)
        hidden = dot_nn(u_ref[...], up_store[:, at]) + dot_nn(z_up_ref[...], b_up_ref[b_up, at])
        gate = jax.nn.sigmoid(hidden)
        active = hidden * gate
        act[:, at] = active.astype(jnp.bfloat16)
        slope[:, at] = (gate + active * (1.0 - gate)).astype(jnp.bfloat16)
    for which, (held, out) in enumerate(((act, act_out), (slope, slope_out))):
        leaving.append(pltpu.make_async_copy(held, out, out_sems.at[which]))
        leaving[-1].start()
    z_down_ref[...] = dot_nt(act[...], a_down_ref[a_down, :]).astype(jnp.bfloat16)
    wait_all(down_copies)
    for begin in range(0, down.width, TALL):
        at = slice(begin, begin + TALL)
        result = dot_nn(act[...], down_store[:, at]) + dot_nn(z_down_ref[...], b_down_ref[b_down, at])
        d_out[:, at] = field_ref[:, at] + 0.5 * result
    gain, bias = gain_ref[...], bias_ref[...]

    def finish(at):
        normed, rate = norm_rows(d_out[at, :])
        d_out[at, :] = norm_back(cot_ref[at, :].astype(jnp.float32), gain, normed, rate)
        return normed * gain + bias

    halves(turn_ref, first_out, second_out, finish)
    for copy in leaving:
        copy.wait()


def feed_forward_last(inputs, up, down, factors, field, gain, bias, cotangent, turn):
    rows, width = inputs.shape
    rank, hidden = factors[0].count, up.width
    return pair_call(
        functools.partial(ffn_kernel, up, down, [part.at for part in factors]), "feed_forward_last", Pair(up, down), [],
        [inputs, *[part.array for part in factors], field, gain, bias, cotangent], turn,
        [shape_of(rows, hidden)] * 2
        + [shape_of(rows, rank)] * 2
        + [shape_of(rows, width, jnp.float32)]
        + [shape_of(rows // 2, width)] * 2,
        2,
        up.scratch([[(0, hidden)]]) + down.scratch([[(0, width)]])
        + [pltpu.VMEM((rows, hidden), jnp.bfloat16)] * 2 + [pltpu.SemaphoreType.DMA((2,))],
        up.bytes + down.bytes + 24 * 1024 * 1024,
    )


def ffn_back_kernel(up, down, rows, turns, places_ref, up_pieces, down_pieces, act_ref, slope_ref,
                    d_ref, a_up_ref, b_up_ref, a_down_ref, b_down_ref, z_up_ref, z_down_ref, u_ref,
                    field_ref, gain_ref, *refs):
    turn_refs, refs = refs[:turns], refs[turns:]
    out_refs, refs = refs[: 1 + turns], refs[1 + turns :]
    da_up_ref, db_up_ref, da_down_ref, db_down_ref = refs[:4]
    up_store, up_sems, down_store, down_sems, act, slope, in_sems, grad, dz, d_hidden, d_inputs = refs[4:]
    whole_up, whole_down = [[(0, up.width)]], [[(0, down.width)]]
    a_up, b_up, a_down, b_down = rows
    down_copies = down.loads(places_ref, down_pieces, down_store, down_sems, whole_down)
    coming = [
        pltpu.make_async_copy(ref, held, in_sems.at[which])
        for which, (ref, held) in enumerate(((slope_ref, slope), (act_ref, act)))
    ]
    coming[0].start()
    grad[...] = (0.5 * d_ref[...]).astype(jnp.bfloat16)
    dz[...] = dot_nt(grad[...], b_down_ref[b_down, :]).astype(jnp.bfloat16)
    db_down_ref[...] = dot_tn(z_down_ref[...], grad[...]).astype(jnp.bfloat16)
    wait_all(down_copies)
    coming[0].wait()
    coming[1].start()
    up_copies = up.loads(places_ref, up_pieces, up_store, up_sems, whole_up)
    for begin in range(0, down.depth, TALL):
        at = slice(begin, begin + TALL)
        result = dot_nt(grad[...], down_store[at, :]) + dot_nn(dz[...], a_down_ref[a_down, at])
        d_hidden[:, at] = (result * slope[:, at].astype(jnp.float32)).astype(jnp.bfloat16)
    coming[1].wait()
    da_down_ref[...] = dot_tn(dz[...], act[...]).astype(jnp.bfloat16)
    dz[...] = dot_nt(d_hidden[...], b_up_ref[b_up, :]).astype(jnp.bfloat16)
    wait_all(up_copies)
    for begin in range(0, up.depth, TALL):
        at = slice(begin, begin + TALL)
        d_inputs[:, at] = dot_nt(d_hidden[...], up_store[at, :]) + dot_nn(dz[...], a_up_ref[a_up, at])
    db_up_ref[...] = dot_tn(z_up_ref[...], d_hidden[...]).astype(jnp.bfloat16)
    da_up_ref[...] = dot_tn(dz[...], u_ref[...]).astype(jnp.bfloat16)

    def finish(at):
        normed, rate = norm_rows(field_ref[at, :].astype(jnp.float32))
        return d_ref[at, :] + norm_back(d_inputs[at, :], gain_ref[...], normed, rate)

    if turns:
        halves(turn_refs[0], *out_refs, finish)
        return

    def store(at):
        out_refs[0][at, :] = finish(at)

    each_rows(d_ref.shape[0], 128, store)


def feed_forward_back(d_field, up, down, factors, kept, field, gain, turn=()):
    rows, width = d_field.shape
    inputs, act, slope, z_up, z_down = kept
    rank, hidden = factors[0].count, up.width
    return pair_call(
        functools.partial(ffn_back_kernel, up, down, [part.at for part in factors], len(turn)), "feed_forward_back", Pair(up, down), [act, slope],
        [d_field, *[part.array for part in factors], z_up, z_down, inputs, field, gain], turn,
        ([shape_of(rows // 2, width)] * 2 if turn else [shape_of(rows, width, jnp.float32)])
        + [shape_of(rank, width), shape_of(rank, hidden)]
        + [shape_of(rank, hidden), shape_of(rank, width)],
        0,
        up.scratch([[(0, hidden)]]) + down.scratch([[(0, width)]])
        + [pltpu.VMEM((rows, hidden), jnp.bfloat16)] * 2
        + [
            pltpu.SemaphoreType.DMA((2,)),
            pltpu.VMEM((rows, width), jnp.bfloat16),
            pltpu.VMEM((rows, rank), jnp.bfloat16),
            pltpu.VMEM((rows, hidden), jnp.bfloat16),
            pltpu.VMEM((rows, width), jnp.float32),
        ],
        up.bytes + down.bytes + 28 * 1024 * 1024,
    )


HALO = 32


def taps_kernel(weight, runs, places_ref, *refs):
    pieces, (out_ref, store, sems) = refs[: weight.count], refs[weight.count :]
    wait_all(weight.loads(places_ref, pieces, store, sems, runs))
    out_ref[...] = jnp.transpose(store[...].astype(jnp.float32))[: out_ref.shape[0], :]


def gather_taps(weight):
    runs = [[(0, TILE)]]
    return pl.pallas_call(
        functools.partial(taps_kernel, weight, runs),
        in_specs=[SCALARS] + [HBM] * weight.count,
        out_specs=VMEM_SPEC,
        out_shape=jax.ShapeDtypeStruct((HALO, weight.depth), jnp.float32),
        scratch_shapes=weight.scratch(runs),
        compiler_params=pltpu.CompilerParams(vmem_limit_bytes=8 * 1024 * 1024),
        name="gather_taps",
    )(weight.places, *weight.pieces)


def slide(lanes, parts, shifted, taps_ref, shifts, rows, store):
    begin = 0
    for part in parts:
        shifted[0, begin : begin + part.shape[0], :] = part
        begin += part.shape[0]
    length = begin - 8
    for turn in range(1, 8):
        shifted[turn, 0:length, :] = shifted[0, turn : turn + length, :]
    step = 64
    for at in range(0, rows, step):
        total = None
        for tap, shift in enumerate(shifts):
            base = shift - shift % 8 + at
            term = shifted[shift % 8, base : base + step, :] * taps_ref[tap : tap + 1, lanes]
            total = term if total is None else total + term
        store(slice(at, at + step), total)


def each_tile(width, body):
    def one(index, carry):
        body(pl.ds(pl.multiple_of(index * TILE, TILE), TILE))
        return carry

    lax.fori_loop(0, width // TILE, one, 0)


def conv_kernel(val_ref, earlier_ref, taps_ref, gain_ref, bias_ref, conv_ref, act_ref, shifted):
    rows, width = val_ref.shape

    def one(lanes):
        parts = [earlier_ref[:, lanes].astype(jnp.float32), val_ref[:, lanes].astype(jnp.float32)]

        def store(at, total):
            conv_ref[at, lanes] = total

        shifts = [HALO - KERNEL + 1 + tap for tap in range(KERNEL)]
        slide(lanes, parts, shifted, taps_ref, shifts, rows, store)

    each_tile(width, one)

    def finish(at):
        shifted_field = norm_rows(conv_ref[at, :])[0] * gain_ref[...] + bias_ref[...]
        act_ref[at, :] = (shifted_field * jax.nn.sigmoid(shifted_field)).astype(jnp.bfloat16)

    each_rows(rows, 128, finish)


def conv_back_kernel(d_ref, later_ref, taps_ref, gate_ref, slope_ref, out_ref, shifted):
    rows, width = d_ref.shape

    def one(lanes):
        parts = [d_ref[:, lanes], later_ref[:, lanes].astype(jnp.float32)]
        high = pl.ds(pl.multiple_of(lanes.start + width, TILE), TILE)

        def store(at, total):
            out_ref[at, lanes] = (total * gate_ref[at, lanes].astype(jnp.float32)).astype(jnp.bfloat16)
            out_ref[at, high] = (total * slope_ref[at, lanes].astype(jnp.float32)).astype(jnp.bfloat16)

        slide(lanes, parts, shifted, taps_ref, [KERNEL - 1 - tap for tap in range(KERNEL)], rows, store)

    each_tile(width, one)


def conv_call(kernel, name, outs, rows, *operands):
    return pl.pallas_call(
        kernel,
        in_specs=[VMEM_SPEC] * len(operands),
        out_specs=[VMEM_SPEC] * len(outs),
        out_shape=outs,
        scratch_shapes=[pltpu.VMEM((8, rows + HALO, TILE), jnp.float32)],
        compiler_params=pltpu.CompilerParams(vmem_limit_bytes=16 * 1024 * 1024),
        cost_estimate=pl.CostEstimate(flops=0, bytes_accessed=32 * rows * operands[0].shape[1], transcendentals=0),
        name=name,
    )(*operands)


def conv_forward(value, earlier, taps, gain, bias):
    rows, width = value.shape
    outs = [shape_of(rows, width, jnp.float32), shape_of(rows, width)]
    return conv_call(conv_kernel, "conv_forward", outs, rows, value, earlier, taps, gain, bias)


def conv_backward(d_conv, later, taps, gate, slope):
    rows, width = d_conv.shape
    outs = [shape_of(rows, 2 * width)]
    return conv_call(conv_back_kernel, "conv_backward", outs, rows, d_conv, later, taps, gate, slope)[0]


class Layout:
    def __init__(self, together, fsdp):
        self.fsdp = fsdp
        self.inner = fsdp // together
        self.group = 2 * self.inner

    def place(self, core, f):
        return core * self.fsdp + f

    def round_route(self, turn):
        route = []
        for core in range(2):
            for f in range(self.fsdp):
                clip = (f % 2 + turn) % 2
                spot = f // 2
                target = self.place(spot % 2, (2 * core + clip) * self.inner + spot // 2)
                route.append((self.place(core, f), target))
        return route

    def gather_rows(self, blocks):
        parity = (lax.axis_index("fz") * self.inner + lax.axis_index("fh")) % 2
        clip = lax.axis_index("fz") % 2
        got = []
        for turn in range(2):
            sent = lax.dynamic_index_in_dim(blocks, (parity + turn) % 2, 0, keepdims=False)
            got.append(lax.ppermute(sent, ("core", "fz", "fh"), self.round_route(turn)))
        swap = clip == 1
        return jnp.concatenate(
            [jnp.where(swap, got[1], got[0]), jnp.where(swap, got[0], got[1])], axis=0
        )

    def scatter_rows(self, sent):
        parity = (lax.axis_index("fz") * self.inner + lax.axis_index("fh")) % 2
        got = []
        for turn in range(2):
            route = [(target, source) for source, target in self.round_route(turn)]
            got.append(lax.ppermute(sent[turn], ("core", "fz", "fh"), route))
        swap = parity == 1
        return jnp.stack([jnp.where(swap, got[1], got[0]), jnp.where(swap, got[0], got[1])])

    def spot_index(self, spot):
        return (spot % 2) * self.inner + spot // 2

    def from_spot(self, block, distance, cyclic):
        route = []
        for spot in range(self.group):
            source = spot + distance
            if cyclic:
                source %= self.group
            if 0 <= source < self.group:
                route.append((self.spot_index(source), self.spot_index(spot)))
        return lax.ppermute(block, ("core", "fh"), route)


def pack_adapters(ids, a_model, a_hidden, b_model, b_hidden):
    slots = a_model.shape[2]
    half = RANK // 2
    core = lax.axis_index("core")
    ranks = core * half + jnp.arange(half, dtype=jnp.int32)
    wanted = ids[:, None] * RANK + ranks[None, :]
    picker = (wanted[:, :, None] == jnp.arange(slots, dtype=jnp.int32)).astype(jnp.bfloat16)
    down = lambda a: jnp.einsum("jrs,pks->jprk", picker, a, preferred_element_type=jnp.float32)
    up = lambda b: jnp.einsum("jrs,psn->jprn", picker, b, preferred_element_type=jnp.float32)
    cut = a_hidden.shape[1] // a_model.shape[1]
    span = a_model.shape[1]

    def short(pack):
        rows = pack.reshape(pack.shape[0], pack.shape[1], half, cut, span)
        return jnp.swapaxes(rows, 2, 3).reshape(pack.shape[0], pack.shape[1] * cut, half, span)

    return jnp.concatenate(
        [down(a_model), up(b_model), short(down(a_hidden)), short(up(b_hidden))], axis=1
    ).astype(jnp.bfloat16)


def join_adapters_kernel(models, cut, plan, spots_ref, mine_ref, theirs_ref, *rest):
    wanted = len(plan)
    outs, full, held, sems = rest[:wanted], rest[wanted], rest[wanted + 1 : -1], rest[-1]
    count, groups, half, span = mine_ref.shape
    for step in range(count):
        at = pl.ds(pl.multiple_of(spots_ref[step] * span, span), span)
        for ref, core in ((mine_ref, spots_ref[count]), (theirs_ref, 1 - spots_ref[count])):
            rows = pl.ds(pl.multiple_of(core * half, half), half)
            full[:, rows, at] = ref[step].astype(jnp.float32)
    copies = []
    for which, (out, kept, parts) in enumerate(zip(outs, held, plan)):
        kept[...] = jnp.zeros_like(kept)
        for group, row, column in parts:
            if group < models:
                kept[row : row + RANK, column : column + count * span] = full[group].astype(kept.dtype)
                continue
            for f in range(count):
                begin = column + f * cut * span
                kept[row : row + RANK, begin : begin + span] = full[
                    group, :, f * span : (f + 1) * span
                ].astype(kept.dtype)
        copies.append(pltpu.make_async_copy(kept, out, sems.at[which]))
        copies[-1].start()
    for copy in copies:
        copy.wait()


def move_adapters(layout, pack, cut, shapes, plan, models):
    core = lax.axis_index("core")
    count = layout.fsdp
    here = lax.axis_index("fz") * layout.inner + lax.axis_index("fh")
    pieces = []
    for step in range(count):
        target = (here + step) % count
        piece = lax.dynamic_index_in_dim(pack, target // layout.inner, 0, keepdims=False)
        if step:
            route = [(f, (f + step) % count) for f in range(count)]
            piece = lax.ppermute(piece, ("fz", "fh"), route)
        pieces.append(piece)
    mine = jnp.stack(pieces)
    theirs = lax.ppermute(mine, "core", [(0, 1), (1, 0)])
    spots = jnp.stack([(here - step) % count for step in range(count)] + [core]).astype(jnp.int32)
    _, groups, half, span = mine.shape
    return pl.pallas_call(
        functools.partial(join_adapters_kernel, models, cut, plan),
        in_specs=[SCALARS, VMEM_SPEC, VMEM_SPEC],
        out_specs=[HBM] * len(shapes),
        out_shape=[shape_of(*shape) for shape in shapes],
        scratch_shapes=[pltpu.VMEM((groups, 2 * half, count * span), jnp.float32)]
        + [pltpu.VMEM(shape, jnp.bfloat16) for shape in shapes]
        + [pltpu.SemaphoreType.DMA((len(shapes),))],
        compiler_params=pltpu.CompilerParams(vmem_limit_bytes=16 * 1024 * 1024),
        name="join_adapters",
    )(spots, mine, theirs)


def factor_plan(models, hiddens, cut, span):
    hidden = [(models + which * cut + q, which * RANK, q * span) for which in range(hiddens) for q in range(cut)]
    return [[(group, group * RANK, 0) for group in range(models)], hidden]


def first_adapters(layout, pack, cut, width, hidden):
    shapes = [(2 * RANK, width), (2 * RANK, hidden)]
    model, inner = move_adapters(layout, pack, cut, shapes, factor_plan(2, 2, cut, pack.shape[3]), 2)
    return model, inner


def other_adapters(layout, pack, cut, width, hidden):
    shapes = [(15 * RANK, width), (2 * RANK, hidden), (3 * RANK, 3 * width), (RANK, 2 * width)]
    plan = factor_plan(15, 2, cut, pack.shape[3]) + [
        [(7 + which, which * RANK, which * width) for which in range(3)],
        [(13, 0, 0), (14, 0, width)],
    ]
    return move_adapters(layout, pack, cut, shapes, plan, 15)


def pack_grads_kernel(models, count, fsdp, *refs):
    core_ref, refs = refs[0], refs[1:]
    out_ref, sems, held = refs[count], refs[count + 1], refs[count + 2 :]
    copies = [pltpu.make_async_copy(refs[i], held[i], sems.at[i]) for i in range(count)]
    for copy in copies:
        copy.start()
    for copy in copies:
        copy.wait()
    model_refs, hidden_refs = held[:models], held[models:]
    _, places, _, _ = out_ref.shape
    lanes = TILE
    model = jnp.concatenate([ref[...].astype(jnp.float32) for ref in model_refs], axis=0)
    tiles = -(-model.shape[0] // TILE)
    if model.shape[0] % TILE:
        rest = jnp.zeros((tiles * TILE - model.shape[0], model.shape[1]), jnp.float32)
        model = jnp.concatenate([model, rest], axis=0)
    turned = [jnp.transpose(model[k * TILE : (k + 1) * TILE]).astype(jnp.bfloat16) for k in range(tiles)]
    share = model.shape[1] // (2 * places)
    for device in range(2 * places):
        chip, other = divmod(device, 2 * fsdp)
        core, f = divmod(other, fsdp)
        place = chip * fsdp + f
        side = core_ref[0] if core == 0 else 1 - core_ref[0]
        row = 0
        for part in turned:
            out_ref[side, place, row : row + share, :] = part[device * share : (device + 1) * share]
            row += share
        for ref in hidden_refs:
            out_ref[side, place, row : row + RANK, :] = ref[:, device * lanes : (device + 1) * lanes]
            row += RANK


def pack_grads(model, hidden):
    core = lax.axis_index("core").astype(jnp.int32).reshape(1)
    devices, fsdp = lax.axis_size(EVERYWHERE), lax.axis_size("fz") * lax.axis_size("fh")
    width = model[0].shape[1]
    share, hidden_share = width // devices, hidden[0].shape[1] // devices
    groups = sum(part.shape[0] for part in model)
    tiles = -(-groups // TILE)
    if hidden_share == TILE and share % RANK == 0:
        rows = tiles * share + RANK * len(hidden)
        return pl.pallas_call(
            functools.partial(pack_grads_kernel, len(model), len(model) + len(hidden), fsdp),
            in_specs=[SCALARS] + [HBM] * (len(model) + len(hidden)),
            out_specs=VMEM_SPEC,
            out_shape=jax.ShapeDtypeStruct((2, devices // 2, rows, TILE), jnp.bfloat16),
            scratch_shapes=[pltpu.SemaphoreType.DMA((len(model) + len(hidden),))]
            + [pltpu.VMEM(item.shape, item.dtype) for item in (*model, *hidden)],
            compiler_params=pltpu.CompilerParams(vmem_limit_bytes=PACK_ROOM),
            name="pack_grads",
        )(core, *model, *hidden)
    rest = jnp.zeros((tiles * TILE - groups, width), jnp.bfloat16)
    turned = jnp.concatenate([*model, rest]).T
    split = jnp.concatenate(hidden).reshape(-1, devices, hidden_share)
    parts = [turned[:, k * TILE : (k + 1) * TILE].reshape(devices, share, TILE) for k in range(tiles)]
    parts.append(jnp.transpose(split, (1, 0, 2)).reshape(devices, -1, TILE))
    part = jnp.concatenate(parts, axis=1).reshape(devices // (2 * fsdp), 2, fsdp, -1, TILE)
    part = jnp.swapaxes(part, 0, 1).reshape(2, devices // 2, -1, TILE)
    return jnp.where(core[0] == 0, part, part[::-1])


def send_grads(model, hidden):
    part = pack_grads(model, hidden)
    ours, theirs = part[0], part[1]
    came = lax.ppermute(theirs, "core", [(0, 1), (1, 0)])
    both = (ours.astype(jnp.float32) + came.astype(jnp.float32)).astype(jnp.bfloat16)
    got = lax.all_to_all(both, ("chip", "fz", "fh"), 0, 0, tiled=True)
    devices = lax.axis_size(EVERYWHERE)
    share, hidden_share = model[0].shape[1] // devices, hidden[0].shape[1] // devices
    begin = -(-sum(item.shape[0] for item in model) // TILE) * share
    if hidden_share == TILE:
        return got, got, begin
    return got, got[:, begin:].reshape(-1, RANK * len(hidden), hidden_share), 0


def place_grads_kernel(batches, ids_ref, *refs):
    sent, outs = refs[: 2 * len(batches)], refs[2 * len(batches) :]
    for out in outs:
        out[...] = jnp.zeros_like(out)
    share = outs[0].shape[1]
    slot = lax.broadcasted_iota(jnp.int32, (share, TILE), 1) // RANK
    in_tile = TILE // RANK

    def one(sender, carry):
        owner = ids_ref[sender]
        at = pl.ds(pl.multiple_of(owner * RANK, RANK), RANK)
        for which, (model_plan, hidden_plan, begin) in enumerate(batches):
            model_ref, hidden_ref = sent[2 * which : 2 * which + 2]
            for group, (out, index) in enumerate(model_plan):
                tile, local_group = divmod(group, in_tile)
                block = model_ref[sender, tile * share : (tile + 1) * share, :].astype(jnp.float32)
                turn = lax.rem(owner - local_group + in_tile, in_tile) * RANK
                outs[out][index] += jnp.where(slot == owner, pltpu.roll(block, turn, 1), 0.0)
            for group, (out, index) in enumerate(hidden_plan):
                rows = slice(begin + group * RANK, begin + (group + 1) * RANK)
                outs[out][index, at, :] += hidden_ref[sender, rows, :].astype(jnp.float32)
        return carry

    lax.fori_loop(0, sent[0].shape[0], one, 0)


def place_grads(ids, batches, shapes):
    arrays, plans = [], []
    for (model, hidden, begin), model_plan, hidden_plan in batches:
        arrays += [model, hidden]
        plans.append((model_plan, hidden_plan, begin))
    return pl.pallas_call(
        functools.partial(place_grads_kernel, plans),
        in_specs=[SCALARS] + [VMEM_SPEC] * len(arrays),
        out_specs=[VMEM_SPEC] * len(shapes),
        out_shape=[jax.ShapeDtypeStruct(shape, jnp.float32) for shape in shapes],
        compiler_params=pltpu.CompilerParams(vmem_limit_bytes=16 * 1024 * 1024),
        name="place_grads",
    )(ids, *arrays)


def local(
    frames,
    cotangent,
    adapter_ids,
    norm_gains,
    norm_biases,
    rel_table,
    w_up,
    w_down,
    w_qkv,
    w_out,
    w_pw1,
    w_depth,
    w_pw2,
    ad_a_model,
    ad_a_hidden,
    ad_b_model,
    ad_b_hidden,
):
    group_clips, frame_span, width = frames.shape
    together = 2 * group_clips
    layout = Layout(together, lax.axis_size("fz") * lax.axis_size("fh"))
    rows = 2 * frame_span
    slots = ad_a_model.shape[2]
    spot = lax.axis_index("fh") * 2 + lax.axis_index("core")
    own = (spot * (rows // TILE)).astype(jnp.int32).reshape(1)
    other_ids = lax.ppermute(adapter_ids, "core", [(0, 1), (1, 0)])
    at_zero = lax.axis_index("core") == 0
    near_ids = jnp.concatenate(
        [jnp.where(at_zero, adapter_ids, other_ids), jnp.where(at_zero, other_ids, adapter_ids)]
    )
    factors = (ad_a_model, ad_a_hidden, ad_b_model, ad_b_hidden)
    cut = ad_a_hidden.shape[1] // ad_a_model.shape[1]
    first_pack = pack_adapters(near_ids, *[factor[:1] for factor in factors])
    other_pack = pack_adapters(near_ids, *[factor[1:] for factor in factors])
    gather = Gather()
    taps = jnp.pad(w_depth.T, ((0, 0), (0, width - KERNEL)))
    shards = [
        w_up[0],
        w_down[0],
        jnp.concatenate([w_qkv, w_out], axis=1),
        jnp.concatenate([w_pw1, w_pw2, taps], axis=1),
        w_up[1],
        w_down[1],
    ]
    used = [shard.shape[1] for shard in shards]
    used[3] = 3 * width + TILE
    turns = gather.stages(shards, used)
    next(turns)

    def weight_of(units, which, begin=0, columns=None):
        return Weight(gather.places, units[which], begin, columns or used[which])

    gains = [norm_gains[index : index + 1] for index in range(6)]
    biases = [norm_biases[index : index + 1] for index in range(6)]

    turns.send([first_pack, other_pack])
    first_pack, other_pack = gather.held
    turns.send([frames, first_pack, other_pack, *rel_tables(rel_table, rows * layout.group)])
    frames, first_pack, other_pack, *tables = gather.held
    layer_in = layout.gather_rows(frames)
    turns.send([])
    hidden_width = w_up.shape[2]
    first_four = first_adapters(layout, first_pack, cut, width, hidden_width)
    units = turns.send([layer_in, *first_four])
    layer_in, *first_four = gather.held
    field = layer_in.astype(jnp.float32)
    first_in = (norm_rows(field)[0] * gains[0] + biases[0]).astype(jnp.bfloat16)
    a_up0, b_down0 = [Rows(first_four[0], row * RANK, RANK) for row in range(2)]
    a_down0, b_up0 = [Rows(first_four[1], row * RANK, RANK) for row in range(2)]
    up0_w = weight_of(units, 0)
    z_up0, act_one, slope_one = project_wide("silu", first_in, up0_w, a_up0, b_up0)
    units = turns.send([act_one, slope_one, other_pack])
    act_one, slope_one, other_pack = gather.held
    others = other_adapters(layout, other_pack, cut, width, hidden_width)
    units = turns.send([])
    down0_w = weight_of(units, 1)
    z_down0, after_ffn, attn_in = project_narrow(
        act_one, down0_w, a_down0, b_down0, layer_in, gains[1], biases[1], 0.5
    )
    units = turns.send([after_ffn, attn_in, *others])
    after_ffn, attn_in, *others = gather.held
    model, inner, qkv_up, glu_up = others
    qkv_down = Rows(model, 0, 3 * RANK)
    qkv_up, glu_up = Rows(qkv_up, 0, 3 * RANK), Rows(glu_up, 0, RANK)
    a_out, a_pw1, a_pw2, a_up1, b_out, b_pw2, b_down1 = [
        Rows(model, row * RANK, RANK) for row in (3, 4, 5, 6, 10, 11, 12)
    ]
    a_down1, b_up1 = [Rows(inner, row * RANK, RANK) for row in range(2)]
    units = turns.send([])
    qkv_w, out_w = weight_of(units, 2, 0, 3 * width), weight_of(units, 2, 3 * width, width)
    z_qkv, query, own_kv = project_wide("plain", attn_in, qkv_w, qkv_down, qkv_up)
    units = turns.send([query, own_kv])
    query, own_kv = gather.held
    units = turns.send([])
    pw1_w, pw2_w = weight_of(units, 3, 0, 2 * width), weight_of(units, 3, 2 * width, width)
    taps = gather_taps(weight_of(units, 3, 3 * width, TILE))
    kv = [own_kv] + [layout.from_spot(own_kv, step, True) for step in range(1, layout.group)]
    mixed, log_total = attention_forward(own, query, kv, tables[0])
    turns.send([mixed, log_total])
    mixed, log_total = gather.held
    units = turns.send([])
    up1_w, down1_w = weight_of(units, 4), weight_of(units, 5)
    mixed, cotangent = lax.optimization_barrier((mixed, cotangent))
    d_out = layout.gather_rows(cotangent)
    z_out, after_attn, conv_in = project_narrow(
        mixed, out_w, a_out, b_out, after_ffn, gains[2], biases[2], 1.0
    )
    z_pw1, gated, gate, gate_slope = project_wide("glu", conv_in, pw1_w, a_pw1, glu_up)
    earlier = layout.from_spot(gated[rows - HALO :], -1, False)
    conv_out, conv_act = conv_forward(gated, earlier, taps, gains[3], biases[3])
    z_pw2, after_conv, second_in = project_narrow(
        conv_act, pw2_w, a_pw2, b_pw2, after_attn, gains[4], biases[4], 1.0
    )
    factors_two = (a_up1, b_up1, a_down1, b_down1)
    turn = [(lax.axis_index("fz") % 2).astype(jnp.int32).reshape(1)]
    act_two, slope_two, z_up1, z_down1, d_fourth, *result = feed_forward_last(
        second_in, up1_w, down1_w, factors_two, after_conv, gains[5], biases[5], d_out, turn
    )
    layer_out = layout.scatter_rows(result)

    d_third, da_up1, db_up1, da_down1, db_down1 = feed_forward_back(
        d_fourth, up1_w, down1_w, factors_two, (second_in, act_two, slope_two, z_up1, z_down1),
        after_conv, gains[4],
    )
    d_conv, da_pw2, db_pw2 = field_back(
        "conv", d_third, pw2_w, a_pw2, b_pw2, conv_act, z_pw2,
        (conv_out, gains[3], biases[3]),
    )
    d_conv, layer_out = lax.optimization_barrier((d_conv, layer_out))
    later = layout.from_spot(d_conv[:HALO].astype(jnp.bfloat16), 1, False)
    d_joined = conv_backward(d_conv, later, taps, gate, gate_slope)
    d_second, da_pw1, db_pw1 = field_back(
        "norm", d_joined, pw1_w, a_pw1, glu_up, conv_in, z_pw1, (d_third, after_attn, gains[2])
    )
    d_mixed, da_out, db_out = field_back(
        "plain", d_second, out_w, a_out, b_out, mixed, z_out, (), jnp.bfloat16
    )
    label = jnp.full((RANK, width), near_ids[lax.axis_index("fz")]).astype(jnp.bfloat16)
    early = send_grads(
        [da_out, da_pw1, da_pw2, da_up1, db_out, db_pw2, db_down1]
        + [db_pw1[:, :width], db_pw1[:, width:], label],
        [da_down1, db_up1],
    )
    d_query, d_own, d_far = attention_backward(own, query, kv, d_mixed, log_total, tables)
    shares = [d_own]
    for step in range(1, layout.group):
        shares.append(layout.from_spot(d_far[:, (step - 1) * rows : step * rows], -step, True))
    d_first, da_qkv, db_qkv = field_back(
        "norm", d_query, qkv_w, qkv_down, qkv_up, attn_in, z_qkv, (d_second, after_ffn, gains[1]),
        shares=shares,
    )
    db_three = [
        db_qkv[index * RANK : (index + 1) * RANK, index * width : (index + 1) * width]
        for index in range(3)
    ]
    *grad_field, da_up0, db_up0, da_down0, db_down0 = feed_forward_back(
        d_first, up0_w, down0_w, (a_up0, b_up0, a_down0, b_down0),
        (first_in, act_one, slope_one, z_up0, z_down0), layer_in, gains[0], turn,
    )
    grad_frames = layout.scatter_rows(grad_field)
    late = send_grads([da_up0, da_qkv, db_down0, *db_three], [da_down0, db_up0])
    devices = lax.axis_size(EVERYWHERE)
    share, hidden_share = width // devices, hidden_width // devices
    ids = (early[0][:, share, RANK] * jnp.bfloat16(0.5)).astype(jnp.int32)
    early_plan = [(0, index) for index in range(4, 8)] + [(1, index) for index in range(4, 9)]
    late_plan = [(0, index) for index in range(4)] + [(1, index) for index in range(4)]
    grad_a_model, grad_b_model, grad_a_hidden, grad_b_hidden = place_grads(
        ids,
        [(early, early_plan, [(2, 1), (3, 1)]), (late, late_plan, [(2, 0), (3, 0)])],
        [(8, share, slots), (9, share, slots), (2, slots, hidden_share), (2, slots, hidden_share)],
    )
    grad_b_model = jnp.swapaxes(grad_b_model, 1, 2)
    grad_a_hidden = jnp.swapaxes(grad_a_hidden, 1, 2)
    return (layer_out, grad_frames, grad_a_model, grad_a_hidden, grad_b_model, grad_b_hidden)


def solution(mesh):
    every = ("chip", "core", "fz", "fh")
    clips, spread = ("chip", "core"), ("fz", "fh")
    in_specs = (
        P(clips, spread, None),
        P(clips, spread, None),
        P(clips),
        P(),
        P(),
        P(),
        P(None, every, None),
        P(None, every, None),
        P(every, None),
        P(every, None),
        P(every, None),
        P(None, every),
        P(every, None),
        P(None, spread, None),
        P(None, spread, None),
        P(None, None, spread),
        P(None, None, spread),
    )
    out_specs = (
        P(clips, spread, None),
        P(clips, spread, None),
        P(None, every, None),
        P(None, every, None),
        P(None, None, every),
        P(None, None, every),
    )

    def run(frames, *rest):
        dp, fsdp = mesh.shape["dp"], mesh.shape["fsdp"]
        together = 2 * frames.shape[0] // dp
        cut = Mesh(
            mesh.devices.reshape(dp // 2, 2, together, fsdp // together), EVERYWHERE
        )
        return jax.shard_map(
            local, mesh=cut, in_specs=in_specs, out_specs=out_specs, check_vma=False
        )(frames, *rest)

    return run
```

```python
import functools
import math

import jax
import jax.numpy as jnp
from jax import lax
from jax.experimental import pallas as pl
from jax.experimental.pallas import tpu as pltpu
from jax.sharding import Mesh
from jax.sharding import PartitionSpec as P

HEADS = 16
KERNEL = 31
RANK = 16
EPSILON = 1e-05
PACK_ROOM = 56 * 1024 * 1024
EVERYWHERE = ("chip", "core", "fz", "fh")

HD = 64
REL_LEFT = 64
REL_RIGHT = 8
TILE = 128
WIDE = 3 * TILE
VMEM = 32 * 1024 * 1024


def dot_nn(a, b):
    return lax.dot_general(a, b, (((1,), (0,)), ((), ())), preferred_element_type=jnp.float32)


def dot_nt(a, b):
    return lax.dot_general(a, b, (((1,), (1,)), ((), ())), preferred_element_type=jnp.float32)


def chunk_plan(tile, chunks):
    return [{chunks - 1: 0, 0: 1, 1: 2}.get((c - tile) % chunks) for c in range(chunks)]


def far_left(c, tile, chunks, own):
    return jnp.logical_or(c + own >= chunks, c < tile)


def wrapped_band(c, tile, chunks, own):
    if tile == 0 and c == chunks - 1:
        return own > 0
    if c == tile + 1:
        return c + own < chunks
    return None


def tile_scores(scores, table, tile, own):
    near = pltpu.roll(table[:, :TILE], TILE // 2, 1, stride=1, stride_axis=0)
    first, last = table[:, TILE : 2 * TILE], table[:, 2 * TILE :]
    ahead = lane_ahead()
    bands = [
        jnp.where(ahead >= TILE // 2, near, first),
        jnp.where(ahead < -(TILE // 2), first, jnp.where(ahead >= TILE // 2, last, near)),
        jnp.where(ahead < -(TILE // 2), near, last),
    ]
    chunks = scores.shape[1] // TILE
    parts = []
    for c, spot in enumerate(chunk_plan(tile, chunks)):
        part = scores[:, c * TILE : (c + 1) * TILE]
        if spot is None:
            bias = first if c < tile else jnp.where(c + own >= chunks, first, last)
        else:
            bias = bands[spot]
            true_band = wrapped_band(c, tile, chunks, own)
            if true_band is not None:
                bias = jnp.where(true_band, bias, jnp.where(far_left(c, tile, chunks, own), first, last))
        parts.append(part + bias)
    return parts


def lane_ahead():
    lane = lax.broadcasted_iota(jnp.int32, (TILE, TILE), 1)
    return lane - lax.broadcasted_iota(jnp.int32, (TILE, TILE), 0)


def stacked(refs):
    return jnp.concatenate([ref[...] for ref in refs], axis=0)


def head_lanes(rows):
    low = lax.broadcasted_iota(jnp.int32, (rows, 2 * HD), 1) < HD
    return low, (low, jnp.logical_not(low))


def row_tiles(rows):
    return [(tile, slice(tile * TILE, (tile + 1) * TILE)) for tile in range(rows // TILE)]


def attn_fwd_kernel(group, own_ref, q_ref, rel_ref, *refs):
    own = own_ref[0]
    keys, values, rel_wide = stacked(refs[:group]), stacked(refs[group : 2 * group]), rel_ref[...]
    o_ref, lse_ref, s_ref, w_ref, p_ref = refs[2 * group :]
    rows_n = q_ref.shape[0]
    low, heads = head_lanes(rows_n)
    q_pair = q_ref[...] * jnp.bfloat16(0.125)
    for head, lanes in enumerate(heads):
        q_head = jnp.where(lanes, q_pair, jnp.zeros_like(q_pair))
        s_ref[head] = dot_nt(q_head, keys)
        w_ref[head] = dot_nt(q_head, rel_wide)
    ones = jnp.ones_like(values)
    values_ones = jnp.concatenate([values, ones], axis=1)
    outs = []
    for head in range(2):
        for tile, rows in row_tiles(rows_n):
            parts = tile_scores(s_ref[head, rows, :], w_ref[head, rows, :], tile, own)
            top = jnp.max(functools.reduce(jnp.maximum, parts), axis=1, keepdims=True)
            top = jnp.broadcast_to(top, (TILE, TILE))
            expo = [jnp.exp(part - top).astype(jnp.bfloat16) for part in parts]
            p_ref[head, rows, :] = jnp.concatenate(expo, axis=1)
            lse_ref[rows, head * TILE : (head + 1) * TILE] = top
        outs.append(dot_nn(p_ref[head], values_ones))
        total = outs[head][:, 2 * HD :]
        at = slice(head * TILE, (head + 1) * TILE)
        lse_ref[:, at] = lse_ref[:, at] + jnp.log(total)
        outs[head] = outs[head][:, : 2 * HD] / total
    o_ref[...] = jnp.where(low, outs[0], outs[1]).astype(jnp.bfloat16)


def attn_bwd_kernel(group, own_ref, q_ref, do_ref, lse_ref, rel_ref, rev_ref, flip_ref, mark_ref, *refs):
    own = own_ref[0]
    keys, values, rel_wide = stacked(refs[:group]), stacked(refs[group : 2 * group]), rel_ref[...]
    dq_ref, own_out, far_out, s_ref, w_ref, dp_ref, ds_ref, p_ref, band_ref = refs[2 * group :]
    rows_n, keys_n = q_ref.shape[0], keys.shape[0]
    chunks = keys_n // TILE
    low, heads = head_lanes(rows_n)
    lane = lax.broadcasted_iota(jnp.int32, (1, TILE), 1)
    q_pair = q_ref[...] * jnp.bfloat16(0.125)
    do_pair = do_ref[...]
    keys_marked = jnp.concatenate([keys, mark_ref[...]], axis=1)
    for head, lanes in enumerate(heads):
        q_head = jnp.where(lanes, q_pair, jnp.zeros_like(q_pair))
        s_ref[head] = dot_nt(q_head, keys)
        w_ref[head] = dot_nt(q_head, rel_wide)
        dp_ref[head] = dot_nt(jnp.where(lanes, do_pair, jnp.zeros_like(do_pair)), values)
    dqs = []
    ahead = lane_ahead()
    for head in range(2):
        edges = []
        for tile, rows in row_tiles(rows_n):
            log_total = lse_ref[rows, head * TILE : (head + 1) * TILE]
            parts = tile_scores(s_ref[head, rows, :], w_ref[head, rows, :], tile, own)
            probs = [jnp.exp(part - log_total) for part in parts]
            d_parts = [dp_ref[head, rows, c * TILE : (c + 1) * TILE] for c in range(chunks)]
            inner = functools.reduce(jnp.add, [p * d for p, d in zip(probs, d_parts)])
            inner = jnp.sum(inner, axis=1, keepdims=True)
            d_scores = [(p * (d - inner)).astype(jnp.bfloat16) for p, d in zip(probs, d_parts)]
            p_ref[head, rows, :] = jnp.concatenate([p.astype(jnp.bfloat16) for p in probs], axis=1)
            ds_ref[head, rows, :] = jnp.concatenate(d_scores, axis=1)
            band = [None, None, None]
            for c, spot in enumerate(chunk_plan(tile, chunks)):
                if spot is not None:
                    near = wrapped_band(c, tile, chunks, own)
                    piece = d_scores[c]
                    band[spot] = piece if near is None else jnp.where(near, piece, jnp.zeros_like(piece))
            behind, beyond = ahead < -(TILE // 2), ahead >= TILE // 2
            none = jnp.zeros_like(band[0])
            band_ref[head, rows, :] = jnp.where(beyond, band[0], jnp.where(behind, band[2], band[1]))
            sides = (
                (jnp.where(beyond, none, band[0]), jnp.where(behind, band[1], none)),
                (jnp.where(behind, none, band[2]), jnp.where(beyond, band[1], none)),
            )
            edges.append([a.astype(jnp.float32) + b.astype(jnp.float32) for a, b in sides])
        turned = dot_nn(band_ref[head], flip_ref[...])
        turned = jnp.concatenate(
            [
                pltpu.roll(turned[rows, :], TILE // 2, 1, stride=1, stride_axis=0).astype(jnp.bfloat16)
                for _, rows in row_tiles(rows_n)
            ],
            axis=0,
        )
        marked = dot_nn(ds_ref[head], keys_marked)
        near_part = dot_nn(turned, rev_ref[...])
        outs = []
        for tile, rows in row_tiles(rows_n):
            weights = [jnp.zeros((1, TILE), jnp.float32)] * 2
            for c, spot in enumerate(chunk_plan(tile, chunks)):
                near = wrapped_band(c, tile, chunks, own)
                if spot is not None and near is None:
                    continue
                left = far_left(c, tile, chunks, own)
                far = 1.0 if spot is None else jnp.where(near, 0.0, 1.0)
                for side, on in enumerate((left, jnp.logical_not(left))):
                    here = jnp.where(on, far, 0.0)
                    weights[side] = weights[side] + jnp.where(lane == c, here, 0.0)
            sums = marked[rows, TILE:]
            before, after = [
                jnp.sum(sums * weight + edge, axis=1, keepdims=True)
                for weight, edge in zip(weights, edges[tile])
            ]
            d_query = marked[rows, :TILE] + near_part[rows, :]
            d_query = d_query + before * rev_ref[TILE - 1 : TILE, :].astype(jnp.float32)
            d_query = d_query + after * rev_ref[0:1, :].astype(jnp.float32)
            outs.append(d_query * 0.125)
        dqs.append(outs)
    for tile, rows in row_tiles(rows_n):
        dq_ref[rows, :] = jnp.where(low[rows, :], dqs[0][tile], dqs[1][tile]).astype(dq_ref.dtype)
    q_turned = jnp.transpose(q_pair)
    do_turned = jnp.transpose(do_pair)
    for which, (turned, kept) in enumerate(((q_turned, ds_ref), (do_turned, p_ref))):
        both = jnp.concatenate(
            [dot_nn(turned[head * HD : (head + 1) * HD, :], kept[head]) for head in range(2)], axis=0
        )
        both = jnp.transpose(both)
        own_out[which] = both[:rows_n].astype(own_out.dtype)
        far_out[which] = both[rows_n:].astype(far_out.dtype)


def rel_tables(rel_table, keys_n):
    count = rel_table.shape[0]
    rows = jnp.concatenate([rel_table, jnp.broadcast_to(rel_table[-1:], (TILE - count, HD))])
    rows = jnp.concatenate([rows, rows], axis=1)
    wide = jnp.concatenate(
        [rows, jnp.broadcast_to(rows[:1], rows.shape), jnp.broadcast_to(rows[-1:], rows.shape)]
    )
    flip = jnp.arange(TILE)[:, None] + jnp.arange(TILE)[None, :] == TILE - 1
    marks = jnp.arange(keys_n)[:, None] // TILE == jnp.arange(TILE)[None, :]
    return wide, rows[::-1], flip.astype(jnp.bfloat16), marks.astype(jnp.bfloat16)


def pair_blocks(rows, width, group):
    pairs = width // (2 * HD)
    one = pl.BlockSpec((rows, 2 * HD), lambda h: (0, h))
    two = pl.BlockSpec((rows, 2 * HD), lambda h: (0, pairs + h))
    return pairs, one, [one] * group + [two] * group


def fixed(array):
    return pl.BlockSpec(array.shape, lambda h: (0, 0))


def attention_forward(own, query, kv, rel_wide):
    rows, width = query.shape
    pairs, block, kv_blocks = pair_blocks(rows, width, len(kv))
    size = rows * rows * len(kv) * width
    return pl.pallas_call(
        functools.partial(attn_fwd_kernel, len(kv)),
        grid=(pairs,),
        in_specs=[pl.BlockSpec(memory_space=pltpu.SMEM), block, fixed(rel_wide)] + kv_blocks,
        out_specs=[block, pl.BlockSpec((rows, 2 * TILE), lambda h: (0, h))],
        out_shape=[
            jax.ShapeDtypeStruct((rows, width), jnp.bfloat16),
            jax.ShapeDtypeStruct((rows, width // HD * TILE), jnp.float32),
        ],
        scratch_shapes=[
            pltpu.VMEM((2, rows, rows * len(kv)), jnp.float32),
            pltpu.VMEM((2, rows, WIDE), jnp.float32),
            pltpu.VMEM((2, rows, rows * len(kv)), jnp.bfloat16),
        ],
        compiler_params=pltpu.CompilerParams(vmem_limit_bytes=VMEM),
        cost_estimate=pl.CostEstimate(flops=12 * size, bytes_accessed=rows * width * 16, transcendentals=0),
        name="attention_forward",
    )(own, query, rel_wide, *kv, *kv)


def attention_backward(own, query, kv, d_out, log_total, tables):
    rows, width = query.shape
    keys_n = rows * len(kv)
    pairs, block, kv_blocks = pair_blocks(rows, width, len(kv))
    size = rows * keys_n * width
    return pl.pallas_call(
        functools.partial(attn_bwd_kernel, len(kv)),
        grid=(pairs,),
        in_specs=[pl.BlockSpec(memory_space=pltpu.SMEM), block, block]
        + [pl.BlockSpec((rows, 2 * TILE), lambda h: (0, h))]
        + [fixed(table) for table in tables]
        + kv_blocks,
        out_specs=[
            block,
            pl.BlockSpec((2, rows, 2 * HD), lambda h: (0, 0, h)),
            pl.BlockSpec((2, keys_n - rows, 2 * HD), lambda h: (0, 0, h)),
        ],
        out_shape=[
            jax.ShapeDtypeStruct((rows, width), jnp.bfloat16),
            jax.ShapeDtypeStruct((2, rows, width), jnp.bfloat16),
            jax.ShapeDtypeStruct((2, keys_n - rows, width), jnp.bfloat16),
        ],
        scratch_shapes=[
            pltpu.VMEM((2, rows, keys_n), jnp.float32),
            pltpu.VMEM((2, rows, WIDE), jnp.float32),
            pltpu.VMEM((2, rows, keys_n), jnp.float32),
            pltpu.VMEM((2, rows, keys_n), jnp.bfloat16),
            pltpu.VMEM((2, rows, keys_n), jnp.bfloat16),
            pltpu.VMEM((2, rows, TILE), jnp.bfloat16),
        ],
        compiler_params=pltpu.CompilerParams(vmem_limit_bytes=VMEM),
        cost_estimate=pl.CostEstimate(flops=24 * size, bytes_accessed=rows * width * 32, transcendentals=0),
        name="attention_backward",
    )(own, query, d_out, log_total, *tables, *kv, *kv)


class Gather:
    def __init__(self):
        self.chips = lax.axis_size("chip")
        side = math.isqrt(self.chips)
        self.first, self.second = (side, side) if side * side == self.chips else (self.chips, 1)
        chip, core = lax.axis_index("chip"), lax.axis_index("core")
        places = []
        for owner in (core, 1 - core):
            for early, late in self.steps():
                one = self.moved(chip, early, late)
                two = self.moved(chip, late, early)
                places.append(jnp.where(owner == 0, one, two) * 2 + owner)
        self.places = jnp.stack(places).astype(jnp.int32)

    def steps(self):
        steps = [(early, 0) for early in range(self.first)]
        steps += [(0, late) for late in range(1, self.second)]
        return steps + [(e, l) for l in range(1, self.second) for e in range(1, self.first)]

    def moved(self, chip, along_first, along_second):
        return chip ^ (along_first * self.second + along_second)

    def hop(self, block, early, late):
        route = []
        for chip in range(self.chips):
            route.append((self.moved(chip, early, late) * 2, chip * 2))
            route.append((self.moved(chip, late, early) * 2 + 1, chip * 2 + 1))
        return lax.ppermute(block, ("chip", "core"), route)

    def stages(self, shards, used):
        swap = lambda block: lax.ppermute(block, "core", [(0, 1), (1, 0)])
        collect = lambda shard: lax.all_gather(shard, ("fz", "fh"), axis=0, tiled=True)
        count = len(shards)
        shards = list(shards)
        blocks = [collect(shard) for shard in shards[:3]]
        kept, traded, last = [[] for _ in shards], [[] for _ in shards], []
        complete, ahead = 0, self.first + self.second - 1
        for turn in range(count + 1):
            onward = kept[turn - 1][1 : self.first] if turn else []
            if turn > 1:
                late, due = kept[turn - 2][ahead if turn == count else 0 :], blocks[turn : turn + 1] if turn > 2 else []
                self.held = yield [kept[which] + traded[which] for which in range(complete)]
                (onward, late, due), last, self.held = lax.optimization_barrier(
                    ((onward, late, due), last, list(self.held))
                )
                if due:
                    blocks[turn] = due[0]
                further = [self.hop(block, 0, step) for step in range(1, self.second) for block in onward]
                kept[turn - 1] = kept[turn - 1] + further
                across = [swap(block) for block in late]
                traded[turn - 2] = traded[turn - 2] + across
                last = further + across
                complete += 1
            self.held = yield [kept[which] + traded[which] for which in range(complete)]
            if turn < count:
                fresh = blocks[turn][:, : used[turn]]
                coming = shards[turn + 3 : turn + 4]
                late = kept[turn - 1][:ahead] if turn == count - 1 else []
                (fresh, onward, coming, late), last, self.held = lax.optimization_barrier(
                    ((fresh, onward, coming, late), last, list(self.held))
                )
                blocks += [collect(shard) for shard in coming]
                early = [self.hop(fresh, step, 0) for step in range(1, self.first)]
                other = [self.hop(fresh, 0, step) for step in range(1, self.second)]
                kept[turn] = [fresh] + early + other
                traded[turn - 1] = traded[turn - 1] + [swap(block) for block in late]
                last = early + other + (traded[turn - 1] if late else [])
                if turn == 1:
                    further = [self.hop(block, 0, step) for step in range(1, self.second) for block in onward]
                    kept[0] = kept[0] + further
                    last = last + further
            else:
                late, last, self.held = lax.optimization_barrier((kept[-1], last, list(self.held)))
                traded[-1] = [swap(block) for block in late]
        yield [own + other for own, other in zip(kept, traded)]


HBM = pl.BlockSpec(memory_space=pltpu.HBM)
SCALARS = pl.BlockSpec(memory_space=pltpu.SMEM)
VMEM_SPEC = pl.BlockSpec(memory_space=pltpu.VMEM)
TALL = 512
HALO = 32
MIB = 1024 * 1024


def dot_tn(a, b):
    return lax.dot_general(a, b, (((0,), (0,)), ((), ())), preferred_element_type=jnp.float32)


def norm_rows(field):
    centred = field - jnp.mean(field, -1, keepdims=True)
    rate = lax.rsqrt(jnp.mean(centred * centred, -1, keepdims=True) + EPSILON)
    return centred * rate, rate


def norm_back(grad, gain, normed, rate):
    scaled = grad * gain
    inner = jnp.mean(scaled * normed, -1, keepdims=True)
    return (scaled - jnp.mean(scaled, -1, keepdims=True) - normed * inner) * rate


def each_rows(rows, step, body):
    def one(index, carry):
        body(pl.ds(pl.multiple_of(index * step, step), step))
        return carry

    lax.fori_loop(0, rows // step, one, 0)


def shape_of(rows, width, dtype=jnp.bfloat16):
    return jax.ShapeDtypeStruct((rows, width), dtype)


class Weight:
    def __init__(self, places, pieces, begin, width):
        self.places, self.pieces, self.begin, self.width = places, pieces, begin, width
        self.count, self.block = len(pieces), pieces[0].shape[0]
        self.depth = self.count * self.block
        self.bytes = 2 * self.depth * width


class Load:
    def __init__(self, weight, places_ref, pieces, store, sems):
        self.store, self.copies = store, []
        for index, piece in enumerate(pieces):
            row = pl.multiple_of(places_ref[index] * weight.block, weight.block)
            self.copies.append(
                pltpu.make_async_copy(
                    piece.at[:, pl.ds(weight.begin, weight.width)],
                    store.at[pl.ds(row, weight.block), :],
                    sems.at[index],
                )
            )

    def start(self):
        for copy in self.copies:
            copy.start()

    def wait(self):
        for copy in self.copies:
            copy.wait()


class Rows:
    def __init__(self, array, begin, count):
        self.array, self.begin, self.count = array, begin, count


class Factor:
    def __init__(self, ref, rows):
        self.ref, self.at = ref, slice(rows.begin, rows.begin + rows.count)

    def all(self):
        return self.ref[self.at, :]

    def columns(self, at):
        return self.ref[self.at, at]


class Refs:
    pass


def fused(body, name, limit, weights, factors, near, far, outs, far_outs=(), scratch=(), turn=()):
    arrays = []
    for rows in factors.values():
        if not any(rows.array is array for array in arrays):
            arrays.append(rows.array)
    far, far_outs, scratch = dict(far), dict(far_outs), dict(scratch)
    places = [weight.places for weight in list(weights.values())[:1]]
    pieces = [piece for weight in weights.values() for piece in weight.pieces]

    def kernel(*refs):
        refs = list(refs)
        take = lambda count: [refs.pop(0) for _ in range(count)]
        r = Refs()
        places_ref = take(len(places))
        blocks = [take(weight.count) for weight in weights.values()]
        factor_refs, turn_ref = take(len(arrays)), take(len(turn))
        r.turn, r.core = (turn_ref + [None, None])[:2]
        for names in (near, far, outs, far_outs):
            for key, ref in zip(names, take(len(names))):
                setattr(r, key, ref)
        for (key, weight), block in zip(weights.items(), blocks):
            setattr(r, key, Load(weight, places_ref[0], block, *take(2)))
        for key, rows in factors.items():
            (which,) = [i for i, array in enumerate(arrays) if array is rows.array]
            setattr(r, key, Factor(factor_refs[which], rows))
        for key, ref in zip(scratch, take(len(scratch))):
            setattr(r, key, ref)
        body(r)

    total = sum(weight.bytes for weight in weights.values())
    everything = [*near.values(), *far.values(), *outs.values(), *far_outs.values()]
    moved = sum(math.prod(item.shape) * item.dtype.itemsize for item in everything)
    rows = list(near.values())[0].shape[0] if near else 0
    stores = []
    for weight in weights.values():
        stores.append(pltpu.VMEM((weight.depth, weight.width), jnp.bfloat16))
        stores.append(pltpu.SemaphoreType.DMA((weight.count,)))
    made = pl.pallas_call(
        kernel,
        in_specs=[SCALARS] * len(places)
        + [HBM] * len(pieces)
        + [VMEM_SPEC] * len(arrays)
        + [SCALARS] * len(turn)
        + [VMEM_SPEC] * len(near)
        + [HBM] * len(far),
        out_specs=[VMEM_SPEC] * len(outs) + [HBM] * len(far_outs),
        out_shape=[*outs.values(), *far_outs.values()],
        scratch_shapes=stores + list(scratch.values()),
        compiler_params=pltpu.CompilerParams(vmem_limit_bytes=total + limit * MIB),
        cost_estimate=pl.CostEstimate(flops=rows * total, bytes_accessed=moved + total, transcendentals=0),
        name=name,
    )(*places, *pieces, *arrays, *turn, *near.values(), *far.values())
    return made


def wide_step(kind, load, u_ref, down, up, z_ref, outs, then=None):
    z_ref[...] = dot_nt(u_ref[...], down.all()).astype(jnp.bfloat16)
    load.wait()
    if then:
        then()
    width = load.store.shape[1]
    out_width = width // 2 if kind == "glu" else width
    for begin in range(0, out_width, TALL):
        at = slice(begin, begin + TALL)
        parts = [slice(base + begin, base + begin + TALL) for base in range(0, width, out_width)]
        result = [
            dot_nn(u_ref[...], load.store[:, part]) + dot_nn(z_ref[...], up.columns(part)) for part in parts
        ]
        if kind == "silu":
            gate = jax.nn.sigmoid(result[0])
            active = result[0] * gate
            outs[0][:, at] = active.astype(jnp.bfloat16)
            outs[1][:, at] = (gate + active * (1.0 - gate)).astype(jnp.bfloat16)
        elif kind == "glu":
            gate = jax.nn.sigmoid(result[1])
            gated = result[0] * gate
            outs[0][:, at] = gated.astype(jnp.bfloat16)
            outs[1][:, at] = gate.astype(jnp.bfloat16)
            outs[2][:, at] = (gated * (1.0 - gate)).astype(jnp.bfloat16)
        else:
            which = min(begin // outs[0].shape[1], 1)
            first = which * outs[0].shape[1]
            outs[which][:, begin - first : begin - first + TALL] = result[0].astype(jnp.bfloat16)


def narrow_step(factor, load, u_ref, down, up, z_ref, field_ref, field_out, then=None):
    z_ref[...] = dot_nt(u_ref[...], down.all()).astype(jnp.bfloat16)
    load.wait()
    if then:
        then()
    for begin in range(0, load.store.shape[1], TALL):
        at = slice(begin, begin + TALL)
        result = dot_nn(u_ref[...], load.store[:, at]) + dot_nn(z_ref[...], up.columns(at))
        field_out[:, at] = field_ref[:, at].astype(jnp.float32) + factor * result


def norm_step(field_ref, gain_ref, bias_ref, out_ref):
    def finish(at):
        normed = norm_rows(field_ref[at, :])[0] * gain_ref[...] + bias_ref[...]
        out_ref[at, :] = normed.astype(jnp.bfloat16)

    each_rows(field_ref.shape[0], 128, finish)


def grads_step(grad, up, z_ref, u_ref, dz, da_ref, db_ref):
    dz[...] = dot_nt(grad[...], up.all()).astype(jnp.bfloat16)
    db_ref[...] = dot_tn(z_ref[...], grad[...]).astype(jnp.bfloat16)
    da_ref[...] = dot_tn(dz[...], u_ref[...]).astype(jnp.bfloat16)


def inputs_step(load, grad, dz, down, out_ref, then=None):
    load.wait()
    if then:
        then()
    for begin in range(0, load.store.shape[0], TALL):
        at = slice(begin, begin + TALL)
        result = dot_nt(grad[...], load.store[at, :]) + dot_nn(dz[...], down.columns(at))
        out_ref[:, at] = result.astype(out_ref.dtype)


def norm_back_step(d_inputs, field_ref, gain_ref, prior_ref, out_ref):
    def finish(at):
        normed, rate = norm_rows(field_ref[at, :].astype(jnp.float32))
        out_ref[at, :] = prior_ref[at, :] + norm_back(d_inputs[at, :], gain_ref[...], normed, rate)

    each_rows(field_ref.shape[0], 128, finish)


def halves_step(turn_ref, first_out, second_out, rows_of):
    half = first_out.shape[0]
    step = half // 2
    for begin in range(0, 2 * half, step):
        made = rows_of(slice(begin, begin + step)).astype(first_out.dtype)
        at = slice(begin % half, begin % half + step)
        for out, turn in ((first_out, begin // half), (second_out, 1 - begin // half)):

            @pl.when(turn_ref[0] == turn)
            def _(out=out):
                out[at, :] = made


def project_wide(kind, inputs, weight, a, b):
    rows, width = inputs.shape[0], weight.width
    sizes = dict(silu=[width] * 2, glu=[width // 2] * 3, plain=[width // 3, width - width // 3])[kind]
    names = ["out%d" % index for index in range(len(sizes))]

    def body(r):
        r.weight.start()
        wide_step(kind, r.weight, r.u, r.a, r.b, r.z, [getattr(r, key) for key in names])

    outs = dict(z=shape_of(rows, a.count), **{key: shape_of(rows, size) for key, size in zip(names, sizes)})
    return fused(body, "project_" + kind, 14, dict(weight=weight), dict(a=a, b=b), dict(u=inputs), {}, outs)


def project_narrow(inputs, weight, a, b, field, gain, bias, factor):
    rows, width = inputs.shape[0], weight.width

    def body(r):
        r.weight.start()
        narrow_step(factor, r.weight, r.u, r.a, r.b, r.z, r.field, r.made)
        norm_step(r.made, r.gain, r.bias, r.normed)

    outs = dict(
        z=shape_of(rows, a.count), made=shape_of(rows, width, jnp.float32),
        normed=shape_of(rows, width),
    )
    near = dict(u=inputs, field=field, gain=gain, bias=bias)
    return fused(body, "project_next", 14, dict(weight=weight), dict(a=a, b=b), near, {}, outs)


def feed_forward_last(inputs, up, down, factors, field, gain, bias, cotangent, turn):
    rows, width = inputs.shape
    rank, hidden = factors["a_up"].count, up.width

    def body(r):
        r.up.start()
        wide_step("silu", r.up, r.u, r.a_up, r.b_up, r.z_up, (r.held_act, r.held_slope), r.down.start)
        leaving = [
            pltpu.make_async_copy(r.held_act, r.act, r.sems.at[0]),
            pltpu.make_async_copy(r.held_slope, r.slope, r.sems.at[1]),
        ]
        for copy in leaving:
            copy.start()
        narrow_step(0.5, r.down, r.held_act, r.a_down, r.b_down, r.z_down, r.field, r.d_out)
        gain, bias = r.gain[...], r.bias[...]

        def finish(at):
            normed, rate = norm_rows(r.d_out[at, :])
            r.d_out[at, :] = norm_back(r.cot[at, :].astype(jnp.float32), gain, normed, rate)
            return normed * gain + bias

        halves_step(r.turn, r.first, r.second, finish)
        for copy in leaving:
            copy.wait()

    outs = dict(
        z_up=shape_of(rows, rank), z_down=shape_of(rows, rank),
        d_out=shape_of(rows, width, jnp.float32), first=shape_of(rows // 2, width),
        second=shape_of(rows // 2, width),
    )
    near = dict(u=inputs, field=field, gain=gain, bias=bias, cot=cotangent)
    return fused(
        body, "feed_forward_last", 30, dict(up=up, down=down), factors, near, {}, outs,
        dict(act=shape_of(rows, hidden), slope=shape_of(rows, hidden)),
        dict(
            held_act=pltpu.VMEM((rows, hidden), jnp.bfloat16),
            held_slope=pltpu.VMEM((rows, hidden), jnp.bfloat16),
            sems=pltpu.SemaphoreType.DMA((2,)),
        ),
        turn,
    )


def ffn_back_steps(r, d_ref, u_ref):
    r.half[...] = (0.5 * d_ref[...]).astype(jnp.bfloat16)
    r.dz_down[...] = dot_nt(r.half[...], r.b_down.all()).astype(jnp.bfloat16)
    r.db_down[...] = dot_tn(r.z_down[...], r.half[...]).astype(jnp.bfloat16)
    r.down.wait()
    pltpu.make_async_copy(r.slope, r.held_slope, r.sems.at[0]).wait()
    act_copy = pltpu.make_async_copy(r.act, r.held_act, r.sems.at[1])
    act_copy.start()
    r.up.start()
    for begin in range(0, r.down.store.shape[0], TALL):
        at = slice(begin, begin + TALL)
        result = dot_nt(r.half[...], r.down.store[at, :]) + dot_nn(r.dz_down[...], r.a_down.columns(at))
        r.d_hidden[:, at] = (result * r.held_slope[:, at].astype(jnp.float32)).astype(jnp.bfloat16)
    r.dz_up[...] = dot_nt(r.d_hidden[...], r.b_up.all()).astype(jnp.bfloat16)
    act_copy.wait()
    r.da_down[...] = dot_tn(r.dz_down[...], r.held_act[...]).astype(jnp.bfloat16)
    inputs_step(r.up, r.d_hidden, r.dz_up, r.a_up, r.d_inputs)
    r.db_up[...] = dot_tn(r.z_up[...], r.d_hidden[...]).astype(jnp.bfloat16)
    r.da_up[...] = dot_tn(r.dz_up[...], u_ref[...]).astype(jnp.bfloat16)


def ffn_back_parts(rows, width, hidden, rank):
    outs = dict(
        da_up=shape_of(rank, width), db_up=shape_of(rank, hidden),
        da_down=shape_of(rank, hidden), db_down=shape_of(rank, width),
    )
    scratch = dict(
        half=pltpu.VMEM((rows, width), jnp.bfloat16),
        dz_down=pltpu.VMEM((rows, rank), jnp.bfloat16),
        dz_up=pltpu.VMEM((rows, rank), jnp.bfloat16),
        d_hidden=pltpu.VMEM((rows, hidden), jnp.bfloat16),
        d_inputs=pltpu.VMEM((rows, width), jnp.float32),
        held_act=pltpu.VMEM((rows, hidden), jnp.bfloat16),
        held_slope=pltpu.VMEM((rows, hidden), jnp.bfloat16),
        sems=pltpu.SemaphoreType.DMA((2,)),
    )
    return outs, scratch


def feed_forward_back(d_field, up, down, factors, kept, field, gain):
    rows, width = d_field.shape
    inputs, act, slope, z_up, z_down = kept

    def body(r):
        r.down.start()
        pltpu.make_async_copy(r.slope, r.held_slope, r.sems.at[0]).start()
        ffn_back_steps(r, r.d_field, r.u)
        norm_back_step(r.d_inputs, r.field, r.gain, r.d_field, r.made)

    outs, scratch = ffn_back_parts(rows, width, up.width, factors["a_up"].count)
    outs = dict(made=shape_of(rows, width, jnp.float32), **outs)
    near = dict(d_field=d_field, u=inputs, z_up=z_up, z_down=z_down, field=field, gain=gain)
    return fused(
        body, "feed_forward_back", 36, dict(down=down, up=up), factors, near,
        dict(act=act, slope=slope), outs, {}, scratch,
    )


def field_back(kind, grad, weight, a, b, inputs, slot_acts, extras=()):
    rows, depth, rank = grad.shape[0], weight.depth, a.count
    low = grad.dtype == jnp.bfloat16
    names = dict(norm=("prior", "field", "gain"), conv=("field", "gain", "bias"), plain=())[kind]

    def body(r):
        r.weight.start()
        grad_ref = r.grad
        if not low:
            grad_ref = r.low
            r.low[...] = r.grad[...].astype(jnp.bfloat16)
        grads_step(grad_ref, r.b, r.z, r.u, r.dz, r.da, r.db)
        if kind == "plain":
            inputs_step(r.weight, grad_ref, r.dz, r.a, r.made)
            return
        inputs_step(r.weight, grad_ref, r.dz, r.a, r.d_inputs)
        if kind == "norm":
            norm_back_step(r.d_inputs, r.field, r.gain, r.prior, r.made)
            return
        gain = r.gain[...]

        def finish(at):
            normed, rate = norm_rows(r.field[at, :])
            shifted = normed * gain + r.bias[...]
            gate = jax.nn.sigmoid(shifted)
            into = gate + shifted * gate * (1.0 - gate)
            r.made[at, :] = norm_back(r.d_inputs[at, :] * into, gain, normed, rate)

        each_rows(rows, 128, finish)

    made = shape_of(rows, depth, jnp.bfloat16 if kind == "plain" else jnp.float32)
    outs = dict(made=made, da=shape_of(rank, depth), db=shape_of(rank, weight.width))
    scratch = dict(dz=pltpu.VMEM((rows, rank), jnp.bfloat16))
    if not low:
        scratch["low"] = pltpu.VMEM((rows, weight.width), jnp.bfloat16)
    if kind != "plain":
        scratch["d_inputs"] = pltpu.VMEM((rows, depth), jnp.float32)
    near = dict(grad=grad, u=inputs, z=slot_acts, **dict(zip(names, extras)))
    return fused(
        body, "field_back_" + kind, 14, dict(weight=weight), dict(a=a, b=b), near, {}, outs, {}, scratch
    )


def first_half_back(d_query, shares, qkv_w, a_qkv, b_qkv, attn_in, z_qkv, prior, field, gain,
                    up, down, factors, kept, layer_in, layer_gain, turn):
    rows, width = d_query.shape
    inputs, act, slope, z_up, z_down = kept
    names = ["share%d" % index for index in range(len(shares))]

    def body(r):
        r.qkv_w.start()
        r.joined[:, :width] = r.d_query[...]
        for which in range(2):
            total = sum(getattr(r, key)[which].astype(jnp.float32) for key in names)
            r.joined[:, (1 + which) * width : (2 + which) * width] = total.astype(jnp.bfloat16)
        grads_step(r.joined, r.b_qkv, r.z_qkv, r.attn_in, r.dz, r.da_qkv, r.db_qkv)

        def then():
            r.down.start()
            pltpu.make_async_copy(r.slope, r.held_slope, r.sems.at[0]).start()

        inputs_step(r.qkv_w, r.joined, r.dz, r.a_qkv, r.d_inputs, then)
        norm_back_step(r.d_inputs, r.field, r.gain, r.prior, r.d_first)
        ffn_back_steps(r, r.d_first, r.u)

        def finish(at):
            normed, rate = norm_rows(r.layer_in[at, :].astype(jnp.float32))
            return r.d_first[at, :] + norm_back(r.d_inputs[at, :], r.layer_gain[...], normed, rate)

        halves_step(r.turn, r.first, r.second, finish)
        if packed:
            three = [
                r.db_qkv[which * rank : (which + 1) * rank, which * width : (which + 1) * width]
                for which in range(3)
            ]
            model = [r.da_up[...], r.da_qkv[...], r.db_down[...], *three]
            pack_step((r.ours, r.theirs), r.core, fsdp, model, [r.da_down[...], r.db_up[...]])

    rank = factors["a_up"].count
    outs, scratch = ffn_back_parts(rows, width, up.width, rank)
    grads = dict(**outs, da_qkv=shape_of(a_qkv.count, width), db_qkv=shape_of(a_qkv.count, 3 * width))
    outs = dict(first=shape_of(rows // 2, width), second=shape_of(rows // 2, width))
    devices, fsdp = lax.axis_size(EVERYWHERE), lax.axis_size("fz") * lax.axis_size("fh")
    packed = packs_whole(devices, width, up.width)
    if packed:
        scratch.update({key: pltpu.VMEM(item.shape, item.dtype) for key, item in grads.items()})
        count = -(-8 * rank // TILE) * (width // devices) + 2 * rank
        outs["ours"] = outs["theirs"] = jax.ShapeDtypeStruct((devices // 2, count, TILE), jnp.bfloat16)
    else:
        outs.update(grads)
    scratch["joined"] = pltpu.VMEM((rows, 3 * width), jnp.bfloat16)
    scratch["dz"] = pltpu.VMEM((rows, a_qkv.count), jnp.bfloat16)
    scratch["d_first"] = pltpu.VMEM((rows, width), jnp.float32)
    near = dict(
        d_query=d_query, **dict(zip(names, shares)), attn_in=attn_in, z_qkv=z_qkv, prior=prior,
        field=field, gain=gain, u=inputs, z_up=z_up, z_down=z_down, layer_in=layer_in,
        layer_gain=layer_gain,
    )
    return fused(
        body, "first_half_back", 38, dict(qkv_w=qkv_w, down=down, up=up),
        dict(a_qkv=a_qkv, b_qkv=b_qkv, **factors), near, dict(act=act, slope=slope), outs, {}, scratch,
        turn,
    )


def slide(lanes, parts, shifted, taps_ref, shifts, rows, store):
    begin = 0
    for part in parts:
        shifted[0, begin : begin + part.shape[0], :] = part
        begin += part.shape[0]
    length = begin - 8
    for turn in range(1, 8):
        shifted[turn, 0:length, :] = shifted[0, turn : turn + length, :]
    step = 64
    for at in range(0, rows, step):
        total = None
        for tap, shift in enumerate(shifts):
            base = shift - shift % 8 + at
            term = shifted[shift % 8, base : base + step, :] * taps_ref[tap : tap + 1, lanes]
            total = term if total is None else total + term
        store(slice(at, at + step), total)


def each_tile(width, body):
    def one(index, carry):
        body(pl.ds(pl.multiple_of(index * TILE, TILE), TILE))
        return carry

    lax.fori_loop(0, width // TILE, one, 0)


def conv_body(r):
    val_ref, earlier_ref, conv_ref, act_ref = r.value, r.earlier, r.conv, r.act
    taps_ref, gain_ref, bias_ref, shifted = r.taps, r.gain, r.bias, r.shifted
    rows, width = val_ref.shape

    def one(lanes):
        parts = [earlier_ref[:, lanes].astype(jnp.float32), val_ref[:, lanes].astype(jnp.float32)]

        def store(at, total):
            conv_ref[at, lanes] = total

        shifts = [HALO - KERNEL + 1 + tap for tap in range(KERNEL)]
        slide(lanes, parts, shifted, taps_ref, shifts, rows, store)

    each_tile(width, one)

    def finish(at):
        shifted_field = norm_rows(conv_ref[at, :])[0] * gain_ref[...] + bias_ref[...]
        act_ref[at, :] = (shifted_field * jax.nn.sigmoid(shifted_field)).astype(jnp.bfloat16)

    each_rows(rows, 128, finish)


def conv_back_body(r):
    d_ref, later_ref, out_ref = r.d_conv, r.later, r.made
    taps_ref, gate_ref, slope_ref, shifted = r.taps, r.gate, r.slope, r.shifted
    rows, width = d_ref.shape

    def one(lanes):
        parts = [d_ref[:, lanes], later_ref[:, lanes].astype(jnp.float32)]
        high = pl.ds(pl.multiple_of(lanes.start + width, TILE), TILE)

        def store(at, total):
            out_ref[at, lanes] = (total * gate_ref[at, lanes].astype(jnp.float32)).astype(jnp.bfloat16)
            out_ref[at, high] = (total * slope_ref[at, lanes].astype(jnp.float32)).astype(jnp.bfloat16)

        slide(lanes, parts, shifted, taps_ref, [KERNEL - 1 - tap for tap in range(KERNEL)], rows, store)

    each_tile(width, one)


def conv_forward(value, earlier, taps, gain, bias):
    rows, width = value.shape
    near = dict(value=value, earlier=earlier, taps=taps, gain=gain, bias=bias)
    outs = dict(conv=shape_of(rows, width, jnp.float32), act=shape_of(rows, width))
    scratch = dict(shifted=pltpu.VMEM((8, rows + HALO, TILE), jnp.float32))
    return fused(conv_body, "conv_forward", 16, {}, {}, near, {}, outs, {}, scratch)


def conv_backward(d_conv, later, taps, gate, slope):
    rows, width = d_conv.shape
    near = dict(d_conv=d_conv, later=later, taps=taps, gate=gate, slope=slope)
    scratch = dict(shifted=pltpu.VMEM((8, rows + HALO, TILE), jnp.float32))
    outs = dict(made=shape_of(rows, 2 * width))
    return fused(conv_back_body, "conv_backward", 16, {}, {}, near, {}, outs, {}, scratch)[0]


def gather_taps(weight):
    def body(r):
        r.weight.start()
        r.weight.wait()
        r.taps[...] = jnp.transpose(r.weight.store[...].astype(jnp.float32))[:HALO, :]

    outs = dict(taps=shape_of(HALO, weight.depth, jnp.float32))
    return fused(body, "gather_taps", 8, dict(weight=weight), {}, {}, {}, outs)[0]


class Layout:
    def __init__(self, together, fsdp):
        self.fsdp = fsdp
        self.inner = fsdp // together
        self.group = 2 * self.inner

    def place(self, core, f):
        return core * self.fsdp + f

    def round_route(self, turn):
        route = []
        for core in range(2):
            for f in range(self.fsdp):
                clip = (f % 2 + turn) % 2
                spot = f // 2
                target = self.place(spot % 2, (2 * core + clip) * self.inner + spot // 2)
                route.append((self.place(core, f), target))
        return route

    def gather_rows(self, blocks):
        parity = (lax.axis_index("fz") * self.inner + lax.axis_index("fh")) % 2
        clip = lax.axis_index("fz") % 2
        got = []
        for turn in range(2):
            sent = lax.dynamic_index_in_dim(blocks, (parity + turn) % 2, 0, keepdims=False)
            got.append(lax.ppermute(sent, ("core", "fz", "fh"), self.round_route(turn)))
        swap = clip == 1
        return jnp.concatenate(
            [jnp.where(swap, got[1], got[0]), jnp.where(swap, got[0], got[1])], axis=0
        )

    def scatter_rows(self, sent):
        parity = (lax.axis_index("fz") * self.inner + lax.axis_index("fh")) % 2
        got = []
        for turn in range(2):
            route = [(target, source) for source, target in self.round_route(turn)]
            got.append(lax.ppermute(sent[turn], ("core", "fz", "fh"), route))
        swap = parity == 1
        return jnp.stack([jnp.where(swap, got[1], got[0]), jnp.where(swap, got[0], got[1])])

    def spot_index(self, spot):
        return (spot % 2) * self.inner + spot // 2

    def from_spot(self, block, distance, cyclic):
        route = []
        for spot in range(self.group):
            source = spot + distance
            if cyclic:
                source %= self.group
            if 0 <= source < self.group:
                route.append((self.spot_index(source), self.spot_index(spot)))
        return lax.ppermute(block, ("core", "fh"), route)


def pack_adapters(ids, a_model, a_hidden, b_model, b_hidden):
    slots = a_model.shape[2]
    half = RANK // 2
    core = lax.axis_index("core")
    ranks = core * half + jnp.arange(half, dtype=jnp.int32)
    wanted = ids[:, None] * RANK + ranks[None, :]
    picker = (wanted[:, :, None] == jnp.arange(slots, dtype=jnp.int32)).astype(jnp.bfloat16)
    down = lambda a: jnp.einsum("jrs,pks->jprk", picker, a, preferred_element_type=jnp.float32)
    up = lambda b: jnp.einsum("jrs,psn->jprn", picker, b, preferred_element_type=jnp.float32)
    cut = a_hidden.shape[1] // a_model.shape[1]
    span = a_model.shape[1]

    def short(pack):
        rows = pack.reshape(pack.shape[0], pack.shape[1], half, cut, span)
        return jnp.swapaxes(rows, 2, 3).reshape(pack.shape[0], pack.shape[1] * cut, half, span)

    return jnp.concatenate(
        [down(a_model), up(b_model), short(down(a_hidden)), short(up(b_hidden))], axis=1
    ).astype(jnp.bfloat16)


def join_adapters_kernel(models, cut, plan, spots_ref, mine_ref, theirs_ref, *rest):
    wanted = len(plan)
    outs, full, held, sems = rest[:wanted], rest[wanted], rest[wanted + 1 : -1], rest[-1]
    count, groups, half, span = mine_ref.shape
    for step in range(count):
        at = pl.ds(pl.multiple_of(spots_ref[step] * span, span), span)
        for ref, core in ((mine_ref, spots_ref[count]), (theirs_ref, 1 - spots_ref[count])):
            rows = pl.ds(pl.multiple_of(core * half, half), half)
            full[:, rows, at] = ref[step].astype(jnp.float32)
    copies = []
    for which, (out, kept, parts) in enumerate(zip(outs, held, plan)):
        kept[...] = jnp.zeros_like(kept)
        for group, row, column in parts:
            if group < models:
                kept[row : row + RANK, column : column + count * span] = full[group].astype(kept.dtype)
                continue
            for f in range(count):
                begin = column + f * cut * span
                kept[row : row + RANK, begin : begin + span] = full[
                    group, :, f * span : (f + 1) * span
                ].astype(kept.dtype)
        copies.append(pltpu.make_async_copy(kept, out, sems.at[which]))
        copies[-1].start()
    for copy in copies:
        copy.wait()


def move_adapters(layout, pack, cut, shapes, plan, models):
    core = lax.axis_index("core")
    count = layout.fsdp
    here = lax.axis_index("fz") * layout.inner + lax.axis_index("fh")
    pieces = []
    for step in range(count):
        target = (here + step) % count
        piece = lax.dynamic_index_in_dim(pack, target // layout.inner, 0, keepdims=False)
        if step:
            route = [(f, (f + step) % count) for f in range(count)]
            piece = lax.ppermute(piece, ("fz", "fh"), route)
        pieces.append(piece)
    mine = jnp.stack(pieces)
    theirs = lax.ppermute(mine, "core", [(0, 1), (1, 0)])
    spots = jnp.stack([(here - step) % count for step in range(count)] + [core]).astype(jnp.int32)
    _, groups, half, span = mine.shape
    return pl.pallas_call(
        functools.partial(join_adapters_kernel, models, cut, plan),
        in_specs=[SCALARS, VMEM_SPEC, VMEM_SPEC],
        out_specs=[HBM] * len(shapes),
        out_shape=[shape_of(*shape) for shape in shapes],
        scratch_shapes=[pltpu.VMEM((groups, 2 * half, count * span), jnp.float32)]
        + [pltpu.VMEM(shape, jnp.bfloat16) for shape in shapes]
        + [pltpu.SemaphoreType.DMA((len(shapes),))],
        compiler_params=pltpu.CompilerParams(vmem_limit_bytes=16 * 1024 * 1024),
        name="join_adapters",
    )(spots, mine, theirs)


def factor_plan(models, hiddens, cut, span):
    hidden = [(models + which * cut + q, which * RANK, q * span) for which in range(hiddens) for q in range(cut)]
    return [[(group, group * RANK, 0) for group in range(models)], hidden]


def first_adapters(layout, pack, cut, width, hidden):
    shapes = [(2 * RANK, width), (2 * RANK, hidden)]
    model, inner = move_adapters(layout, pack, cut, shapes, factor_plan(2, 2, cut, pack.shape[3]), 2)
    return model, inner


def other_adapters(layout, pack, cut, width, hidden):
    shapes = [(15 * RANK, width), (2 * RANK, hidden), (3 * RANK, 3 * width), (RANK, 2 * width)]
    plan = factor_plan(15, 2, cut, pack.shape[3]) + [
        [(7 + which, which * RANK, which * width) for which in range(3)],
        [(13, 0, 0), (14, 0, width)],
    ]
    return move_adapters(layout, pack, cut, shapes, plan, 15)


def pack_step(outs, core_ref, fsdp, model, hidden):
    places, _, lanes = outs[0].shape
    model = jnp.concatenate([part.astype(jnp.float32) for part in model], axis=0)
    tiles = -(-model.shape[0] // TILE)
    if model.shape[0] % TILE:
        rest = jnp.zeros((tiles * TILE - model.shape[0], model.shape[1]), jnp.float32)
        model = jnp.concatenate([model, rest], axis=0)
    turned = [jnp.transpose(model[k * TILE : (k + 1) * TILE]).astype(jnp.bfloat16) for k in range(tiles)]
    share = model.shape[1] // (2 * places)

    def write(here):
        for device in range(2 * places):
            chip, other = divmod(device, 2 * fsdp)
            core, f = divmod(other, fsdp)
            out, place, row = outs[0 if core == here else 1], chip * fsdp + f, 0
            for part in turned:
                out[place, row : row + share, :] = part[device * share : (device + 1) * share]
                row += share
            for part in hidden:
                out[place, row : row + RANK, :] = part[:, device * lanes : (device + 1) * lanes]
                row += RANK

    for here in range(2):
        pl.when(core_ref[0] == here)(functools.partial(write, here))


def packs_whole(devices, width, hidden):
    return hidden // devices == TILE and width // devices % RANK == 0


def pack_grads_kernel(models, count, fsdp, *refs):
    core_ref, refs = refs[0], refs[1:]
    outs, sems, held = refs[count : count + 2], refs[count + 2], refs[count + 3 :]
    copies = [pltpu.make_async_copy(refs[i], held[i], sems.at[i]) for i in range(count)]
    for copy in copies:
        copy.start()
    for copy in copies:
        copy.wait()
    pack_step(outs, core_ref, fsdp, [ref[...] for ref in held[:models]], [ref[...] for ref in held[models:]])


def pack_grads(model, hidden):
    core = lax.axis_index("core").astype(jnp.int32).reshape(1)
    devices, fsdp = lax.axis_size(EVERYWHERE), lax.axis_size("fz") * lax.axis_size("fh")
    width = model[0].shape[1]
    share, hidden_share = width // devices, hidden[0].shape[1] // devices
    groups = sum(part.shape[0] for part in model)
    tiles = -(-groups // TILE)
    if packs_whole(devices, width, hidden[0].shape[1]):
        rows = tiles * share + RANK * len(hidden)
        return pl.pallas_call(
            functools.partial(pack_grads_kernel, len(model), len(model) + len(hidden), fsdp),
            in_specs=[SCALARS] + [HBM] * (len(model) + len(hidden)),
            out_specs=[VMEM_SPEC] * 2,
            out_shape=[jax.ShapeDtypeStruct((devices // 2, rows, TILE), jnp.bfloat16)] * 2,
            scratch_shapes=[pltpu.SemaphoreType.DMA((len(model) + len(hidden),))]
            + [pltpu.VMEM(item.shape, item.dtype) for item in (*model, *hidden)],
            compiler_params=pltpu.CompilerParams(vmem_limit_bytes=PACK_ROOM),
            name="pack_grads",
        )(core, *model, *hidden)
    rest = jnp.zeros((tiles * TILE - groups, width), jnp.bfloat16)
    turned = jnp.concatenate([*model, rest]).T
    split = jnp.concatenate(hidden).reshape(-1, devices, hidden_share)
    parts = [turned[:, k * TILE : (k + 1) * TILE].reshape(devices, share, TILE) for k in range(tiles)]
    parts.append(jnp.transpose(split, (1, 0, 2)).reshape(devices, -1, TILE))
    part = jnp.concatenate(parts, axis=1).reshape(devices // (2 * fsdp), 2, fsdp, -1, TILE)
    part = jnp.swapaxes(part, 0, 1).reshape(2, devices // 2, -1, TILE)
    return tuple(jnp.where(core[0] == 0, part, part[::-1]))


def send_grads(model, hidden):
    groups = sum(item.shape[0] for item in model)
    return send_packed(pack_grads(model, hidden), groups, len(hidden), model[0].shape[1], hidden[0].shape[1])


def send_packed(part, groups, hiddens, width, features):
    ours, theirs = part
    came = lax.ppermute(theirs, "core", [(0, 1), (1, 0)])
    both = (ours.astype(jnp.float32) + came.astype(jnp.float32)).astype(jnp.bfloat16)
    got = lax.all_to_all(both, ("chip", "fz", "fh"), 0, 0, tiled=True)
    devices = lax.axis_size(EVERYWHERE)
    share, hidden_share = width // devices, features // devices
    begin = -(-groups // TILE) * share
    if hidden_share == TILE:
        return got, got, begin
    return got, got[:, begin:].reshape(-1, RANK * hiddens, hidden_share), 0


def place_grads_kernel(batches, ids_ref, *refs):
    sent, outs = refs[: 2 * len(batches)], refs[2 * len(batches) :]
    for out in outs:
        out[...] = jnp.zeros_like(out)
    share = outs[0].shape[1]
    slot = lax.broadcasted_iota(jnp.int32, (share, TILE), 1) // RANK
    in_tile = TILE // RANK

    def one(sender, carry):
        owner = ids_ref[sender]
        at = pl.ds(pl.multiple_of(owner * RANK, RANK), RANK)
        for which, (model_plan, hidden_plan, begin) in enumerate(batches):
            model_ref, hidden_ref = sent[2 * which : 2 * which + 2]
            for group, (out, index) in enumerate(model_plan):
                tile, local_group = divmod(group, in_tile)
                block = model_ref[sender, tile * share : (tile + 1) * share, :].astype(jnp.float32)
                turn = lax.rem(owner - local_group + in_tile, in_tile) * RANK
                outs[out][index] += jnp.where(slot == owner, pltpu.roll(block, turn, 1), 0.0)
            for group, (out, index) in enumerate(hidden_plan):
                rows = slice(begin + group * RANK, begin + (group + 1) * RANK)
                outs[out][index, at, :] += hidden_ref[sender, rows, :].astype(jnp.float32)
        return carry

    lax.fori_loop(0, sent[0].shape[0], one, 0)


def place_grads(ids, batches, shapes):
    arrays, plans = [], []
    for (model, hidden, begin), model_plan, hidden_plan in batches:
        arrays += [model, hidden]
        plans.append((model_plan, hidden_plan, begin))
    return pl.pallas_call(
        functools.partial(place_grads_kernel, plans),
        in_specs=[SCALARS] + [VMEM_SPEC] * len(arrays),
        out_specs=[VMEM_SPEC] * len(shapes),
        out_shape=[jax.ShapeDtypeStruct(shape, jnp.float32) for shape in shapes],
        compiler_params=pltpu.CompilerParams(vmem_limit_bytes=16 * 1024 * 1024),
        name="place_grads",
    )(ids, *arrays)


def local(
    frames,
    cotangent,
    adapter_ids,
    norm_gains,
    norm_biases,
    rel_table,
    w_up,
    w_down,
    w_qkv,
    w_out,
    w_pw1,
    w_depth,
    w_pw2,
    ad_a_model,
    ad_a_hidden,
    ad_b_model,
    ad_b_hidden,
):
    group_clips, frame_span, width = frames.shape
    together = 2 * group_clips
    layout = Layout(together, lax.axis_size("fz") * lax.axis_size("fh"))
    rows = 2 * frame_span
    slots = ad_a_model.shape[2]
    spot = lax.axis_index("fh") * 2 + lax.axis_index("core")
    own = (spot * (rows // TILE)).astype(jnp.int32).reshape(1)
    other_ids = lax.ppermute(adapter_ids, "core", [(0, 1), (1, 0)])
    at_zero = lax.axis_index("core") == 0
    near_ids = jnp.concatenate(
        [jnp.where(at_zero, adapter_ids, other_ids), jnp.where(at_zero, other_ids, adapter_ids)]
    )
    factors = (ad_a_model, ad_a_hidden, ad_b_model, ad_b_hidden)
    cut = ad_a_hidden.shape[1] // ad_a_model.shape[1]
    first_pack = pack_adapters(near_ids, *[factor[:1] for factor in factors])
    other_pack = pack_adapters(near_ids, *[factor[1:] for factor in factors])
    gather = Gather()
    taps = jnp.pad(w_depth.T, ((0, 0), (0, width - KERNEL)))
    shards = [
        w_up[0],
        w_down[0],
        jnp.concatenate([w_qkv, w_out], axis=1),
        jnp.concatenate([w_pw1, w_pw2, taps], axis=1),
        w_up[1],
        w_down[1],
    ]
    used = [shard.shape[1] for shard in shards]
    used[3] = 3 * width + TILE
    turns = gather.stages(shards, used)
    next(turns)

    def weight_of(units, which, begin=0, columns=None):
        return Weight(gather.places, units[which], begin, columns or used[which])

    gains = [norm_gains[index : index + 1] for index in range(6)]
    biases = [norm_biases[index : index + 1] for index in range(6)]

    turns.send([first_pack, other_pack])
    first_pack, other_pack = gather.held
    turns.send([frames, first_pack, other_pack, *rel_tables(rel_table, rows * layout.group)])
    frames, first_pack, other_pack, *tables = gather.held
    layer_in = layout.gather_rows(frames)
    turns.send([])
    hidden_width = w_up.shape[2]
    first_four = first_adapters(layout, first_pack, cut, width, hidden_width)
    units = turns.send([layer_in, *first_four])
    layer_in, *first_four = gather.held
    field = layer_in.astype(jnp.float32)
    first_in = (norm_rows(field)[0] * gains[0] + biases[0]).astype(jnp.bfloat16)
    a_up0, b_down0 = [Rows(first_four[0], row * RANK, RANK) for row in range(2)]
    a_down0, b_up0 = [Rows(first_four[1], row * RANK, RANK) for row in range(2)]
    up0_w = weight_of(units, 0)
    z_up0, act_one, slope_one = project_wide("silu", first_in, up0_w, a_up0, b_up0)
    units = turns.send([act_one, slope_one, other_pack])
    act_one, slope_one, other_pack = gather.held
    others = other_adapters(layout, other_pack, cut, width, hidden_width)
    units = turns.send([])
    down0_w = weight_of(units, 1)
    z_down0, after_ffn, attn_in = project_narrow(
        act_one, down0_w, a_down0, b_down0, layer_in, gains[1], biases[1], 0.5
    )
    units = turns.send([after_ffn, attn_in, *others])
    after_ffn, attn_in, *others = gather.held
    model, inner, qkv_up, glu_up = others
    qkv_down = Rows(model, 0, 3 * RANK)
    qkv_up, glu_up = Rows(qkv_up, 0, 3 * RANK), Rows(glu_up, 0, RANK)
    a_out, a_pw1, a_pw2, a_up1, b_out, b_pw2, b_down1 = [
        Rows(model, row * RANK, RANK) for row in (3, 4, 5, 6, 10, 11, 12)
    ]
    a_down1, b_up1 = [Rows(inner, row * RANK, RANK) for row in range(2)]
    units = turns.send([])
    qkv_w, out_w = weight_of(units, 2, 0, 3 * width), weight_of(units, 2, 3 * width, width)
    z_qkv, query, own_kv = project_wide("plain", attn_in, qkv_w, qkv_down, qkv_up)
    units = turns.send([query, own_kv])
    query, own_kv = gather.held
    units = turns.send([])
    pw1_w, pw2_w = weight_of(units, 3, 0, 2 * width), weight_of(units, 3, 2 * width, width)
    taps = gather_taps(weight_of(units, 3, 3 * width, TILE))
    kv = [own_kv] + [layout.from_spot(own_kv, step, True) for step in range(1, layout.group)]
    mixed, log_total = attention_forward(own, query, kv, tables[0])
    turns.send([mixed, log_total])
    mixed, log_total = gather.held
    units = turns.send([])
    up1_w, down1_w = weight_of(units, 4), weight_of(units, 5)
    mixed, cotangent = lax.optimization_barrier((mixed, cotangent))
    d_out = layout.gather_rows(cotangent)
    z_out, after_attn, conv_in = project_narrow(
        mixed, out_w, a_out, b_out, after_ffn, gains[2], biases[2], 1.0
    )
    z_pw1, gated, gate, gate_slope = project_wide("glu", conv_in, pw1_w, a_pw1, glu_up)
    earlier = layout.from_spot(gated[rows - HALO :], -1, False)
    conv_out, conv_act = conv_forward(gated, earlier, taps, gains[3], biases[3])
    z_pw2, after_conv, second_in = project_narrow(
        conv_act, pw2_w, a_pw2, b_pw2, after_attn, gains[4], biases[4], 1.0
    )
    factors_two = dict(a_up=a_up1, b_up=b_up1, a_down=a_down1, b_down=b_down1)
    turn = [(lax.axis_index("fz") % 2).astype(jnp.int32).reshape(1)]
    z_up1, z_down1, d_fourth, *result, act_two, slope_two = feed_forward_last(
        second_in, up1_w, down1_w, factors_two, after_conv, gains[5], biases[5], d_out, turn
    )
    layer_out = layout.scatter_rows(result)

    d_third, da_up1, db_up1, da_down1, db_down1 = feed_forward_back(
        d_fourth, up1_w, down1_w, factors_two, (second_in, act_two, slope_two, z_up1, z_down1),
        after_conv, gains[4],
    )
    d_conv, da_pw2, db_pw2 = field_back(
        "conv", d_third, pw2_w, a_pw2, b_pw2, conv_act, z_pw2,
        (conv_out, gains[3], biases[3]),
    )
    d_conv, layer_out = lax.optimization_barrier((d_conv, layer_out))
    later = layout.from_spot(d_conv[:HALO].astype(jnp.bfloat16), 1, False)
    d_joined = conv_backward(d_conv, later, taps, gate, gate_slope)
    d_second, da_pw1, db_pw1 = field_back(
        "norm", d_joined, pw1_w, a_pw1, glu_up, conv_in, z_pw1, (d_third, after_attn, gains[2])
    )
    d_mixed, da_out, db_out = field_back(
        "plain", d_second, out_w, a_out, b_out, mixed, z_out, ()
    )
    label = jnp.full((RANK, width), near_ids[lax.axis_index("fz")]).astype(jnp.bfloat16)
    early = send_grads(
        [da_out, da_pw1, da_pw2, da_up1, db_out, db_pw2, db_down1]
        + [db_pw1[:, :width], db_pw1[:, width:], label],
        [da_down1, db_up1],
    )
    d_query, d_own, d_far = attention_backward(own, query, kv, d_mixed, log_total, tables)
    shares = [d_own]
    for step in range(1, layout.group):
        shares.append(layout.from_spot(d_far[:, (step - 1) * rows : step * rows], -step, True))
    first_half, second_half_rows, *grads = first_half_back(
        d_query, shares, qkv_w, qkv_down, qkv_up, attn_in, z_qkv, d_second, after_ffn, gains[1],
        up0_w, down0_w, dict(a_up=a_up0, b_up=b_up0, a_down=a_down0, b_down=b_down0),
        (first_in, act_one, slope_one, z_up0, z_down0), layer_in, gains[0],
        [*turn, lax.axis_index("core").astype(jnp.int32).reshape(1)],
    )
    grad_frames = layout.scatter_rows([first_half, second_half_rows])
    if len(grads) == 2:
        late = send_packed(grads, 8 * RANK, 2, width, hidden_width)
    else:
        da_up0, db_up0, da_down0, db_down0, da_qkv, db_qkv = grads
        db_three = [
            db_qkv[index * RANK : (index + 1) * RANK, index * width : (index + 1) * width]
            for index in range(3)
        ]
        late = send_grads([da_up0, da_qkv, db_down0, *db_three], [da_down0, db_up0])
    devices = lax.axis_size(EVERYWHERE)
    share, hidden_share = width // devices, hidden_width // devices
    ids = (early[0][:, share, RANK] * jnp.bfloat16(0.5)).astype(jnp.int32)
    early_plan = [(0, index) for index in range(4, 8)] + [(1, index) for index in range(4, 9)]
    late_plan = [(0, index) for index in range(4)] + [(1, index) for index in range(4)]
    grad_a_model, grad_b_model, grad_a_hidden, grad_b_hidden = place_grads(
        ids,
        [(early, early_plan, [(2, 1), (3, 1)]), (late, late_plan, [(2, 0), (3, 0)])],
        [(8, share, slots), (9, share, slots), (2, slots, hidden_share), (2, slots, hidden_share)],
    )
    grad_b_model = jnp.swapaxes(grad_b_model, 1, 2)
    grad_a_hidden = jnp.swapaxes(grad_a_hidden, 1, 2)
    return (layer_out, grad_frames, grad_a_model, grad_a_hidden, grad_b_model, grad_b_hidden)


def solution(mesh):
    every = ("chip", "core", "fz", "fh")
    clips, spread = ("chip", "core"), ("fz", "fh")
    in_specs = (
        P(clips, spread, None),
        P(clips, spread, None),
        P(clips),
        P(),
        P(),
        P(),
        P(None, every, None),
        P(None, every, None),
        P(every, None),
        P(every, None),
        P(every, None),
        P(None, every),
        P(every, None),
        P(None, spread, None),
        P(None, spread, None),
        P(None, None, spread),
        P(None, None, spread),
    )
    out_specs = (
        P(clips, spread, None),
        P(clips, spread, None),
        P(None, every, None),
        P(None, every, None),
        P(None, None, every),
        P(None, None, every),
    )

    def run(frames, *rest):
        dp, fsdp = mesh.shape["dp"], mesh.shape["fsdp"]
        together = 2 * frames.shape[0] // dp
        cut = Mesh(
            mesh.devices.reshape(dp // 2, 2, together, fsdp // together), EVERYWHERE
        )
        return jax.shard_map(
            local, mesh=cut, in_specs=in_specs, out_specs=out_specs, check_vma=False
        )(frames, *rest)

    return run
```

```python
import functools
import math

import jax
import jax.numpy as jnp
from jax import lax
from jax.experimental import pallas as pl
from jax.experimental.pallas import tpu as pltpu
from jax.sharding import Mesh
from jax.sharding import PartitionSpec as P

HEADS = 16
KERNEL = 31
RANK = 16
EPSILON = 1e-05
PACK_ROOM = 56 * 1024 * 1024
EVERYWHERE = ("chip", "core", "fz", "fh")

HD = 64
REL_LEFT = 64
REL_RIGHT = 8
TILE = 128
WIDE = 3 * TILE
VMEM = 32 * 1024 * 1024


def dot_nn(a, b):
    return lax.dot_general(a, b, (((1,), (0,)), ((), ())), preferred_element_type=jnp.float32)


def dot_nt(a, b):
    return lax.dot_general(a, b, (((1,), (1,)), ((), ())), preferred_element_type=jnp.float32)


def chunk_plan(tile, chunks):
    return [{chunks - 1: 0, 0: 1, 1: 2}.get((c - tile) % chunks) for c in range(chunks)]


def far_left(c, tile, chunks, own):
    return jnp.logical_or(c + own >= chunks, c < tile)


def wrapped_band(c, tile, chunks, own):
    if tile == 0 and c == chunks - 1:
        return own > 0
    if c == tile + 1:
        return c + own < chunks
    return None


def tile_scores(scores, table, tile, own):
    near = pltpu.roll(table[:, :TILE], TILE // 2, 1, stride=1, stride_axis=0)
    first, last = table[:, TILE : 2 * TILE], table[:, 2 * TILE :]
    ahead = lane_ahead()
    bands = [
        jnp.where(ahead >= TILE // 2, near, first),
        jnp.where(ahead < -(TILE // 2), first, jnp.where(ahead >= TILE // 2, last, near)),
        jnp.where(ahead < -(TILE // 2), near, last),
    ]
    chunks = scores.shape[1] // TILE
    parts = []
    for c, spot in enumerate(chunk_plan(tile, chunks)):
        part = scores[:, c * TILE : (c + 1) * TILE]
        if spot is None:
            bias = first if c < tile else jnp.where(c + own >= chunks, first, last)
        else:
            bias = bands[spot]
            true_band = wrapped_band(c, tile, chunks, own)
            if true_band is not None:
                bias = jnp.where(true_band, bias, jnp.where(far_left(c, tile, chunks, own), first, last))
        parts.append(part + bias)
    return parts


def lane_ahead():
    lane = lax.broadcasted_iota(jnp.int32, (TILE, TILE), 1)
    return lane - lax.broadcasted_iota(jnp.int32, (TILE, TILE), 0)


def stacked(refs):
    return jnp.concatenate([ref[...] for ref in refs], axis=0)


def head_lanes(rows):
    low = lax.broadcasted_iota(jnp.int32, (rows, 2 * HD), 1) < HD
    return low, (low, jnp.logical_not(low))


def row_tiles(rows):
    return [(tile, slice(tile * TILE, (tile + 1) * TILE)) for tile in range(rows // TILE)]


def attn_fwd_kernel(group, own_ref, q_ref, rel_ref, *refs):
    own = own_ref[0]
    keys, values, rel_wide = stacked(refs[:group]), stacked(refs[group : 2 * group]), rel_ref[...]
    o_ref, rate_ref, p_ref, s_ref, w_ref = refs[2 * group :]
    rows_n = q_ref.shape[0]
    low, heads = head_lanes(rows_n)
    q_pair = q_ref[...] * jnp.bfloat16(0.125)
    for head, lanes in enumerate(heads):
        q_head = jnp.where(lanes, q_pair, jnp.zeros_like(q_pair))
        s_ref[head] = dot_nt(q_head, keys)
        w_ref[head] = dot_nt(q_head, rel_wide)
    ones = jnp.ones_like(values)
    values_ones = jnp.concatenate([values, ones], axis=1)
    outs = []
    for head in range(2):
        for tile, rows in row_tiles(rows_n):
            parts = tile_scores(s_ref[head, rows, :], w_ref[head, rows, :], tile, own)
            top = jnp.max(functools.reduce(jnp.maximum, parts), axis=1, keepdims=True)
            top = jnp.broadcast_to(top, (TILE, TILE))
            expo = [jnp.exp(part - top).astype(jnp.bfloat16) for part in parts]
            p_ref[head, rows, :] = jnp.concatenate(expo, axis=1)
        outs.append(dot_nn(p_ref[head], values_ones))
        total = outs[head][:, 2 * HD :]
        rate_ref[:, head * TILE : (head + 1) * TILE] = 1.0 / total
        outs[head] = outs[head][:, : 2 * HD] / total
    o_ref[...] = jnp.where(low, outs[0], outs[1]).astype(jnp.bfloat16)


def attn_bwd_kernel(group, own_ref, q_ref, do_ref, rate_ref, e_ref, rev_ref, flip_ref, mark_ref, *refs):
    own = own_ref[0]
    keys, values = stacked(refs[:group]), stacked(refs[group : 2 * group])
    dq_ref, own_out, far_out, dp_ref, ds_ref, p_ref, band_ref = refs[2 * group :]
    rows_n, keys_n = q_ref.shape[0], keys.shape[0]
    chunks = keys_n // TILE
    low, heads = head_lanes(rows_n)
    lane = lax.broadcasted_iota(jnp.int32, (1, TILE), 1)
    q_pair = q_ref[...] * jnp.bfloat16(0.125)
    do_pair = do_ref[...]
    keys_marked = jnp.concatenate([keys, mark_ref[...]], axis=1)
    for head, lanes in enumerate(heads):
        dp_ref[head] = dot_nt(jnp.where(lanes, do_pair, jnp.zeros_like(do_pair)), values)
    dqs = []
    ahead = lane_ahead()
    for head in range(2):
        edges = []
        for tile, rows in row_tiles(rows_n):
            rate = rate_ref[rows, head * TILE : (head + 1) * TILE]
            parts = [e_ref[head, rows, c * TILE : (c + 1) * TILE] for c in range(chunks)]
            probs = [part.astype(jnp.float32) * rate for part in parts]
            d_parts = [dp_ref[head, rows, c * TILE : (c + 1) * TILE] for c in range(chunks)]
            inner = functools.reduce(jnp.add, [p * d for p, d in zip(probs, d_parts)])
            inner = jnp.sum(inner, axis=1, keepdims=True)
            d_scores = [(p * (d - inner)).astype(jnp.bfloat16) for p, d in zip(probs, d_parts)]
            p_ref[head, rows, :] = jnp.concatenate([p.astype(jnp.bfloat16) for p in probs], axis=1)
            ds_ref[head, rows, :] = jnp.concatenate(d_scores, axis=1)
            band = [None, None, None]
            for c, spot in enumerate(chunk_plan(tile, chunks)):
                if spot is not None:
                    near = wrapped_band(c, tile, chunks, own)
                    piece = d_scores[c]
                    band[spot] = piece if near is None else jnp.where(near, piece, jnp.zeros_like(piece))
            behind, beyond = ahead < -(TILE // 2), ahead >= TILE // 2
            none = jnp.zeros_like(band[0])
            band_ref[head, rows, :] = jnp.where(beyond, band[0], jnp.where(behind, band[2], band[1]))
            sides = (
                (jnp.where(beyond, none, band[0]), jnp.where(behind, band[1], none)),
                (jnp.where(behind, none, band[2]), jnp.where(beyond, band[1], none)),
            )
            edges.append([a.astype(jnp.float32) + b.astype(jnp.float32) for a, b in sides])
        turned = dot_nn(band_ref[head], flip_ref[...])
        turned = jnp.concatenate(
            [
                pltpu.roll(turned[rows, :], TILE // 2, 1, stride=1, stride_axis=0).astype(jnp.bfloat16)
                for _, rows in row_tiles(rows_n)
            ],
            axis=0,
        )
        marked = dot_nn(ds_ref[head], keys_marked)
        near_part = dot_nn(turned, rev_ref[...])
        outs = []
        for tile, rows in row_tiles(rows_n):
            weights = [jnp.zeros((1, TILE), jnp.float32)] * 2
            for c, spot in enumerate(chunk_plan(tile, chunks)):
                near = wrapped_band(c, tile, chunks, own)
                if spot is not None and near is None:
                    continue
                left = far_left(c, tile, chunks, own)
                far = 1.0 if spot is None else jnp.where(near, 0.0, 1.0)
                for side, on in enumerate((left, jnp.logical_not(left))):
                    here = jnp.where(on, far, 0.0)
                    weights[side] = weights[side] + jnp.where(lane == c, here, 0.0)
            sums = marked[rows, TILE:]
            before, after = [
                jnp.sum(sums * weight + edge, axis=1, keepdims=True)
                for weight, edge in zip(weights, edges[tile])
            ]
            d_query = marked[rows, :TILE] + near_part[rows, :]
            d_query = d_query + before * rev_ref[TILE - 1 : TILE, :].astype(jnp.float32)
            d_query = d_query + after * rev_ref[0:1, :].astype(jnp.float32)
            outs.append(d_query * 0.125)
        dqs.append(outs)
    for tile, rows in row_tiles(rows_n):
        dq_ref[rows, :] = jnp.where(low[rows, :], dqs[0][tile], dqs[1][tile]).astype(dq_ref.dtype)
    q_turned = jnp.transpose(q_pair)
    do_turned = jnp.transpose(do_pair)
    for which, (turned, kept) in enumerate(((q_turned, ds_ref), (do_turned, p_ref))):
        both = jnp.concatenate(
            [dot_nn(turned[head * HD : (head + 1) * HD, :], kept[head]) for head in range(2)], axis=0
        )
        both = jnp.transpose(both)
        own_out[which] = both[:rows_n].astype(own_out.dtype)
        far_out[which] = both[rows_n:].astype(far_out.dtype)


def rel_tables(rel_table, keys_n):
    count = rel_table.shape[0]
    rows = jnp.concatenate([rel_table, jnp.broadcast_to(rel_table[-1:], (TILE - count, HD))])
    rows = jnp.concatenate([rows, rows], axis=1)
    wide = jnp.concatenate(
        [rows, jnp.broadcast_to(rows[:1], rows.shape), jnp.broadcast_to(rows[-1:], rows.shape)]
    )
    flip = jnp.arange(TILE)[:, None] + jnp.arange(TILE)[None, :] == TILE - 1
    marks = jnp.arange(keys_n)[:, None] // TILE == jnp.arange(TILE)[None, :]
    return wide, rows[::-1], flip.astype(jnp.bfloat16), marks.astype(jnp.bfloat16)


def pair_blocks(rows, width, group):
    pairs = width // (2 * HD)
    one = pl.BlockSpec((rows, 2 * HD), lambda h: (0, h))
    two = pl.BlockSpec((rows, 2 * HD), lambda h: (0, pairs + h))
    return pairs, one, [one] * group + [two] * group


def fixed(array):
    return pl.BlockSpec(array.shape, lambda h: (0, 0))


def attention_forward(own, query, kv, rel_wide):
    rows, width = query.shape
    pairs, block, kv_blocks = pair_blocks(rows, width, len(kv))
    size = rows * rows * len(kv) * width
    return pl.pallas_call(
        functools.partial(attn_fwd_kernel, len(kv)),
        grid=(pairs,),
        in_specs=[pl.BlockSpec(memory_space=pltpu.SMEM), block, fixed(rel_wide)] + kv_blocks,
        out_specs=[
            block,
            pl.BlockSpec((rows, 2 * TILE), lambda h: (0, h)),
            pl.BlockSpec((2, rows, rows * len(kv)), lambda h: (h, 0, 0)),
        ],
        out_shape=[
            jax.ShapeDtypeStruct((rows, width), jnp.bfloat16),
            jax.ShapeDtypeStruct((rows, width // HD * TILE), jnp.float32),
            jax.ShapeDtypeStruct((width // HD, rows, rows * len(kv)), jnp.bfloat16),
        ],
        scratch_shapes=[
            pltpu.VMEM((2, rows, rows * len(kv)), jnp.float32),
            pltpu.VMEM((2, rows, WIDE), jnp.float32),
        ],
        compiler_params=pltpu.CompilerParams(vmem_limit_bytes=VMEM),
        cost_estimate=pl.CostEstimate(flops=12 * size, bytes_accessed=rows * width * 16, transcendentals=0),
        name="attention_forward",
    )(own, query, rel_wide, *kv, *kv)


def attention_backward(own, query, kv, d_out, rate, expo, tables):
    rows, width = query.shape
    keys_n = rows * len(kv)
    pairs, block, kv_blocks = pair_blocks(rows, width, len(kv))
    size = rows * keys_n * width
    return pl.pallas_call(
        functools.partial(attn_bwd_kernel, len(kv)),
        grid=(pairs,),
        in_specs=[pl.BlockSpec(memory_space=pltpu.SMEM), block, block]
        + [pl.BlockSpec((rows, 2 * TILE), lambda h: (0, h))]
        + [pl.BlockSpec((2, rows, keys_n), lambda h: (h, 0, 0))]
        + [fixed(table) for table in tables[1:]]
        + kv_blocks,
        out_specs=[
            block,
            pl.BlockSpec((2, rows, 2 * HD), lambda h: (0, 0, h)),
            pl.BlockSpec((2, keys_n - rows, 2 * HD), lambda h: (0, 0, h)),
        ],
        out_shape=[
            jax.ShapeDtypeStruct((rows, width), jnp.bfloat16),
            jax.ShapeDtypeStruct((2, rows, width), jnp.bfloat16),
            jax.ShapeDtypeStruct((2, keys_n - rows, width), jnp.bfloat16),
        ],
        scratch_shapes=[
            pltpu.VMEM((2, rows, keys_n), jnp.float32),
            pltpu.VMEM((2, rows, keys_n), jnp.bfloat16),
            pltpu.VMEM((2, rows, keys_n), jnp.bfloat16),
            pltpu.VMEM((2, rows, TILE), jnp.bfloat16),
        ],
        compiler_params=pltpu.CompilerParams(vmem_limit_bytes=VMEM),
        cost_estimate=pl.CostEstimate(flops=24 * size, bytes_accessed=rows * width * 32, transcendentals=0),
        name="attention_backward",
    )(own, query, d_out, rate, expo, *tables[1:], *kv, *kv)


class Gather:
    def __init__(self):
        self.chips = lax.axis_size("chip")
        side = math.isqrt(self.chips)
        self.first, self.second = (side, side) if side * side == self.chips else (self.chips, 1)
        chip, core = lax.axis_index("chip"), lax.axis_index("core")
        places = []
        for owner in (core, 1 - core):
            for early, late in self.steps():
                one = self.moved(chip, early, late)
                two = self.moved(chip, late, early)
                places.append(jnp.where(owner == 0, one, two) * 2 + owner)
        self.places = jnp.stack(places).astype(jnp.int32)

    def steps(self):
        steps = [(early, 0) for early in range(self.first)]
        steps += [(0, late) for late in range(1, self.second)]
        return steps + [(e, l) for l in range(1, self.second) for e in range(1, self.first)]

    def moved(self, chip, along_first, along_second):
        return chip ^ (along_first * self.second + along_second)

    def hop(self, block, early, late):
        route = []
        for chip in range(self.chips):
            route.append((self.moved(chip, early, late) * 2, chip * 2))
            route.append((self.moved(chip, late, early) * 2 + 1, chip * 2 + 1))
        return lax.ppermute(block, ("chip", "core"), route)

    def stages(self, shards, used):
        swap = lambda block: lax.ppermute(block, "core", [(0, 1), (1, 0)])
        collect = lambda shard: lax.all_gather(shard, ("fz", "fh"), axis=0, tiled=True)
        count = len(shards)
        shards = list(shards)
        blocks = [collect(shard) for shard in shards[:3]]
        kept, traded, last = [[] for _ in shards], [[] for _ in shards], []
        complete, ahead = 0, self.first + self.second - 1
        for turn in range(count + 1):
            onward = kept[turn - 1][1 : self.first] if turn else []
            if turn > 1:
                late, due = kept[turn - 2][ahead if turn == count else 0 :], blocks[turn : turn + 1] if turn > 2 else []
                self.held = yield [kept[which] + traded[which] for which in range(complete)]
                (onward, late, due), last, self.held = lax.optimization_barrier(
                    ((onward, late, due), last, list(self.held))
                )
                if due:
                    blocks[turn] = due[0]
                further = [self.hop(block, 0, step) for step in range(1, self.second) for block in onward]
                kept[turn - 1] = kept[turn - 1] + further
                across = [swap(block) for block in late]
                traded[turn - 2] = traded[turn - 2] + across
                last = further + across
                complete += 1
            self.held = yield [kept[which] + traded[which] for which in range(complete)]
            if turn < count:
                fresh = blocks[turn][:, : used[turn]]
                coming = shards[turn + 3 : turn + 4]
                late = kept[turn - 1][:ahead] if turn == count - 1 else []
                (fresh, onward, coming, late), last, self.held = lax.optimization_barrier(
                    ((fresh, onward, coming, late), last, list(self.held))
                )
                blocks += [collect(shard) for shard in coming]
                early = [self.hop(fresh, step, 0) for step in range(1, self.first)]
                other = [self.hop(fresh, 0, step) for step in range(1, self.second)]
                kept[turn] = [fresh] + early + other
                traded[turn - 1] = traded[turn - 1] + [swap(block) for block in late]
                last = early + other + (traded[turn - 1] if late else [])
                if turn == 1:
                    further = [self.hop(block, 0, step) for step in range(1, self.second) for block in onward]
                    kept[0] = kept[0] + further
                    last = last + further
            else:
                late, last, self.held = lax.optimization_barrier((kept[-1], last, list(self.held)))
                traded[-1] = [swap(block) for block in late]
        yield [own + other for own, other in zip(kept, traded)]


HBM = pl.BlockSpec(memory_space=pltpu.HBM)
SCALARS = pl.BlockSpec(memory_space=pltpu.SMEM)
VMEM_SPEC = pl.BlockSpec(memory_space=pltpu.VMEM)
TALL = 512
HALO = 32
MIB = 1024 * 1024


def dot_tn(a, b):
    return lax.dot_general(a, b, (((0,), (0,)), ((), ())), preferred_element_type=jnp.float32)


def norm_rows(field):
    centred = field - jnp.mean(field, -1, keepdims=True)
    rate = lax.rsqrt(jnp.mean(centred * centred, -1, keepdims=True) + EPSILON)
    return centred * rate, rate


def norm_back(grad, gain, normed, rate):
    scaled = grad * gain
    inner = jnp.mean(scaled * normed, -1, keepdims=True)
    return (scaled - jnp.mean(scaled, -1, keepdims=True) - normed * inner) * rate


def each_rows(rows, step, body):
    for begin in range(0, rows, step):
        body(slice(begin, begin + step))


def shape_of(rows, width, dtype=jnp.bfloat16):
    return jax.ShapeDtypeStruct((rows, width), dtype)


class Weight:
    def __init__(self, places, pieces, begin, width):
        self.places, self.pieces, self.begin, self.width = places, pieces, begin, width
        self.count, self.block = len(pieces), pieces[0].shape[0]
        self.depth = self.count * self.block
        self.bytes = 2 * self.depth * width


class Load:
    def __init__(self, weight, places_ref, pieces, store, sems):
        self.store, self.copies = store, []
        for index, piece in enumerate(pieces):
            row = pl.multiple_of(places_ref[index] * weight.block, weight.block)
            self.copies.append(
                pltpu.make_async_copy(
                    piece.at[:, pl.ds(weight.begin, weight.width)],
                    store.at[pl.ds(row, weight.block), :],
                    sems.at[index],
                )
            )

    def start(self):
        for copy in self.copies:
            copy.start()

    def wait(self):
        for copy in self.copies:
            copy.wait()


class Rows:
    def __init__(self, array, begin, count):
        self.array, self.begin, self.count = array, begin, count


class Factor:
    def __init__(self, ref, rows):
        self.ref, self.at = ref, slice(rows.begin, rows.begin + rows.count)

    def all(self):
        return self.ref[self.at, :]

    def columns(self, at):
        return self.ref[self.at, at]


class Refs:
    pass


def fused(body, name, limit, weights, factors, near, far, outs, far_outs=(), scratch=(), turn=()):
    arrays = []
    for rows in factors.values():
        if not any(rows.array is array for array in arrays):
            arrays.append(rows.array)
    far, far_outs, scratch = dict(far), dict(far_outs), dict(scratch)
    places = [weight.places for weight in list(weights.values())[:1]]
    pieces = [piece for weight in weights.values() for piece in weight.pieces]

    def kernel(*refs):
        refs = list(refs)
        take = lambda count: [refs.pop(0) for _ in range(count)]
        r = Refs()
        places_ref = take(len(places))
        blocks = [take(weight.count) for weight in weights.values()]
        factor_refs, turn_ref = take(len(arrays)), take(len(turn))
        r.turn, r.core = (turn_ref + [None, None])[:2]
        for names in (near, far, outs, far_outs):
            for key, ref in zip(names, take(len(names))):
                setattr(r, key, ref)
        for (key, weight), block in zip(weights.items(), blocks):
            setattr(r, key, Load(weight, places_ref[0], block, *take(2)))
        for key, rows in factors.items():
            (which,) = [i for i, array in enumerate(arrays) if array is rows.array]
            setattr(r, key, Factor(factor_refs[which], rows))
        for key, ref in zip(scratch, take(len(scratch))):
            setattr(r, key, ref)
        body(r)

    total = sum(weight.bytes for weight in weights.values())
    everything = [*near.values(), *far.values(), *outs.values(), *far_outs.values()]
    moved = sum(math.prod(item.shape) * item.dtype.itemsize for item in everything)
    rows = list(near.values())[0].shape[0] if near else 0
    stores = []
    for weight in weights.values():
        stores.append(pltpu.VMEM((weight.depth, weight.width), jnp.bfloat16))
        stores.append(pltpu.SemaphoreType.DMA((weight.count,)))
    made = pl.pallas_call(
        kernel,
        in_specs=[SCALARS] * len(places)
        + [HBM] * len(pieces)
        + [VMEM_SPEC] * len(arrays)
        + [SCALARS] * len(turn)
        + [VMEM_SPEC] * len(near)
        + [HBM] * len(far),
        out_specs=[VMEM_SPEC] * len(outs) + [HBM] * len(far_outs),
        out_shape=[*outs.values(), *far_outs.values()],
        scratch_shapes=stores + list(scratch.values()),
        compiler_params=pltpu.CompilerParams(vmem_limit_bytes=total + limit * MIB),
        cost_estimate=pl.CostEstimate(flops=rows * total, bytes_accessed=moved + total, transcendentals=0),
        name=name,
    )(*places, *pieces, *arrays, *turn, *near.values(), *far.values())
    return made


def wide_step(kind, load, u_ref, down, up, z_ref, outs, then=None):
    z_ref[...] = dot_nt(u_ref[...], down.all()).astype(jnp.bfloat16)
    load.wait()
    if then:
        then()
    width = load.store.shape[1]
    out_width = width // 2 if kind == "glu" else width
    for begin in range(0, out_width, TALL):
        at = slice(begin, begin + TALL)
        parts = [slice(base + begin, base + begin + TALL) for base in range(0, width, out_width)]
        result = [
            dot_nn(u_ref[...], load.store[:, part]) + dot_nn(z_ref[...], up.columns(part)) for part in parts
        ]
        if kind == "silu":
            gate = jax.nn.sigmoid(result[0])
            active = result[0] * gate
            outs[0][:, at] = active.astype(jnp.bfloat16)
            outs[1][:, at] = (gate + active * (1.0 - gate)).astype(jnp.bfloat16)
        elif kind == "glu":
            gate = jax.nn.sigmoid(result[1])
            gated = result[0] * gate
            outs[0][:, at] = gated.astype(jnp.bfloat16)
            outs[1][:, at] = gate.astype(jnp.bfloat16)
            outs[2][:, at] = (gated * (1.0 - gate)).astype(jnp.bfloat16)
        else:
            which = min(begin // outs[0].shape[1], 1)
            first = which * outs[0].shape[1]
            outs[which][:, begin - first : begin - first + TALL] = result[0].astype(jnp.bfloat16)


def narrow_step(factor, load, u_ref, down, up, z_ref, field_ref, field_out, then=None):
    z_ref[...] = dot_nt(u_ref[...], down.all()).astype(jnp.bfloat16)
    load.wait()
    if then:
        then()
    for begin in range(0, load.store.shape[1], TALL):
        at = slice(begin, begin + TALL)
        result = dot_nn(u_ref[...], load.store[:, at]) + dot_nn(z_ref[...], up.columns(at))
        field_out[:, at] = field_ref[:, at].astype(jnp.float32) + factor * result


def norm_step(field_ref, gain_ref, bias_ref, out_ref):
    def finish(at):
        normed = norm_rows(field_ref[at, :])[0] * gain_ref[...] + bias_ref[...]
        out_ref[at, :] = normed.astype(jnp.bfloat16)

    each_rows(field_ref.shape[0], 128, finish)


def grads_step(grad, up, z_ref, u_ref, dz, da_ref, db_ref):
    dz[...] = dot_nt(grad[...], up.all()).astype(jnp.bfloat16)
    db_ref[...] = dot_tn(z_ref[...], grad[...]).astype(jnp.bfloat16)
    da_ref[...] = dot_tn(dz[...], u_ref[...]).astype(jnp.bfloat16)


def inputs_step(load, grad, dz, down, out_ref, then=None):
    load.wait()
    if then:
        then()
    for begin in range(0, load.store.shape[0], TALL):
        at = slice(begin, begin + TALL)
        result = dot_nt(grad[...], load.store[at, :]) + dot_nn(dz[...], down.columns(at))
        out_ref[:, at] = result.astype(out_ref.dtype)


def norm_back_step(d_inputs, field_ref, gain_ref, prior_ref, out_ref):
    def finish(at):
        normed, rate = norm_rows(field_ref[at, :].astype(jnp.float32))
        out_ref[at, :] = prior_ref[at, :] + norm_back(d_inputs[at, :], gain_ref[...], normed, rate)

    each_rows(field_ref.shape[0], 128, finish)


def halves_step(turn_ref, first_out, second_out, rows_of):
    half = first_out.shape[0]
    step = half // 2
    for begin in range(0, 2 * half, step):
        made = rows_of(slice(begin, begin + step)).astype(first_out.dtype)
        at = slice(begin % half, begin % half + step)
        for out, turn in ((first_out, begin // half), (second_out, 1 - begin // half)):

            @pl.when(turn_ref[0] == turn)
            def _(out=out):
                out[at, :] = made


def project_wide(kind, inputs, weight, a, b):
    rows, width = inputs.shape[0], weight.width
    sizes = dict(silu=[width] * 2, glu=[width // 2] * 3, plain=[width // 3, width - width // 3])[kind]
    names = ["out%d" % index for index in range(len(sizes))]

    def body(r):
        r.weight.start()
        wide_step(kind, r.weight, r.u, r.a, r.b, r.z, [getattr(r, key) for key in names])

    outs = dict(z=shape_of(rows, a.count), **{key: shape_of(rows, size) for key, size in zip(names, sizes)})
    return fused(body, "project_" + kind, 14, dict(weight=weight), dict(a=a, b=b), dict(u=inputs), {}, outs)


def project_narrow(inputs, weight, a, b, field, gain, bias, factor):
    rows, width = inputs.shape[0], weight.width

    def body(r):
        r.weight.start()
        narrow_step(factor, r.weight, r.u, r.a, r.b, r.z, r.field, r.made)
        norm_step(r.made, r.gain, r.bias, r.normed)

    outs = dict(
        z=shape_of(rows, a.count), made=shape_of(rows, width, jnp.float32),
        normed=shape_of(rows, width),
    )
    near = dict(u=inputs, field=field, gain=gain, bias=bias)
    return fused(body, "project_next", 14, dict(weight=weight), dict(a=a, b=b), near, {}, outs)


def feed_forward_last(inputs, up, down, factors, field, gain, bias, cotangent, turn):
    rows, width = inputs.shape
    rank, hidden = factors["a_up"].count, up.width

    def body(r):
        r.up.start()
        wide_step("silu", r.up, r.u, r.a_up, r.b_up, r.z_up, (r.held_act, r.held_slope), r.down.start)
        leaving = [
            pltpu.make_async_copy(r.held_act, r.act, r.sems.at[0]),
            pltpu.make_async_copy(r.held_slope, r.slope, r.sems.at[1]),
        ]
        for copy in leaving:
            copy.start()
        narrow_step(0.5, r.down, r.held_act, r.a_down, r.b_down, r.z_down, r.field, r.d_out)
        gain, bias = r.gain[...], r.bias[...]

        def finish(at):
            normed, rate = norm_rows(r.d_out[at, :])
            r.d_out[at, :] = norm_back(r.cot[at, :].astype(jnp.float32), gain, normed, rate)
            return normed * gain + bias

        halves_step(r.turn, r.first, r.second, finish)
        for copy in leaving:
            copy.wait()

    outs = dict(
        z_up=shape_of(rows, rank), z_down=shape_of(rows, rank),
        d_out=shape_of(rows, width, jnp.float32), first=shape_of(rows // 2, width),
        second=shape_of(rows // 2, width),
    )
    near = dict(u=inputs, field=field, gain=gain, bias=bias, cot=cotangent)
    return fused(
        body, "feed_forward_last", 30, dict(up=up, down=down), factors, near, {}, outs,
        dict(act=shape_of(rows, hidden), slope=shape_of(rows, hidden)),
        dict(
            held_act=pltpu.VMEM((rows, hidden), jnp.bfloat16),
            held_slope=pltpu.VMEM((rows, hidden), jnp.bfloat16),
            sems=pltpu.SemaphoreType.DMA((2,)),
        ),
        turn,
    )


def ffn_back_steps(r, d_ref, u_ref):
    r.half[...] = (0.5 * d_ref[...]).astype(jnp.bfloat16)
    r.dz_down[...] = dot_nt(r.half[...], r.b_down.all()).astype(jnp.bfloat16)
    r.db_down[...] = dot_tn(r.z_down[...], r.half[...]).astype(jnp.bfloat16)
    r.down.wait()
    pltpu.make_async_copy(r.slope, r.held_slope, r.sems.at[0]).wait()
    act_copy = pltpu.make_async_copy(r.act, r.held_act, r.sems.at[1])
    act_copy.start()
    r.up.start()
    for begin in range(0, r.down.store.shape[0], TALL):
        at = slice(begin, begin + TALL)
        result = dot_nt(r.half[...], r.down.store[at, :]) + dot_nn(r.dz_down[...], r.a_down.columns(at))
        r.d_hidden[:, at] = (result * r.held_slope[:, at].astype(jnp.float32)).astype(jnp.bfloat16)
    r.dz_up[...] = dot_nt(r.d_hidden[...], r.b_up.all()).astype(jnp.bfloat16)
    act_copy.wait()
    r.da_down[...] = dot_tn(r.dz_down[...], r.held_act[...]).astype(jnp.bfloat16)
    inputs_step(r.up, r.d_hidden, r.dz_up, r.a_up, r.d_inputs)
    r.db_up[...] = dot_tn(r.z_up[...], r.d_hidden[...]).astype(jnp.bfloat16)
    r.da_up[...] = dot_tn(r.dz_up[...], u_ref[...]).astype(jnp.bfloat16)


def ffn_back_parts(rows, width, hidden, rank):
    outs = dict(
        da_up=shape_of(rank, width), db_up=shape_of(rank, hidden),
        da_down=shape_of(rank, hidden), db_down=shape_of(rank, width),
    )
    scratch = dict(
        half=pltpu.VMEM((rows, width), jnp.bfloat16),
        dz_down=pltpu.VMEM((rows, rank), jnp.bfloat16),
        dz_up=pltpu.VMEM((rows, rank), jnp.bfloat16),
        d_hidden=pltpu.VMEM((rows, hidden), jnp.bfloat16),
        d_inputs=pltpu.VMEM((rows, width), jnp.float32),
        held_act=pltpu.VMEM((rows, hidden), jnp.bfloat16),
        held_slope=pltpu.VMEM((rows, hidden), jnp.bfloat16),
        sems=pltpu.SemaphoreType.DMA((2,)),
    )
    return outs, scratch


def feed_forward_back(d_field, up, down, factors, kept, field, gain):
    rows, width = d_field.shape
    inputs, act, slope, z_up, z_down = kept

    def body(r):
        r.down.start()
        pltpu.make_async_copy(r.slope, r.held_slope, r.sems.at[0]).start()
        ffn_back_steps(r, r.d_field, r.u)
        norm_back_step(r.d_inputs, r.field, r.gain, r.d_field, r.made)

    outs, scratch = ffn_back_parts(rows, width, up.width, factors["a_up"].count)
    outs = dict(made=shape_of(rows, width, jnp.float32), **outs)
    near = dict(d_field=d_field, u=inputs, z_up=z_up, z_down=z_down, field=field, gain=gain)
    return fused(
        body, "feed_forward_back", 36, dict(down=down, up=up), factors, near,
        dict(act=act, slope=slope), outs, {}, scratch,
    )


def field_back(kind, grad, weight, a, b, inputs, slot_acts, extras=()):
    rows, depth, rank = grad.shape[0], weight.depth, a.count
    low = grad.dtype == jnp.bfloat16
    names = dict(norm=("prior", "field", "gain"), conv=("field", "gain", "bias"), plain=())[kind]

    def body(r):
        r.weight.start()
        grad_ref = r.grad
        if not low:
            grad_ref = r.low
            r.low[...] = r.grad[...].astype(jnp.bfloat16)
        grads_step(grad_ref, r.b, r.z, r.u, r.dz, r.da, r.db)
        if kind == "plain":
            inputs_step(r.weight, grad_ref, r.dz, r.a, r.made)
            return
        inputs_step(r.weight, grad_ref, r.dz, r.a, r.d_inputs)
        if kind == "norm":
            norm_back_step(r.d_inputs, r.field, r.gain, r.prior, r.made)
            return
        gain = r.gain[...]

        def finish(at):
            normed, rate = norm_rows(r.field[at, :])
            shifted = normed * gain + r.bias[...]
            gate = jax.nn.sigmoid(shifted)
            into = gate + shifted * gate * (1.0 - gate)
            r.made[at, :] = norm_back(r.d_inputs[at, :] * into, gain, normed, rate)

        each_rows(rows, 128, finish)

    made = shape_of(rows, depth, jnp.bfloat16 if kind == "plain" else jnp.float32)
    outs = dict(made=made, da=shape_of(rank, depth), db=shape_of(rank, weight.width))
    scratch = dict(dz=pltpu.VMEM((rows, rank), jnp.bfloat16))
    if not low:
        scratch["low"] = pltpu.VMEM((rows, weight.width), jnp.bfloat16)
    if kind != "plain":
        scratch["d_inputs"] = pltpu.VMEM((rows, depth), jnp.float32)
    near = dict(grad=grad, u=inputs, z=slot_acts, **dict(zip(names, extras)))
    return fused(
        body, "field_back_" + kind, 14, dict(weight=weight), dict(a=a, b=b), near, {}, outs, {}, scratch
    )


def first_half_back(d_query, shares, qkv_w, a_qkv, b_qkv, attn_in, z_qkv, prior, field, gain,
                    up, down, factors, kept, layer_in, layer_gain, turn):
    rows, width = d_query.shape
    inputs, act, slope, z_up, z_down = kept
    names = ["share%d" % index for index in range(len(shares))]

    def body(r):
        r.qkv_w.start()
        r.joined[:, :width] = r.d_query[...]
        for which in range(2):
            total = sum(getattr(r, key)[which].astype(jnp.float32) for key in names)
            r.joined[:, (1 + which) * width : (2 + which) * width] = total.astype(jnp.bfloat16)
        grads_step(r.joined, r.b_qkv, r.z_qkv, r.attn_in, r.dz, r.da_qkv, r.db_qkv)

        def then():
            r.down.start()
            pltpu.make_async_copy(r.slope, r.held_slope, r.sems.at[0]).start()

        inputs_step(r.qkv_w, r.joined, r.dz, r.a_qkv, r.d_inputs, then)
        norm_back_step(r.d_inputs, r.field, r.gain, r.prior, r.d_first)
        ffn_back_steps(r, r.d_first, r.u)

        def finish(at):
            normed, rate = norm_rows(r.layer_in[at, :].astype(jnp.float32))
            return r.d_first[at, :] + norm_back(r.d_inputs[at, :], r.layer_gain[...], normed, rate)

        halves_step(r.turn, r.first, r.second, finish)
        if packed:
            three = [
                r.db_qkv[which * rank : (which + 1) * rank, which * width : (which + 1) * width]
                for which in range(3)
            ]
            model = [r.da_up[...], r.da_qkv[...], r.db_down[...], *three]
            pack_step((r.ours, r.theirs), r.core, fsdp, model, [r.da_down[...], r.db_up[...]])

    rank = factors["a_up"].count
    outs, scratch = ffn_back_parts(rows, width, up.width, rank)
    grads = dict(**outs, da_qkv=shape_of(a_qkv.count, width), db_qkv=shape_of(a_qkv.count, 3 * width))
    outs = dict(first=shape_of(rows // 2, width), second=shape_of(rows // 2, width))
    devices, fsdp = lax.axis_size(EVERYWHERE), lax.axis_size("fz") * lax.axis_size("fh")
    packed = packs_whole(devices, width, up.width)
    if packed:
        scratch.update({key: pltpu.VMEM(item.shape, item.dtype) for key, item in grads.items()})
        count = -(-8 * rank // TILE) * (width // devices) + 2 * rank
        outs["ours"] = outs["theirs"] = jax.ShapeDtypeStruct((devices // 2, count, TILE), jnp.bfloat16)
    else:
        outs.update(grads)
    scratch["joined"] = pltpu.VMEM((rows, 3 * width), jnp.bfloat16)
    scratch["dz"] = pltpu.VMEM((rows, a_qkv.count), jnp.bfloat16)
    scratch["d_first"] = pltpu.VMEM((rows, width), jnp.float32)
    near = dict(
        d_query=d_query, **dict(zip(names, shares)), attn_in=attn_in, z_qkv=z_qkv, prior=prior,
        field=field, gain=gain, u=inputs, z_up=z_up, z_down=z_down, layer_in=layer_in,
        layer_gain=layer_gain,
    )
    return fused(
        body, "first_half_back", 38, dict(qkv_w=qkv_w, down=down, up=up),
        dict(a_qkv=a_qkv, b_qkv=b_qkv, **factors), near, dict(act=act, slope=slope), outs, {}, scratch,
        turn,
    )


def slide(lanes, parts, shifted, taps_ref, shifts, rows, store):
    begin = 0
    for part in parts:
        shifted[0, begin : begin + part.shape[0], :] = part
        begin += part.shape[0]
    length = begin - 8
    for turn in range(1, 8):
        shifted[turn, 0:length, :] = shifted[0, turn : turn + length, :]
    step = 64
    for at in range(0, rows, step):
        total = None
        for tap, shift in enumerate(shifts):
            base = shift - shift % 8 + at
            term = shifted[shift % 8, base : base + step, :] * taps_ref[tap : tap + 1, lanes]
            total = term if total is None else total + term
        store(slice(at, at + step), total)


def each_tile(width, body):
    def one(index, carry):
        body(pl.ds(pl.multiple_of(index * TILE, TILE), TILE))
        return carry

    lax.fori_loop(0, width // TILE, one, 0)


def conv_body(r):
    val_ref, earlier_ref, conv_ref, act_ref = r.value, r.earlier, r.conv, r.act
    taps_ref, gain_ref, bias_ref, shifted = r.taps, r.gain, r.bias, r.shifted
    rows, width = val_ref.shape

    def one(lanes):
        parts = [earlier_ref[:, lanes].astype(jnp.float32), val_ref[:, lanes].astype(jnp.float32)]

        def store(at, total):
            conv_ref[at, lanes] = total

        shifts = [HALO - KERNEL + 1 + tap for tap in range(KERNEL)]
        slide(lanes, parts, shifted, taps_ref, shifts, rows, store)

    each_tile(width, one)

    def finish(at):
        shifted_field = norm_rows(conv_ref[at, :])[0] * gain_ref[...] + bias_ref[...]
        act_ref[at, :] = (shifted_field * jax.nn.sigmoid(shifted_field)).astype(jnp.bfloat16)

    each_rows(rows, 128, finish)


def conv_back_body(r):
    d_ref, later_ref, out_ref = r.d_conv, r.later, r.made
    taps_ref, gate_ref, slope_ref, shifted = r.taps, r.gate, r.slope, r.shifted
    rows, width = d_ref.shape

    def one(lanes):
        parts = [d_ref[:, lanes], later_ref[:, lanes].astype(jnp.float32)]
        high = pl.ds(pl.multiple_of(lanes.start + width, TILE), TILE)

        def store(at, total):
            out_ref[at, lanes] = (total * gate_ref[at, lanes].astype(jnp.float32)).astype(jnp.bfloat16)
            out_ref[at, high] = (total * slope_ref[at, lanes].astype(jnp.float32)).astype(jnp.bfloat16)

        slide(lanes, parts, shifted, taps_ref, [KERNEL - 1 - tap for tap in range(KERNEL)], rows, store)

    each_tile(width, one)


def conv_forward(value, earlier, taps, gain, bias):
    rows, width = value.shape
    near = dict(value=value, earlier=earlier, taps=taps, gain=gain, bias=bias)
    outs = dict(conv=shape_of(rows, width, jnp.float32), act=shape_of(rows, width))
    scratch = dict(shifted=pltpu.VMEM((8, rows + HALO, TILE), jnp.float32))
    return fused(conv_body, "conv_forward", 16, {}, {}, near, {}, outs, {}, scratch)


def conv_backward(d_conv, later, taps, gate, slope):
    rows, width = d_conv.shape
    near = dict(d_conv=d_conv, later=later, taps=taps, gate=gate, slope=slope)
    scratch = dict(shifted=pltpu.VMEM((8, rows + HALO, TILE), jnp.float32))
    outs = dict(made=shape_of(rows, 2 * width))
    return fused(conv_back_body, "conv_backward", 16, {}, {}, near, {}, outs, {}, scratch)[0]


def gather_taps(weight):
    def body(r):
        r.weight.start()
        r.weight.wait()
        r.taps[...] = jnp.transpose(r.weight.store[...].astype(jnp.float32))[:HALO, :]

    outs = dict(taps=shape_of(HALO, weight.depth, jnp.float32))
    return fused(body, "gather_taps", 8, dict(weight=weight), {}, {}, {}, outs)[0]


class Layout:
    def __init__(self, together, fsdp):
        self.fsdp = fsdp
        self.inner = fsdp // together
        self.group = 2 * self.inner

    def place(self, core, f):
        return core * self.fsdp + f

    def round_route(self, turn):
        route = []
        for core in range(2):
            for f in range(self.fsdp):
                clip = (f % 2 + turn) % 2
                spot = f // 2
                target = self.place(spot % 2, (2 * core + clip) * self.inner + spot // 2)
                route.append((self.place(core, f), target))
        return route

    def gather_rows(self, blocks):
        parity = (lax.axis_index("fz") * self.inner + lax.axis_index("fh")) % 2
        clip = lax.axis_index("fz") % 2
        got = []
        for turn in range(2):
            sent = lax.dynamic_index_in_dim(blocks, (parity + turn) % 2, 0, keepdims=False)
            got.append(lax.ppermute(sent, ("core", "fz", "fh"), self.round_route(turn)))
        swap = clip == 1
        return jnp.concatenate(
            [jnp.where(swap, got[1], got[0]), jnp.where(swap, got[0], got[1])], axis=0
        )

    def scatter_rows(self, sent):
        parity = (lax.axis_index("fz") * self.inner + lax.axis_index("fh")) % 2
        got = []
        for turn in range(2):
            route = [(target, source) for source, target in self.round_route(turn)]
            got.append(lax.ppermute(sent[turn], ("core", "fz", "fh"), route))
        swap = parity == 1
        return jnp.stack([jnp.where(swap, got[1], got[0]), jnp.where(swap, got[0], got[1])])

    def spot_index(self, spot):
        return (spot % 2) * self.inner + spot // 2

    def from_spot(self, block, distance, cyclic):
        route = []
        for spot in range(self.group):
            source = spot + distance
            if cyclic:
                source %= self.group
            if 0 <= source < self.group:
                route.append((self.spot_index(source), self.spot_index(spot)))
        return lax.ppermute(block, ("core", "fh"), route)


def pack_adapters(ids, a_model, a_hidden, b_model, b_hidden):
    slots = a_model.shape[2]
    half = RANK // 2
    core = lax.axis_index("core")
    ranks = core * half + jnp.arange(half, dtype=jnp.int32)
    wanted = ids[:, None] * RANK + ranks[None, :]
    picker = (wanted[:, :, None] == jnp.arange(slots, dtype=jnp.int32)).astype(jnp.bfloat16)
    down = lambda a: jnp.einsum("jrs,pks->jprk", picker, a, preferred_element_type=jnp.float32)
    up = lambda b: jnp.einsum("jrs,psn->jprn", picker, b, preferred_element_type=jnp.float32)
    cut = a_hidden.shape[1] // a_model.shape[1]
    span = a_model.shape[1]

    def short(pack):
        rows = pack.reshape(pack.shape[0], pack.shape[1], half, cut, span)
        return jnp.swapaxes(rows, 2, 3).reshape(pack.shape[0], pack.shape[1] * cut, half, span)

    return jnp.concatenate(
        [down(a_model), up(b_model), short(down(a_hidden)), short(up(b_hidden))], axis=1
    ).astype(jnp.bfloat16)


def join_adapters_kernel(models, cut, plan, spots_ref, mine_ref, theirs_ref, *rest):
    wanted = len(plan)
    outs, full, held, sems = rest[:wanted], rest[wanted], rest[wanted + 1 : -1], rest[-1]
    count, groups, half, span = mine_ref.shape
    for step in range(count):
        at = pl.ds(pl.multiple_of(spots_ref[step] * span, span), span)
        for ref, core in ((mine_ref, spots_ref[count]), (theirs_ref, 1 - spots_ref[count])):
            rows = pl.ds(pl.multiple_of(core * half, half), half)
            full[:, rows, at] = ref[step].astype(jnp.float32)
    copies = []
    for which, (out, kept, parts) in enumerate(zip(outs, held, plan)):
        kept[...] = jnp.zeros_like(kept)
        for group, row, column in parts:
            if group < models:
                kept[row : row + RANK, column : column + count * span] = full[group].astype(kept.dtype)
                continue
            for f in range(count):
                begin = column + f * cut * span
                kept[row : row + RANK, begin : begin + span] = full[
                    group, :, f * span : (f + 1) * span
                ].astype(kept.dtype)
        copies.append(pltpu.make_async_copy(kept, out, sems.at[which]))
        copies[-1].start()
    for copy in copies:
        copy.wait()


def move_adapters(layout, pack, cut, shapes, plan, models):
    core = lax.axis_index("core")
    count = layout.fsdp
    here = lax.axis_index("fz") * layout.inner + lax.axis_index("fh")
    pieces = []
    for step in range(count):
        target = (here + step) % count
        piece = lax.dynamic_index_in_dim(pack, target // layout.inner, 0, keepdims=False)
        if step:
            route = [(f, (f + step) % count) for f in range(count)]
            piece = lax.ppermute(piece, ("fz", "fh"), route)
        pieces.append(piece)
    mine = jnp.stack(pieces)
    theirs = lax.ppermute(mine, "core", [(0, 1), (1, 0)])
    spots = jnp.stack([(here - step) % count for step in range(count)] + [core]).astype(jnp.int32)
    _, groups, half, span = mine.shape
    return pl.pallas_call(
        functools.partial(join_adapters_kernel, models, cut, plan),
        in_specs=[SCALARS, VMEM_SPEC, VMEM_SPEC],
        out_specs=[HBM] * len(shapes),
        out_shape=[shape_of(*shape) for shape in shapes],
        scratch_shapes=[pltpu.VMEM((groups, 2 * half, count * span), jnp.float32)]
        + [pltpu.VMEM(shape, jnp.bfloat16) for shape in shapes]
        + [pltpu.SemaphoreType.DMA((len(shapes),))],
        compiler_params=pltpu.CompilerParams(vmem_limit_bytes=16 * 1024 * 1024),
        name="join_adapters",
    )(spots, mine, theirs)


def factor_plan(models, hiddens, cut, span):
    hidden = [(models + which * cut + q, which * RANK, q * span) for which in range(hiddens) for q in range(cut)]
    return [[(group, group * RANK, 0) for group in range(models)], hidden]


def first_adapters(layout, pack, cut, width, hidden):
    shapes = [(2 * RANK, width), (2 * RANK, hidden)]
    model, inner = move_adapters(layout, pack, cut, shapes, factor_plan(2, 2, cut, pack.shape[3]), 2)
    return model, inner


def other_adapters(layout, pack, cut, width, hidden):
    shapes = [(15 * RANK, width), (2 * RANK, hidden), (3 * RANK, 3 * width), (RANK, 2 * width)]
    plan = factor_plan(15, 2, cut, pack.shape[3]) + [
        [(7 + which, which * RANK, which * width) for which in range(3)],
        [(13, 0, 0), (14, 0, width)],
    ]
    return move_adapters(layout, pack, cut, shapes, plan, 15)


def pack_step(outs, core_ref, fsdp, model, hidden):
    places, _, lanes = outs[0].shape
    model = jnp.concatenate([part.astype(jnp.float32) for part in model], axis=0)
    tiles = -(-model.shape[0] // TILE)
    if model.shape[0] % TILE:
        rest = jnp.zeros((tiles * TILE - model.shape[0], model.shape[1]), jnp.float32)
        model = jnp.concatenate([model, rest], axis=0)
    turned = [jnp.transpose(model[k * TILE : (k + 1) * TILE]).astype(jnp.bfloat16) for k in range(tiles)]
    share = model.shape[1] // (2 * places)

    def write(here):
        for device in range(2 * places):
            chip, other = divmod(device, 2 * fsdp)
            core, f = divmod(other, fsdp)
            out, place, row = outs[0 if core == here else 1], chip * fsdp + f, 0
            for part in turned:
                out[place, row : row + share, :] = part[device * share : (device + 1) * share]
                row += share
            for part in hidden:
                out[place, row : row + RANK, :] = part[:, device * lanes : (device + 1) * lanes]
                row += RANK

    for here in range(2):
        pl.when(core_ref[0] == here)(functools.partial(write, here))


def packs_whole(devices, width, hidden):
    return hidden // devices == TILE and width // devices % RANK == 0


def pack_grads_kernel(models, count, fsdp, *refs):
    core_ref, refs = refs[0], refs[1:]
    outs, sems, held = refs[count : count + 2], refs[count + 2], refs[count + 3 :]
    copies = [pltpu.make_async_copy(refs[i], held[i], sems.at[i]) for i in range(count)]
    for copy in copies:
        copy.start()
    for copy in copies:
        copy.wait()
    pack_step(outs, core_ref, fsdp, [ref[...] for ref in held[:models]], [ref[...] for ref in held[models:]])


def pack_grads(model, hidden):
    core = lax.axis_index("core").astype(jnp.int32).reshape(1)
    devices, fsdp = lax.axis_size(EVERYWHERE), lax.axis_size("fz") * lax.axis_size("fh")
    width = model[0].shape[1]
    share, hidden_share = width // devices, hidden[0].shape[1] // devices
    groups = sum(part.shape[0] for part in model)
    tiles = -(-groups // TILE)
    if packs_whole(devices, width, hidden[0].shape[1]):
        rows = tiles * share + RANK * len(hidden)
        return pl.pallas_call(
            functools.partial(pack_grads_kernel, len(model), len(model) + len(hidden), fsdp),
            in_specs=[SCALARS] + [HBM] * (len(model) + len(hidden)),
            out_specs=[VMEM_SPEC] * 2,
            out_shape=[jax.ShapeDtypeStruct((devices // 2, rows, TILE), jnp.bfloat16)] * 2,
            scratch_shapes=[pltpu.SemaphoreType.DMA((len(model) + len(hidden),))]
            + [pltpu.VMEM(item.shape, item.dtype) for item in (*model, *hidden)],
            compiler_params=pltpu.CompilerParams(vmem_limit_bytes=PACK_ROOM),
            name="pack_grads",
        )(core, *model, *hidden)
    rest = jnp.zeros((tiles * TILE - groups, width), jnp.bfloat16)
    turned = jnp.concatenate([*model, rest]).T
    split = jnp.concatenate(hidden).reshape(-1, devices, hidden_share)
    parts = [turned[:, k * TILE : (k + 1) * TILE].reshape(devices, share, TILE) for k in range(tiles)]
    parts.append(jnp.transpose(split, (1, 0, 2)).reshape(devices, -1, TILE))
    part = jnp.concatenate(parts, axis=1).reshape(devices // (2 * fsdp), 2, fsdp, -1, TILE)
    part = jnp.swapaxes(part, 0, 1).reshape(2, devices // 2, -1, TILE)
    return tuple(jnp.where(core[0] == 0, part, part[::-1]))


def send_grads(model, hidden):
    groups = sum(item.shape[0] for item in model)
    return send_packed(pack_grads(model, hidden), groups, len(hidden), model[0].shape[1], hidden[0].shape[1])


def send_packed(part, groups, hiddens, width, features):
    ours, theirs = part
    came = lax.ppermute(theirs, "core", [(0, 1), (1, 0)])
    both = (ours.astype(jnp.float32) + came.astype(jnp.float32)).astype(jnp.bfloat16)
    got = lax.all_to_all(both, ("chip", "fz", "fh"), 0, 0, tiled=True)
    devices = lax.axis_size(EVERYWHERE)
    share, hidden_share = width // devices, features // devices
    begin = -(-groups // TILE) * share
    if hidden_share == TILE:
        return got, got, begin
    return got, got[:, begin:].reshape(-1, RANK * hiddens, hidden_share), 0


def place_grads_kernel(batches, ids_ref, *refs):
    sent, outs = refs[: 2 * len(batches)], refs[2 * len(batches) :]
    for out in outs:
        out[...] = jnp.zeros_like(out)
    share = outs[0].shape[1]
    slot = lax.broadcasted_iota(jnp.int32, (share, TILE), 1) // RANK
    in_tile = TILE // RANK

    def one(sender, carry):
        owner = ids_ref[sender]
        at = pl.ds(pl.multiple_of(owner * RANK, RANK), RANK)
        for which, (model_plan, hidden_plan, begin) in enumerate(batches):
            model_ref, hidden_ref = sent[2 * which : 2 * which + 2]
            for group, (out, index) in enumerate(model_plan):
                tile, local_group = divmod(group, in_tile)
                block = model_ref[sender, tile * share : (tile + 1) * share, :].astype(jnp.float32)
                turn = lax.rem(owner - local_group + in_tile, in_tile) * RANK
                outs[out][index] += jnp.where(slot == owner, pltpu.roll(block, turn, 1), 0.0)
            for group, (out, index) in enumerate(hidden_plan):
                rows = slice(begin + group * RANK, begin + (group + 1) * RANK)
                outs[out][index, at, :] += hidden_ref[sender, rows, :].astype(jnp.float32)
        return carry

    lax.fori_loop(0, sent[0].shape[0], one, 0)


def place_grads(ids, batches, shapes):
    arrays, plans = [], []
    for (model, hidden, begin), model_plan, hidden_plan in batches:
        arrays += [model, hidden]
        plans.append((model_plan, hidden_plan, begin))
    return pl.pallas_call(
        functools.partial(place_grads_kernel, plans),
        in_specs=[SCALARS] + [VMEM_SPEC] * len(arrays),
        out_specs=[VMEM_SPEC] * len(shapes),
        out_shape=[jax.ShapeDtypeStruct(shape, jnp.float32) for shape in shapes],
        compiler_params=pltpu.CompilerParams(vmem_limit_bytes=16 * 1024 * 1024),
        name="place_grads",
    )(ids, *arrays)


def local(
    frames,
    cotangent,
    adapter_ids,
    norm_gains,
    norm_biases,
    rel_table,
    w_up,
    w_down,
    w_qkv,
    w_out,
    w_pw1,
    w_depth,
    w_pw2,
    ad_a_model,
    ad_a_hidden,
    ad_b_model,
    ad_b_hidden,
):
    group_clips, frame_span, width = frames.shape
    together = 2 * group_clips
    layout = Layout(together, lax.axis_size("fz") * lax.axis_size("fh"))
    rows = 2 * frame_span
    slots = ad_a_model.shape[2]
    spot = lax.axis_index("fh") * 2 + lax.axis_index("core")
    own = (spot * (rows // TILE)).astype(jnp.int32).reshape(1)
    other_ids = lax.ppermute(adapter_ids, "core", [(0, 1), (1, 0)])
    at_zero = lax.axis_index("core") == 0
    near_ids = jnp.concatenate(
        [jnp.where(at_zero, adapter_ids, other_ids), jnp.where(at_zero, other_ids, adapter_ids)]
    )
    factors = (ad_a_model, ad_a_hidden, ad_b_model, ad_b_hidden)
    cut = ad_a_hidden.shape[1] // ad_a_model.shape[1]
    first_pack = pack_adapters(near_ids, *[factor[:1] for factor in factors])
    other_pack = pack_adapters(near_ids, *[factor[1:] for factor in factors])
    gather = Gather()
    taps = jnp.pad(w_depth.T, ((0, 0), (0, width - KERNEL)))
    shards = [
        w_up[0],
        w_down[0],
        jnp.concatenate([w_qkv, w_out], axis=1),
        jnp.concatenate([w_pw1, w_pw2, taps], axis=1),
        w_up[1],
        w_down[1],
    ]
    used = [shard.shape[1] for shard in shards]
    used[3] = 3 * width + TILE
    turns = gather.stages(shards, used)
    next(turns)

    def weight_of(units, which, begin=0, columns=None):
        return Weight(gather.places, units[which], begin, columns or used[which])

    gains = [norm_gains[index : index + 1] for index in range(6)]
    biases = [norm_biases[index : index + 1] for index in range(6)]

    turns.send([first_pack, other_pack])
    first_pack, other_pack = gather.held
    turns.send([frames, first_pack, other_pack, *rel_tables(rel_table, rows * layout.group)])
    frames, first_pack, other_pack, *tables = gather.held
    layer_in = layout.gather_rows(frames)
    turns.send([])
    hidden_width = w_up.shape[2]
    first_four = first_adapters(layout, first_pack, cut, width, hidden_width)
    units = turns.send([layer_in, *first_four])
    layer_in, *first_four = gather.held
    field = layer_in.astype(jnp.float32)
    first_in = (norm_rows(field)[0] * gains[0] + biases[0]).astype(jnp.bfloat16)
    a_up0, b_down0 = [Rows(first_four[0], row * RANK, RANK) for row in range(2)]
    a_down0, b_up0 = [Rows(first_four[1], row * RANK, RANK) for row in range(2)]
    up0_w = weight_of(units, 0)
    z_up0, act_one, slope_one = project_wide("silu", first_in, up0_w, a_up0, b_up0)
    units = turns.send([act_one, slope_one, other_pack])
    act_one, slope_one, other_pack = gather.held
    others = other_adapters(layout, other_pack, cut, width, hidden_width)
    units = turns.send([])
    down0_w = weight_of(units, 1)
    z_down0, after_ffn, attn_in = project_narrow(
        act_one, down0_w, a_down0, b_down0, layer_in, gains[1], biases[1], 0.5
    )
    units = turns.send([after_ffn, attn_in, *others])
    after_ffn, attn_in, *others = gather.held
    model, inner, qkv_up, glu_up = others
    qkv_down = Rows(model, 0, 3 * RANK)
    qkv_up, glu_up = Rows(qkv_up, 0, 3 * RANK), Rows(glu_up, 0, RANK)
    a_out, a_pw1, a_pw2, a_up1, b_out, b_pw2, b_down1 = [
        Rows(model, row * RANK, RANK) for row in (3, 4, 5, 6, 10, 11, 12)
    ]
    a_down1, b_up1 = [Rows(inner, row * RANK, RANK) for row in range(2)]
    units = turns.send([])
    qkv_w, out_w = weight_of(units, 2, 0, 3 * width), weight_of(units, 2, 3 * width, width)
    z_qkv, query, own_kv = project_wide("plain", attn_in, qkv_w, qkv_down, qkv_up)
    units = turns.send([query, own_kv])
    query, own_kv = gather.held
    units = turns.send([])
    pw1_w, pw2_w = weight_of(units, 3, 0, 2 * width), weight_of(units, 3, 2 * width, width)
    taps = gather_taps(weight_of(units, 3, 3 * width, TILE))
    kv = [own_kv] + [layout.from_spot(own_kv, step, True) for step in range(1, layout.group)]
    mixed, rate, expo = attention_forward(own, query, kv, tables[0])
    turns.send([mixed, rate])
    mixed, rate = gather.held
    units = turns.send([])
    up1_w, down1_w = weight_of(units, 4), weight_of(units, 5)
    mixed, cotangent = lax.optimization_barrier((mixed, cotangent))
    d_out = layout.gather_rows(cotangent)
    z_out, after_attn, conv_in = project_narrow(
        mixed, out_w, a_out, b_out, after_ffn, gains[2], biases[2], 1.0
    )
    z_pw1, gated, gate, gate_slope = project_wide("glu", conv_in, pw1_w, a_pw1, glu_up)
    earlier = layout.from_spot(gated[rows - HALO :], -1, False)
    conv_out, conv_act = conv_forward(gated, earlier, taps, gains[3], biases[3])
    z_pw2, after_conv, second_in = project_narrow(
        conv_act, pw2_w, a_pw2, b_pw2, after_attn, gains[4], biases[4], 1.0
    )
    factors_two = dict(a_up=a_up1, b_up=b_up1, a_down=a_down1, b_down=b_down1)
    turn = [(lax.axis_index("fz") % 2).astype(jnp.int32).reshape(1)]
    z_up1, z_down1, d_fourth, *result, act_two, slope_two = feed_forward_last(
        second_in, up1_w, down1_w, factors_two, after_conv, gains[5], biases[5], d_out, turn
    )
    layer_out = layout.scatter_rows(result)

    d_third, da_up1, db_up1, da_down1, db_down1 = feed_forward_back(
        d_fourth, up1_w, down1_w, factors_two, (second_in, act_two, slope_two, z_up1, z_down1),
        after_conv, gains[4],
    )
    d_conv, da_pw2, db_pw2 = field_back(
        "conv", d_third, pw2_w, a_pw2, b_pw2, conv_act, z_pw2,
        (conv_out, gains[3], biases[3]),
    )
    d_conv, layer_out = lax.optimization_barrier((d_conv, layer_out))
    later = layout.from_spot(d_conv[:HALO].astype(jnp.bfloat16), 1, False)
    d_joined = conv_backward(d_conv, later, taps, gate, gate_slope)
    d_second, da_pw1, db_pw1 = field_back(
        "norm", d_joined, pw1_w, a_pw1, glu_up, conv_in, z_pw1, (d_third, after_attn, gains[2])
    )
    d_mixed, da_out, db_out = field_back(
        "plain", d_second, out_w, a_out, b_out, mixed, z_out, ()
    )
    label = jnp.full((RANK, width), near_ids[lax.axis_index("fz")]).astype(jnp.bfloat16)
    early = send_grads(
        [da_out, da_pw1, da_pw2, da_up1, db_out, db_pw2, db_down1]
        + [db_pw1[:, :width], db_pw1[:, width:], label],
        [da_down1, db_up1],
    )
    d_query, d_own, d_far = attention_backward(own, query, kv, d_mixed, rate, expo, tables)
    shares = [d_own]
    for step in range(1, layout.group):
        shares.append(layout.from_spot(d_far[:, (step - 1) * rows : step * rows], -step, True))
    first_half, second_half_rows, *grads = first_half_back(
        d_query, shares, qkv_w, qkv_down, qkv_up, attn_in, z_qkv, d_second, after_ffn, gains[1],
        up0_w, down0_w, dict(a_up=a_up0, b_up=b_up0, a_down=a_down0, b_down=b_down0),
        (first_in, act_one, slope_one, z_up0, z_down0), layer_in, gains[0],
        [*turn, lax.axis_index("core").astype(jnp.int32).reshape(1)],
    )
    grad_frames = layout.scatter_rows([first_half, second_half_rows])
    if len(grads) == 2:
        late = send_packed(grads, 8 * RANK, 2, width, hidden_width)
    else:
        da_up0, db_up0, da_down0, db_down0, da_qkv, db_qkv = grads
        db_three = [
            db_qkv[index * RANK : (index + 1) * RANK, index * width : (index + 1) * width]
            for index in range(3)
        ]
        late = send_grads([da_up0, da_qkv, db_down0, *db_three], [da_down0, db_up0])
    devices = lax.axis_size(EVERYWHERE)
    share, hidden_share = width // devices, hidden_width // devices
    ids = (early[0][:, share, RANK] * jnp.bfloat16(0.5)).astype(jnp.int32)
    early_plan = [(0, index) for index in range(4, 8)] + [(1, index) for index in range(4, 9)]
    late_plan = [(0, index) for index in range(4)] + [(1, index) for index in range(4)]
    grad_a_model, grad_b_model, grad_a_hidden, grad_b_hidden = place_grads(
        ids,
        [(early, early_plan, [(2, 1), (3, 1)]), (late, late_plan, [(2, 0), (3, 0)])],
        [(8, share, slots), (9, share, slots), (2, slots, hidden_share), (2, slots, hidden_share)],
    )
    grad_b_model = jnp.swapaxes(grad_b_model, 1, 2)
    grad_a_hidden = jnp.swapaxes(grad_a_hidden, 1, 2)
    return (layer_out, grad_frames, grad_a_model, grad_a_hidden, grad_b_model, grad_b_hidden)


def solution(mesh):
    every = ("chip", "core", "fz", "fh")
    clips, spread = ("chip", "core"), ("fz", "fh")
    in_specs = (
        P(clips, spread, None),
        P(clips, spread, None),
        P(clips),
        P(),
        P(),
        P(),
        P(None, every, None),
        P(None, every, None),
        P(every, None),
        P(every, None),
        P(every, None),
        P(None, every),
        P(every, None),
        P(None, spread, None),
        P(None, spread, None),
        P(None, None, spread),
        P(None, None, spread),
    )
    out_specs = (
        P(clips, spread, None),
        P(clips, spread, None),
        P(None, every, None),
        P(None, every, None),
        P(None, None, every),
        P(None, None, every),
    )

    def run(frames, *rest):
        dp, fsdp = mesh.shape["dp"], mesh.shape["fsdp"]
        together = 2 * frames.shape[0] // dp
        cut = Mesh(
            mesh.devices.reshape(dp // 2, 2, together, fsdp // together), EVERYWHERE
        )
        return jax.shard_map(
            local, mesh=cut, in_specs=in_specs, out_specs=out_specs, check_vma=False
        )(frames, *rest)

    return run
```

```python
import functools
import math

import jax
import jax.numpy as jnp
from jax import lax
from jax.experimental import pallas as pl
from jax.experimental.pallas import tpu as pltpu
from jax.sharding import Mesh
from jax.sharding import PartitionSpec as P

HEADS = 16
KERNEL = 31
RANK = 16
EPSILON = 1e-05
PACK_ROOM = 56 * 1024 * 1024
EVERYWHERE = ("chip", "core", "fz", "fh")

HD = 64
REL_LEFT = 64
REL_RIGHT = 8
TILE = 128
WIDE = 3 * TILE
VMEM = 32 * 1024 * 1024


def dot_nn(a, b):
    return lax.dot_general(a, b, (((1,), (0,)), ((), ())), preferred_element_type=jnp.float32)


def dot_nt(a, b):
    return lax.dot_general(a, b, (((1,), (1,)), ((), ())), preferred_element_type=jnp.float32)


def chunk_plan(tile, chunks):
    return [{chunks - 1: 0, 0: 1, 1: 2}.get((c - tile) % chunks) for c in range(chunks)]


def far_left(c, tile, chunks, own):
    return jnp.logical_or(c + own >= chunks, c < tile)


def wrapped_band(c, tile, chunks, own):
    if tile == 0 and c == chunks - 1:
        return own > 0
    if c == tile + 1:
        return c + own < chunks
    return None


def tile_scores(scores, table, tile, own):
    near = pltpu.roll(table[:, :TILE], TILE // 2, 1, stride=1, stride_axis=0)
    first, last = table[:, TILE : 2 * TILE], table[:, 2 * TILE :]
    ahead = lane_ahead()
    bands = [
        jnp.where(ahead >= TILE // 2, near, first),
        jnp.where(ahead < -(TILE // 2), first, jnp.where(ahead >= TILE // 2, last, near)),
        jnp.where(ahead < -(TILE // 2), near, last),
    ]
    chunks = scores.shape[1] // TILE
    parts = []
    for c, spot in enumerate(chunk_plan(tile, chunks)):
        part = scores[:, c * TILE : (c + 1) * TILE]
        if spot is None:
            bias = first if c < tile else jnp.where(c + own >= chunks, first, last)
        else:
            bias = bands[spot]
            true_band = wrapped_band(c, tile, chunks, own)
            if true_band is not None:
                bias = jnp.where(true_band, bias, jnp.where(far_left(c, tile, chunks, own), first, last))
        parts.append(part + bias)
    return parts


def lane_ahead():
    lane = lax.broadcasted_iota(jnp.int32, (TILE, TILE), 1)
    return lane - lax.broadcasted_iota(jnp.int32, (TILE, TILE), 0)


def stacked(refs):
    return jnp.concatenate([ref[...] for ref in refs], axis=0)


def head_lanes(rows):
    low = lax.broadcasted_iota(jnp.int32, (rows, 2 * HD), 1) < HD
    return low, (low, jnp.logical_not(low))


def row_tiles(rows):
    return [(tile, slice(tile * TILE, (tile + 1) * TILE)) for tile in range(rows // TILE)]


def attn_fwd_kernel(group, own_ref, q_ref, rel_ref, *refs):
    own = own_ref[0]
    keys, values, rel_wide = stacked(refs[:group]), stacked(refs[group : 2 * group]), rel_ref[...]
    o_ref, rate_ref, p_ref, s_ref, w_ref = refs[2 * group :]
    rows_n = q_ref.shape[0]
    low, heads = head_lanes(rows_n)
    q_pair = q_ref[...] * jnp.bfloat16(0.125)
    for head, lanes in enumerate(heads):
        q_head = jnp.where(lanes, q_pair, jnp.zeros_like(q_pair))
        s_ref[head] = dot_nt(q_head, keys)
        w_ref[head] = dot_nt(q_head, rel_wide)
    ones = jnp.ones_like(values)
    values_ones = jnp.concatenate([values, ones], axis=1)
    outs = []
    for head in range(2):
        for tile, rows in row_tiles(rows_n):
            parts = tile_scores(s_ref[head, rows, :], w_ref[head, rows, :], tile, own)
            top = jnp.max(functools.reduce(jnp.maximum, parts), axis=1, keepdims=True)
            top = jnp.broadcast_to(top, (TILE, TILE))
            expo = [jnp.exp(part - top).astype(jnp.bfloat16) for part in parts]
            p_ref[head, rows, :] = jnp.concatenate(expo, axis=1)
        outs.append(dot_nn(p_ref[head], values_ones))
        total = outs[head][:, 2 * HD :]
        rate_ref[:, head * TILE : (head + 1) * TILE] = 1.0 / total
        outs[head] = outs[head][:, : 2 * HD] / total
    o_ref[...] = jnp.where(low, outs[0], outs[1]).astype(jnp.bfloat16)


def attn_bwd_kernel(group, own_ref, q_ref, do_ref, rate_ref, e_ref, rev_ref, flip_ref, mark_ref, *refs):
    own = own_ref[0]
    keys, values = stacked(refs[:group]), stacked(refs[group : 2 * group])
    dq_ref, own_out, far_out, dp_ref, ds_ref, p_ref, band_ref = refs[2 * group :]
    rows_n, keys_n = q_ref.shape[0], keys.shape[0]
    chunks = keys_n // TILE
    low, heads = head_lanes(rows_n)
    lane = lax.broadcasted_iota(jnp.int32, (1, TILE), 1)
    q_pair = q_ref[...] * jnp.bfloat16(0.125)
    do_pair = do_ref[...]
    keys_marked = jnp.concatenate([keys, mark_ref[...]], axis=1)
    for head, lanes in enumerate(heads):
        dp_ref[head] = dot_nt(jnp.where(lanes, do_pair, jnp.zeros_like(do_pair)), values)
    dqs = []
    ahead = lane_ahead()
    for head in range(2):
        edges = []
        for tile, rows in row_tiles(rows_n):
            rate = rate_ref[rows, head * TILE : (head + 1) * TILE]
            parts = [e_ref[head, rows, c * TILE : (c + 1) * TILE] for c in range(chunks)]
            probs = [part.astype(jnp.float32) * rate for part in parts]
            d_parts = [dp_ref[head, rows, c * TILE : (c + 1) * TILE] for c in range(chunks)]
            inner = functools.reduce(jnp.add, [p * d for p, d in zip(probs, d_parts)])
            inner = jnp.sum(inner, axis=1, keepdims=True)
            d_scores = [(p * (d - inner)).astype(jnp.bfloat16) for p, d in zip(probs, d_parts)]
            p_ref[head, rows, :] = jnp.concatenate([p.astype(jnp.bfloat16) for p in probs], axis=1)
            ds_ref[head, rows, :] = jnp.concatenate(d_scores, axis=1)
            band = [None, None, None]
            for c, spot in enumerate(chunk_plan(tile, chunks)):
                if spot is not None:
                    near = wrapped_band(c, tile, chunks, own)
                    piece = d_scores[c]
                    band[spot] = piece if near is None else jnp.where(near, piece, jnp.zeros_like(piece))
            behind, beyond = ahead < -(TILE // 2), ahead >= TILE // 2
            none = jnp.zeros_like(band[0])
            band_ref[head, rows, :] = jnp.where(beyond, band[0], jnp.where(behind, band[2], band[1]))
            sides = (
                (jnp.where(beyond, none, band[0]), jnp.where(behind, band[1], none)),
                (jnp.where(behind, none, band[2]), jnp.where(beyond, band[1], none)),
            )
            edges.append([a.astype(jnp.float32) + b.astype(jnp.float32) for a, b in sides])
        turned = dot_nn(band_ref[head], flip_ref[...])
        turned = jnp.concatenate(
            [
                pltpu.roll(turned[rows, :], TILE // 2, 1, stride=1, stride_axis=0).astype(jnp.bfloat16)
                for _, rows in row_tiles(rows_n)
            ],
            axis=0,
        )
        marked = dot_nn(ds_ref[head], keys_marked)
        near_part = dot_nn(turned, rev_ref[...])
        outs = []
        for tile, rows in row_tiles(rows_n):
            weights = [jnp.zeros((1, TILE), jnp.float32)] * 2
            for c, spot in enumerate(chunk_plan(tile, chunks)):
                near = wrapped_band(c, tile, chunks, own)
                if spot is not None and near is None:
                    continue
                left = far_left(c, tile, chunks, own)
                far = 1.0 if spot is None else jnp.where(near, 0.0, 1.0)
                for side, on in enumerate((left, jnp.logical_not(left))):
                    here = jnp.where(on, far, 0.0)
                    weights[side] = weights[side] + jnp.where(lane == c, here, 0.0)
            sums = marked[rows, TILE:]
            before, after = [
                jnp.sum(sums * weight + edge, axis=1, keepdims=True)
                for weight, edge in zip(weights, edges[tile])
            ]
            d_query = marked[rows, :TILE] + near_part[rows, :]
            d_query = d_query + before * rev_ref[TILE - 1 : TILE, :].astype(jnp.float32)
            d_query = d_query + after * rev_ref[0:1, :].astype(jnp.float32)
            outs.append(d_query * 0.125)
        dqs.append(outs)
    for tile, rows in row_tiles(rows_n):
        dq_ref[rows, :] = jnp.where(low[rows, :], dqs[0][tile], dqs[1][tile]).astype(dq_ref.dtype)
    q_turned = jnp.transpose(q_pair)
    do_turned = jnp.transpose(do_pair)
    for which, (turned, kept) in enumerate(((q_turned, ds_ref), (do_turned, p_ref))):
        both = jnp.concatenate(
            [dot_nn(turned[head * HD : (head + 1) * HD, :], kept[head]) for head in range(2)], axis=0
        )
        both = jnp.transpose(both)
        own_out[which] = both[:rows_n].astype(own_out.dtype)
        far_out[which] = both[rows_n:].astype(far_out.dtype)


def rel_tables(rel_table, keys_n):
    count = rel_table.shape[0]
    rows = jnp.concatenate([rel_table, jnp.broadcast_to(rel_table[-1:], (TILE - count, HD))])
    rows = jnp.concatenate([rows, rows], axis=1)
    wide = jnp.concatenate(
        [rows, jnp.broadcast_to(rows[:1], rows.shape), jnp.broadcast_to(rows[-1:], rows.shape)]
    )
    flip = jnp.arange(TILE)[:, None] + jnp.arange(TILE)[None, :] == TILE - 1
    marks = jnp.arange(keys_n)[:, None] // TILE == jnp.arange(TILE)[None, :]
    return wide, rows[::-1], flip.astype(jnp.bfloat16), marks.astype(jnp.bfloat16)


def pair_blocks(rows, width, group):
    pairs = width // (2 * HD)
    one = pl.BlockSpec((rows, 2 * HD), lambda h: (0, h))
    two = pl.BlockSpec((rows, 2 * HD), lambda h: (0, pairs + h))
    return pairs, one, [one] * group + [two] * group


def fixed(array):
    return pl.BlockSpec(array.shape, lambda h: (0, 0))


def attention_forward(own, query, kv, rel_wide):
    rows, width = query.shape
    pairs, block, kv_blocks = pair_blocks(rows, width, len(kv))
    size = rows * rows * len(kv) * width
    return pl.pallas_call(
        functools.partial(attn_fwd_kernel, len(kv)),
        grid=(pairs,),
        in_specs=[pl.BlockSpec(memory_space=pltpu.SMEM), block, fixed(rel_wide)] + kv_blocks,
        out_specs=[
            block,
            pl.BlockSpec((rows, 2 * TILE), lambda h: (0, h)),
            pl.BlockSpec((2, rows, rows * len(kv)), lambda h: (h, 0, 0)),
        ],
        out_shape=[
            jax.ShapeDtypeStruct((rows, width), jnp.bfloat16),
            jax.ShapeDtypeStruct((rows, width // HD * TILE), jnp.float32),
            jax.ShapeDtypeStruct((width // HD, rows, rows * len(kv)), jnp.bfloat16),
        ],
        scratch_shapes=[
            pltpu.VMEM((2, rows, rows * len(kv)), jnp.float32),
            pltpu.VMEM((2, rows, WIDE), jnp.float32),
        ],
        compiler_params=pltpu.CompilerParams(vmem_limit_bytes=VMEM),
        cost_estimate=pl.CostEstimate(flops=12 * size, bytes_accessed=rows * width * 16, transcendentals=0),
        name="attention_forward",
    )(own, query, rel_wide, *kv, *kv)


def attention_backward(own, query, kv, d_out, rate, expo, tables):
    rows, width = query.shape
    keys_n = rows * len(kv)
    pairs, block, kv_blocks = pair_blocks(rows, width, len(kv))
    size = rows * keys_n * width
    return pl.pallas_call(
        functools.partial(attn_bwd_kernel, len(kv)),
        grid=(pairs,),
        in_specs=[pl.BlockSpec(memory_space=pltpu.SMEM), block, block]
        + [pl.BlockSpec((rows, 2 * TILE), lambda h: (0, h))]
        + [pl.BlockSpec((2, rows, keys_n), lambda h: (h, 0, 0))]
        + [fixed(table) for table in tables[1:]]
        + kv_blocks,
        out_specs=[
            block,
            pl.BlockSpec((2, rows, 2 * HD), lambda h: (0, 0, h)),
            pl.BlockSpec((2, keys_n - rows, 2 * HD), lambda h: (0, 0, h)),
        ],
        out_shape=[
            jax.ShapeDtypeStruct((rows, width), jnp.bfloat16),
            jax.ShapeDtypeStruct((2, rows, width), jnp.bfloat16),
            jax.ShapeDtypeStruct((2, keys_n - rows, width), jnp.bfloat16),
        ],
        scratch_shapes=[
            pltpu.VMEM((2, rows, keys_n), jnp.float32),
            pltpu.VMEM((2, rows, keys_n), jnp.bfloat16),
            pltpu.VMEM((2, rows, keys_n), jnp.bfloat16),
            pltpu.VMEM((2, rows, TILE), jnp.bfloat16),
        ],
        compiler_params=pltpu.CompilerParams(vmem_limit_bytes=VMEM),
        cost_estimate=pl.CostEstimate(flops=24 * size, bytes_accessed=rows * width * 32, transcendentals=0),
        name="attention_backward",
    )(own, query, d_out, rate, expo, *tables[1:], *kv, *kv)


class Gather:
    def __init__(self):
        self.chips = lax.axis_size("chip")
        side = math.isqrt(self.chips)
        self.first, self.second = (side, side) if side * side == self.chips else (self.chips, 1)
        chip, core = lax.axis_index("chip"), lax.axis_index("core")
        places = []
        for owner in (core, 1 - core):
            for early, late in self.steps():
                one = self.moved(chip, early, late)
                two = self.moved(chip, late, early)
                places.append(jnp.where(owner == 0, one, two) * 2 + owner)
        self.places = jnp.stack(places).astype(jnp.int32)

    def steps(self):
        steps = [(early, 0) for early in range(self.first)]
        steps += [(0, late) for late in range(1, self.second)]
        return steps + [(e, l) for l in range(1, self.second) for e in range(1, self.first)]

    def moved(self, chip, along_first, along_second):
        return chip ^ (along_first * self.second + along_second)

    def hop(self, block, early, late):
        route = []
        for chip in range(self.chips):
            route.append((self.moved(chip, early, late) * 2, chip * 2))
            route.append((self.moved(chip, late, early) * 2 + 1, chip * 2 + 1))
        return lax.ppermute(block, ("chip", "core"), route)

    def stages(self, shards, used):
        swap = lambda block: lax.ppermute(block, "core", [(0, 1), (1, 0)])
        collect = lambda shard: lax.all_gather(shard, ("fz", "fh"), axis=0, tiled=True)
        count = len(shards)
        shards = list(shards)
        blocks = [collect(shard) for shard in shards[:3]]
        kept, traded, last = [[] for _ in shards], [[] for _ in shards], []
        complete, ahead = 0, self.first + self.second - 1
        for turn in range(count + 1):
            onward = kept[turn - 1][1 : self.first] if turn else []
            if turn > 1:
                late, due = kept[turn - 2][ahead if turn == count else 0 :], blocks[turn : turn + 1] if turn > 2 else []
                self.held = yield [kept[which] + traded[which] for which in range(complete)]
                (onward, late, due), last, self.held = lax.optimization_barrier(
                    ((onward, late, due), last, list(self.held))
                )
                if due:
                    blocks[turn] = due[0]
                further = [self.hop(block, 0, step) for step in range(1, self.second) for block in onward]
                kept[turn - 1] = kept[turn - 1] + further
                across = [swap(block) for block in late]
                traded[turn - 2] = traded[turn - 2] + across
                last = further + across
                complete += 1
            self.held = yield [kept[which] + traded[which] for which in range(complete)]
            if turn < count:
                fresh = blocks[turn][:, : used[turn]]
                coming = shards[turn + 3 : turn + 4]
                late = kept[turn - 1][:ahead] if turn == count - 1 else []
                (fresh, onward, coming, late), last, self.held = lax.optimization_barrier(
                    ((fresh, onward, coming, late), last, list(self.held))
                )
                blocks += [collect(shard) for shard in coming]
                early = [self.hop(fresh, step, 0) for step in range(1, self.first)]
                other = [self.hop(fresh, 0, step) for step in range(1, self.second)]
                kept[turn] = [fresh] + early + other
                traded[turn - 1] = traded[turn - 1] + [swap(block) for block in late]
                last = early + other + (traded[turn - 1] if late else [])
                if turn == 1:
                    further = [self.hop(block, 0, step) for step in range(1, self.second) for block in onward]
                    kept[0] = kept[0] + further
                    last = last + further
            else:
                late, last, self.held = lax.optimization_barrier((kept[-1], last, list(self.held)))
                traded[-1] = [swap(block) for block in late]
        yield [own + other for own, other in zip(kept, traded)]


HBM = pl.BlockSpec(memory_space=pltpu.HBM)
SCALARS = pl.BlockSpec(memory_space=pltpu.SMEM)
VMEM_SPEC = pl.BlockSpec(memory_space=pltpu.VMEM)
TALL = 512
HALO = 32
MIB = 1024 * 1024


def dot_tn(a, b):
    return lax.dot_general(a, b, (((0,), (0,)), ((), ())), preferred_element_type=jnp.float32)


def norm_rows(field):
    centred = field - jnp.mean(field, -1, keepdims=True)
    rate = lax.rsqrt(jnp.mean(centred * centred, -1, keepdims=True) + EPSILON)
    return centred * rate, rate


def norm_back(grad, gain, normed, rate):
    scaled = grad * gain
    inner = jnp.mean(scaled * normed, -1, keepdims=True)
    return (scaled - jnp.mean(scaled, -1, keepdims=True) - normed * inner) * rate


def each_rows(rows, step, body):
    for begin in range(0, rows, step):
        body(slice(begin, begin + step))


def shape_of(rows, width, dtype=jnp.bfloat16):
    return jax.ShapeDtypeStruct((rows, width), dtype)


class Weight:
    def __init__(self, places, pieces, begin, width):
        self.places, self.pieces, self.begin, self.width = places, pieces, begin, width
        self.count, self.block = len(pieces), pieces[0].shape[0]
        self.depth = self.count * self.block
        self.bytes = 2 * self.depth * width


class Load:
    def __init__(self, weight, places_ref, pieces, store, sems):
        self.store, self.copies = store, []
        for index, piece in enumerate(pieces):
            row = pl.multiple_of(places_ref[index] * weight.block, weight.block)
            self.copies.append(
                pltpu.make_async_copy(
                    piece.at[:, pl.ds(weight.begin, weight.width)],
                    store.at[pl.ds(row, weight.block), :],
                    sems.at[index],
                )
            )

    def start(self):
        for copy in self.copies:
            copy.start()

    def wait(self):
        for copy in self.copies:
            copy.wait()


class Rows:
    def __init__(self, array, begin, count):
        self.array, self.begin, self.count = array, begin, count


class Factor:
    def __init__(self, ref, rows):
        self.ref, self.at = ref, slice(rows.begin, rows.begin + rows.count)

    def all(self):
        return self.ref[self.at, :]

    def columns(self, at):
        return self.ref[self.at, at]


class Refs:
    pass


def fused(body, name, limit, weights, factors, near, far, outs, far_outs=(), scratch=(), turn=()):
    arrays = []
    for rows in factors.values():
        if not any(rows.array is array for array in arrays):
            arrays.append(rows.array)
    far, far_outs, scratch = dict(far), dict(far_outs), dict(scratch)
    places = [weight.places for weight in list(weights.values())[:1]]
    pieces = [piece for weight in weights.values() for piece in weight.pieces]

    def kernel(*refs):
        refs = list(refs)
        take = lambda count: [refs.pop(0) for _ in range(count)]
        r = Refs()
        places_ref = take(len(places))
        blocks = [take(weight.count) for weight in weights.values()]
        factor_refs, turn_ref = take(len(arrays)), take(len(turn))
        r.turn, r.core = (turn_ref + [None, None])[:2]
        for names in (near, far, outs, far_outs):
            for key, ref in zip(names, take(len(names))):
                setattr(r, key, ref)
        for (key, weight), block in zip(weights.items(), blocks):
            setattr(r, key, Load(weight, places_ref[0], block, *take(2)))
        for key, rows in factors.items():
            (which,) = [i for i, array in enumerate(arrays) if array is rows.array]
            setattr(r, key, Factor(factor_refs[which], rows))
        for key, ref in zip(scratch, take(len(scratch))):
            setattr(r, key, ref)
        body(r)

    total = sum(weight.bytes for weight in weights.values())
    everything = [*near.values(), *far.values(), *outs.values(), *far_outs.values()]
    moved = sum(math.prod(item.shape) * item.dtype.itemsize for item in everything)
    rows = list(near.values())[0].shape[0] if near else 0
    stores = []
    for weight in weights.values():
        stores.append(pltpu.VMEM((weight.depth, weight.width), jnp.bfloat16))
        stores.append(pltpu.SemaphoreType.DMA((weight.count,)))
    made = pl.pallas_call(
        kernel,
        in_specs=[SCALARS] * len(places)
        + [HBM] * len(pieces)
        + [VMEM_SPEC] * len(arrays)
        + [SCALARS] * len(turn)
        + [VMEM_SPEC] * len(near)
        + [HBM] * len(far),
        out_specs=[VMEM_SPEC] * len(outs) + [HBM] * len(far_outs),
        out_shape=[*outs.values(), *far_outs.values()],
        scratch_shapes=stores + list(scratch.values()),
        compiler_params=pltpu.CompilerParams(vmem_limit_bytes=total + limit * MIB),
        cost_estimate=pl.CostEstimate(flops=rows * total, bytes_accessed=moved + total, transcendentals=0),
        name=name,
    )(*places, *pieces, *arrays, *turn, *near.values(), *far.values())
    return made


def wide_step(kind, load, u_ref, down, up, z_ref, outs, then=None):
    z_ref[...] = dot_nt(u_ref[...], down.all()).astype(jnp.bfloat16)
    load.wait()
    if then:
        then()
    width = load.store.shape[1]
    out_width = width // 2 if kind == "glu" else width
    for begin in range(0, out_width, TALL):
        at = slice(begin, begin + TALL)
        parts = [slice(base + begin, base + begin + TALL) for base in range(0, width, out_width)]
        result = [
            dot_nn(u_ref[...], load.store[:, part]) + dot_nn(z_ref[...], up.columns(part)) for part in parts
        ]
        if kind == "silu":
            gate = jax.nn.sigmoid(result[0])
            active = result[0] * gate
            outs[0][:, at] = active.astype(jnp.bfloat16)
            outs[1][:, at] = (gate + active * (1.0 - gate)).astype(jnp.bfloat16)
        elif kind == "glu":
            gate = jax.nn.sigmoid(result[1])
            gated = result[0] * gate
            outs[0][:, at] = gated.astype(jnp.bfloat16)
            outs[1][:, at] = gate.astype(jnp.bfloat16)
            outs[2][:, at] = (gated * (1.0 - gate)).astype(jnp.bfloat16)
        else:
            which = min(begin // outs[0].shape[1], 1)
            first = which * outs[0].shape[1]
            outs[which][:, begin - first : begin - first + TALL] = result[0].astype(jnp.bfloat16)


def narrow_step(factor, load, u_ref, down, up, z_ref, field_ref, field_out, then=None):
    z_ref[...] = dot_nt(u_ref[...], down.all()).astype(jnp.bfloat16)
    load.wait()
    if then:
        then()
    for begin in range(0, load.store.shape[1], TALL):
        at = slice(begin, begin + TALL)
        result = dot_nn(u_ref[...], load.store[:, at]) + dot_nn(z_ref[...], up.columns(at))
        field_out[:, at] = field_ref[:, at].astype(jnp.float32) + factor * result


def norm_step(field_ref, gain_ref, bias_ref, out_ref):
    def finish(at):
        normed = norm_rows(field_ref[at, :])[0] * gain_ref[...] + bias_ref[...]
        out_ref[at, :] = normed.astype(jnp.bfloat16)

    each_rows(field_ref.shape[0], 128, finish)


def grads_step(grad, up, z_ref, u_ref, dz, da_ref, db_ref):
    dz[...] = dot_nt(grad[...], up.all()).astype(jnp.bfloat16)
    db_ref[...] = dot_tn(z_ref[...], grad[...]).astype(jnp.bfloat16)
    da_ref[...] = dot_tn(dz[...], u_ref[...]).astype(jnp.bfloat16)


def inputs_step(load, grad, dz, down, out_ref, then=None):
    load.wait()
    if then:
        then()
    for begin in range(0, load.store.shape[0], TALL):
        at = slice(begin, begin + TALL)
        result = dot_nt(grad[...], load.store[at, :]) + dot_nn(dz[...], down.columns(at))
        out_ref[:, at] = result.astype(out_ref.dtype)


def norm_back_step(d_inputs, field_ref, gain_ref, prior_ref, out_ref):
    def finish(at):
        normed, rate = norm_rows(field_ref[at, :].astype(jnp.float32))
        out_ref[at, :] = prior_ref[at, :] + norm_back(d_inputs[at, :], gain_ref[...], normed, rate)

    each_rows(field_ref.shape[0], 128, finish)


def halves_step(turn_ref, first_out, second_out, rows_of):
    half = first_out.shape[0]
    step = half // 2
    for begin in range(0, 2 * half, step):
        made = rows_of(slice(begin, begin + step)).astype(first_out.dtype)
        at = slice(begin % half, begin % half + step)
        for out, turn in ((first_out, begin // half), (second_out, 1 - begin // half)):

            @pl.when(turn_ref[0] == turn)
            def _(out=out):
                out[at, :] = made


def project_wide(kind, inputs, weight, a, b):
    rows, width = inputs.shape[0], weight.width
    sizes = dict(silu=[width] * 2, glu=[width // 2] * 3, plain=[width // 3, width - width // 3])[kind]
    names = ["out%d" % index for index in range(len(sizes))]

    def body(r):
        r.weight.start()
        wide_step(kind, r.weight, r.u, r.a, r.b, r.z, [getattr(r, key) for key in names])

    outs = dict(z=shape_of(rows, a.count), **{key: shape_of(rows, size) for key, size in zip(names, sizes)})
    return fused(body, "project_" + kind, 14, dict(weight=weight), dict(a=a, b=b), dict(u=inputs), {}, outs)


def project_narrow(inputs, weight, a, b, field, gain, bias, factor):
    rows, width = inputs.shape[0], weight.width

    def body(r):
        r.weight.start()
        narrow_step(factor, r.weight, r.u, r.a, r.b, r.z, r.field, r.made)
        norm_step(r.made, r.gain, r.bias, r.normed)

    outs = dict(
        z=shape_of(rows, a.count), made=shape_of(rows, width, jnp.float32),
        normed=shape_of(rows, width),
    )
    near = dict(u=inputs, field=field, gain=gain, bias=bias)
    return fused(body, "project_next", 14, dict(weight=weight), dict(a=a, b=b), near, {}, outs)


def feed_forward_last(inputs, up, down, factors, field, gain, bias, cotangent, turn):
    rows, width = inputs.shape
    rank, hidden = factors["a_up"].count, up.width

    def body(r):
        r.up.start()
        wide_step("silu", r.up, r.u, r.a_up, r.b_up, r.z_up, (r.held_act, r.held_slope), r.down.start)
        leaving = [
            pltpu.make_async_copy(r.held_act, r.act, r.sems.at[0]),
            pltpu.make_async_copy(r.held_slope, r.slope, r.sems.at[1]),
        ]
        for copy in leaving:
            copy.start()
        narrow_step(0.5, r.down, r.held_act, r.a_down, r.b_down, r.z_down, r.field, r.d_out)
        gain, bias = r.gain[...], r.bias[...]

        def finish(at):
            normed, rate = norm_rows(r.d_out[at, :])
            r.d_out[at, :] = norm_back(r.cot[at, :].astype(jnp.float32), gain, normed, rate)
            return normed * gain + bias

        halves_step(r.turn, r.first, r.second, finish)
        for copy in leaving:
            copy.wait()

    outs = dict(
        z_up=shape_of(rows, rank), z_down=shape_of(rows, rank),
        d_out=shape_of(rows, width, jnp.float32), first=shape_of(rows // 2, width),
        second=shape_of(rows // 2, width),
    )
    near = dict(u=inputs, field=field, gain=gain, bias=bias, cot=cotangent)
    return fused(
        body, "feed_forward_last", 30, dict(up=up, down=down), factors, near, {}, outs,
        dict(act=shape_of(rows, hidden), slope=shape_of(rows, hidden)),
        dict(
            held_act=pltpu.VMEM((rows, hidden), jnp.bfloat16),
            held_slope=pltpu.VMEM((rows, hidden), jnp.bfloat16),
            sems=pltpu.SemaphoreType.DMA((2,)),
        ),
        turn,
    )


def ffn_back_steps(r, d_ref, u_ref):
    r.half[...] = (0.5 * d_ref[...]).astype(jnp.bfloat16)
    r.dz_down[...] = dot_nt(r.half[...], r.b_down.all()).astype(jnp.bfloat16)
    r.db_down[...] = dot_tn(r.z_down[...], r.half[...]).astype(jnp.bfloat16)
    r.down.wait()
    pltpu.make_async_copy(r.slope, r.held_slope, r.sems.at[0]).wait()
    act_copy = pltpu.make_async_copy(r.act, r.held_act, r.sems.at[1])
    act_copy.start()
    r.up.start()
    for begin in range(0, r.down.store.shape[0], TALL):
        at = slice(begin, begin + TALL)
        result = dot_nt(r.half[...], r.down.store[at, :]) + dot_nn(r.dz_down[...], r.a_down.columns(at))
        r.d_hidden[:, at] = (result * r.held_slope[:, at].astype(jnp.float32)).astype(jnp.bfloat16)
    r.dz_up[...] = dot_nt(r.d_hidden[...], r.b_up.all()).astype(jnp.bfloat16)
    act_copy.wait()
    r.da_down[...] = dot_tn(r.dz_down[...], r.held_act[...]).astype(jnp.bfloat16)
    inputs_step(r.up, r.d_hidden, r.dz_up, r.a_up, r.d_inputs)
    r.db_up[...] = dot_tn(r.z_up[...], r.d_hidden[...]).astype(jnp.bfloat16)
    r.da_up[...] = dot_tn(r.dz_up[...], u_ref[...]).astype(jnp.bfloat16)


def ffn_back_parts(rows, width, hidden, rank):
    outs = dict(
        da_up=shape_of(rank, width), db_up=shape_of(rank, hidden),
        da_down=shape_of(rank, hidden), db_down=shape_of(rank, width),
    )
    scratch = dict(
        half=pltpu.VMEM((rows, width), jnp.bfloat16),
        dz_down=pltpu.VMEM((rows, rank), jnp.bfloat16),
        dz_up=pltpu.VMEM((rows, rank), jnp.bfloat16),
        d_hidden=pltpu.VMEM((rows, hidden), jnp.bfloat16),
        d_inputs=pltpu.VMEM((rows, width), jnp.float32),
        held_act=pltpu.VMEM((rows, hidden), jnp.bfloat16),
        held_slope=pltpu.VMEM((rows, hidden), jnp.bfloat16),
        sems=pltpu.SemaphoreType.DMA((2,)),
    )
    return outs, scratch


def feed_forward_back(d_field, up, down, factors, kept, field, gain):
    rows, width = d_field.shape
    inputs, act, slope, z_up, z_down = kept

    def body(r):
        r.down.start()
        pltpu.make_async_copy(r.slope, r.held_slope, r.sems.at[0]).start()
        ffn_back_steps(r, r.d_field, r.u)
        norm_back_step(r.d_inputs, r.field, r.gain, r.d_field, r.made)

    outs, scratch = ffn_back_parts(rows, width, up.width, factors["a_up"].count)
    outs = dict(made=shape_of(rows, width, jnp.float32), **outs)
    near = dict(d_field=d_field, u=inputs, z_up=z_up, z_down=z_down, field=field, gain=gain)
    return fused(
        body, "feed_forward_back", 41, dict(down=down, up=up), factors, near,
        dict(act=act, slope=slope), outs, {}, scratch,
    )


def field_back(kind, grad, weight, a, b, inputs, slot_acts, extras=()):
    rows, depth, rank = grad.shape[0], weight.depth, a.count
    low = grad.dtype == jnp.bfloat16
    names = dict(norm=("prior", "field", "gain"), conv=("field", "gain", "bias"), plain=())[kind]

    def body(r):
        r.weight.start()
        grad_ref = r.grad
        if not low:
            grad_ref = r.low
            r.low[...] = r.grad[...].astype(jnp.bfloat16)
        grads_step(grad_ref, r.b, r.z, r.u, r.dz, r.da, r.db)
        if kind == "plain":
            inputs_step(r.weight, grad_ref, r.dz, r.a, r.made)
            return
        inputs_step(r.weight, grad_ref, r.dz, r.a, r.d_inputs)
        if kind == "norm":
            norm_back_step(r.d_inputs, r.field, r.gain, r.prior, r.made)
            return
        gain = r.gain[...]

        def finish(at):
            normed, rate = norm_rows(r.field[at, :])
            shifted = normed * gain + r.bias[...]
            gate = jax.nn.sigmoid(shifted)
            into = gate + shifted * gate * (1.0 - gate)
            r.made[at, :] = norm_back(r.d_inputs[at, :] * into, gain, normed, rate)

        each_rows(rows, 128, finish)

    made = shape_of(rows, depth, jnp.bfloat16 if kind == "plain" else jnp.float32)
    outs = dict(made=made, da=shape_of(rank, depth), db=shape_of(rank, weight.width))
    scratch = dict(dz=pltpu.VMEM((rows, rank), jnp.bfloat16))
    if not low:
        scratch["low"] = pltpu.VMEM((rows, weight.width), jnp.bfloat16)
    if kind != "plain":
        scratch["d_inputs"] = pltpu.VMEM((rows, depth), jnp.float32)
    near = dict(grad=grad, u=inputs, z=slot_acts, **dict(zip(names, extras)))
    return fused(
        body, "field_back_" + kind, 22, dict(weight=weight), dict(a=a, b=b), near, {}, outs, {}, scratch
    )


def first_half_back(d_query, shares, qkv_w, a_qkv, b_qkv, attn_in, z_qkv, prior, field, gain,
                    up, down, factors, kept, layer_in, layer_gain, turn):
    rows, width = d_query.shape
    inputs, act, slope, z_up, z_down = kept
    names = ["share%d" % index for index in range(len(shares))]

    def body(r):
        r.qkv_w.start()
        r.joined[:, :width] = r.d_query[...]
        for which in range(2):
            total = sum(getattr(r, key)[which].astype(jnp.float32) for key in names)
            r.joined[:, (1 + which) * width : (2 + which) * width] = total.astype(jnp.bfloat16)
        grads_step(r.joined, r.b_qkv, r.z_qkv, r.attn_in, r.dz, r.da_qkv, r.db_qkv)

        def then():
            r.down.start()
            pltpu.make_async_copy(r.slope, r.held_slope, r.sems.at[0]).start()

        inputs_step(r.qkv_w, r.joined, r.dz, r.a_qkv, r.d_inputs, then)
        norm_back_step(r.d_inputs, r.field, r.gain, r.prior, r.d_first)
        ffn_back_steps(r, r.d_first, r.u)

        def finish(at):
            normed, rate = norm_rows(r.layer_in[at, :].astype(jnp.float32))
            return r.d_first[at, :] + norm_back(r.d_inputs[at, :], r.layer_gain[...], normed, rate)

        halves_step(r.turn, r.first, r.second, finish)
        if packed:
            three = [
                r.db_qkv[which * rank : (which + 1) * rank, which * width : (which + 1) * width]
                for which in range(3)
            ]
            model = [r.da_up[...], r.da_qkv[...], r.db_down[...], *three]
            pack_step((r.ours, r.theirs), r.core, fsdp, model, [r.da_down[...], r.db_up[...]])

    rank = factors["a_up"].count
    outs, scratch = ffn_back_parts(rows, width, up.width, rank)
    grads = dict(**outs, da_qkv=shape_of(a_qkv.count, width), db_qkv=shape_of(a_qkv.count, 3 * width))
    outs = dict(first=shape_of(rows // 2, width), second=shape_of(rows // 2, width))
    devices, fsdp = lax.axis_size(EVERYWHERE), lax.axis_size("fz") * lax.axis_size("fh")
    packed = packs_whole(devices, width, up.width)
    if packed:
        scratch.update({key: pltpu.VMEM(item.shape, item.dtype) for key, item in grads.items()})
        count = -(-8 * rank // TILE) * (width // devices) + 2 * rank
        outs["ours"] = outs["theirs"] = jax.ShapeDtypeStruct((devices // 2, count, TILE), jnp.bfloat16)
    else:
        outs.update(grads)
    scratch["joined"] = pltpu.VMEM((rows, 3 * width), jnp.bfloat16)
    scratch["dz"] = pltpu.VMEM((rows, a_qkv.count), jnp.bfloat16)
    scratch["d_first"] = pltpu.VMEM((rows, width), jnp.float32)
    near = dict(
        d_query=d_query, **dict(zip(names, shares)), attn_in=attn_in, z_qkv=z_qkv, prior=prior,
        field=field, gain=gain, u=inputs, z_up=z_up, z_down=z_down, layer_in=layer_in,
        layer_gain=layer_gain,
    )
    return fused(
        body, "first_half_back", 42, dict(qkv_w=qkv_w, down=down, up=up),
        dict(a_qkv=a_qkv, b_qkv=b_qkv, **factors), near, dict(act=act, slope=slope), outs, {}, scratch,
        turn,
    )


def slide(lanes, parts, shifted, taps_ref, shifts, rows, store):
    begin = 0
    for part in parts:
        shifted[0, begin : begin + part.shape[0], :] = part
        begin += part.shape[0]
    length = begin - 8
    for turn in range(1, 8):
        shifted[turn, 0:length, :] = shifted[0, turn : turn + length, :]
    step = 64
    for at in range(0, rows, step):
        total = None
        for tap, shift in enumerate(shifts):
            base = shift - shift % 8 + at
            term = shifted[shift % 8, base : base + step, :] * taps_ref[tap : tap + 1, lanes]
            total = term if total is None else total + term
        store(slice(at, at + step), total)


def each_tile(width, body):
    def one(index, carry):
        body(pl.ds(pl.multiple_of(index * TILE, TILE), TILE))
        return carry

    lax.fori_loop(0, width // TILE, one, 0)


def conv_body(r):
    val_ref, earlier_ref, conv_ref, act_ref = r.value, r.earlier, r.conv, r.act
    taps_ref, gain_ref, bias_ref, shifted = r.taps, r.gain, r.bias, r.shifted
    rows, width = val_ref.shape

    def one(lanes):
        parts = [earlier_ref[:, lanes].astype(jnp.float32), val_ref[:, lanes].astype(jnp.float32)]

        def store(at, total):
            conv_ref[at, lanes] = total

        shifts = [HALO - KERNEL + 1 + tap for tap in range(KERNEL)]
        slide(lanes, parts, shifted, taps_ref, shifts, rows, store)

    each_tile(width, one)

    def finish(at):
        shifted_field = norm_rows(conv_ref[at, :])[0] * gain_ref[...] + bias_ref[...]
        act_ref[at, :] = (shifted_field * jax.nn.sigmoid(shifted_field)).astype(jnp.bfloat16)

    each_rows(rows, 128, finish)


def conv_back_body(r):
    d_ref, later_ref, out_ref = r.d_conv, r.later, r.made
    taps_ref, gate_ref, slope_ref, shifted = r.taps, r.gate, r.slope, r.shifted
    rows, width = d_ref.shape

    def one(lanes):
        parts = [d_ref[:, lanes], later_ref[:, lanes].astype(jnp.float32)]
        high = pl.ds(pl.multiple_of(lanes.start + width, TILE), TILE)

        def store(at, total):
            out_ref[at, lanes] = (total * gate_ref[at, lanes].astype(jnp.float32)).astype(jnp.bfloat16)
            out_ref[at, high] = (total * slope_ref[at, lanes].astype(jnp.float32)).astype(jnp.bfloat16)

        slide(lanes, parts, shifted, taps_ref, [KERNEL - 1 - tap for tap in range(KERNEL)], rows, store)

    each_tile(width, one)


def conv_forward(value, earlier, taps, gain, bias):
    rows, width = value.shape
    near = dict(value=value, earlier=earlier, taps=taps, gain=gain, bias=bias)
    outs = dict(conv=shape_of(rows, width, jnp.float32), act=shape_of(rows, width))
    scratch = dict(shifted=pltpu.VMEM((8, rows + HALO, TILE), jnp.float32))
    return fused(conv_body, "conv_forward", 16, {}, {}, near, {}, outs, {}, scratch)


def conv_backward(d_conv, later, taps, gate, slope):
    rows, width = d_conv.shape
    near = dict(d_conv=d_conv, later=later, taps=taps, gate=gate, slope=slope)
    scratch = dict(shifted=pltpu.VMEM((8, rows + HALO, TILE), jnp.float32))
    outs = dict(made=shape_of(rows, 2 * width))
    return fused(conv_back_body, "conv_backward", 16, {}, {}, near, {}, outs, {}, scratch)[0]


def gather_taps(weight):
    def body(r):
        r.weight.start()
        r.weight.wait()
        r.taps[...] = jnp.transpose(r.weight.store[...].astype(jnp.float32))[:HALO, :]

    outs = dict(taps=shape_of(HALO, weight.depth, jnp.float32))
    return fused(body, "gather_taps", 8, dict(weight=weight), {}, {}, {}, outs)[0]


class Layout:
    def __init__(self, together, fsdp):
        self.fsdp = fsdp
        self.inner = fsdp // together
        self.group = 2 * self.inner

    def place(self, core, f):
        return core * self.fsdp + f

    def round_route(self, turn):
        route = []
        for core in range(2):
            for f in range(self.fsdp):
                clip = (f % 2 + turn) % 2
                spot = f // 2
                target = self.place(spot % 2, (2 * core + clip) * self.inner + spot // 2)
                route.append((self.place(core, f), target))
        return route

    def gather_rows(self, blocks):
        parity = (lax.axis_index("fz") * self.inner + lax.axis_index("fh")) % 2
        clip = lax.axis_index("fz") % 2
        got = []
        for turn in range(2):
            sent = lax.dynamic_index_in_dim(blocks, (parity + turn) % 2, 0, keepdims=False)
            got.append(lax.ppermute(sent, ("core", "fz", "fh"), self.round_route(turn)))
        swap = clip == 1
        return jnp.concatenate(
            [jnp.where(swap, got[1], got[0]), jnp.where(swap, got[0], got[1])], axis=0
        )

    def scatter_rows(self, sent):
        parity = (lax.axis_index("fz") * self.inner + lax.axis_index("fh")) % 2
        got = []
        for turn in range(2):
            route = [(target, source) for source, target in self.round_route(turn)]
            got.append(lax.ppermute(sent[turn], ("core", "fz", "fh"), route))
        swap = parity == 1
        return jnp.stack([jnp.where(swap, got[1], got[0]), jnp.where(swap, got[0], got[1])])

    def spot_index(self, spot):
        return (spot % 2) * self.inner + spot // 2

    def from_spot(self, block, distance, cyclic):
        route = []
        for spot in range(self.group):
            source = spot + distance
            if cyclic:
                source %= self.group
            if 0 <= source < self.group:
                route.append((self.spot_index(source), self.spot_index(spot)))
        return lax.ppermute(block, ("core", "fh"), route)


def pack_adapters(ids, a_model, a_hidden, b_model, b_hidden):
    slots = a_model.shape[2]
    half = RANK // 2
    core = lax.axis_index("core")
    ranks = core * half + jnp.arange(half, dtype=jnp.int32)
    wanted = ids[:, None] * RANK + ranks[None, :]
    picker = (wanted[:, :, None] == jnp.arange(slots, dtype=jnp.int32)).astype(jnp.bfloat16)
    down = lambda a: jnp.einsum("jrs,pks->jprk", picker, a, preferred_element_type=jnp.float32)
    up = lambda b: jnp.einsum("jrs,psn->jprn", picker, b, preferred_element_type=jnp.float32)
    cut = a_hidden.shape[1] // a_model.shape[1]
    span = a_model.shape[1]

    def short(pack):
        rows = pack.reshape(pack.shape[0], pack.shape[1], half, cut, span)
        return jnp.swapaxes(rows, 2, 3).reshape(pack.shape[0], pack.shape[1] * cut, half, span)

    return jnp.concatenate(
        [down(a_model), up(b_model), short(down(a_hidden)), short(up(b_hidden))], axis=1
    ).astype(jnp.bfloat16)


def join_adapters_kernel(models, cut, plan, spots_ref, mine_ref, theirs_ref, *rest):
    wanted = len(plan)
    outs, full, held, sems = rest[:wanted], rest[wanted], rest[wanted + 1 : -1], rest[-1]
    count, groups, half, span = mine_ref.shape
    for step in range(count):
        at = pl.ds(pl.multiple_of(spots_ref[step] * span, span), span)
        for ref, core in ((mine_ref, spots_ref[count]), (theirs_ref, 1 - spots_ref[count])):
            rows = pl.ds(pl.multiple_of(core * half, half), half)
            full[:, rows, at] = ref[step].astype(jnp.float32)
    copies = []
    for which, (out, kept, parts) in enumerate(zip(outs, held, plan)):
        kept[...] = jnp.zeros_like(kept)
        for group, row, column in parts:
            if group < models:
                kept[row : row + RANK, column : column + count * span] = full[group].astype(kept.dtype)
                continue
            for f in range(count):
                begin = column + f * cut * span
                kept[row : row + RANK, begin : begin + span] = full[
                    group, :, f * span : (f + 1) * span
                ].astype(kept.dtype)
        copies.append(pltpu.make_async_copy(kept, out, sems.at[which]))
        copies[-1].start()
    for copy in copies:
        copy.wait()


def move_adapters(layout, pack, cut, shapes, plan, models):
    core = lax.axis_index("core")
    count = layout.fsdp
    here = lax.axis_index("fz") * layout.inner + lax.axis_index("fh")
    pieces = []
    for step in range(count):
        target = (here + step) % count
        piece = lax.dynamic_index_in_dim(pack, target // layout.inner, 0, keepdims=False)
        if step:
            route = [(f, (f + step) % count) for f in range(count)]
            piece = lax.ppermute(piece, ("fz", "fh"), route)
        pieces.append(piece)
    mine = jnp.stack(pieces)
    theirs = lax.ppermute(mine, "core", [(0, 1), (1, 0)])
    spots = jnp.stack([(here - step) % count for step in range(count)] + [core]).astype(jnp.int32)
    _, groups, half, span = mine.shape
    return pl.pallas_call(
        functools.partial(join_adapters_kernel, models, cut, plan),
        in_specs=[SCALARS, VMEM_SPEC, VMEM_SPEC],
        out_specs=[HBM] * len(shapes),
        out_shape=[shape_of(*shape) for shape in shapes],
        scratch_shapes=[pltpu.VMEM((groups, 2 * half, count * span), jnp.float32)]
        + [pltpu.VMEM(shape, jnp.bfloat16) for shape in shapes]
        + [pltpu.SemaphoreType.DMA((len(shapes),))],
        compiler_params=pltpu.CompilerParams(vmem_limit_bytes=16 * 1024 * 1024),
        name="join_adapters",
    )(spots, mine, theirs)


def factor_plan(models, hiddens, cut, span):
    hidden = [(models + which * cut + q, which * RANK, q * span) for which in range(hiddens) for q in range(cut)]
    return [[(group, group * RANK, 0) for group in range(models)], hidden]


def first_adapters(layout, pack, cut, width, hidden):
    shapes = [(2 * RANK, width), (2 * RANK, hidden)]
    model, inner = move_adapters(layout, pack, cut, shapes, factor_plan(2, 2, cut, pack.shape[3]), 2)
    return model, inner


def other_adapters(layout, pack, cut, width, hidden):
    shapes = [(15 * RANK, width), (2 * RANK, hidden), (3 * RANK, 3 * width), (RANK, 2 * width)]
    plan = factor_plan(15, 2, cut, pack.shape[3]) + [
        [(7 + which, which * RANK, which * width) for which in range(3)],
        [(13, 0, 0), (14, 0, width)],
    ]
    return move_adapters(layout, pack, cut, shapes, plan, 15)


def pack_step(outs, core_ref, fsdp, model, hidden):
    places, _, lanes = outs[0].shape
    model = jnp.concatenate([part.astype(jnp.float32) for part in model], axis=0)
    tiles = -(-model.shape[0] // TILE)
    if model.shape[0] % TILE:
        rest = jnp.zeros((tiles * TILE - model.shape[0], model.shape[1]), jnp.float32)
        model = jnp.concatenate([model, rest], axis=0)
    turned = [jnp.transpose(model[k * TILE : (k + 1) * TILE]).astype(jnp.bfloat16) for k in range(tiles)]
    share = model.shape[1] // (2 * places)

    def write(here):
        for device in range(2 * places):
            chip, other = divmod(device, 2 * fsdp)
            core, f = divmod(other, fsdp)
            out, place, row = outs[0 if core == here else 1], chip * fsdp + f, 0
            for part in turned:
                out[place, row : row + share, :] = part[device * share : (device + 1) * share]
                row += share
            for part in hidden:
                out[place, row : row + RANK, :] = part[:, device * lanes : (device + 1) * lanes]
                row += RANK

    for here in range(2):
        pl.when(core_ref[0] == here)(functools.partial(write, here))


def packs_whole(devices, width, hidden):
    return hidden // devices == TILE and width // devices % RANK == 0


def pack_grads_kernel(models, count, fsdp, *refs):
    core_ref, refs = refs[0], refs[1:]
    outs, sems, held = refs[count : count + 2], refs[count + 2], refs[count + 3 :]
    copies = [pltpu.make_async_copy(refs[i], held[i], sems.at[i]) for i in range(count)]
    for copy in copies:
        copy.start()
    for copy in copies:
        copy.wait()
    pack_step(outs, core_ref, fsdp, [ref[...] for ref in held[:models]], [ref[...] for ref in held[models:]])


def pack_grads(model, hidden):
    core = lax.axis_index("core").astype(jnp.int32).reshape(1)
    devices, fsdp = lax.axis_size(EVERYWHERE), lax.axis_size("fz") * lax.axis_size("fh")
    width = model[0].shape[1]
    share, hidden_share = width // devices, hidden[0].shape[1] // devices
    groups = sum(part.shape[0] for part in model)
    tiles = -(-groups // TILE)
    if packs_whole(devices, width, hidden[0].shape[1]):
        rows = tiles * share + RANK * len(hidden)
        return pl.pallas_call(
            functools.partial(pack_grads_kernel, len(model), len(model) + len(hidden), fsdp),
            in_specs=[SCALARS] + [HBM] * (len(model) + len(hidden)),
            out_specs=[VMEM_SPEC] * 2,
            out_shape=[jax.ShapeDtypeStruct((devices // 2, rows, TILE), jnp.bfloat16)] * 2,
            scratch_shapes=[pltpu.SemaphoreType.DMA((len(model) + len(hidden),))]
            + [pltpu.VMEM(item.shape, item.dtype) for item in (*model, *hidden)],
            compiler_params=pltpu.CompilerParams(vmem_limit_bytes=PACK_ROOM),
            name="pack_grads",
        )(core, *model, *hidden)
    rest = jnp.zeros((tiles * TILE - groups, width), jnp.bfloat16)
    turned = jnp.concatenate([*model, rest]).T
    split = jnp.concatenate(hidden).reshape(-1, devices, hidden_share)
    parts = [turned[:, k * TILE : (k + 1) * TILE].reshape(devices, share, TILE) for k in range(tiles)]
    parts.append(jnp.transpose(split, (1, 0, 2)).reshape(devices, -1, TILE))
    part = jnp.concatenate(parts, axis=1).reshape(devices // (2 * fsdp), 2, fsdp, -1, TILE)
    part = jnp.swapaxes(part, 0, 1).reshape(2, devices // 2, -1, TILE)
    return tuple(jnp.where(core[0] == 0, part, part[::-1]))


def send_grads(model, hidden):
    groups = sum(item.shape[0] for item in model)
    return send_packed(pack_grads(model, hidden), groups, len(hidden), model[0].shape[1], hidden[0].shape[1])


def send_packed(part, groups, hiddens, width, features):
    ours, theirs = part
    came = lax.ppermute(theirs, "core", [(0, 1), (1, 0)])
    both = (ours.astype(jnp.float32) + came.astype(jnp.float32)).astype(jnp.bfloat16)
    got = lax.all_to_all(both, ("chip", "fz", "fh"), 0, 0, tiled=True)
    devices = lax.axis_size(EVERYWHERE)
    share, hidden_share = width // devices, features // devices
    begin = -(-groups // TILE) * share
    if hidden_share == TILE:
        return got, got, begin
    return got, got[:, begin:].reshape(-1, RANK * hiddens, hidden_share), 0


def place_grads_kernel(batches, ids_ref, *refs):
    sent, outs = refs[: 2 * len(batches)], refs[2 * len(batches) :]
    for out in outs:
        out[...] = jnp.zeros_like(out)
    share = outs[0].shape[1]
    slot = lax.broadcasted_iota(jnp.int32, (share, TILE), 1) // RANK
    in_tile = TILE // RANK

    def one(sender, carry):
        owner = ids_ref[sender]
        at = pl.ds(pl.multiple_of(owner * RANK, RANK), RANK)
        for which, (model_plan, hidden_plan, begin) in enumerate(batches):
            model_ref, hidden_ref = sent[2 * which : 2 * which + 2]
            for group, (out, index) in enumerate(model_plan):
                tile, local_group = divmod(group, in_tile)
                block = model_ref[sender, tile * share : (tile + 1) * share, :].astype(jnp.float32)
                turn = lax.rem(owner - local_group + in_tile, in_tile) * RANK
                outs[out][index] += jnp.where(slot == owner, pltpu.roll(block, turn, 1), 0.0)
            for group, (out, index) in enumerate(hidden_plan):
                rows = slice(begin + group * RANK, begin + (group + 1) * RANK)
                outs[out][index, at, :] += hidden_ref[sender, rows, :].astype(jnp.float32)
        return carry

    lax.fori_loop(0, sent[0].shape[0], one, 0, unroll=4)


def place_grads(ids, batches, shapes):
    arrays, plans = [], []
    for (model, hidden, begin), model_plan, hidden_plan in batches:
        arrays += [model, hidden]
        plans.append((model_plan, hidden_plan, begin))
    return pl.pallas_call(
        functools.partial(place_grads_kernel, plans),
        in_specs=[SCALARS] + [VMEM_SPEC] * len(arrays),
        out_specs=[VMEM_SPEC] * len(shapes),
        out_shape=[jax.ShapeDtypeStruct(shape, jnp.float32) for shape in shapes],
        compiler_params=pltpu.CompilerParams(vmem_limit_bytes=16 * 1024 * 1024),
        name="place_grads",
    )(ids, *arrays)


def local(
    frames,
    cotangent,
    adapter_ids,
    norm_gains,
    norm_biases,
    rel_table,
    w_up,
    w_down,
    w_qkv,
    w_out,
    w_pw1,
    w_depth,
    w_pw2,
    ad_a_model,
    ad_a_hidden,
    ad_b_model,
    ad_b_hidden,
):
    group_clips, frame_span, width = frames.shape
    together = 2 * group_clips
    layout = Layout(together, lax.axis_size("fz") * lax.axis_size("fh"))
    rows = 2 * frame_span
    slots = ad_a_model.shape[2]
    spot = lax.axis_index("fh") * 2 + lax.axis_index("core")
    own = (spot * (rows // TILE)).astype(jnp.int32).reshape(1)
    other_ids = lax.ppermute(adapter_ids, "core", [(0, 1), (1, 0)])
    at_zero = lax.axis_index("core") == 0
    near_ids = jnp.concatenate(
        [jnp.where(at_zero, adapter_ids, other_ids), jnp.where(at_zero, other_ids, adapter_ids)]
    )
    factors = (ad_a_model, ad_a_hidden, ad_b_model, ad_b_hidden)
    cut = ad_a_hidden.shape[1] // ad_a_model.shape[1]
    first_pack = pack_adapters(near_ids, *[factor[:1] for factor in factors])
    other_pack = pack_adapters(near_ids, *[factor[1:] for factor in factors])
    gather = Gather()
    taps = jnp.pad(w_depth.T, ((0, 0), (0, width - KERNEL)))
    shards = [
        w_up[0],
        w_down[0],
        jnp.concatenate([w_qkv, w_out], axis=1),
        jnp.concatenate([w_pw1, w_pw2, taps], axis=1),
        w_up[1],
        w_down[1],
    ]
    used = [shard.shape[1] for shard in shards]
    used[3] = 3 * width + TILE
    turns = gather.stages(shards, used)
    next(turns)

    def weight_of(units, which, begin=0, columns=None):
        return Weight(gather.places, units[which], begin, columns or used[which])

    gains = [norm_gains[index : index + 1] for index in range(6)]
    biases = [norm_biases[index : index + 1] for index in range(6)]

    turns.send([first_pack, other_pack])
    first_pack, other_pack = gather.held
    turns.send([frames, first_pack, other_pack, *rel_tables(rel_table, rows * layout.group)])
    frames, first_pack, other_pack, *tables = gather.held
    layer_in = layout.gather_rows(frames)
    turns.send([])
    hidden_width = w_up.shape[2]
    first_four = first_adapters(layout, first_pack, cut, width, hidden_width)
    units = turns.send([layer_in, *first_four])
    layer_in, *first_four = gather.held
    field = layer_in.astype(jnp.float32)
    first_in = (norm_rows(field)[0] * gains[0] + biases[0]).astype(jnp.bfloat16)
    a_up0, b_down0 = [Rows(first_four[0], row * RANK, RANK) for row in range(2)]
    a_down0, b_up0 = [Rows(first_four[1], row * RANK, RANK) for row in range(2)]
    up0_w = weight_of(units, 0)
    z_up0, act_one, slope_one = project_wide("silu", first_in, up0_w, a_up0, b_up0)
    units = turns.send([act_one, slope_one, other_pack])
    act_one, slope_one, other_pack = gather.held
    others = other_adapters(layout, other_pack, cut, width, hidden_width)
    units = turns.send([])
    down0_w = weight_of(units, 1)
    z_down0, after_ffn, attn_in = project_narrow(
        act_one, down0_w, a_down0, b_down0, layer_in, gains[1], biases[1], 0.5
    )
    units = turns.send([after_ffn, attn_in, *others])
    after_ffn, attn_in, *others = gather.held
    model, inner, qkv_up, glu_up = others
    qkv_down = Rows(model, 0, 3 * RANK)
    qkv_up, glu_up = Rows(qkv_up, 0, 3 * RANK), Rows(glu_up, 0, RANK)
    a_out, a_pw1, a_pw2, a_up1, b_out, b_pw2, b_down1 = [
        Rows(model, row * RANK, RANK) for row in (3, 4, 5, 6, 10, 11, 12)
    ]
    a_down1, b_up1 = [Rows(inner, row * RANK, RANK) for row in range(2)]
    units = turns.send([])
    qkv_w, out_w = weight_of(units, 2, 0, 3 * width), weight_of(units, 2, 3 * width, width)
    z_qkv, query, own_kv = project_wide("plain", attn_in, qkv_w, qkv_down, qkv_up)
    units = turns.send([query, own_kv])
    query, own_kv = gather.held
    units = turns.send([])
    pw1_w, pw2_w = weight_of(units, 3, 0, 2 * width), weight_of(units, 3, 2 * width, width)
    taps = gather_taps(weight_of(units, 3, 3 * width, TILE))
    kv = [own_kv] + [layout.from_spot(own_kv, step, True) for step in range(1, layout.group)]
    mixed, rate, expo = attention_forward(own, query, kv, tables[0])
    turns.send([mixed, rate])
    mixed, rate = gather.held
    units = turns.send([])
    up1_w, down1_w = weight_of(units, 4), weight_of(units, 5)
    mixed, cotangent = lax.optimization_barrier((mixed, cotangent))
    d_out = layout.gather_rows(cotangent)
    z_out, after_attn, conv_in = project_narrow(
        mixed, out_w, a_out, b_out, after_ffn, gains[2], biases[2], 1.0
    )
    z_pw1, gated, gate, gate_slope = project_wide("glu", conv_in, pw1_w, a_pw1, glu_up)
    earlier = layout.from_spot(gated[rows - HALO :], -1, False)
    conv_out, conv_act = conv_forward(gated, earlier, taps, gains[3], biases[3])
    z_pw2, after_conv, second_in = project_narrow(
        conv_act, pw2_w, a_pw2, b_pw2, after_attn, gains[4], biases[4], 1.0
    )
    factors_two = dict(a_up=a_up1, b_up=b_up1, a_down=a_down1, b_down=b_down1)
    turn = [(lax.axis_index("fz") % 2).astype(jnp.int32).reshape(1)]
    z_up1, z_down1, d_fourth, *result, act_two, slope_two = feed_forward_last(
        second_in, up1_w, down1_w, factors_two, after_conv, gains[5], biases[5], d_out, turn
    )
    layer_out = layout.scatter_rows(result)

    d_third, da_up1, db_up1, da_down1, db_down1 = feed_forward_back(
        d_fourth, up1_w, down1_w, factors_two, (second_in, act_two, slope_two, z_up1, z_down1),
        after_conv, gains[4],
    )
    d_conv, da_pw2, db_pw2 = field_back(
        "conv", d_third, pw2_w, a_pw2, b_pw2, conv_act, z_pw2,
        (conv_out, gains[3], biases[3]),
    )
    d_conv, layer_out = lax.optimization_barrier((d_conv, layer_out))
    later = layout.from_spot(d_conv[:HALO].astype(jnp.bfloat16), 1, False)
    d_joined = conv_backward(d_conv, later, taps, gate, gate_slope)
    d_second, da_pw1, db_pw1 = field_back(
        "norm", d_joined, pw1_w, a_pw1, glu_up, conv_in, z_pw1, (d_third, after_attn, gains[2])
    )
    d_mixed, da_out, db_out = field_back(
        "plain", d_second, out_w, a_out, b_out, mixed, z_out, ()
    )
    label = jnp.full((RANK, width), near_ids[lax.axis_index("fz")]).astype(jnp.bfloat16)
    early = send_grads(
        [da_out, da_pw1, da_pw2, da_up1, db_out, db_pw2, db_down1]
        + [db_pw1[:, :width], db_pw1[:, width:], label],
        [da_down1, db_up1],
    )
    d_query, d_own, d_far = attention_backward(own, query, kv, d_mixed, rate, expo, tables)
    shares = [d_own]
    for step in range(1, layout.group):
        shares.append(layout.from_spot(d_far[:, (step - 1) * rows : step * rows], -step, True))
    first_half, second_half_rows, *grads = first_half_back(
        d_query, shares, qkv_w, qkv_down, qkv_up, attn_in, z_qkv, d_second, after_ffn, gains[1],
        up0_w, down0_w, dict(a_up=a_up0, b_up=b_up0, a_down=a_down0, b_down=b_down0),
        (first_in, act_one, slope_one, z_up0, z_down0), layer_in, gains[0],
        [*turn, lax.axis_index("core").astype(jnp.int32).reshape(1)],
    )
    grad_frames = layout.scatter_rows([first_half, second_half_rows])
    if len(grads) == 2:
        late = send_packed(grads, 8 * RANK, 2, width, hidden_width)
    else:
        da_up0, db_up0, da_down0, db_down0, da_qkv, db_qkv = grads
        db_three = [
            db_qkv[index * RANK : (index + 1) * RANK, index * width : (index + 1) * width]
            for index in range(3)
        ]
        late = send_grads([da_up0, da_qkv, db_down0, *db_three], [da_down0, db_up0])
    devices = lax.axis_size(EVERYWHERE)
    share, hidden_share = width // devices, hidden_width // devices
    ids = (early[0][:, share, RANK] * jnp.bfloat16(0.5)).astype(jnp.int32)
    early_plan = [(0, index) for index in range(4, 8)] + [(1, index) for index in range(4, 9)]
    late_plan = [(0, index) for index in range(4)] + [(1, index) for index in range(4)]
    grad_a_model, grad_b_model, grad_a_hidden, grad_b_hidden = place_grads(
        ids,
        [(early, early_plan, [(2, 1), (3, 1)]), (late, late_plan, [(2, 0), (3, 0)])],
        [(8, share, slots), (9, share, slots), (2, slots, hidden_share), (2, slots, hidden_share)],
    )
    grad_b_model = jnp.swapaxes(grad_b_model, 1, 2)
    grad_a_hidden = jnp.swapaxes(grad_a_hidden, 1, 2)
    return (layer_out, grad_frames, grad_a_model, grad_a_hidden, grad_b_model, grad_b_hidden)


def solution(mesh):
    every = ("chip", "core", "fz", "fh")
    clips, spread = ("chip", "core"), ("fz", "fh")
    in_specs = (
        P(clips, spread, None),
        P(clips, spread, None),
        P(clips),
        P(),
        P(),
        P(),
        P(None, every, None),
        P(None, every, None),
        P(every, None),
        P(every, None),
        P(every, None),
        P(None, every),
        P(every, None),
        P(None, spread, None),
        P(None, spread, None),
        P(None, None, spread),
        P(None, None, spread),
    )
    out_specs = (
        P(clips, spread, None),
        P(clips, spread, None),
        P(None, every, None),
        P(None, every, None),
        P(None, None, every),
        P(None, None, every),
    )

    def run(frames, *rest):
        dp, fsdp = mesh.shape["dp"], mesh.shape["fsdp"]
        together = 2 * frames.shape[0] // dp
        cut = Mesh(
            mesh.devices.reshape(dp // 2, 2, together, fsdp // together), EVERYWHERE
        )
        return jax.shard_map(
            local, mesh=cut, in_specs=in_specs, out_specs=out_specs, check_vma=False
        )(frames, *rest)

    return run
```

```python
import functools
import math

import jax
import jax.numpy as jnp
from jax import lax
from jax.experimental import pallas as pl
from jax.experimental.pallas import tpu as pltpu
from jax.sharding import Mesh
from jax.sharding import PartitionSpec as P

HEADS = 16
KERNEL = 31
RANK = 16
EPSILON = 1e-05
PACK_ROOM = 56 * 1024 * 1024
EVERYWHERE = ("chip", "core", "fz", "fh")

HD = 64
REL_LEFT = 64
REL_RIGHT = 8
TILE = 128
WIDE = 3 * TILE
VMEM = 32 * 1024 * 1024


def dot_nn(a, b):
    return lax.dot_general(a, b, (((1,), (0,)), ((), ())), preferred_element_type=jnp.float32)


def dot_nt(a, b):
    return lax.dot_general(a, b, (((1,), (1,)), ((), ())), preferred_element_type=jnp.float32)


def chunk_plan(tile, chunks):
    return [{chunks - 1: 0, 0: 1, 1: 2}.get((c - tile) % chunks) for c in range(chunks)]


def far_left(c, tile, chunks, own):
    return jnp.logical_or(c + own >= chunks, c < tile)


def wrapped_band(c, tile, chunks, own):
    if tile == 0 and c == chunks - 1:
        return own > 0
    if c == tile + 1:
        return c + own < chunks
    return None


def tile_scores(scores, table, tile, own):
    near = pltpu.roll(table[:, :TILE], TILE // 2, 1, stride=1, stride_axis=0)
    first, last = table[:, TILE : 2 * TILE], table[:, 2 * TILE :]
    ahead = lane_ahead()
    bands = [
        jnp.where(ahead >= TILE // 2, near, first),
        jnp.where(ahead < -(TILE // 2), first, jnp.where(ahead >= TILE // 2, last, near)),
        jnp.where(ahead < -(TILE // 2), near, last),
    ]
    chunks = scores.shape[1] // TILE
    parts = []
    for c, spot in enumerate(chunk_plan(tile, chunks)):
        part = scores[:, c * TILE : (c + 1) * TILE]
        if spot is None:
            bias = first if c < tile else jnp.where(c + own >= chunks, first, last)
        else:
            bias = bands[spot]
            true_band = wrapped_band(c, tile, chunks, own)
            if true_band is not None:
                bias = jnp.where(true_band, bias, jnp.where(far_left(c, tile, chunks, own), first, last))
        parts.append(part + bias)
    return parts


def lane_ahead():
    lane = lax.broadcasted_iota(jnp.int32, (TILE, TILE), 1)
    return lane - lax.broadcasted_iota(jnp.int32, (TILE, TILE), 0)


def stacked(refs):
    return jnp.concatenate([ref[...] for ref in refs], axis=0)


def head_lanes(rows):
    low = lax.broadcasted_iota(jnp.int32, (rows, 2 * HD), 1) < HD
    return low, (low, jnp.logical_not(low))


def row_tiles(rows):
    return [(tile, slice(tile * TILE, (tile + 1) * TILE)) for tile in range(rows // TILE)]


def attn_fwd_kernel(group, own_ref, q_ref, rel_ref, *refs):
    own = own_ref[0]
    keys, values, rel_wide = stacked(refs[:group]), stacked(refs[group : 2 * group]), rel_ref[...]
    o_ref, rate_ref, p_ref, s_ref, w_ref = refs[2 * group :]
    rows_n = q_ref.shape[0]
    low, heads = head_lanes(rows_n)
    q_pair = q_ref[...] * jnp.bfloat16(0.125)
    for head, lanes in enumerate(heads):
        q_head = jnp.where(lanes, q_pair, jnp.zeros_like(q_pair))
        s_ref[head] = dot_nt(q_head, keys)
        w_ref[head] = dot_nt(q_head, rel_wide)
    ones = jnp.ones_like(values)
    values_ones = jnp.concatenate([values, ones], axis=1)
    outs = []
    for head in range(2):
        for tile, rows in row_tiles(rows_n):
            parts = tile_scores(s_ref[head, rows, :], w_ref[head, rows, :], tile, own)
            top = jnp.max(functools.reduce(jnp.maximum, parts), axis=1, keepdims=True)
            top = jnp.broadcast_to(top, (TILE, TILE))
            expo = [jnp.exp(part - top).astype(jnp.bfloat16) for part in parts]
            p_ref[head, rows, :] = jnp.concatenate(expo, axis=1)
        outs.append(dot_nn(p_ref[head], values_ones))
        total = outs[head][:, 2 * HD :]
        rate_ref[:, head * TILE : (head + 1) * TILE] = 1.0 / total
        outs[head] = outs[head][:, : 2 * HD] / total
    o_ref[...] = jnp.where(low, outs[0], outs[1]).astype(jnp.bfloat16)


def attn_bwd_kernel(group, own_ref, q_ref, do_ref, rate_ref, e_ref, rev_ref, flip_ref, mark_ref, *refs):
    own = own_ref[0]
    keys, values = stacked(refs[:group]), stacked(refs[group : 2 * group])
    dq_ref, own_out, far_out, dp_ref, ds_ref, p_ref, band_ref = refs[2 * group :]
    rows_n, keys_n = q_ref.shape[0], keys.shape[0]
    chunks = keys_n // TILE
    low, heads = head_lanes(rows_n)
    lane = lax.broadcasted_iota(jnp.int32, (1, TILE), 1)
    q_pair = q_ref[...] * jnp.bfloat16(0.125)
    do_pair = do_ref[...]
    keys_marked = jnp.concatenate([keys, mark_ref[...]], axis=1)
    for head, lanes in enumerate(heads):
        dp_ref[head] = dot_nt(jnp.where(lanes, do_pair, jnp.zeros_like(do_pair)), values)
    dqs = []
    ahead = lane_ahead()
    for head in range(2):
        edges = []
        for tile, rows in row_tiles(rows_n):
            rate = rate_ref[rows, head * TILE : (head + 1) * TILE]
            parts = [e_ref[head, rows, c * TILE : (c + 1) * TILE] for c in range(chunks)]
            probs = [part.astype(jnp.float32) * rate for part in parts]
            d_parts = [dp_ref[head, rows, c * TILE : (c + 1) * TILE] for c in range(chunks)]
            inner = functools.reduce(jnp.add, [p * d for p, d in zip(probs, d_parts)])
            inner = jnp.sum(inner, axis=1, keepdims=True)
            d_scores = [(p * (d - inner)).astype(jnp.bfloat16) for p, d in zip(probs, d_parts)]
            p_ref[head, rows, :] = jnp.concatenate([p.astype(jnp.bfloat16) for p in probs], axis=1)
            ds_ref[head, rows, :] = jnp.concatenate(d_scores, axis=1)
            band = [None, None, None]
            for c, spot in enumerate(chunk_plan(tile, chunks)):
                if spot is not None:
                    near = wrapped_band(c, tile, chunks, own)
                    piece = d_scores[c]
                    band[spot] = piece if near is None else jnp.where(near, piece, jnp.zeros_like(piece))
            behind, beyond = ahead < -(TILE // 2), ahead >= TILE // 2
            none = jnp.zeros_like(band[0])
            band_ref[head, rows, :] = jnp.where(beyond, band[0], jnp.where(behind, band[2], band[1]))
            sides = (
                (jnp.where(beyond, none, band[0]), jnp.where(behind, band[1], none)),
                (jnp.where(behind, none, band[2]), jnp.where(beyond, band[1], none)),
            )
            edges.append([a.astype(jnp.float32) + b.astype(jnp.float32) for a, b in sides])
        turned = dot_nn(band_ref[head], flip_ref[...])
        turned = jnp.concatenate(
            [
                pltpu.roll(turned[rows, :], TILE // 2, 1, stride=1, stride_axis=0).astype(jnp.bfloat16)
                for _, rows in row_tiles(rows_n)
            ],
            axis=0,
        )
        marked = dot_nn(ds_ref[head], keys_marked)
        near_part = dot_nn(turned, rev_ref[...])
        outs = []
        for tile, rows in row_tiles(rows_n):
            weights = [jnp.zeros((1, TILE), jnp.float32)] * 2
            for c, spot in enumerate(chunk_plan(tile, chunks)):
                near = wrapped_band(c, tile, chunks, own)
                if spot is not None and near is None:
                    continue
                left = far_left(c, tile, chunks, own)
                far = 1.0 if spot is None else jnp.where(near, 0.0, 1.0)
                for side, on in enumerate((left, jnp.logical_not(left))):
                    here = jnp.where(on, far, 0.0)
                    weights[side] = weights[side] + jnp.where(lane == c, here, 0.0)
            sums = marked[rows, TILE:]
            before, after = [
                jnp.sum(sums * weight + edge, axis=1, keepdims=True)
                for weight, edge in zip(weights, edges[tile])
            ]
            d_query = marked[rows, :TILE] + near_part[rows, :]
            d_query = d_query + before * rev_ref[TILE - 1 : TILE, :].astype(jnp.float32)
            d_query = d_query + after * rev_ref[0:1, :].astype(jnp.float32)
            outs.append(d_query * 0.125)
        dqs.append(outs)
    for tile, rows in row_tiles(rows_n):
        dq_ref[rows, :] = jnp.where(low[rows, :], dqs[0][tile], dqs[1][tile]).astype(dq_ref.dtype)
    q_turned = jnp.transpose(q_pair)
    do_turned = jnp.transpose(do_pair)
    for which, (turned, kept) in enumerate(((q_turned, ds_ref), (do_turned, p_ref))):
        both = jnp.concatenate(
            [dot_nn(turned[head * HD : (head + 1) * HD, :], kept[head]) for head in range(2)], axis=0
        )
        both = jnp.transpose(both)
        own_out[which] = both[:rows_n].astype(own_out.dtype)
        far_out[which] = both[rows_n:].astype(far_out.dtype)


def rel_tables(rel_table, keys_n):
    count = rel_table.shape[0]
    rows = jnp.concatenate([rel_table, jnp.broadcast_to(rel_table[-1:], (TILE - count, HD))])
    rows = jnp.concatenate([rows, rows], axis=1)
    wide = jnp.concatenate(
        [rows, jnp.broadcast_to(rows[:1], rows.shape), jnp.broadcast_to(rows[-1:], rows.shape)]
    )
    flip = jnp.arange(TILE)[:, None] + jnp.arange(TILE)[None, :] == TILE - 1
    marks = jnp.arange(keys_n)[:, None] // TILE == jnp.arange(TILE)[None, :]
    return wide, rows[::-1], flip.astype(jnp.bfloat16), marks.astype(jnp.bfloat16)


def pair_blocks(rows, width, group):
    pairs = width // (2 * HD)
    one = pl.BlockSpec((rows, 2 * HD), lambda h: (0, h))
    two = pl.BlockSpec((rows, 2 * HD), lambda h: (0, pairs + h))
    return pairs, one, [one] * group + [two] * group


def fixed(array):
    return pl.BlockSpec(array.shape, lambda h: (0, 0))


def attention_forward(own, query, kv, rel_wide):
    rows, width = query.shape
    pairs, block, kv_blocks = pair_blocks(rows, width, len(kv))
    size = rows * rows * len(kv) * width
    return pl.pallas_call(
        functools.partial(attn_fwd_kernel, len(kv)),
        grid=(pairs,),
        in_specs=[pl.BlockSpec(memory_space=pltpu.SMEM), block, fixed(rel_wide)] + kv_blocks,
        out_specs=[
            block,
            pl.BlockSpec((rows, 2 * TILE), lambda h: (0, h)),
            pl.BlockSpec((2, rows, rows * len(kv)), lambda h: (h, 0, 0)),
        ],
        out_shape=[
            jax.ShapeDtypeStruct((rows, width), jnp.bfloat16),
            jax.ShapeDtypeStruct((rows, width // HD * TILE), jnp.float32),
            jax.ShapeDtypeStruct((width // HD, rows, rows * len(kv)), jnp.bfloat16),
        ],
        scratch_shapes=[
            pltpu.VMEM((2, rows, rows * len(kv)), jnp.float32),
            pltpu.VMEM((2, rows, WIDE), jnp.float32),
        ],
        compiler_params=pltpu.CompilerParams(vmem_limit_bytes=VMEM),
        cost_estimate=pl.CostEstimate(flops=12 * size, bytes_accessed=rows * width * 16, transcendentals=0),
        name="attention_forward",
    )(own, query, rel_wide, *kv, *kv)


def attention_backward(own, query, kv, d_out, rate, expo, tables):
    rows, width = query.shape
    keys_n = rows * len(kv)
    pairs, block, kv_blocks = pair_blocks(rows, width, len(kv))
    size = rows * keys_n * width
    return pl.pallas_call(
        functools.partial(attn_bwd_kernel, len(kv)),
        grid=(pairs,),
        in_specs=[pl.BlockSpec(memory_space=pltpu.SMEM), block, block]
        + [pl.BlockSpec((rows, 2 * TILE), lambda h: (0, h))]
        + [pl.BlockSpec((2, rows, keys_n), lambda h: (h, 0, 0))]
        + [fixed(table) for table in tables[1:]]
        + kv_blocks,
        out_specs=[
            block,
            pl.BlockSpec((2, rows, 2 * HD), lambda h: (0, 0, h)),
            pl.BlockSpec((2, keys_n - rows, 2 * HD), lambda h: (0, 0, h)),
        ],
        out_shape=[
            jax.ShapeDtypeStruct((rows, width), jnp.bfloat16),
            jax.ShapeDtypeStruct((2, rows, width), jnp.bfloat16),
            jax.ShapeDtypeStruct((2, keys_n - rows, width), jnp.bfloat16),
        ],
        scratch_shapes=[
            pltpu.VMEM((2, rows, keys_n), jnp.float32),
            pltpu.VMEM((2, rows, keys_n), jnp.bfloat16),
            pltpu.VMEM((2, rows, keys_n), jnp.bfloat16),
            pltpu.VMEM((2, rows, TILE), jnp.bfloat16),
        ],
        compiler_params=pltpu.CompilerParams(vmem_limit_bytes=3 * VMEM // 4),
        cost_estimate=pl.CostEstimate(flops=24 * size, bytes_accessed=rows * width * 32, transcendentals=0),
        name="attention_backward",
    )(own, query, d_out, rate, expo, *tables[1:], *kv, *kv)


class Gather:
    def __init__(self):
        self.chips = lax.axis_size("chip")
        side = math.isqrt(self.chips)
        self.first, self.second = (side, side) if side * side == self.chips else (self.chips, 1)
        chip, core = lax.axis_index("chip"), lax.axis_index("core")
        places = []
        for owner in (core, 1 - core):
            for early, late in self.steps():
                one = self.moved(chip, early, late)
                two = self.moved(chip, late, early)
                places.append(jnp.where(owner == 0, one, two) * 2 + owner)
        self.places = jnp.stack(places).astype(jnp.int32)

    def steps(self):
        steps = [(early, 0) for early in range(self.first)]
        steps += [(0, late) for late in range(1, self.second)]
        return steps + [(e, l) for l in range(1, self.second) for e in range(1, self.first)]

    def moved(self, chip, along_first, along_second):
        return chip ^ (along_first * self.second + along_second)

    def hop(self, block, early, late):
        route = []
        for chip in range(self.chips):
            route.append((self.moved(chip, early, late) * 2, chip * 2))
            route.append((self.moved(chip, late, early) * 2 + 1, chip * 2 + 1))
        return lax.ppermute(block, ("chip", "core"), route)

    def stages(self, shards, used):
        swap = lambda block: lax.ppermute(block, "core", [(0, 1), (1, 0)])
        collect = lambda shard: lax.all_gather(shard, ("fz", "fh"), axis=0, tiled=True)
        count = len(shards)
        shards = list(shards)
        blocks = [collect(shard) for shard in shards[:3]]
        kept, traded, last = [[] for _ in shards], [[] for _ in shards], []
        complete, ahead = 0, self.first + self.second - 1
        for turn in range(count + 1):
            onward = kept[turn - 1][1 : self.first] if turn else []
            if turn > 1:
                late, due = kept[turn - 2][ahead if turn == count else 0 :], blocks[turn : turn + 1] if turn > 2 else []
                self.held = yield [kept[which] + traded[which] for which in range(complete)]
                (onward, late, due), last, self.held = lax.optimization_barrier(
                    ((onward, late, due), last, list(self.held))
                )
                if due:
                    blocks[turn] = due[0]
                further = [self.hop(block, 0, step) for step in range(1, self.second) for block in onward]
                kept[turn - 1] = kept[turn - 1] + further
                across = [swap(block) for block in late]
                traded[turn - 2] = traded[turn - 2] + across
                last = further + across
                complete += 1
            self.held = yield [kept[which] + traded[which] for which in range(complete)]
            if turn < count:
                fresh = blocks[turn][:, : used[turn]]
                coming = shards[turn + 3 : turn + 4]
                late = kept[turn - 1][:ahead] if turn == count - 1 else []
                (fresh, onward, coming, late), last, self.held = lax.optimization_barrier(
                    ((fresh, onward, coming, late), last, list(self.held))
                )
                blocks += [collect(shard) for shard in coming]
                early = [self.hop(fresh, step, 0) for step in range(1, self.first)]
                other = [self.hop(fresh, 0, step) for step in range(1, self.second)]
                kept[turn] = [fresh] + early + other
                traded[turn - 1] = traded[turn - 1] + [swap(block) for block in late]
                last = early + other + (traded[turn - 1] if late else [])
                if turn == 1:
                    further = [self.hop(block, 0, step) for step in range(1, self.second) for block in onward]
                    kept[0] = kept[0] + further
                    last = last + further
            else:
                late, last, self.held = lax.optimization_barrier((kept[-1], last, list(self.held)))
                traded[-1] = [swap(block) for block in late]
        yield [own + other for own, other in zip(kept, traded)]


HBM = pl.BlockSpec(memory_space=pltpu.HBM)
SCALARS = pl.BlockSpec(memory_space=pltpu.SMEM)
VMEM_SPEC = pl.BlockSpec(memory_space=pltpu.VMEM)
TALL = 512
HALO = 32
MIB = 1024 * 1024


def dot_tn(a, b):
    return lax.dot_general(a, b, (((0,), (0,)), ((), ())), preferred_element_type=jnp.float32)


def norm_rows(field):
    centred = field - jnp.mean(field, -1, keepdims=True)
    rate = lax.rsqrt(jnp.mean(centred * centred, -1, keepdims=True) + EPSILON)
    return centred * rate, rate


def norm_back(grad, gain, normed, rate):
    scaled = grad * gain
    inner = jnp.mean(scaled * normed, -1, keepdims=True)
    return (scaled - jnp.mean(scaled, -1, keepdims=True) - normed * inner) * rate


def each_rows(rows, step, body):
    for begin in range(0, rows, step):
        body(slice(begin, begin + step))


def shape_of(rows, width, dtype=jnp.bfloat16):
    return jax.ShapeDtypeStruct((rows, width), dtype)


class Weight:
    def __init__(self, places, pieces, begin, width):
        self.places, self.pieces, self.begin, self.width = places, pieces, begin, width
        self.count, self.block = len(pieces), pieces[0].shape[0]
        self.depth = self.count * self.block
        self.bytes = 2 * self.depth * width


class Load:
    def __init__(self, weight, places_ref, pieces, store, sems):
        self.store, self.copies = store, []
        for index, piece in enumerate(pieces):
            row = pl.multiple_of(places_ref[index] * weight.block, weight.block)
            self.copies.append(
                pltpu.make_async_copy(
                    piece.at[:, pl.ds(weight.begin, weight.width)],
                    store.at[pl.ds(row, weight.block), :],
                    sems.at[index],
                )
            )

    def start(self):
        for copy in self.copies:
            copy.start()

    def wait(self):
        for copy in self.copies:
            copy.wait()


class Rows:
    def __init__(self, array, begin, count):
        self.array, self.begin, self.count = array, begin, count


class Factor:
    def __init__(self, ref, rows):
        self.ref, self.at = ref, slice(rows.begin, rows.begin + rows.count)

    def all(self):
        return self.ref[self.at, :]

    def columns(self, at):
        return self.ref[self.at, at]


class Refs:
    pass


def fused(body, name, limit, weights, factors, near, far, outs, far_outs=(), scratch=(), turn=()):
    arrays = []
    for rows in factors.values():
        if not any(rows.array is array for array in arrays):
            arrays.append(rows.array)
    far, far_outs, scratch = dict(far), dict(far_outs), dict(scratch)
    places = [weight.places for weight in list(weights.values())[:1]]
    pieces = [piece for weight in weights.values() for piece in weight.pieces]

    def kernel(*refs):
        refs = list(refs)
        take = lambda count: [refs.pop(0) for _ in range(count)]
        r = Refs()
        places_ref = take(len(places))
        blocks = [take(weight.count) for weight in weights.values()]
        factor_refs, turn_ref = take(len(arrays)), take(len(turn))
        r.turn, r.core = (turn_ref + [None, None])[:2]
        for names in (near, far, outs, far_outs):
            for key, ref in zip(names, take(len(names))):
                setattr(r, key, ref)
        for (key, weight), block in zip(weights.items(), blocks):
            setattr(r, key, Load(weight, places_ref[0], block, *take(2)))
        for key, rows in factors.items():
            (which,) = [i for i, array in enumerate(arrays) if array is rows.array]
            setattr(r, key, Factor(factor_refs[which], rows))
        for key, ref in zip(scratch, take(len(scratch))):
            setattr(r, key, ref)
        body(r)

    total = sum(weight.bytes for weight in weights.values())
    everything = [*near.values(), *far.values(), *outs.values(), *far_outs.values()]
    moved = sum(math.prod(item.shape) * item.dtype.itemsize for item in everything)
    rows = list(near.values())[0].shape[0] if near else 0
    stores = []
    for weight in weights.values():
        stores.append(pltpu.VMEM((weight.depth, weight.width), jnp.bfloat16))
        stores.append(pltpu.SemaphoreType.DMA((weight.count,)))
    made = pl.pallas_call(
        kernel,
        in_specs=[SCALARS] * len(places)
        + [HBM] * len(pieces)
        + [VMEM_SPEC] * len(arrays)
        + [SCALARS] * len(turn)
        + [VMEM_SPEC] * len(near)
        + [HBM] * len(far),
        out_specs=[VMEM_SPEC] * len(outs) + [HBM] * len(far_outs),
        out_shape=[*outs.values(), *far_outs.values()],
        scratch_shapes=stores + list(scratch.values()),
        compiler_params=pltpu.CompilerParams(vmem_limit_bytes=total + limit * MIB),
        cost_estimate=pl.CostEstimate(flops=rows * total, bytes_accessed=moved + total, transcendentals=0),
        name=name,
    )(*places, *pieces, *arrays, *turn, *near.values(), *far.values())
    return made


def wide_step(kind, load, u_ref, down, up, z_ref, outs, then=None):
    z_ref[...] = dot_nt(u_ref[...], down.all()).astype(jnp.bfloat16)
    load.wait()
    if then:
        then()
    width = load.store.shape[1]
    out_width = width // 2 if kind == "glu" else width
    for begin in range(0, out_width, TALL):
        at = slice(begin, begin + TALL)
        parts = [slice(base + begin, base + begin + TALL) for base in range(0, width, out_width)]
        result = [
            dot_nn(u_ref[...], load.store[:, part]) + dot_nn(z_ref[...], up.columns(part)) for part in parts
        ]
        if kind == "silu":
            gate = jax.nn.sigmoid(result[0])
            active = result[0] * gate
            outs[0][:, at] = active.astype(jnp.bfloat16)
            outs[1][:, at] = (gate + active * (1.0 - gate)).astype(jnp.bfloat16)
        elif kind == "glu":
            gate = jax.nn.sigmoid(result[1])
            gated = result[0] * gate
            outs[0][:, at] = gated.astype(jnp.bfloat16)
            outs[1][:, at] = gate.astype(jnp.bfloat16)
            outs[2][:, at] = (gated * (1.0 - gate)).astype(jnp.bfloat16)
        else:
            which = min(begin // outs[0].shape[1], 1)
            first = which * outs[0].shape[1]
            outs[which][:, begin - first : begin - first + TALL] = result[0].astype(jnp.bfloat16)


def narrow_step(factor, load, u_ref, down, up, z_ref, field_ref, field_out, then=None):
    z_ref[...] = dot_nt(u_ref[...], down.all()).astype(jnp.bfloat16)
    load.wait()
    if then:
        then()
    for begin in range(0, load.store.shape[1], TALL):
        at = slice(begin, begin + TALL)
        result = dot_nn(u_ref[...], load.store[:, at]) + dot_nn(z_ref[...], up.columns(at))
        field_out[:, at] = field_ref[:, at].astype(jnp.float32) + factor * result


def norm_step(field_ref, gain_ref, bias_ref, out_ref):
    def finish(at):
        normed = norm_rows(field_ref[at, :])[0] * gain_ref[...] + bias_ref[...]
        out_ref[at, :] = normed.astype(jnp.bfloat16)

    each_rows(field_ref.shape[0], 128, finish)


def grads_step(grad, up, z_ref, u_ref, dz, da_ref, db_ref):
    dz[...] = dot_nt(grad[...], up.all()).astype(jnp.bfloat16)
    db_ref[...] = dot_tn(z_ref[...], grad[...]).astype(jnp.bfloat16)
    da_ref[...] = dot_tn(dz[...], u_ref[...]).astype(jnp.bfloat16)


def inputs_step(load, grad, dz, down, out_ref, then=None):
    load.wait()
    if then:
        then()
    for begin in range(0, load.store.shape[0], TALL):
        at = slice(begin, begin + TALL)
        result = dot_nt(grad[...], load.store[at, :]) + dot_nn(dz[...], down.columns(at))
        out_ref[:, at] = result.astype(out_ref.dtype)


def norm_back_step(d_inputs, field_ref, gain_ref, prior_ref, out_ref):
    def finish(at):
        normed, rate = norm_rows(field_ref[at, :].astype(jnp.float32))
        out_ref[at, :] = prior_ref[at, :] + norm_back(d_inputs[at, :], gain_ref[...], normed, rate)

    each_rows(field_ref.shape[0], 128, finish)


def halves_step(turn_ref, first_out, second_out, rows_of):
    half = first_out.shape[0]
    step = half // 2
    for begin in range(0, 2 * half, step):
        made = rows_of(slice(begin, begin + step)).astype(first_out.dtype)
        at = slice(begin % half, begin % half + step)
        for out, turn in ((first_out, begin // half), (second_out, 1 - begin // half)):

            @pl.when(turn_ref[0] == turn)
            def _(out=out):
                out[at, :] = made


def project_wide(kind, inputs, weight, a, b):
    rows, width = inputs.shape[0], weight.width
    sizes = dict(silu=[width] * 2, glu=[width // 2] * 3, plain=[width // 3, width - width // 3])[kind]
    names = ["out%d" % index for index in range(len(sizes))]

    def body(r):
        r.weight.start()
        wide_step(kind, r.weight, r.u, r.a, r.b, r.z, [getattr(r, key) for key in names])

    outs = dict(z=shape_of(rows, a.count), **{key: shape_of(rows, size) for key, size in zip(names, sizes)})
    return fused(body, "project_" + kind, 14, dict(weight=weight), dict(a=a, b=b), dict(u=inputs), {}, outs)


def project_narrow(inputs, weight, a, b, field, gain, bias, factor):
    rows, width = inputs.shape[0], weight.width

    def body(r):
        r.weight.start()
        narrow_step(factor, r.weight, r.u, r.a, r.b, r.z, r.field, r.made)
        norm_step(r.made, r.gain, r.bias, r.normed)

    outs = dict(
        z=shape_of(rows, a.count), made=shape_of(rows, width, jnp.float32),
        normed=shape_of(rows, width),
    )
    near = dict(u=inputs, field=field, gain=gain, bias=bias)
    return fused(body, "project_next", 14, dict(weight=weight), dict(a=a, b=b), near, {}, outs)


def feed_forward_last(inputs, up, down, factors, field, gain, bias, cotangent, turn):
    rows, width = inputs.shape
    rank, hidden = factors["a_up"].count, up.width

    def body(r):
        r.up.start()
        wide_step("silu", r.up, r.u, r.a_up, r.b_up, r.z_up, (r.held_act, r.held_slope), r.down.start)
        leaving = [
            pltpu.make_async_copy(r.held_act, r.act, r.sems.at[0]),
            pltpu.make_async_copy(r.held_slope, r.slope, r.sems.at[1]),
        ]
        for copy in leaving:
            copy.start()
        narrow_step(0.5, r.down, r.held_act, r.a_down, r.b_down, r.z_down, r.field, r.d_out)
        gain, bias = r.gain[...], r.bias[...]

        def finish(at):
            normed, rate = norm_rows(r.d_out[at, :])
            r.d_out[at, :] = norm_back(r.cot[at, :].astype(jnp.float32), gain, normed, rate)
            return normed * gain + bias

        halves_step(r.turn, r.first, r.second, finish)
        for copy in leaving:
            copy.wait()

    outs = dict(
        z_up=shape_of(rows, rank), z_down=shape_of(rows, rank),
        d_out=shape_of(rows, width, jnp.float32), first=shape_of(rows // 2, width),
        second=shape_of(rows // 2, width),
    )
    near = dict(u=inputs, field=field, gain=gain, bias=bias, cot=cotangent)
    return fused(
        body, "feed_forward_last", 30, dict(up=up, down=down), factors, near, {}, outs,
        dict(act=shape_of(rows, hidden), slope=shape_of(rows, hidden)),
        dict(
            held_act=pltpu.VMEM((rows, hidden), jnp.bfloat16),
            held_slope=pltpu.VMEM((rows, hidden), jnp.bfloat16),
            sems=pltpu.SemaphoreType.DMA((2,)),
        ),
        turn,
    )


def ffn_back_steps(r, d_ref, u_ref):
    r.half[...] = (0.5 * d_ref[...]).astype(jnp.bfloat16)
    r.dz_down[...] = dot_nt(r.half[...], r.b_down.all()).astype(jnp.bfloat16)
    r.db_down[...] = dot_tn(r.z_down[...], r.half[...]).astype(jnp.bfloat16)
    r.down.wait()
    pltpu.make_async_copy(r.slope, r.held_slope, r.sems.at[0]).wait()
    act_copy = pltpu.make_async_copy(r.act, r.held_act, r.sems.at[1])
    act_copy.start()
    r.up.start()
    for begin in range(0, r.down.store.shape[0], TALL):
        at = slice(begin, begin + TALL)
        result = dot_nt(r.half[...], r.down.store[at, :]) + dot_nn(r.dz_down[...], r.a_down.columns(at))
        r.d_hidden[:, at] = (result * r.held_slope[:, at].astype(jnp.float32)).astype(jnp.bfloat16)
    r.dz_up[...] = dot_nt(r.d_hidden[...], r.b_up.all()).astype(jnp.bfloat16)
    act_copy.wait()
    r.da_down[...] = dot_tn(r.dz_down[...], r.held_act[...]).astype(jnp.bfloat16)
    inputs_step(r.up, r.d_hidden, r.dz_up, r.a_up, r.d_inputs)
    r.db_up[...] = dot_tn(r.z_up[...], r.d_hidden[...]).astype(jnp.bfloat16)
    r.da_up[...] = dot_tn(r.dz_up[...], u_ref[...]).astype(jnp.bfloat16)


def ffn_back_parts(rows, width, hidden, rank):
    outs = dict(
        da_up=shape_of(rank, width), db_up=shape_of(rank, hidden),
        da_down=shape_of(rank, hidden), db_down=shape_of(rank, width),
    )
    scratch = dict(
        half=pltpu.VMEM((rows, width), jnp.bfloat16),
        dz_down=pltpu.VMEM((rows, rank), jnp.bfloat16),
        dz_up=pltpu.VMEM((rows, rank), jnp.bfloat16),
        d_hidden=pltpu.VMEM((rows, hidden), jnp.bfloat16),
        d_inputs=pltpu.VMEM((rows, width), jnp.float32),
        held_act=pltpu.VMEM((rows, hidden), jnp.bfloat16),
        held_slope=pltpu.VMEM((rows, hidden), jnp.bfloat16),
        sems=pltpu.SemaphoreType.DMA((2,)),
    )
    return outs, scratch


def feed_forward_back(d_field, up, down, factors, kept, field, gain):
    rows, width = d_field.shape
    inputs, act, slope, z_up, z_down = kept

    def body(r):
        r.down.start()
        pltpu.make_async_copy(r.slope, r.held_slope, r.sems.at[0]).start()
        ffn_back_steps(r, r.d_field, r.u)
        norm_back_step(r.d_inputs, r.field, r.gain, r.d_field, r.made)

    outs, scratch = ffn_back_parts(rows, width, up.width, factors["a_up"].count)
    outs = dict(made=shape_of(rows, width, jnp.float32), **outs)
    near = dict(d_field=d_field, u=inputs, z_up=z_up, z_down=z_down, field=field, gain=gain)
    return fused(
        body, "feed_forward_back", 41, dict(down=down, up=up), factors, near,
        dict(act=act, slope=slope), outs, {}, scratch,
    )


def field_back(kind, grad, weight, a, b, inputs, slot_acts, extras=()):
    rows, depth, rank = grad.shape[0], weight.depth, a.count
    low = grad.dtype == jnp.bfloat16
    names = dict(norm=("prior", "field", "gain"), conv=("field", "gain", "bias"), plain=())[kind]

    def body(r):
        r.weight.start()
        grad_ref = r.grad
        if not low:
            grad_ref = r.low
            r.low[...] = r.grad[...].astype(jnp.bfloat16)
        grads_step(grad_ref, r.b, r.z, r.u, r.dz, r.da, r.db)
        if kind == "plain":
            inputs_step(r.weight, grad_ref, r.dz, r.a, r.made)
            return
        inputs_step(r.weight, grad_ref, r.dz, r.a, r.d_inputs)
        if kind == "norm":
            norm_back_step(r.d_inputs, r.field, r.gain, r.prior, r.made)
            return
        gain = r.gain[...]

        def finish(at):
            normed, rate = norm_rows(r.field[at, :])
            shifted = normed * gain + r.bias[...]
            gate = jax.nn.sigmoid(shifted)
            into = gate + shifted * gate * (1.0 - gate)
            r.made[at, :] = norm_back(r.d_inputs[at, :] * into, gain, normed, rate)

        each_rows(rows, 128, finish)

    made = shape_of(rows, depth, jnp.bfloat16 if kind == "plain" else jnp.float32)
    outs = dict(made=made, da=shape_of(rank, depth), db=shape_of(rank, weight.width))
    scratch = dict(dz=pltpu.VMEM((rows, rank), jnp.bfloat16))
    if not low:
        scratch["low"] = pltpu.VMEM((rows, weight.width), jnp.bfloat16)
    if kind != "plain":
        scratch["d_inputs"] = pltpu.VMEM((rows, depth), jnp.float32)
    near = dict(grad=grad, u=inputs, z=slot_acts, **dict(zip(names, extras)))
    return fused(
        body, "field_back_" + kind, 22, dict(weight=weight), dict(a=a, b=b), near, {}, outs, {}, scratch
    )


def first_half_back(d_query, shares, qkv_w, a_qkv, b_qkv, attn_in, z_qkv, prior, field, gain,
                    up, down, factors, kept, layer_in, layer_gain, turn):
    rows, width = d_query.shape
    inputs, act, slope, z_up, z_down = kept
    names = ["share%d" % index for index in range(len(shares))]

    def body(r):
        r.qkv_w.start()
        r.joined[:, :width] = r.d_query[...]
        for which in range(2):
            total = sum(getattr(r, key)[which].astype(jnp.float32) for key in names)
            r.joined[:, (1 + which) * width : (2 + which) * width] = total.astype(jnp.bfloat16)
        grads_step(r.joined, r.b_qkv, r.z_qkv, r.attn_in, r.dz, r.da_qkv, r.db_qkv)

        def then():
            r.down.start()
            pltpu.make_async_copy(r.slope, r.held_slope, r.sems.at[0]).start()

        inputs_step(r.qkv_w, r.joined, r.dz, r.a_qkv, r.d_inputs, then)
        norm_back_step(r.d_inputs, r.field, r.gain, r.prior, r.d_first)
        ffn_back_steps(r, r.d_first, r.u)

        def finish(at):
            normed, rate = norm_rows(r.layer_in[at, :].astype(jnp.float32))
            return r.d_first[at, :] + norm_back(r.d_inputs[at, :], r.layer_gain[...], normed, rate)

        halves_step(r.turn, r.first, r.second, finish)
        if packed:
            three = [
                r.db_qkv[which * rank : (which + 1) * rank, which * width : (which + 1) * width]
                for which in range(3)
            ]
            model = [r.da_up[...], r.da_qkv[...], r.db_down[...], *three]
            pack_step((r.ours, r.theirs), r.core, fsdp, model, [r.da_down[...], r.db_up[...]])

    rank = factors["a_up"].count
    outs, scratch = ffn_back_parts(rows, width, up.width, rank)
    grads = dict(**outs, da_qkv=shape_of(a_qkv.count, width), db_qkv=shape_of(a_qkv.count, 3 * width))
    outs = dict(first=shape_of(rows // 2, width), second=shape_of(rows // 2, width))
    devices, fsdp = lax.axis_size(EVERYWHERE), lax.axis_size("fz") * lax.axis_size("fh")
    packed = packs_whole(devices, width, up.width)
    if packed:
        scratch.update({key: pltpu.VMEM(item.shape, item.dtype) for key, item in grads.items()})
        count = -(-8 * rank // TILE) * (width // devices) + 2 * rank
        outs["ours"] = outs["theirs"] = jax.ShapeDtypeStruct((devices // 2, count, TILE), jnp.bfloat16)
    else:
        outs.update(grads)
    scratch["joined"] = pltpu.VMEM((rows, 3 * width), jnp.bfloat16)
    scratch["dz"] = pltpu.VMEM((rows, a_qkv.count), jnp.bfloat16)
    scratch["d_first"] = pltpu.VMEM((rows, width), jnp.float32)
    near = dict(
        d_query=d_query, **dict(zip(names, shares)), attn_in=attn_in, z_qkv=z_qkv, prior=prior,
        field=field, gain=gain, u=inputs, z_up=z_up, z_down=z_down, layer_in=layer_in,
        layer_gain=layer_gain,
    )
    return fused(
        body, "first_half_back", 42, dict(qkv_w=qkv_w, down=down, up=up),
        dict(a_qkv=a_qkv, b_qkv=b_qkv, **factors), near, dict(act=act, slope=slope), outs, {}, scratch,
        turn,
    )


def slide(lanes, parts, shifted, taps_ref, shifts, rows, store):
    begin = 0
    for part in parts:
        shifted[0, begin : begin + part.shape[0], :] = part
        begin += part.shape[0]
    length = begin - 8
    for turn in range(1, 8):
        shifted[turn, 0:length, :] = shifted[0, turn : turn + length, :]
    step = 64
    for at in range(0, rows, step):
        total = None
        for tap, shift in enumerate(shifts):
            base = shift - shift % 8 + at
            term = shifted[shift % 8, base : base + step, :] * taps_ref[tap : tap + 1, lanes]
            total = term if total is None else total + term
        store(slice(at, at + step), total)


def each_tile(width, body):
    def one(index, carry):
        body(pl.ds(pl.multiple_of(index * TILE, TILE), TILE))
        return carry

    lax.fori_loop(0, width // TILE, one, 0)


def conv_body(r):
    val_ref, earlier_ref, conv_ref, act_ref = r.value, r.earlier, r.conv, r.act
    taps_ref, gain_ref, bias_ref, shifted = r.taps, r.gain, r.bias, r.shifted
    rows, width = val_ref.shape

    def one(lanes):
        parts = [earlier_ref[:, lanes].astype(jnp.float32), val_ref[:, lanes].astype(jnp.float32)]

        def store(at, total):
            conv_ref[at, lanes] = total

        shifts = [HALO - KERNEL + 1 + tap for tap in range(KERNEL)]
        slide(lanes, parts, shifted, taps_ref, shifts, rows, store)

    each_tile(width, one)

    def finish(at):
        shifted_field = norm_rows(conv_ref[at, :])[0] * gain_ref[...] + bias_ref[...]
        act_ref[at, :] = (shifted_field * jax.nn.sigmoid(shifted_field)).astype(jnp.bfloat16)

    each_rows(rows, 128, finish)


def conv_back_body(r):
    d_ref, later_ref, out_ref = r.d_conv, r.later, r.made
    taps_ref, gate_ref, slope_ref, shifted = r.taps, r.gate, r.slope, r.shifted
    rows, width = d_ref.shape

    def one(lanes):
        parts = [d_ref[:, lanes], later_ref[:, lanes].astype(jnp.float32)]
        high = slice(lanes.start + width, lanes.stop + width)

        def store(at, total):
            out_ref[at, lanes] = (total * gate_ref[at, lanes].astype(jnp.float32)).astype(jnp.bfloat16)
            out_ref[at, high] = (total * slope_ref[at, lanes].astype(jnp.float32)).astype(jnp.bfloat16)

        slide(lanes, parts, shifted.at[lanes.start // TILE % 2], taps_ref, [KERNEL - 1 - tap for tap in range(KERNEL)], rows, store)

    for begin in range(0, width, TILE):
        one(slice(begin, begin + TILE))


def conv_forward(value, earlier, taps, gain, bias):
    rows, width = value.shape
    near = dict(value=value, earlier=earlier, taps=taps, gain=gain, bias=bias)
    outs = dict(conv=shape_of(rows, width, jnp.float32), act=shape_of(rows, width))
    scratch = dict(shifted=pltpu.VMEM((8, rows + HALO, TILE), jnp.float32))
    return fused(conv_body, "conv_forward", 16, {}, {}, near, {}, outs, {}, scratch)


def conv_backward(d_conv, later, taps, gate, slope):
    rows, width = d_conv.shape
    near = dict(d_conv=d_conv, later=later, taps=taps, gate=gate, slope=slope)
    scratch = dict(shifted=pltpu.VMEM((2, 8, rows + HALO, TILE), jnp.float32))
    outs = dict(made=shape_of(rows, 2 * width))
    return fused(conv_back_body, "conv_backward", 16, {}, {}, near, {}, outs, {}, scratch)[0]


def gather_taps(weight):
    def body(r):
        r.weight.start()
        r.weight.wait()
        r.taps[...] = jnp.transpose(r.weight.store[...].astype(jnp.float32))[:HALO, :]

    outs = dict(taps=shape_of(HALO, weight.depth, jnp.float32))
    return fused(body, "gather_taps", 8, dict(weight=weight), {}, {}, {}, outs)[0]


class Layout:
    def __init__(self, together, fsdp):
        self.fsdp = fsdp
        self.inner = fsdp // together
        self.group = 2 * self.inner

    def place(self, core, f):
        return core * self.fsdp + f

    def round_route(self, turn):
        route = []
        for core in range(2):
            for f in range(self.fsdp):
                clip = (f % 2 + turn) % 2
                spot = f // 2
                target = self.place(spot % 2, (2 * core + clip) * self.inner + spot // 2)
                route.append((self.place(core, f), target))
        return route

    def gather_rows(self, blocks):
        parity = (lax.axis_index("fz") * self.inner + lax.axis_index("fh")) % 2
        clip = lax.axis_index("fz") % 2
        got = []
        for turn in range(2):
            sent = lax.dynamic_index_in_dim(blocks, (parity + turn) % 2, 0, keepdims=False)
            got.append(lax.ppermute(sent, ("core", "fz", "fh"), self.round_route(turn)))
        swap = clip == 1
        return jnp.concatenate(
            [jnp.where(swap, got[1], got[0]), jnp.where(swap, got[0], got[1])], axis=0
        )

    def scatter_rows(self, sent):
        parity = (lax.axis_index("fz") * self.inner + lax.axis_index("fh")) % 2
        got = []
        for turn in range(2):
            route = [(target, source) for source, target in self.round_route(turn)]
            got.append(lax.ppermute(sent[turn], ("core", "fz", "fh"), route))
        swap = parity == 1
        return jnp.stack([jnp.where(swap, got[1], got[0]), jnp.where(swap, got[0], got[1])])

    def spot_index(self, spot):
        return (spot % 2) * self.inner + spot // 2

    def from_spot(self, block, distance, cyclic):
        route = []
        for spot in range(self.group):
            source = spot + distance
            if cyclic:
                source %= self.group
            if 0 <= source < self.group:
                route.append((self.spot_index(source), self.spot_index(spot)))
        return lax.ppermute(block, ("core", "fh"), route)


def pack_adapters(ids, a_model, a_hidden, b_model, b_hidden):
    slots = a_model.shape[2]
    half = RANK // 2
    core = lax.axis_index("core")
    ranks = core * half + jnp.arange(half, dtype=jnp.int32)
    wanted = ids[:, None] * RANK + ranks[None, :]
    picker = (wanted[:, :, None] == jnp.arange(slots, dtype=jnp.int32)).astype(jnp.bfloat16)
    down = lambda a: jnp.einsum("jrs,pks->jprk", picker, a, preferred_element_type=jnp.float32)
    up = lambda b: jnp.einsum("jrs,psn->jprn", picker, b, preferred_element_type=jnp.float32)
    cut = a_hidden.shape[1] // a_model.shape[1]
    span = a_model.shape[1]

    def short(pack):
        rows = pack.reshape(pack.shape[0], pack.shape[1], half, cut, span)
        return jnp.swapaxes(rows, 2, 3).reshape(pack.shape[0], pack.shape[1] * cut, half, span)

    return jnp.concatenate(
        [down(a_model), up(b_model), short(down(a_hidden)), short(up(b_hidden))], axis=1
    ).astype(jnp.bfloat16)


def join_adapters_kernel(models, cut, plan, spots_ref, mine_ref, theirs_ref, *rest):
    wanted = len(plan)
    outs, full, held, sems = rest[:wanted], rest[wanted], rest[wanted + 1 : -1], rest[-1]
    count, groups, half, span = mine_ref.shape
    for step in range(count):
        at = pl.ds(pl.multiple_of(spots_ref[step] * span, span), span)
        for ref, core in ((mine_ref, spots_ref[count]), (theirs_ref, 1 - spots_ref[count])):
            rows = pl.ds(pl.multiple_of(core * half, half), half)
            full[:, rows, at] = ref[step].astype(jnp.float32)
    copies = []
    for which, (out, kept, parts) in enumerate(zip(outs, held, plan)):
        kept[...] = jnp.zeros_like(kept)
        for group, row, column in parts:
            if group < models:
                kept[row : row + RANK, column : column + count * span] = full[group].astype(kept.dtype)
                continue
            for f in range(count):
                begin = column + f * cut * span
                kept[row : row + RANK, begin : begin + span] = full[
                    group, :, f * span : (f + 1) * span
                ].astype(kept.dtype)
        copies.append(pltpu.make_async_copy(kept, out, sems.at[which]))
        copies[-1].start()
    for copy in copies:
        copy.wait()


def move_adapters(layout, pack, cut, shapes, plan, models):
    core = lax.axis_index("core")
    count = layout.fsdp
    here = lax.axis_index("fz") * layout.inner + lax.axis_index("fh")
    pieces = []
    for step in range(count):
        target = (here + step) % count
        piece = lax.dynamic_index_in_dim(pack, target // layout.inner, 0, keepdims=False)
        if step:
            route = [(f, (f + step) % count) for f in range(count)]
            piece = lax.ppermute(piece, ("fz", "fh"), route)
        pieces.append(piece)
    mine = jnp.stack(pieces)
    theirs = lax.ppermute(mine, "core", [(0, 1), (1, 0)])
    spots = jnp.stack([(here - step) % count for step in range(count)] + [core]).astype(jnp.int32)
    _, groups, half, span = mine.shape
    return pl.pallas_call(
        functools.partial(join_adapters_kernel, models, cut, plan),
        in_specs=[SCALARS, VMEM_SPEC, VMEM_SPEC],
        out_specs=[HBM] * len(shapes),
        out_shape=[shape_of(*shape) for shape in shapes],
        scratch_shapes=[pltpu.VMEM((groups, 2 * half, count * span), jnp.float32)]
        + [pltpu.VMEM(shape, jnp.bfloat16) for shape in shapes]
        + [pltpu.SemaphoreType.DMA((len(shapes),))],
        compiler_params=pltpu.CompilerParams(vmem_limit_bytes=16 * 1024 * 1024),
        name="join_adapters",
    )(spots, mine, theirs)


def factor_plan(models, hiddens, cut, span):
    hidden = [(models + which * cut + q, which * RANK, q * span) for which in range(hiddens) for q in range(cut)]
    return [[(group, group * RANK, 0) for group in range(models)], hidden]


def first_adapters(layout, pack, cut, width, hidden):
    shapes = [(2 * RANK, width), (2 * RANK, hidden)]
    model, inner = move_adapters(layout, pack, cut, shapes, factor_plan(2, 2, cut, pack.shape[3]), 2)
    return model, inner


def other_adapters(layout, pack, cut, width, hidden):
    shapes = [(15 * RANK, width), (2 * RANK, hidden), (3 * RANK, 3 * width), (RANK, 2 * width)]
    plan = factor_plan(15, 2, cut, pack.shape[3]) + [
        [(7 + which, which * RANK, which * width) for which in range(3)],
        [(13, 0, 0), (14, 0, width)],
    ]
    return move_adapters(layout, pack, cut, shapes, plan, 15)


def pack_step(outs, core_ref, fsdp, model, hidden):
    places, _, lanes = outs[0].shape
    model = jnp.concatenate([part.astype(jnp.float32) for part in model], axis=0)
    tiles = -(-model.shape[0] // TILE)
    if model.shape[0] % TILE:
        rest = jnp.zeros((tiles * TILE - model.shape[0], model.shape[1]), jnp.float32)
        model = jnp.concatenate([model, rest], axis=0)
    turned = [jnp.transpose(model[k * TILE : (k + 1) * TILE]).astype(jnp.bfloat16) for k in range(tiles)]
    share = model.shape[1] // (2 * places)

    def write(here):
        for device in range(2 * places):
            chip, other = divmod(device, 2 * fsdp)
            core, f = divmod(other, fsdp)
            out, place, row = outs[0 if core == here else 1], chip * fsdp + f, 0
            for part in turned:
                out[place, row : row + share, :] = part[device * share : (device + 1) * share]
                row += share
            for part in hidden:
                out[place, row : row + RANK, :] = part[:, device * lanes : (device + 1) * lanes]
                row += RANK

    for here in range(2):
        pl.when(core_ref[0] == here)(functools.partial(write, here))


def packs_whole(devices, width, hidden):
    return hidden // devices == TILE and width // devices % RANK == 0


def pack_grads_kernel(models, count, fsdp, *refs):
    core_ref, refs = refs[0], refs[1:]
    outs, sems, held = refs[count : count + 2], refs[count + 2], refs[count + 3 :]
    copies = [pltpu.make_async_copy(refs[i], held[i], sems.at[i]) for i in range(count)]
    for copy in copies:
        copy.start()
    for copy in copies:
        copy.wait()
    pack_step(outs, core_ref, fsdp, [ref[...] for ref in held[:models]], [ref[...] for ref in held[models:]])


def pack_grads(model, hidden):
    core = lax.axis_index("core").astype(jnp.int32).reshape(1)
    devices, fsdp = lax.axis_size(EVERYWHERE), lax.axis_size("fz") * lax.axis_size("fh")
    width = model[0].shape[1]
    share, hidden_share = width // devices, hidden[0].shape[1] // devices
    groups = sum(part.shape[0] for part in model)
    tiles = -(-groups // TILE)
    if packs_whole(devices, width, hidden[0].shape[1]):
        rows = tiles * share + RANK * len(hidden)
        return pl.pallas_call(
            functools.partial(pack_grads_kernel, len(model), len(model) + len(hidden), fsdp),
            in_specs=[SCALARS] + [HBM] * (len(model) + len(hidden)),
            out_specs=[VMEM_SPEC] * 2,
            out_shape=[jax.ShapeDtypeStruct((devices // 2, rows, TILE), jnp.bfloat16)] * 2,
            scratch_shapes=[pltpu.SemaphoreType.DMA((len(model) + len(hidden),))]
            + [pltpu.VMEM(item.shape, item.dtype) for item in (*model, *hidden)],
            compiler_params=pltpu.CompilerParams(vmem_limit_bytes=PACK_ROOM),
            name="pack_grads",
        )(core, *model, *hidden)
    rest = jnp.zeros((tiles * TILE - groups, width), jnp.bfloat16)
    turned = jnp.concatenate([*model, rest]).T
    split = jnp.concatenate(hidden).reshape(-1, devices, hidden_share)
    parts = [turned[:, k * TILE : (k + 1) * TILE].reshape(devices, share, TILE) for k in range(tiles)]
    parts.append(jnp.transpose(split, (1, 0, 2)).reshape(devices, -1, TILE))
    part = jnp.concatenate(parts, axis=1).reshape(devices // (2 * fsdp), 2, fsdp, -1, TILE)
    part = jnp.swapaxes(part, 0, 1).reshape(2, devices // 2, -1, TILE)
    return tuple(jnp.where(core[0] == 0, part, part[::-1]))


def send_grads(model, hidden):
    groups = sum(item.shape[0] for item in model)
    return send_packed(pack_grads(model, hidden), groups, len(hidden), model[0].shape[1], hidden[0].shape[1])


def send_packed(part, groups, hiddens, width, features):
    ours, theirs = part
    came = lax.ppermute(theirs, "core", [(0, 1), (1, 0)])
    both = (ours.astype(jnp.float32) + came.astype(jnp.float32)).astype(jnp.bfloat16)
    got = lax.all_to_all(both, ("chip", "fz", "fh"), 0, 0, tiled=True)
    devices = lax.axis_size(EVERYWHERE)
    share, hidden_share = width // devices, features // devices
    begin = -(-groups // TILE) * share
    if hidden_share == TILE:
        return got, got, begin
    return got, got[:, begin:].reshape(-1, RANK * hiddens, hidden_share), 0


def place_grads_kernel(batches, ids_ref, *refs):
    sent, outs = refs[: 2 * len(batches)], refs[2 * len(batches) :]
    for out in outs:
        out[...] = jnp.zeros_like(out)
    share = outs[0].shape[1]
    slot = lax.broadcasted_iota(jnp.int32, (share, TILE), 1) // RANK
    in_tile = TILE // RANK

    def one(sender, carry):
        owner = ids_ref[sender]
        at = pl.ds(pl.multiple_of(owner * RANK, RANK), RANK)
        for which, (model_plan, hidden_plan, begin) in enumerate(batches):
            model_ref, hidden_ref = sent[2 * which : 2 * which + 2]
            for group, (out, index) in enumerate(model_plan):
                tile, local_group = divmod(group, in_tile)
                block = model_ref[sender, tile * share : (tile + 1) * share, :].astype(jnp.float32)
                turn = lax.rem(owner - local_group + in_tile, in_tile) * RANK
                outs[out][index] += jnp.where(slot == owner, pltpu.roll(block, turn, 1), 0.0)
            for group, (out, index) in enumerate(hidden_plan):
                rows = slice(begin + group * RANK, begin + (group + 1) * RANK)
                outs[out][index, at, :] += hidden_ref[sender, rows, :].astype(jnp.float32)
        return carry

    lax.fori_loop(0, sent[0].shape[0], one, 0, unroll=4)


def place_grads(ids, batches, shapes):
    arrays, plans = [], []
    for (model, hidden, begin), model_plan, hidden_plan in batches:
        arrays += [model, hidden]
        plans.append((model_plan, hidden_plan, begin))
    return pl.pallas_call(
        functools.partial(place_grads_kernel, plans),
        in_specs=[SCALARS] + [VMEM_SPEC] * len(arrays),
        out_specs=[VMEM_SPEC] * len(shapes),
        out_shape=[jax.ShapeDtypeStruct(shape, jnp.float32) for shape in shapes],
        compiler_params=pltpu.CompilerParams(vmem_limit_bytes=16 * 1024 * 1024),
        name="place_grads",
    )(ids, *arrays)


def local(
    frames,
    cotangent,
    adapter_ids,
    norm_gains,
    norm_biases,
    rel_table,
    w_up,
    w_down,
    w_qkv,
    w_out,
    w_pw1,
    w_depth,
    w_pw2,
    ad_a_model,
    ad_a_hidden,
    ad_b_model,
    ad_b_hidden,
):
    group_clips, frame_span, width = frames.shape
    together = 2 * group_clips
    layout = Layout(together, lax.axis_size("fz") * lax.axis_size("fh"))
    rows = 2 * frame_span
    slots = ad_a_model.shape[2]
    spot = lax.axis_index("fh") * 2 + lax.axis_index("core")
    own = (spot * (rows // TILE)).astype(jnp.int32).reshape(1)
    other_ids = lax.ppermute(adapter_ids, "core", [(0, 1), (1, 0)])
    at_zero = lax.axis_index("core") == 0
    near_ids = jnp.concatenate(
        [jnp.where(at_zero, adapter_ids, other_ids), jnp.where(at_zero, other_ids, adapter_ids)]
    )
    factors = (ad_a_model, ad_a_hidden, ad_b_model, ad_b_hidden)
    cut = ad_a_hidden.shape[1] // ad_a_model.shape[1]
    first_pack = pack_adapters(near_ids, *[factor[:1] for factor in factors])
    other_pack = pack_adapters(near_ids, *[factor[1:] for factor in factors])
    gather = Gather()
    taps = jnp.pad(w_depth.T, ((0, 0), (0, width - KERNEL)))
    shards = [
        w_up[0],
        w_down[0],
        jnp.concatenate([w_qkv, w_out], axis=1),
        jnp.concatenate([w_pw1, w_pw2, taps], axis=1),
        w_up[1],
        w_down[1],
    ]
    used = [shard.shape[1] for shard in shards]
    used[3] = 3 * width + TILE
    turns = gather.stages(shards, used)
    next(turns)

    def weight_of(units, which, begin=0, columns=None):
        return Weight(gather.places, units[which], begin, columns or used[which])

    gains = [norm_gains[index : index + 1] for index in range(6)]
    biases = [norm_biases[index : index + 1] for index in range(6)]

    turns.send([first_pack, other_pack])
    first_pack, other_pack = gather.held
    turns.send([frames, first_pack, other_pack, *rel_tables(rel_table, rows * layout.group)])
    frames, first_pack, other_pack, *tables = gather.held
    layer_in = layout.gather_rows(frames)
    turns.send([])
    hidden_width = w_up.shape[2]
    first_four = first_adapters(layout, first_pack, cut, width, hidden_width)
    units = turns.send([layer_in, *first_four])
    layer_in, *first_four = gather.held
    field = layer_in.astype(jnp.float32)
    first_in = (norm_rows(field)[0] * gains[0] + biases[0]).astype(jnp.bfloat16)
    a_up0, b_down0 = [Rows(first_four[0], row * RANK, RANK) for row in range(2)]
    a_down0, b_up0 = [Rows(first_four[1], row * RANK, RANK) for row in range(2)]
    up0_w = weight_of(units, 0)
    z_up0, act_one, slope_one = project_wide("silu", first_in, up0_w, a_up0, b_up0)
    units = turns.send([act_one, slope_one, other_pack])
    act_one, slope_one, other_pack = gather.held
    others = other_adapters(layout, other_pack, cut, width, hidden_width)
    units = turns.send([])
    down0_w = weight_of(units, 1)
    z_down0, after_ffn, attn_in = project_narrow(
        act_one, down0_w, a_down0, b_down0, layer_in, gains[1], biases[1], 0.5
    )
    units = turns.send([after_ffn, attn_in, *others])
    after_ffn, attn_in, *others = gather.held
    model, inner, qkv_up, glu_up = others
    qkv_down = Rows(model, 0, 3 * RANK)
    qkv_up, glu_up = Rows(qkv_up, 0, 3 * RANK), Rows(glu_up, 0, RANK)
    a_out, a_pw1, a_pw2, a_up1, b_out, b_pw2, b_down1 = [
        Rows(model, row * RANK, RANK) for row in (3, 4, 5, 6, 10, 11, 12)
    ]
    a_down1, b_up1 = [Rows(inner, row * RANK, RANK) for row in range(2)]
    units = turns.send([])
    qkv_w, out_w = weight_of(units, 2, 0, 3 * width), weight_of(units, 2, 3 * width, width)
    z_qkv, query, own_kv = project_wide("plain", attn_in, qkv_w, qkv_down, qkv_up)
    units = turns.send([query, own_kv])
    query, own_kv = gather.held
    units = turns.send([])
    pw1_w, pw2_w = weight_of(units, 3, 0, 2 * width), weight_of(units, 3, 2 * width, width)
    taps = gather_taps(weight_of(units, 3, 3 * width, TILE))
    kv = [own_kv] + [layout.from_spot(own_kv, step, True) for step in range(1, layout.group)]
    mixed, rate, expo = attention_forward(own, query, kv, tables[0])
    turns.send([mixed, rate])
    mixed, rate = gather.held
    units = turns.send([])
    up1_w, down1_w = weight_of(units, 4), weight_of(units, 5)
    mixed, cotangent = lax.optimization_barrier((mixed, cotangent))
    d_out = layout.gather_rows(cotangent)
    z_out, after_attn, conv_in = project_narrow(
        mixed, out_w, a_out, b_out, after_ffn, gains[2], biases[2], 1.0
    )
    z_pw1, gated, gate, gate_slope = project_wide("glu", conv_in, pw1_w, a_pw1, glu_up)
    earlier = layout.from_spot(gated[rows - HALO :], -1, False)
    conv_out, conv_act = conv_forward(gated, earlier, taps, gains[3], biases[3])
    z_pw2, after_conv, second_in = project_narrow(
        conv_act, pw2_w, a_pw2, b_pw2, after_attn, gains[4], biases[4], 1.0
    )
    factors_two = dict(a_up=a_up1, b_up=b_up1, a_down=a_down1, b_down=b_down1)
    turn = [(lax.axis_index("fz") % 2).astype(jnp.int32).reshape(1)]
    z_up1, z_down1, d_fourth, *result, act_two, slope_two = feed_forward_last(
        second_in, up1_w, down1_w, factors_two, after_conv, gains[5], biases[5], d_out, turn
    )
    layer_out = layout.scatter_rows(result)

    d_third, da_up1, db_up1, da_down1, db_down1 = feed_forward_back(
        d_fourth, up1_w, down1_w, factors_two, (second_in, act_two, slope_two, z_up1, z_down1),
        after_conv, gains[4],
    )
    d_conv, da_pw2, db_pw2 = field_back(
        "conv", d_third, pw2_w, a_pw2, b_pw2, conv_act, z_pw2,
        (conv_out, gains[3], biases[3]),
    )
    d_conv, layer_out = lax.optimization_barrier((d_conv, layer_out))
    later = layout.from_spot(d_conv[:HALO].astype(jnp.bfloat16), 1, False)
    d_joined = conv_backward(d_conv, later, taps, gate, gate_slope)
    d_second, da_pw1, db_pw1 = field_back(
        "norm", d_joined, pw1_w, a_pw1, glu_up, conv_in, z_pw1, (d_third, after_attn, gains[2])
    )
    d_mixed, da_out, db_out = field_back(
        "plain", d_second, out_w, a_out, b_out, mixed, z_out, ()
    )
    label = jnp.full((RANK, width), near_ids[lax.axis_index("fz")]).astype(jnp.bfloat16)
    early = send_grads(
        [da_out, da_pw1, da_pw2, da_up1, db_out, db_pw2, db_down1]
        + [db_pw1[:, :width], db_pw1[:, width:], label],
        [da_down1, db_up1],
    )
    d_query, d_own, d_far = attention_backward(own, query, kv, d_mixed, rate, expo, tables)
    shares = [d_own]
    for step in range(1, layout.group):
        shares.append(layout.from_spot(d_far[:, (step - 1) * rows : step * rows], -step, True))
    first_half, second_half_rows, *grads = first_half_back(
        d_query, shares, qkv_w, qkv_down, qkv_up, attn_in, z_qkv, d_second, after_ffn, gains[1],
        up0_w, down0_w, dict(a_up=a_up0, b_up=b_up0, a_down=a_down0, b_down=b_down0),
        (first_in, act_one, slope_one, z_up0, z_down0), layer_in, gains[0],
        [*turn, lax.axis_index("core").astype(jnp.int32).reshape(1)],
    )
    grad_frames = layout.scatter_rows([first_half, second_half_rows])
    if len(grads) == 2:
        late = send_packed(grads, 8 * RANK, 2, width, hidden_width)
    else:
        da_up0, db_up0, da_down0, db_down0, da_qkv, db_qkv = grads
        db_three = [
            db_qkv[index * RANK : (index + 1) * RANK, index * width : (index + 1) * width]
            for index in range(3)
        ]
        late = send_grads([da_up0, da_qkv, db_down0, *db_three], [da_down0, db_up0])
    devices = lax.axis_size(EVERYWHERE)
    share, hidden_share = width // devices, hidden_width // devices
    ids = (early[0][:, share, RANK] * jnp.bfloat16(0.5)).astype(jnp.int32)
    early_plan = [(0, index) for index in range(4, 8)] + [(1, index) for index in range(4, 9)]
    late_plan = [(0, index) for index in range(4)] + [(1, index) for index in range(4)]
    grad_a_model, grad_b_model, grad_a_hidden, grad_b_hidden = place_grads(
        ids,
        [(early, early_plan, [(2, 1), (3, 1)]), (late, late_plan, [(2, 0), (3, 0)])],
        [(8, share, slots), (9, share, slots), (2, slots, hidden_share), (2, slots, hidden_share)],
    )
    grad_b_model = jnp.swapaxes(grad_b_model, 1, 2)
    grad_a_hidden = jnp.swapaxes(grad_a_hidden, 1, 2)
    return (layer_out, grad_frames, grad_a_model, grad_a_hidden, grad_b_model, grad_b_hidden)


def solution(mesh):
    every = ("chip", "core", "fz", "fh")
    clips, spread = ("chip", "core"), ("fz", "fh")
    in_specs = (
        P(clips, spread, None),
        P(clips, spread, None),
        P(clips),
        P(),
        P(),
        P(),
        P(None, every, None),
        P(None, every, None),
        P(every, None),
        P(every, None),
        P(every, None),
        P(None, every),
        P(every, None),
        P(None, spread, None),
        P(None, spread, None),
        P(None, None, spread),
        P(None, None, spread),
    )
    out_specs = (
        P(clips, spread, None),
        P(clips, spread, None),
        P(None, every, None),
        P(None, every, None),
        P(None, None, every),
        P(None, None, every),
    )

    def run(frames, *rest):
        dp, fsdp = mesh.shape["dp"], mesh.shape["fsdp"]
        together = 2 * frames.shape[0] // dp
        cut = Mesh(
            mesh.devices.reshape(dp // 2, 2, together, fsdp // together), EVERYWHERE
        )
        return jax.shard_map(
            local, mesh=cut, in_specs=in_specs, out_specs=out_specs, check_vma=False
        )(frames, *rest)

    return run
```
